32 devices in a mesh: dp: 8 (over z, y), group: 4 (over x, core).
Axes of the slice: x: 2, y: 2, z: 4, core: 2. Of those that a mesh axis runs over, the one named last changes fastest.
Arguments:
- patches: bfloat16 [192, 144, 640], P(('dp', 'group')), may hold values from -6 to 6
- vis_index: int32 [192, 3, 48], P(('dp', 'group')), may hold values from 0 to 143, as said below
- vis_count: int32 [192, 3], P(('dp', 'group')), may hold values from 24 to 48, as said below
- w_stem: bfloat16 [640, 1024], replicated, may hold values from -0.375 to 0.375
- ln_gain: float32 [1024], replicated, may hold values from 0.5 to 1.5
- w_qkv: bfloat16 [1024, 3, 1024], P('dp', None, 'group'), may hold values from -7.5 to 7.5
- w_out: bfloat16 [1024, 1024], P('group', 'dp'), may hold values from -0.1875 to 0.1875
- out_grad: bfloat16 [192, 3, 48, 1024], P(('dp', 'group')), may hold values from -6 to 6
Outputs:
- output: bfloat16 [192, 3, 48, 1024], P(('dp', 'group'))
- grad_w_stem: float32 [640, 1024], replicated
- grad_w_qkv: float32 [1024, 3, 1024], P('dp', None, 'group')
- grad_w_out: float32 [1024, 1024], P('group', 'dp')
The draws below stay inside these ranges and needn't reach their ends.
Inputs may be any that keep to these rules, and one draw needn't show every extreme that they name: `vis_index`: for each scene and band group the 48 entries are distinct patch numbers; only the first vis_count entries are visible tokens, the rest are padding. `vis_count`: equals 48 for at least one scene and band group of every draw.
All inputs are finite; a program needn't handle non-finite values.
Results may differ from the reference program's by a relative error of at most 0.0025.
The reference program's roundings to bfloat16 on the way count: a program that leaves them out, or rounds other values in their place, can miss the bound.
Values may be sent and summed in bfloat16 or wider, within the bound.
No kernel may reach another device: no remote copies, remote signals or barrier semaphores. Data moves between devices by JAX's collectives and lax.ppermute only.
A program may use at most 192 MiB of HBM per device.

```python
import jax
import jax.numpy as jnp
from jax import lax

D = 1024
HD = 64
GROUPS = 3
CAP = 48
SC_DEV = 6
GRID = 12
PATCHES = 144
PIX = 64
IN = 640
SCENES = 192


def draw_vis_index(key, part):
    split_keys = jax.random.split(jax.random.fold_in(key, 101), SCENES * GROUPS)
    orders = jax.vmap(lambda one_key: jax.random.permutation(one_key, PATCHES)[:CAP])(split_keys)
    return orders.reshape(SCENES, GROUPS, CAP).astype(jnp.int32)


def draw_vis_count(key, part):
    counts = jax.random.randint(jax.random.fold_in(key, 202), (SCENES, GROUPS), CAP // 2, CAP + 1)
    chosen = jax.random.randint(jax.random.fold_in(key, 303), (), 0, SCENES * GROUPS)
    position = jnp.arange(SCENES * GROUPS, dtype=jnp.int32).reshape(SCENES, GROUPS)
    return jnp.where(position == chosen, CAP, counts).astype(jnp.int32)


def draw_w_qkv(key, part):
    base = jax.random.truncated_normal(jax.random.fold_in(key, 404), -6.0, 6.0, (D, 3, D), jnp.float32) * D ** (-0.5)
    return base.astype(jnp.bfloat16)


def levels(rng, dims, shards, least, high):
    loudness = 1.0
    for dim, shards_of in shards:
        steps = jax.random.uniform(jax.random.fold_in(jax.random.fold_in(rng, 6), dim), (shards_of,), jnp.float32, least / len(shards), high / len(shards))
        loudness = loudness * jnp.repeat(jnp.exp(steps), dims[dim] // shards_of).reshape((-1,) + (1,) * (len(dims) - 1 - dim))
    return loudness


def normal_values(rng, dims, scale, reach, shards=(), held_as=jnp.bfloat16):
    array = jax.random.normal(rng, dims, jnp.float32) * scale
    if len(shards) > 0:
        array = levels(rng, dims, shards, -0.22, 0.18) * array
    return jnp.clip(array, min=-reach, max=reach).astype(held_as)


def setup_inputs(seed: int = 0) -> dict:
    key_of = jax.random.split(jax.random.key(seed), 9)
    patches = normal_values(key_of[0], (SCENES, PATCHES, IN), 1.0, 6.0, ((0, 32),))
    vis_index = draw_vis_index(jax.random.fold_in(key_of[8], 71), 0)
    vis_count = draw_vis_count(jax.random.fold_in(key_of[8], 71), 0)
    w_stem = normal_values(key_of[3], (IN, D), (4 * PIX) ** -0.5, 0.375)
    ln_gain = jnp.clip(1.0 + 0.1 * jax.random.normal(key_of[4], (D,), jnp.float32), 0.5, 1.5)
    w_qkv = draw_w_qkv(jax.random.fold_in(key_of[8], 71), 0)
    w_out = normal_values(key_of[6], (D, D), D ** -0.5, 0.1875, ((0, 4), (1, 8)))
    out_grad = normal_values(key_of[7], (SCENES, GROUPS, CAP, D), 1.0, 6.0, ((0, 32),))
    return {"patches": patches, "vis_index": vis_index, "vis_count": vis_count, "w_stem": w_stem, "ln_gain": ln_gain, "w_qkv": w_qkv, "w_out": w_out, "out_grad": out_grad}


GROUP_BANDS = ((0, 4), (4, 8), (8, 10))
NORM_EPS = 1e-06

def encodings(patch_ids, group_id):
    quarter = D // 4
    half_width = D // 2
    row_freq = jnp.power(10000.0, -jnp.arange(quarter, dtype=jnp.float32) / quarter)
    group_freq = jnp.power(10000.0, -jnp.arange(half_width, dtype=jnp.float32) / half_width)
    row_at = (patch_ids // GRID).astype(jnp.float32)[..., None] * row_freq
    col_at = (patch_ids % GRID).astype(jnp.float32)[..., None] * row_freq
    spatial = jnp.concatenate([jnp.sin(row_at), jnp.cos(row_at), jnp.sin(col_at), jnp.cos(col_at)], axis=-1)
    group_at = float(group_id) * group_freq
    return spatial + jnp.concatenate([jnp.sin(group_at), jnp.cos(group_at)])

def embed_tokens(patches, vis_index, w_stem):
    scene_count = patches.shape[0]
    flat_ids = vis_index.reshape(scene_count, GROUPS * CAP).astype(jnp.int32)
    picked = jnp.take_along_axis(patches, flat_ids[:, :, None], axis=1)
    pieces = []
    for group_id, (band_start, band_end) in enumerate(GROUP_BANDS):
        columns = picked[:, group_id * CAP:(group_id + 1) * CAP, band_start * PIX:band_end * PIX]
        weights = w_stem[band_start * PIX:band_end * PIX]
        summed = jnp.einsum('str,rd->std', columns.astype(jnp.float32), weights.astype(jnp.float32))
        pieces.append((summed + encodings(vis_index[:, group_id], group_id)).astype(jnp.bfloat16))
    return (jnp.stack(pieces, axis=1), picked)

def layer_norm(embedded, ln_gain):
    values = embedded.astype(jnp.float32)
    centre = lax.optimization_barrier(jnp.mean(values, axis=-1, keepdims=True))
    spread = lax.optimization_barrier(jnp.mean(jnp.square(values - centre), axis=-1, keepdims=True))
    inv_std = lax.rsqrt(spread + NORM_EPS)
    centred = (values - centre) * inv_std
    return ((centred * ln_gain).astype(jnp.bfloat16), centred, inv_std)

def norm_back(grad_normed, centred, inv_std, ln_gain):
    scaled = grad_normed * ln_gain
    first_mean = lax.optimization_barrier(jnp.mean(scaled, axis=-1, keepdims=True))
    second_mean = lax.optimization_barrier(jnp.mean(scaled * centred, axis=-1, keepdims=True))
    return inv_std * (scaled - first_mean - centred * second_mean)

def attend_forward(normed, key_flags, w_qkv):
    scene_count, token_count, _ = normed.shape
    width = w_qkv.shape[2]
    head_count = width // HD
    qkv = jnp.einsum('ntd,dcw->ntcw', normed.astype(jnp.float32), w_qkv.astype(jnp.float32)).astype(jnp.bfloat16)
    query_rows = qkv[:, :, 0].reshape(scene_count, token_count, head_count, HD).astype(jnp.float32)
    key_rows = qkv[:, :, 1].reshape(scene_count, token_count, head_count, HD).astype(jnp.float32)
    value_rows = qkv[:, :, 2].reshape(scene_count, token_count, head_count, HD).astype(jnp.float32)
    scores = jnp.einsum('nqhe,nkhe->nhqk', query_rows, key_rows) * HD ** (-0.5)
    scores = jnp.where(key_flags[:, None, None, :], scores, -1e+30)
    row_top = lax.optimization_barrier(jnp.max(scores, axis=-1, keepdims=True))
    lifted = jnp.exp(scores - row_top)
    attn_probs = lifted / lax.optimization_barrier(jnp.sum(lifted, axis=-1, keepdims=True))
    probs_half = attn_probs.astype(jnp.bfloat16)
    context = jnp.einsum('nhqk,nkhe->nqhe', probs_half.astype(jnp.float32), value_rows)
    context = context.astype(jnp.bfloat16).reshape(scene_count, token_count, width)
    return (qkv, attn_probs, probs_half, context)

def attend_backward(grad_rows, normed, w_qkv, w_out, qkv, attn_probs, probs_half, context):
    scene_count, token_count, _ = normed.shape
    width = w_qkv.shape[2]
    head_count = width // HD
    grad_out_w = jnp.einsum('ntw,ntd->wd', context.astype(jnp.float32), grad_rows.astype(jnp.float32))
    grad_context = jnp.einsum('ntd,wd->ntw', grad_rows.astype(jnp.float32), w_out.astype(jnp.float32))
    grad_context = grad_context.astype(jnp.bfloat16).reshape(scene_count, token_count, head_count, HD).astype(jnp.float32)
    query_rows = qkv[:, :, 0].reshape(scene_count, token_count, head_count, HD).astype(jnp.float32)
    key_rows = qkv[:, :, 1].reshape(scene_count, token_count, head_count, HD).astype(jnp.float32)
    value_rows = qkv[:, :, 2].reshape(scene_count, token_count, head_count, HD).astype(jnp.float32)
    grad_probs = jnp.einsum('nqhe,nkhe->nhqk', grad_context, value_rows)
    grad_value = jnp.einsum('nhqk,nqhe->nkhe', probs_half.astype(jnp.float32), grad_context).astype(jnp.bfloat16)
    inner = lax.optimization_barrier(jnp.sum(attn_probs * grad_probs, axis=-1, keepdims=True))
    grad_score = (attn_probs * (grad_probs - inner) * HD ** (-0.5)).astype(jnp.bfloat16).astype(jnp.float32)
    grad_query = jnp.einsum('nhqk,nkhe->nqhe', grad_score, key_rows).astype(jnp.bfloat16)
    grad_key = jnp.einsum('nhqk,nqhe->nkhe', grad_score, query_rows).astype(jnp.bfloat16)
    grad_qkv = jnp.stack([grad_query.reshape(scene_count, token_count, width), grad_key.reshape(scene_count, token_count, width), grad_value.reshape(scene_count, token_count, width)], axis=2)
    grad_qkv_w = jnp.einsum('ntd,ntcw->dcw', normed.astype(jnp.float32), grad_qkv.astype(jnp.float32))
    return (grad_qkv_w, grad_out_w, grad_qkv)

def stem_grads(picked, grad_in):
    pieces = []
    for group_id, (band_start, band_end) in enumerate(GROUP_BANDS):
        columns = picked[:, group_id * CAP:(group_id + 1) * CAP, band_start * PIX:band_end * PIX]
        pieces.append(jnp.einsum('str,std->rd', columns.astype(jnp.float32), grad_in[:, group_id].astype(jnp.float32)))
    return jnp.concatenate(pieces, axis=0)

def reference(patches, vis_index, vis_count, w_stem, ln_gain, w_qkv, w_out, out_grad):
    block_count = SCENES // SC_DEV
    token_count = GROUPS * CAP

    def one_block(carry, block):
        patch_blk, index_blk, count_blk, grad_blk = block
        stem_acc, qkv_acc, out_acc = carry
        embedded, picked = embed_tokens(patch_blk, index_blk, w_stem)
        live_slots = jnp.arange(CAP, dtype=jnp.int32)[None, None, :] < count_blk[:, :, None]
        normed, centred, inv_std = layer_norm(embedded, ln_gain)
        normed_rows = normed.reshape(SC_DEV, token_count, D)
        key_flags = live_slots.reshape(SC_DEV, token_count)
        qkv, attn_probs, probs_half, context = attend_forward(normed_rows, key_flags, w_qkv)
        mixed = jnp.einsum('ntw,wd->ntd', context.astype(jnp.float32), w_out.astype(jnp.float32))
        mixed = mixed.reshape(SC_DEV, GROUPS, CAP, D)
        output = jnp.where(live_slots[..., None], embedded.astype(jnp.float32) + mixed, 0.0).astype(jnp.bfloat16)
        grad_live = jnp.where(live_slots[..., None], grad_blk, jnp.zeros((), jnp.bfloat16))
        grad_rows = grad_live.reshape(SC_DEV, token_count, D)
        grad_qkv_w, grad_out_w, grad_qkv = attend_backward(grad_rows, normed_rows, w_qkv, w_out, qkv, attn_probs, probs_half, context)
        grad_normed = jnp.einsum('ntcw,dcw->ntd', grad_qkv.astype(jnp.float32), w_qkv.astype(jnp.float32))
        grad_normed = grad_normed.reshape(SC_DEV, GROUPS, CAP, D)
        grad_in = (grad_live.astype(jnp.float32) + norm_back(grad_normed, centred, inv_std, ln_gain)).astype(jnp.bfloat16)
        stem_part = stem_grads(picked, grad_in)
        return ((stem_acc + stem_part, qkv_acc + grad_qkv_w, out_acc + grad_out_w), output)
    blocks = (patches.reshape(block_count, SC_DEV, PATCHES, IN), vis_index.reshape(block_count, SC_DEV, GROUPS, CAP), vis_count.reshape(block_count, SC_DEV, GROUPS), out_grad.reshape(block_count, SC_DEV, GROUPS, CAP, D))
    start = (jnp.zeros((IN, D), jnp.float32), jnp.zeros((D, 3, D), jnp.float32), jnp.zeros((D, D), jnp.float32))
    (grad_w_stem, grad_w_qkv, grad_w_out), outputs = lax.scan(one_block, start, blocks)
    return (outputs.reshape(SCENES, GROUPS, CAP, D), grad_w_stem, grad_w_qkv, grad_w_out)
```

```python
import functools

import jax
import jax.numpy as jnp
from jax import lax
from jax.experimental import pallas as pl
from jax.experimental.pallas import tpu as pltpu
from jax.sharding import PartitionSpec as P

D = 1024
HD = 64
GROUPS = 3
CAP = 48
GRID = 12
PIX = 64
TOK = GROUPS * CAP
PAIR = 128
GROUP_BANDS = ((0, 4), (4, 8), (8, 10))
NORM_EPS = 1e-06
F32 = jnp.float32
BF16 = jnp.bfloat16
VMEM_LIMIT = 48 * 1024 * 1024


def dot_nn(a, b):
    return lax.dot_general(a, b, (((1,), (0,)), ((), ())), preferred_element_type=F32)


def dot_nt(a, b):
    return lax.dot_general(a, b, (((1,), (1,)), ((), ())), preferred_element_type=F32)


def dot_tn(a, b):
    return lax.dot_general(a, b, (((0,), (0,)), ((), ())), preferred_element_type=F32)


def live_column(c0, c1, c2):
    row = lax.broadcasted_iota(jnp.int32, (TOK, 1), 0)
    return (
        (row < c0)
        | ((row >= CAP) & (row < CAP + c1))
        | ((row >= 2 * CAP) & (row < 2 * CAP + c2))
    )


def params():
    return pltpu.CompilerParams(vmem_limit_bytes=VMEM_LIMIT)


def cost(flops, nbytes):
    return pl.CostEstimate(flops=int(flops), bytes_accessed=int(nbytes), transcendentals=0)


def stem_kernel(
    cnt_ref, idx_ref, patch_ref, w_ref, gain_ref, table_ref, genc_ref, og_ref,
    emb_ref, normed_ref, gl_ref, cols_ref, parts,
):
    step = pl.program_id(0)
    scenes = patch_ref.shape[0]

    @pl.when(step == 0)
    def _():
        whole = table_ref[...]
        high = whole.astype(BF16)
        rest = whole - high.astype(F32)
        mid = rest.astype(BF16)
        low = (rest - mid.astype(F32)).astype(BF16)
        parts[0] = high
        parts[1] = mid
        parts[2] = low

    patch_iota = lax.broadcasted_iota(jnp.int32, (TOK, table_ref.shape[0]), 1)
    picked, placed = [], []
    for s in range(scenes):
        onehot = (idx_ref[s] == patch_iota).astype(F32).astype(BF16)
        picked.append(dot_nn(onehot, patch_ref[s]).astype(BF16))
        placed.append(
            (dot_nn(onehot, parts[0]) + dot_nn(onehot, parts[1])) + dot_nn(onehot, parts[2])
        )
        live = live_column(
            cnt_ref[step * scenes + s, 0], cnt_ref[step * scenes + s, 1], cnt_ref[step * scenes + s, 2]
        )
        gl_ref[s] = jnp.where(live, og_ref[s].astype(F32), 0.0).astype(BF16)
    for g, (start, end) in enumerate(GROUP_BANDS):
        rows = slice(g * CAP, (g + 1) * CAP)
        columns = jnp.concatenate([p[rows, start * PIX : end * PIX] for p in picked], axis=0)
        summed = dot_nn(columns, w_ref[start * PIX : end * PIX, :])
        width = (end - start) * PIX
        for s in range(scenes):
            values = summed[s * CAP : (s + 1) * CAP] + (placed[s][rows] + genc_ref[g : g + 1, :])
            emb = values.astype(BF16)
            emb_ref[s, rows, :] = emb
            x = emb.astype(F32)
            centre = jnp.mean(x, axis=-1, keepdims=True)
            dev = x - centre
            spread = jnp.mean(dev * dev, axis=-1, keepdims=True)
            centred = dev * lax.rsqrt(spread + NORM_EPS)
            normed_ref[s, rows, :] = (centred * gain_ref[...]).astype(BF16)
            cols_ref[s, rows, :width] = columns[s * CAP : (s + 1) * CAP]
            if width < cols_ref.shape[2]:
                cols_ref[s, rows, width:] = jnp.zeros((CAP, cols_ref.shape[2] - width), BF16)


def stem_call(counts, index_col, patches, w_stem, gain, table, genc, out_grad):
    scenes, patch_count, width = patches.shape
    block = 3 if scenes % 3 == 0 else 1
    col_width = max(e - s for s, e in GROUP_BANDS) * PIX
    per = lambda shape: pl.BlockSpec((block,) + shape, lambda i: (i, 0, 0))
    whole = lambda a: pl.BlockSpec(a.shape, lambda i: (0,) * a.ndim)
    rows = jax.ShapeDtypeStruct((scenes, TOK, D), BF16)
    return pl.pallas_call(
        stem_kernel,
        grid=(scenes // block,),
        in_specs=[
            pl.BlockSpec(memory_space=pltpu.SMEM),
            per((TOK, 1)),
            per((patch_count, width)),
            whole(w_stem),
            whole(gain),
            whole(table),
            whole(genc),
            per((TOK, D)),
        ],
        out_specs=[per((TOK, D)), per((TOK, D)), per((TOK, D)), per((TOK, col_width))],
        out_shape=[rows, rows, rows, jax.ShapeDtypeStruct((scenes, TOK, col_width), BF16)],
        scratch_shapes=[pltpu.VMEM((3,) + table.shape, BF16)],
        compiler_params=params(),
        cost_estimate=cost(8e9, 12e6),
        name="stem_norm",
    )(counts, index_col, patches, w_stem, gain, table, genc, out_grad)


def attention_kernel(cnt_ref, na_ref, nb_ref, ga_ref, gb_ref, p_ref, out_ref, n_s, g_s, qkv):
    half, step = pl.program_id(0), pl.program_id(1)
    rows = n_s.shape[0]
    scenes = rows // TOK
    width = p_ref.shape[1] // 4

    @pl.when(half == 0)
    def _():
        n_s[...] = na_ref[...]
        g_s[...] = ga_ref[...]

    @pl.when(half != 0)
    def _():
        n_s[...] = nb_ref[...]
        g_s[...] = gb_ref[...]

    qkv[:, : 3 * width] = dot_nn(n_s[...], p_ref[:, : 3 * width]).astype(BF16)
    qkv[:, 3 * width :] = dot_nn(g_s[...], p_ref[:, 3 * width :]).astype(BF16)
    lane = lax.broadcasted_iota(jnp.int32, (1, PAIR), 1)
    masks = [
        (lane // HD == h).astype(F32).astype(BF16) for h in range(PAIR // HD)
    ]

    def scene_body(s, _):
        base = pl.multiple_of(s * TOK, 16)
        at = pl.ds(base, TOK)
        scene = step * scenes + s
        live = live_column(cnt_ref[half, scene, 0], cnt_ref[half, scene, 1], cnt_ref[half, scene, 2])
        bias = jnp.where(live, 0.0, -1e30)
        for pair in range(width // PAIR):
            cols = [slice(part * width + pair * PAIR, part * width + (pair + 1) * PAIR) for part in range(4)]
            q, k, v, dc = [qkv[at, c] for c in cols]
            gq = gk = gv = ctx = None
            for mask in masks:
                qm = q * (mask * jnp.asarray(HD ** (-0.5), BF16))
                km, vm, dcm = k * mask, v * mask, dc * mask
                scores = dot_nt(k, qm) + bias
                lifted = jnp.exp(scores - jnp.max(scores, axis=0, keepdims=True))
                probs = lifted * (1.0 / jnp.sum(lifted, axis=0, keepdims=True))
                half_probs = probs.astype(BF16)
                grad_probs = dot_nt(v, dcm)
                inner = jnp.sum(probs * grad_probs, axis=0, keepdims=True)
                grad_score = (probs * (grad_probs - inner)).astype(BF16)
                new = (
                    dot_tn(grad_score, km),
                    dot_nn(grad_score, qm),
                    dot_nn(half_probs, dcm),
                    dot_tn(half_probs, vm),
                )
                if gq is None:
                    gq, gk, gv, ctx = new
                else:
                    gq, gk, gv, ctx = gq + new[0], gk + new[1], gv + new[2], ctx + new[3]
            out_ref[at, cols[0]] = (gq * HD ** (-0.5)).astype(BF16)
            out_ref[at, cols[1]] = gk.astype(BF16)
            out_ref[at, cols[2]] = gv.astype(BF16)
            out_ref[at, cols[3]] = ctx.astype(BF16)
        return 0

    lax.fori_loop(0, scenes, scene_body, 0)


def attention_call(counts, na, nb, ga, gb, packed):
    tokens = na.shape[0]
    rows = 3 * TOK if tokens % (3 * TOK) == 0 else TOK
    steps = tokens // rows
    first = pl.BlockSpec((rows, D), lambda h, i: (jnp.where(h == 0, i, steps - 1), 0))
    second = pl.BlockSpec((rows, D), lambda h, i: (jnp.where(h == 0, 0, i), 0))
    return pl.pallas_call(
        attention_kernel,
        grid=(2, steps),
        in_specs=[
            pl.BlockSpec(memory_space=pltpu.SMEM),
            first, second, first, second,
            pl.BlockSpec(packed.shape, lambda h, i: (0, 0)),
        ],
        out_specs=pl.BlockSpec((rows, packed.shape[1]), lambda h, i: (h * steps + i, 0)),
        out_shape=jax.ShapeDtypeStruct((2 * tokens, packed.shape[1]), BF16),
        scratch_shapes=[
            pltpu.VMEM((rows, D), BF16),
            pltpu.VMEM((rows, D), BF16),
            pltpu.VMEM((rows, packed.shape[1]), BF16),
        ],
        compiler_params=params(),
        cost_estimate=cost(22e9, 14e6),
        name="attention",
    )(counts, na, nb, ga, gb, packed)


def weight_grad_kernel(na_ref, nb_ref, ga_ref, gb_ref, pack_ref, out_ref):
    half, step = pl.program_id(0), pl.program_id(1)
    width = pack_ref.shape[1] // 4

    @pl.when((half == 0) & (step == 0))
    def _():
        out_ref[...] = jnp.zeros_like(out_ref)

    def add(n_ref, g_ref):
        out_ref[:, : 3 * width] += dot_tn(n_ref[...], pack_ref[:, : 3 * width])
        out_ref[:, 3 * width :] += dot_tn(g_ref[...], pack_ref[:, 3 * width :])

    pl.when(half == 0)(lambda: add(na_ref, ga_ref))
    pl.when(half != 0)(lambda: add(nb_ref, gb_ref))


def weight_grad_call(na, nb, ga, gb, pack):
    tokens = na.shape[0]
    rows = 3 * TOK if tokens % (3 * TOK) == 0 else TOK
    steps = tokens // rows
    first = pl.BlockSpec((rows, D), lambda h, i: (jnp.where(h == 0, i, steps - 1), 0))
    second = pl.BlockSpec((rows, D), lambda h, i: (jnp.where(h == 0, 0, i), 0))
    return pl.pallas_call(
        weight_grad_kernel,
        grid=(2, steps),
        in_specs=[
            first, second, first, second,
            pl.BlockSpec((rows, pack.shape[1]), lambda h, i: (h * steps + i, 0)),
        ],
        out_specs=pl.BlockSpec((D, pack.shape[1]), lambda h, i: (0, 0)),
        out_shape=jax.ShapeDtypeStruct((D, pack.shape[1]), F32),
        compiler_params=params(),
        cost_estimate=cost(4e9, 15e6),
        name="weight_grad",
    )(na, nb, ga, gb, pack)


def back_kernel(blocks, first_col, last_col, out_dtype, *refs):
    packs, weights, out_ref = refs[:blocks], refs[blocks : 2 * blocks], refs[2 * blocks]
    total = None
    for pack_ref, w_ref in zip(packs, weights):
        new = dot_nt(pack_ref[...], w_ref[:, first_col:last_col])
        total = new if total is None else total + new
    out_ref[...] = total.astype(out_dtype)


def back_call(packs, weights, half, context, out_dtype):
    blocks = len(packs)
    tokens = packs[0].shape[0] // 2
    rows = 3 * TOK if tokens % (3 * TOK) == 0 else TOK
    steps = tokens // rows
    width = packs[0].shape[1] // 4
    span = (3 * width, 4 * width) if context else (0, 3 * width)
    if context:
        pack_spec = pl.BlockSpec((rows, width), lambda i: (half * steps + i, 3))
    else:
        pack_spec = pl.BlockSpec((rows, 3 * width), lambda i: (half * steps + i, 0))
    return pl.pallas_call(
        functools.partial(back_kernel, blocks, span[0], span[1], out_dtype),
        grid=(steps,),
        in_specs=[pack_spec] * blocks + [pl.BlockSpec(w.shape, lambda i: (0, 0)) for w in weights],
        out_specs=pl.BlockSpec((rows, D), lambda i: (i, 0)),
        out_shape=jax.ShapeDtypeStruct((tokens, D), out_dtype),
        compiler_params=params(),
        cost_estimate=cost(3e9, 10e6),
        name="back_context" if context else "back_qkv",
    )(*packs, *weights)


def tail_kernel(
    blocks, cnt_ref, recv_ref, emb_ref, gl_ref, cols_ref, gain_ref, *refs
):
    packs, weights, out_ref = refs[:blocks], refs[blocks : 2 * blocks], refs[2 * blocks]
    step = pl.program_id(0)
    rows = emb_ref.shape[0]
    scenes = rows // TOK

    @pl.when(step == 0)
    def _():
        out_ref[...] = jnp.zeros_like(out_ref)

    grad_normed = recv_ref[...]
    for pack_ref, w_ref in zip(packs, weights):
        grad_normed = grad_normed + dot_nt(pack_ref[...], w_ref[:, : pack_ref.shape[1]])
    x = emb_ref[...].astype(F32)
    dev = x - jnp.mean(x, axis=-1, keepdims=True)
    inv_std = lax.rsqrt(jnp.mean(dev * dev, axis=-1, keepdims=True) + NORM_EPS)
    centred = dev * inv_std
    scaled = grad_normed * gain_ref[...]
    first_mean = jnp.mean(scaled, axis=-1, keepdims=True)
    second_mean = jnp.mean(scaled * centred, axis=-1, keepdims=True)
    back = inv_std * (scaled - first_mean - centred * second_mean)
    grad_in = (gl_ref[...].astype(F32) + back).astype(BF16)
    for g, (start, end) in enumerate(GROUP_BANDS):
        at = [slice(s * TOK + g * CAP, s * TOK + (g + 1) * CAP) for s in range(scenes)]
        columns = jnp.concatenate([cols_ref[a, : (end - start) * PIX] for a in at], axis=0)
        grads = jnp.concatenate([grad_in[a] for a in at], axis=0)
        out_ref[start * PIX : end * PIX, :] += dot_tn(columns, grads)


def tail_call(counts, recv, emb, gl, cols, gain, packs, weights):
    blocks = len(packs)
    tokens = emb.shape[0]
    rows = 3 * TOK if tokens % (3 * TOK) == 0 else TOK
    width = packs[0].shape[1] // 4
    per = lambda a: pl.BlockSpec((rows, a.shape[1]), lambda i: (i, 0))
    return pl.pallas_call(
        functools.partial(tail_kernel, blocks),
        grid=(tokens // rows,),
        in_specs=[pl.BlockSpec(memory_space=pltpu.SMEM), per(recv), per(emb), per(gl), per(cols)]
        + [pl.BlockSpec(gain.shape, lambda i: (0, 0))]
        + [pl.BlockSpec((rows, 3 * width), lambda i: (i, 0))] * blocks
        + [pl.BlockSpec(w.shape, lambda i: (0, 0)) for w in weights],
        out_specs=pl.BlockSpec((GROUP_BANDS[-1][1] * PIX, D), lambda i: (0, 0)),
        out_shape=jax.ShapeDtypeStruct((GROUP_BANDS[-1][1] * PIX, D), F32),
        compiler_params=params(),
        cost_estimate=cost(5e9, 18e6),
        name="tail",
    )(counts, recv, emb, gl, cols, gain, *packs, *weights)


def output_kernel(blocks, cnt_ref, recv_ref, emb_ref, *refs):
    packs, weights, out_ref = refs[:blocks], refs[blocks : 2 * blocks], refs[2 * blocks]
    step = pl.program_id(0)
    scenes = emb_ref.shape[0] // TOK
    mixed = recv_ref[...].astype(F32)
    for pack_ref, w_ref in zip(packs, weights):
        mixed = mixed + dot_nt(pack_ref[...], w_ref[:, 3 * pack_ref.shape[1] :])
    total = emb_ref[...].astype(F32) + mixed
    for s in range(scenes):
        scene = step * scenes + s
        live = live_column(cnt_ref[scene, 0], cnt_ref[scene, 1], cnt_ref[scene, 2])
        at = slice(s * TOK, (s + 1) * TOK)
        out_ref[at, :] = jnp.where(live, total[at], 0.0).astype(BF16)


def output_call(counts, recv, emb, packs, weights):
    blocks = len(packs)
    tokens = emb.shape[0]
    rows = 3 * TOK if tokens % (3 * TOK) == 0 else TOK
    width = packs[0].shape[1] // 4
    per = lambda a: pl.BlockSpec((rows, a.shape[1]), lambda i: (i, 0))
    return pl.pallas_call(
        functools.partial(output_kernel, blocks),
        grid=(tokens // rows,),
        in_specs=[pl.BlockSpec(memory_space=pltpu.SMEM), per(recv), per(emb)]
        + [pl.BlockSpec((rows, width), lambda i: (i, 3))] * blocks
        + [pl.BlockSpec(w.shape, lambda i: (0, 0)) for w in weights],
        out_specs=per(emb),
        out_shape=jax.ShapeDtypeStruct(emb.shape, BF16),
        compiler_params=params(),
        cost_estimate=cost(1e9, 10e6),
        name="layer_output",
    )(counts, recv, emb, *packs, *weights)


def swap(x, axis, size, bit):
    return lax.ppermute(x, axis, [(i, i ^ bit) for i in range(size)])


def ring_order(size):
    return list(range(0, size, 2)) + list(range(size - 1, 0, -2)) if size % 2 == 0 else list(range(size))


def ring_gather(x, axis, size):
    order = ring_order(size)
    place = [order.index(i) for i in range(size)]
    forward = [(order[i], order[(i + 1) % size]) for i in range(size)]
    backward = [(order[(i + 1) % size], order[i]) for i in range(size)]
    here = jnp.array(place, jnp.int32)[lax.axis_index(axis)]
    owners = jnp.array(order, jnp.int32)
    rows = x.shape[0]
    full = jnp.zeros((size * rows,) + x.shape[1:], x.dtype)

    def put(full, block, distance):
        owner = owners[(here + distance + size) % size]
        return lax.dynamic_update_slice_in_dim(full, block, owner * rows, 0)

    full = put(full, x, 0)
    ahead = behind = x
    for s in range(1, size // 2 + 1):
        ahead = lax.ppermute(ahead, axis, forward)
        full = put(full, ahead, -s)
        if s <= (size - 1) // 2:
            behind = lax.ppermute(behind, axis, backward)
            full = put(full, behind, s)
    return full


def reduce_rows(x, axis, size, chunks):
    rows = x.shape[0] // size
    cols = x.shape[1] // chunks
    me = lax.axis_index(axis)
    low, high = me % 2, me // 2
    count = size // 2
    out = []
    for c in range(chunks):
        part = x[:, c * cols : (c + 1) * cols].reshape(count, 2, rows, cols)
        send = lax.dynamic_index_in_dim(part, 1 - low, 1, keepdims=False).astype(BF16)
        keep = lax.dynamic_index_in_dim(part, low, 1, keepdims=False)
        part = keep + swap(send, axis, size, 1).astype(F32)
        total = lax.dynamic_index_in_dim(part, high, 0, keepdims=False)
        for j in range(1, count):
            away = lax.dynamic_index_in_dim(part, high ^ j, 0, keepdims=False).astype(BF16)
            total = total + swap(away, axis, size, 2 * j).astype(F32)
        out.append(total)
    return jnp.concatenate(out, axis=1)


def sum_stem(x, dp, group):
    core = lax.axis_index("group") % 2
    far = lax.axis_index("group") // 2
    low = lax.axis_index("dp") % 2
    high = lax.axis_index("dp") // 2
    fars, highs = group // 2, dp // 2
    rows = x.shape[0] // 2
    own = lax.dynamic_slice_in_dim(x, core * rows, rows, 0)
    other = lax.dynamic_slice_in_dim(x, (1 - core) * rows, rows, 0)
    own = own + swap(other, "group", group, 1)
    small = rows // (2 * fars)
    mine = far * 2 + low
    total = lax.dynamic_slice_in_dim(own, mine * small, small, 0)

    def hop(block, f, b):
        if f:
            block_axis = [
                ((d, g), (d ^ b, g ^ (2 * f))) for d in range(dp) for g in range(group)
            ]
            pairs = [(s[0] * group + s[1], t[0] * group + t[1]) for s, t in block_axis]
            return lax.ppermute(block, ("dp", "group"), pairs)
        return swap(block, "dp", dp, b)

    hops = [(f, b) for f in range(fars) for b in range(2) if f or b]
    for f, b in hops:
        target = (far ^ f) * 2 + (low ^ b)
        away = lax.dynamic_slice_in_dim(own, target * small, small, 0).astype(BF16)
        total = total + hop(away, f, b).astype(F32)
    cols = x.shape[1] // highs
    part = lax.dynamic_slice_in_dim(total, high * cols, cols, 1)
    for j in range(1, highs):
        away = lax.dynamic_slice_in_dim(total, (high ^ j) * cols, cols, 1)
        part = part + swap(away, "dp", dp, 2 * j)
    part = part.astype(BF16)
    line = jnp.zeros((small, x.shape[1]), BF16)
    line = lax.dynamic_update_slice_in_dim(line, part, high * cols, 1)
    for j in range(1, highs):
        line = lax.dynamic_update_slice_in_dim(
            line, swap(part, "dp", dp, 2 * j), (high ^ j) * cols, 1
        )
    block = jnp.zeros((rows, x.shape[1]), BF16)
    block = lax.dynamic_update_slice_in_dim(block, line, mine * small, 0)
    for f, b in hops:
        target = (far ^ f) * 2 + (low ^ b)
        block = lax.dynamic_update_slice_in_dim(block, hop(line, f, b), target * small, 0)
    partner = swap(block, "group", group, 1)
    whole = jnp.zeros(x.shape, BF16)
    whole = lax.dynamic_update_slice_in_dim(whole, block, core * rows, 0)
    whole = lax.dynamic_update_slice_in_dim(whole, partner, (1 - core) * rows, 0)
    return whole.astype(F32)


def spatial_table(patch_count):
    quarter = D // 4
    half_width = D // 2
    row_freq = jnp.power(10000.0, -jnp.arange(quarter, dtype=F32) / quarter)
    group_freq = jnp.power(10000.0, -jnp.arange(half_width, dtype=F32) / half_width)
    at = jnp.arange(GRID).astype(F32)[:, None] * row_freq
    both = jnp.concatenate([jnp.sin(at), jnp.cos(at)], axis=-1)
    rows = patch_count // GRID
    by_row = jnp.broadcast_to(both[:rows, None], (rows, GRID, 2 * quarter))
    by_col = jnp.broadcast_to(both[None], (rows, GRID, 2 * quarter))
    table = jnp.concatenate([by_row, by_col], axis=-1).reshape(patch_count, D)
    group_at = jnp.arange(GROUPS).astype(F32)[:, None] * group_freq
    return table, jnp.concatenate([jnp.sin(group_at), jnp.cos(group_at)], axis=-1)


def on_device(dp, group, patches, vis_index, vis_count, w_stem, ln_gain, w_qkv, w_out, out_grad):
    scenes = patches.shape[0]
    tokens = scenes * TOK
    width = w_qkv.shape[2]
    fars = group // 2

    shard = jnp.concatenate([w_qkv.reshape(w_qkv.shape[0], 3 * width), w_out.T], axis=1)
    shards = [shard] + [swap(shard, "group", group, 2 * f) for f in range(1, fars)]
    weights = [ring_gather(s, "dp", dp) for s in shards]

    counts = vis_count.astype(jnp.int32)
    both_counts = jnp.stack([counts, swap(counts, "group", group, 1)])
    table, genc = spatial_table(patches.shape[1])
    gain = ln_gain.reshape(1, D)
    emb, normed, gl, cols = stem_call(
        counts,
        vis_index.reshape(scenes, TOK, 1),
        patches,
        w_stem,
        gain,
        table,
        genc,
        out_grad.reshape(scenes, TOK, D),
    )
    emb, normed, gl = [a.reshape(tokens, D) for a in (emb, normed, gl)]
    cols = cols.reshape(tokens, cols.shape[2])
    normed_far = swap(normed, "group", group, 1)
    gl_far = swap(gl, "group", group, 1)

    packs, grads = [], []
    for f in range(fars):
        packs.append(attention_call(both_counts, normed, normed_far, gl, gl_far, weights[f]))
        grads.append(weight_grad_call(normed, normed_far, gl, gl_far, packs[f]))
    shares = [reduce_rows(g, "dp", dp, 2) for g in grads]
    total = shares[0]
    for f in range(1, fars):
        total = total + swap(shares[f].astype(BF16), "group", group, 2 * f).astype(F32)
    grad_w_qkv = total[:, : 3 * width].reshape(total.shape[0], 3, width)
    grad_w_out = total[:, 3 * width :].T

    back_far = swap(back_call(packs, weights, 1, False, F32), "group", group, 1)
    mixed_far = swap(back_call(packs, weights, 1, True, BF16), "group", group, 1)
    stem_local = tail_call(counts, back_far, emb, gl, cols, gain, packs, weights)
    grad_w_stem = sum_stem(stem_local, dp, group)
    output = output_call(counts, mixed_far, emb, packs, weights)
    return (output.reshape(scenes, GROUPS, CAP, D), grad_w_stem, grad_w_qkv, grad_w_out)


def solution(mesh):
    sizes = dict(mesh.shape)
    return jax.shard_map(
        functools.partial(on_device, sizes["dp"], sizes["group"]),
        mesh=mesh,
        in_specs=(
            P(("dp", "group"), None, None),
            P(("dp", "group"), None, None),
            P(("dp", "group"), None),
            P(),
            P(),
            P("dp", None, "group"),
            P("group", "dp"),
            P(("dp", "group"), None, None, None),
        ),
        out_specs=(
            P(("dp", "group"), None, None, None),
            P(),
            P("dp", None, "group"),
            P("group", "dp"),
        ),
        check_vma=False,
    )
```

```python
import functools

import jax
import jax.numpy as jnp
from jax import lax
from jax.experimental import pallas as pl
from jax.experimental.pallas import tpu as pltpu
from jax.sharding import PartitionSpec as P

D = 1024
HD = 64
GROUPS = 3
CAP = 48
GRID = 12
PIX = 64
TOK = GROUPS * CAP
PAIR = 128
GROUP_BANDS = ((0, 4), (4, 8), (8, 10))
NORM_EPS = 1e-06
F32 = jnp.float32
BF16 = jnp.bfloat16
VMEM_LIMIT = 48 * 1024 * 1024


def dot_nn(a, b):
    return lax.dot_general(a, b, (((1,), (0,)), ((), ())), preferred_element_type=F32)


def dot_nt(a, b):
    return lax.dot_general(a, b, (((1,), (1,)), ((), ())), preferred_element_type=F32)


def dot_tn(a, b):
    return lax.dot_general(a, b, (((0,), (0,)), ((), ())), preferred_element_type=F32)


def live_column(c0, c1, c2):
    row = lax.broadcasted_iota(jnp.int32, (TOK, 1), 0)
    return (
        (row < c0)
        | ((row >= CAP) & (row < CAP + c1))
        | ((row >= 2 * CAP) & (row < 2 * CAP + c2))
    )


def params():
    return pltpu.CompilerParams(vmem_limit_bytes=VMEM_LIMIT)


def cost(flops, nbytes):
    return pl.CostEstimate(flops=int(flops), bytes_accessed=int(nbytes), transcendentals=0)


def stem_kernel(
    cnt_ref, idx_ref, patch_ref, w_ref, gain_ref, table_ref, genc_ref, og_ref,
    emb_ref, normed_ref, gl_ref, cols_ref, parts,
):
    step = pl.program_id(0)
    scenes = patch_ref.shape[0]

    @pl.when(step == 0)
    def _():
        whole = table_ref[...]
        high = whole.astype(BF16)
        rest = whole - high.astype(F32)
        mid = rest.astype(BF16)
        low = (rest - mid.astype(F32)).astype(BF16)
        parts[0] = high
        parts[1] = mid
        parts[2] = low

    patch_iota = lax.broadcasted_iota(jnp.int32, (TOK, table_ref.shape[0]), 1)
    picked, placed = [], []
    for s in range(scenes):
        onehot = (idx_ref[s] == patch_iota).astype(F32).astype(BF16)
        picked.append(dot_nn(onehot, patch_ref[s]).astype(BF16))
        placed.append(
            (dot_nn(onehot, parts[0]) + dot_nn(onehot, parts[1])) + dot_nn(onehot, parts[2])
        )
        live = live_column(
            cnt_ref[step * scenes + s, 0], cnt_ref[step * scenes + s, 1], cnt_ref[step * scenes + s, 2]
        )
        gl_ref[s] = jnp.where(live, og_ref[s].astype(F32), 0.0).astype(BF16)
    for g, (start, end) in enumerate(GROUP_BANDS):
        rows = slice(g * CAP, (g + 1) * CAP)
        columns = jnp.concatenate([p[rows, start * PIX : end * PIX] for p in picked], axis=0)
        summed = dot_nn(columns, w_ref[start * PIX : end * PIX, :])
        width = (end - start) * PIX
        for s in range(scenes):
            values = summed[s * CAP : (s + 1) * CAP] + (placed[s][rows] + genc_ref[g : g + 1, :])
            emb = values.astype(BF16)
            emb_ref[s, rows, :] = emb
            x = emb.astype(F32)
            centre = jnp.mean(x, axis=-1, keepdims=True)
            dev = x - centre
            spread = jnp.mean(dev * dev, axis=-1, keepdims=True)
            centred = dev * lax.rsqrt(spread + NORM_EPS)
            normed_ref[s, rows, :] = (centred * gain_ref[...]).astype(BF16)
            cols_ref[s, rows, :width] = columns[s * CAP : (s + 1) * CAP]
            if width < cols_ref.shape[2]:
                cols_ref[s, rows, width:] = jnp.zeros((CAP, cols_ref.shape[2] - width), BF16)


def stem_call(counts, index_col, patches, w_stem, gain, table, genc, out_grad):
    scenes, patch_count, width = patches.shape
    block = 3 if scenes % 3 == 0 else 1
    col_width = max(e - s for s, e in GROUP_BANDS) * PIX
    per = lambda shape: pl.BlockSpec((block,) + shape, lambda i: (i, 0, 0))
    whole = lambda a: pl.BlockSpec(a.shape, lambda i: (0,) * a.ndim)
    rows = jax.ShapeDtypeStruct((scenes, TOK, D), BF16)
    return pl.pallas_call(
        stem_kernel,
        grid=(scenes // block,),
        in_specs=[
            pl.BlockSpec(memory_space=pltpu.SMEM),
            per((TOK, 1)),
            per((patch_count, width)),
            whole(w_stem),
            whole(gain),
            whole(table),
            whole(genc),
            per((TOK, D)),
        ],
        out_specs=[per((TOK, D)), per((TOK, D)), per((TOK, D)), per((TOK, col_width))],
        out_shape=[rows, rows, rows, jax.ShapeDtypeStruct((scenes, TOK, col_width), BF16)],
        scratch_shapes=[pltpu.VMEM((3,) + table.shape, BF16)],
        compiler_params=params(),
        cost_estimate=cost(8e9, 12e6),
        name="stem_norm",
    )(counts, index_col, patches, w_stem, gain, table, genc, out_grad)


def attention_kernel(
    deps, cnt_ref, na_ref, nb_ref, ga_ref, gb_ref, wq_ref, wk_ref, wv_ref, wo_ref, *refs
):
    out_ref, n_s, g_s, qkv = refs[deps:]
    half, step = pl.program_id(0), pl.program_id(1)
    rows = n_s.shape[0]
    scenes = rows // TOK
    width = wq_ref.shape[1]

    @pl.when(half == 0)
    def _():
        n_s[...] = na_ref[...]
        g_s[...] = ga_ref[...]

    @pl.when(half != 0)
    def _():
        n_s[...] = nb_ref[...]
        g_s[...] = gb_ref[...]

    into = jnp.concatenate([wq_ref[...], wk_ref[...], wv_ref[...]], axis=1)
    qkv[:, : 3 * width] = dot_nn(n_s[...], into).astype(BF16)
    qkv[:, 3 * width :] = dot_nn(g_s[...], wo_ref[...]).astype(BF16)
    lane = lax.broadcasted_iota(jnp.int32, (1, PAIR), 1)
    masks = [(lane // HD == h).astype(F32).astype(BF16) for h in range(PAIR // HD)]

    def scene_body(s, _):
        base = pl.multiple_of(s * TOK, 16)
        at = pl.ds(base, TOK)
        scene = step * scenes + s
        live = live_column(cnt_ref[half, scene, 0], cnt_ref[half, scene, 1], cnt_ref[half, scene, 2])
        bias = jnp.where(live, 0.0, -1e30)
        for pair in range(width // PAIR):
            cols = [slice(part * width + pair * PAIR, part * width + (pair + 1) * PAIR) for part in range(4)]
            q, k, v, dc = [qkv[at, c] for c in cols]
            gq = gk = gv = ctx = None
            for mask in masks:
                qm = q * (mask * jnp.asarray(HD ** (-0.5), BF16))
                km, vm, dcm = k * mask, v * mask, dc * mask
                scores = dot_nt(k, qm) + bias
                lifted = jnp.exp(scores - jnp.max(scores, axis=0, keepdims=True))
                probs = lifted * (1.0 / jnp.sum(lifted, axis=0, keepdims=True))
                half_probs = probs.astype(BF16)
                grad_probs = dot_nt(v, dcm)
                inner = jnp.sum(probs * grad_probs, axis=0, keepdims=True)
                grad_score = (probs * (grad_probs - inner)).astype(BF16)
                new = (
                    dot_tn(grad_score, km),
                    dot_nn(grad_score, qm),
                    dot_nn(half_probs, dcm),
                    dot_tn(half_probs, vm),
                )
                if gq is None:
                    gq, gk, gv, ctx = new
                else:
                    gq, gk, gv, ctx = gq + new[0], gk + new[1], gv + new[2], ctx + new[3]
            out_ref[at, cols[0]] = (gq * HD ** (-0.5)).astype(BF16)
            out_ref[at, cols[1]] = gk.astype(BF16)
            out_ref[at, cols[2]] = gv.astype(BF16)
            out_ref[at, cols[3]] = ctx.astype(BF16)
        return 0

    lax.fori_loop(0, scenes, scene_body, 0)


def block_rows(tokens):
    return 3 * TOK if tokens % (3 * TOK) == 0 else TOK


def two_halves(rows, steps):
    first = pl.BlockSpec((rows, D), lambda h, i: (jnp.where(h == 0, i, steps - 1), 0))
    second = pl.BlockSpec((rows, D), lambda h, i: (jnp.where(h == 0, 0, i), 0))
    return [first, second, first, second]


ANYWHERE = pl.BlockSpec(memory_space=pl.ANY)
SCALARS = pl.BlockSpec(memory_space=pltpu.SMEM)


def attention_call(counts, na, nb, ga, gb, packed, part, parts, deps=()):
    tokens = na.shape[0]
    rows = block_rows(tokens)
    steps = tokens // rows
    first, second = packed
    width = first.shape[1] // 2 // parts
    weight = lambda c: pl.BlockSpec((D, width), lambda h, i: (0, (c % 2) * parts + part))
    return pl.pallas_call(
        functools.partial(attention_kernel, len(deps)),
        grid=(2, steps),
        in_specs=[SCALARS] + two_halves(rows, steps) + [weight(c) for c in range(4)] + [ANYWHERE] * len(deps),
        out_specs=pl.BlockSpec((rows, 4 * width), lambda h, i: (h * steps + i, 0)),
        out_shape=jax.ShapeDtypeStruct((2 * tokens, 4 * width), BF16),
        scratch_shapes=[
            pltpu.VMEM((rows, D), BF16),
            pltpu.VMEM((rows, D), BF16),
            pltpu.VMEM((rows, 4 * width), BF16),
        ],
        compiler_params=params(),
        cost_estimate=cost(24e9 / parts, 14e6),
        name="attention",
    )(counts, na, nb, ga, gb, first, first, second, second, *deps)


def weight_grad_kernel(
    deps, blocks, low_ref, na_ref, nb_ref, ga_ref, gb_ref, pack_ref, *refs
):
    send_ref, keep_ref, total = refs[deps:]
    half, step = pl.program_id(0), pl.program_id(1)
    width = pack_ref.shape[1] // 4

    @pl.when((half == 0) & (step == 0))
    def _():
        total[...] = jnp.zeros_like(total)

    def add(n_ref, g_ref):
        total[:, : 3 * width] += dot_tn(n_ref[...], pack_ref[:, : 3 * width])
        total[:, 3 * width :] += dot_tn(g_ref[...], pack_ref[:, 3 * width :])

    pl.when(half == 0)(lambda: add(na_ref, ga_ref))
    pl.when(half != 0)(lambda: add(nb_ref, gb_ref))

    @pl.when((half == pl.num_programs(0) - 1) & (step == pl.num_programs(1) - 1))
    def _():
        rows = total.shape[0] // blocks
        low = low_ref[0]
        for b in range(blocks // 2):
            at = slice(b * rows, (b + 1) * rows)
            mine = pl.multiple_of((2 * b + low) * rows, rows)
            other = pl.multiple_of((2 * b + 1 - low) * rows, rows)
            keep_ref[at, :] = total[pl.ds(mine, rows), :]
            send_ref[at, :] = total[pl.ds(other, rows), :].astype(BF16)


def weight_grad_call(low, na, nb, ga, gb, pack, blocks, deps=()):
    tokens = na.shape[0]
    rows = block_rows(tokens)
    steps = tokens // rows
    cols = pack.shape[1]
    whole = pl.BlockSpec((D // 2, cols), lambda h, i: (0, 0))
    return pl.pallas_call(
        functools.partial(weight_grad_kernel, len(deps), blocks),
        grid=(2, steps),
        in_specs=[SCALARS]
        + two_halves(rows, steps)
        + [pl.BlockSpec((rows, cols), lambda h, i: (h * steps + i, 0))]
        + [ANYWHERE] * len(deps),
        out_specs=[whole, whole],
        out_shape=[jax.ShapeDtypeStruct((D // 2, cols), BF16), jax.ShapeDtypeStruct((D // 2, cols), F32)],
        scratch_shapes=[pltpu.VMEM((D, cols), F32)],
        compiler_params=params(),
        cost_estimate=cost(10e9 * cols / D, 12e6),
        name="weight_grad",
    )(low, na, nb, ga, gb, pack, *deps)


def combine_kernel(deps, place_ref, keep_ref, recv_ref, *refs):
    refs = refs[deps:]
    rows = refs[0].shape[0]
    place = place_ref[0]
    for j, ref in enumerate(refs):
        at = pl.ds(pl.multiple_of((place ^ j) * rows, rows), rows)
        ref[...] = (keep_ref[at, :] + recv_ref[at, :].astype(F32)).astype(ref.dtype)


def combine_call(place, keep, recv, blocks, dtype, deps=()):
    rows, cols = keep.shape[0] // blocks, keep.shape[1]
    whole = lambda a: pl.BlockSpec(a.shape, lambda: (0, 0))
    shapes = [jax.ShapeDtypeStruct((rows, cols), F32 if j == 0 else dtype) for j in range(blocks)]
    return pl.pallas_call(
        functools.partial(combine_kernel, len(deps)),
        in_specs=[SCALARS, whole(keep), whole(recv)] + [ANYWHERE] * len(deps),
        out_specs=[pl.BlockSpec((rows, cols), lambda: (0, 0))] * blocks,
        out_shape=shapes,
        compiler_params=params(),
        cost_estimate=cost(1e6, 5e6),
        name="combine",
    )(place, keep, recv, *deps)


def add_kernel(count, *refs):
    total = refs[0][...]
    for ref in refs[1:count]:
        total = total + ref[...].astype(F32)
    refs[-1][...] = total


def add_call(parts, deps=()):
    spec = pl.BlockSpec(parts[0].shape, lambda: (0, 0))
    return pl.pallas_call(
        functools.partial(add_kernel, len(parts)),
        in_specs=[spec] * len(parts) + [ANYWHERE] * len(deps),
        out_specs=spec,
        out_shape=jax.ShapeDtypeStruct(parts[0].shape, F32),
        compiler_params=params(),
        cost_estimate=cost(1e6, 2e6),
        name="add_parts",
    )(*parts, *deps)


def weight_columns(w_refs, first, count, part, parts):
    width = w_refs[0].shape[1] // 2
    size = width // parts
    pieces = []
    for c in range(first, first + count):
        start = (c % 2) * width + part * size
        pieces.append(w_refs[c // 2][:, start : start + size])
    return pieces[0] if count == 1 else jnp.concatenate(pieces, axis=1)


def back_product(layout, pack_refs, weight_refs, first, count):
    total = None
    for pack_ref, (block, part, parts) in zip(pack_refs, layout):
        columns = weight_columns(weight_refs[2 * block : 2 * block + 2], first, count, part, parts)
        new = dot_nt(pack_ref[...], columns)
        total = new if total is None else total + new
    return total


def back_kernel(layout, deps, first, count, *refs):
    packs, refs = refs[: len(layout)], refs[len(layout) :]
    out_ref = refs[-1]
    out_ref[...] = back_product(layout, packs, refs, first, count).astype(out_ref.dtype)


def back_call(layout, packs, weights, half, context, out_dtype, deps=()):
    tokens = packs[0].shape[0] // 2
    rows = block_rows(tokens)
    steps = tokens // rows

    def pack_spec(pack):
        width = pack.shape[1] // 4
        if context:
            return pl.BlockSpec((rows, width), lambda i: (half * steps + i, 3))
        return pl.BlockSpec((rows, 3 * width), lambda i: (half * steps + i, 0))

    return pl.pallas_call(
        functools.partial(back_kernel, layout, len(deps), 3 if context else 0, 1 if context else 3),
        grid=(steps,),
        in_specs=[pack_spec(p) for p in packs]
        + [pl.BlockSpec(w.shape, lambda i: (0, 0)) for w in weights]
        + [ANYWHERE] * len(deps),
        out_specs=pl.BlockSpec((rows, D), lambda i: (i, 0)),
        out_shape=jax.ShapeDtypeStruct((tokens, D), out_dtype),
        compiler_params=params(),
        cost_estimate=cost(3.5e9 if context else 6e9, 8e6),
        name="back_context" if context else "back_qkv",
    )(*packs, *weights, *deps)


def tail_kernel(layout, blocks, deps, core_ref, recv_ref, emb_ref, gl_ref, cols_ref, gain_ref, *refs):
    packs, refs = refs[: len(layout)], refs[len(layout) :]
    weights = refs[:blocks]
    send_ref, keep_ref, acc = refs[blocks + deps :]
    step = pl.program_id(0)
    rows = emb_ref.shape[0]
    scenes = rows // TOK

    @pl.when(step == 0)
    def _():
        acc[...] = jnp.zeros_like(acc)

    grad_normed = recv_ref[...] + back_product(layout, packs, weights, 0, 3)
    x = emb_ref[...].astype(F32)
    dev = x - jnp.mean(x, axis=-1, keepdims=True)
    inv_std = lax.rsqrt(jnp.mean(dev * dev, axis=-1, keepdims=True) + NORM_EPS)
    centred = dev * inv_std
    scaled = grad_normed * gain_ref[...]
    first_mean = jnp.mean(scaled, axis=-1, keepdims=True)
    second_mean = jnp.mean(scaled * centred, axis=-1, keepdims=True)
    back = inv_std * (scaled - first_mean - centred * second_mean)
    grad_in = (gl_ref[...].astype(F32) + back).astype(BF16)
    for g, (start, end) in enumerate(GROUP_BANDS):
        at = [slice(s * TOK + g * CAP, s * TOK + (g + 1) * CAP) for s in range(scenes)]
        columns = jnp.concatenate([cols_ref[a, : (end - start) * PIX] for a in at], axis=0)
        grads = jnp.concatenate([grad_in[a] for a in at], axis=0)
        acc[start * PIX : end * PIX, :] += dot_tn(columns, grads)

    @pl.when(step == pl.num_programs(0) - 1)
    def _():
        size = keep_ref.shape[0]
        core = core_ref[0]
        keep_ref[...] = acc[pl.ds(pl.multiple_of(core * size, size), size), :]
        send_ref[...] = acc[pl.ds(pl.multiple_of((1 - core) * size, size), size), :]


def tail_call(layout, core, recv, emb, gl, cols, gain, packs, weights, deps=()):
    tokens = emb.shape[0]
    rows = block_rows(tokens)
    per = lambda a: pl.BlockSpec((rows, a.shape[1]), lambda i: (i, 0))
    stem_rows = GROUP_BANDS[-1][1] * PIX
    half = jax.ShapeDtypeStruct((stem_rows // 2, D), F32)
    return pl.pallas_call(
        functools.partial(tail_kernel, layout, len(weights), len(deps)),
        grid=(tokens // rows,),
        in_specs=[SCALARS, per(recv), per(emb), per(gl), per(cols)]
        + [pl.BlockSpec(gain.shape, lambda i: (0, 0))]
        + [pl.BlockSpec((rows, 3 * (p.shape[1] // 4)), lambda i: (i, 0)) for p in packs]
        + [pl.BlockSpec(w.shape, lambda i: (0, 0)) for w in weights]
        + [ANYWHERE] * len(deps),
        out_specs=[pl.BlockSpec(half.shape, lambda i: (0, 0))] * 2,
        out_shape=[half, half],
        scratch_shapes=[pltpu.VMEM((stem_rows, D), F32)],
        compiler_params=params(),
        cost_estimate=cost(10e9, 12e6),
        name="tail",
    )(core, recv, emb, gl, cols, gain, *packs, *weights, *deps)


def output_kernel(layout, blocks, cnt_ref, recv_ref, emb_ref, *refs):
    packs, weights, out_ref = refs[: len(layout)], refs[len(layout) : len(layout) + blocks], refs[-1]
    step = pl.program_id(0)
    scenes = emb_ref.shape[0] // TOK
    mixed = recv_ref[...].astype(F32) + back_product(layout, packs, weights, 3, 1)
    total = emb_ref[...].astype(F32) + mixed
    for s in range(scenes):
        scene = step * scenes + s
        live = live_column(cnt_ref[scene, 0], cnt_ref[scene, 1], cnt_ref[scene, 2])
        at = slice(s * TOK, (s + 1) * TOK)
        out_ref[at, :] = jnp.where(live, total[at], 0.0).astype(BF16)


def output_call(layout, counts, recv, emb, packs, weights, deps=()):
    tokens = emb.shape[0]
    rows = block_rows(tokens)
    per = lambda a: pl.BlockSpec((rows, a.shape[1]), lambda i: (i, 0))
    return pl.pallas_call(
        functools.partial(output_kernel, layout, len(weights)),
        grid=(tokens // rows,),
        in_specs=[SCALARS, per(recv), per(emb)]
        + [pl.BlockSpec((rows, p.shape[1] // 4), lambda i: (i, 3)) for p in packs]
        + [pl.BlockSpec(w.shape, lambda i: (0, 0)) for w in weights]
        + [ANYWHERE] * len(deps),
        out_specs=per(emb),
        out_shape=jax.ShapeDtypeStruct(emb.shape, BF16),
        compiler_params=params(),
        cost_estimate=cost(5e9, 10e6),
        name="layer_output",
    )(counts, recv, emb, *packs, *weights, *deps)


def swap(x, axis, size, bit):
    return lax.ppermute(x, axis, [(i, i ^ bit) for i in range(size)])


def ring_gather(pieces, axis, size):
    order = list(range(0, size, 2)) + list(range(size - 1, 0, -2))
    forward = [(order[i], order[(i + 1) % size]) for i in range(size)]
    backward = [(order[(i + 1) % size], order[i]) for i in range(size)]
    me = lax.axis_index(axis)
    here = jnp.where(me % 2 == 0, me // 2, size - 1 - me // 2)
    rows = pieces[0].shape[0]

    def put(full, block, distance):
        at = (here + distance + size) % size
        owner = jnp.where(at < size // 2, 2 * at, 2 * (size - 1 - at) + 1)
        return lax.dynamic_update_slice_in_dim(full, block, owner * rows, 0)

    fulls = [put(jnp.zeros((size * rows,) + x.shape[1:], x.dtype), x, 0) for x in pieces]
    ahead, behind = list(pieces), list(pieces)
    for s in range(1, size // 2 + 1):
        for i in range(len(pieces)):
            ahead[i] = lax.ppermute(ahead[i], axis, forward)
            fulls[i] = put(fulls[i], ahead[i], -s)
            if s <= (size - 1) // 2:
                behind[i] = lax.ppermute(behind[i], axis, backward)
                fulls[i] = put(fulls[i], behind[i], s)
    return fulls


def halve_stem(send, keep, group, after):
    recv = swap(send, "group", group, 1)
    mine = lax.axis_index("group") // 2 * 2 + lax.axis_index("dp") % 2
    return combine_call(mine.reshape(1), keep, recv, group // 2 * 2, F32, (after,))


def sum_stem(parts, dp, group):
    core = lax.axis_index("group") % 2
    far = lax.axis_index("group") // 2
    low = lax.axis_index("dp") % 2
    high = lax.axis_index("dp") // 2
    fars, highs = group // 2, dp // 2
    mine = far * 2 + low
    small, width = parts[0].shape
    rows = 2 * fars * small

    def hop(block, f, b):
        if f:
            pairs = [
                (d * group + g, (d ^ b) * group + (g ^ (2 * f))) for d in range(dp) for g in range(group)
            ]
            return lax.ppermute(block, ("dp", "group"), pairs)
        return swap(block, "dp", dp, b)

    hops = [(k // 2, k % 2) for k in range(1, 2 * fars)]
    total = add_call([parts[0]] + [hop(part, f, b) for part, (f, b) in zip(parts[1:], hops)])
    cols = width // highs
    part = lax.dynamic_slice_in_dim(total, high * cols, cols, 1)
    for j in range(1, highs):
        away = lax.dynamic_slice_in_dim(total, (high ^ j) * cols, cols, 1)
        part = part + swap(away, "dp", dp, 2 * j)
    part = part.astype(BF16)
    line = jnp.zeros((small, width), BF16)
    line = lax.dynamic_update_slice_in_dim(line, part, high * cols, 1)
    for j in range(1, highs):
        line = lax.dynamic_update_slice_in_dim(
            line, swap(part, "dp", dp, 2 * j), (high ^ j) * cols, 1
        )
    block = jnp.zeros((rows, width), BF16)
    block = lax.dynamic_update_slice_in_dim(block, line, mine * small, 0)
    for f, b in hops:
        target = (far ^ f) * 2 + (low ^ b)
        block = lax.dynamic_update_slice_in_dim(block, hop(line, f, b), target * small, 0)
    partner = swap(block, "group", group, 1)
    first = jnp.where(core == 0, block, partner)
    second = jnp.where(core == 0, partner, block)
    return jnp.concatenate([first, second], axis=0).astype(F32), total


def spatial_table(patch_count):
    quarter = D // 4
    half_width = D // 2
    row_freq = jnp.power(10000.0, -jnp.arange(quarter, dtype=F32) / quarter)
    group_freq = jnp.power(10000.0, -jnp.arange(half_width, dtype=F32) / half_width)
    at = jnp.arange(GRID).astype(F32)[:, None] * row_freq
    both = jnp.concatenate([jnp.sin(at), jnp.cos(at)], axis=-1)
    rows = patch_count // GRID
    by_row = jnp.broadcast_to(both[:rows, None], (rows, GRID, 2 * quarter))
    by_col = jnp.broadcast_to(both[None], (rows, GRID, 2 * quarter))
    table = jnp.concatenate([by_row, by_col], axis=-1).reshape(patch_count, D)
    group_at = jnp.arange(GROUPS).astype(F32)[:, None] * group_freq
    return table, jnp.concatenate([jnp.sin(group_at), jnp.cos(group_at)], axis=-1)


def on_device(dp, group, patches, vis_index, vis_count, w_stem, ln_gain, w_qkv, w_out, out_grad):
    scenes = patches.shape[0]
    tokens = scenes * TOK
    width = w_qkv.shape[2]
    fars = group // 2
    low = (lax.axis_index("dp") % 2).astype(jnp.int32).reshape(1)
    high = (lax.axis_index("dp") // 2).astype(jnp.int32).reshape(1)
    core = (lax.axis_index("group") % 2).astype(jnp.int32).reshape(1)

    pieces = [
        w_qkv[:, :2].reshape(w_qkv.shape[0], 2 * width),
        jnp.concatenate([w_qkv[:, 2], w_out.T], axis=1),
    ]
    own = ring_gather(pieces, "dp", dp)
    weights = [own] + [[swap(w, "group", group, 2 * f) for w in own] for f in range(1, fars)]
    flat = [w for pair in weights for w in pair]

    counts = vis_count.astype(jnp.int32)
    both_counts = jnp.stack([counts, swap(counts, "group", group, 1)])
    table, genc = spatial_table(patches.shape[1])
    gain = ln_gain.reshape(1, D)
    emb, normed, gl, cols = stem_call(
        counts,
        vis_index.reshape(scenes, TOK, 1),
        patches,
        w_stem,
        gain,
        table,
        genc,
        out_grad.reshape(scenes, TOK, D),
    )
    emb, normed, gl = [a.reshape(tokens, D) for a in (emb, normed, gl)]
    cols = cols.reshape(tokens, cols.shape[2])
    both = (normed, swap(normed, "group", group, 1), gl, swap(gl, "group", group, 1))

    layout = [(0, 0, 1)] + [(f, part, 2) for f in range(1, fars) for part in range(2)]
    packs, kept, coming, landing = [], [], [], []

    def first_leg(deps=()):
        send, keep = weight_grad_call(low, *both, packs[-1], dp, deps)
        kept.append(keep)
        coming.append(swap(send, "dp", dp, 1))
        return send

    def second_leg(n, deps):
        blocks = combine_call(high, kept[n], coming[n], dp // 2, BF16, deps)
        landing.append([blocks[0]] + [swap(blocks[j], "dp", dp, 2 * j) for j in range(1, dp // 2)])
        return blocks[-1]

    deps = ()
    for n, (f, part, parts) in enumerate(layout):
        packs.append(attention_call(both_counts, *both, weights[f], part, parts, deps))
        if n + 1 < len(layout):
            send = first_leg()
            deps = (send,) if n == 0 else (second_leg(n - 1, (send,)),)

    near = dp // 2 * 3 // 4
    back = back_call(layout, packs, flat, 1, False, F32, (coming[-1], *landing[-1][1:near]))
    back_far = swap(back, "group", group, 1)
    last = second_leg(len(layout) - 2, (back,))
    send = first_leg((last,))
    mixed = back_call(layout, packs, flat, 1, True, BF16, (send, *landing[-2][near:], *landing[-1][1:near]))
    mixed_far = swap(mixed, "group", group, 1)
    stem_send, stem_keep = tail_call(
        layout, core, back_far, emb, gl, cols, gain, packs, flat, (mixed, *landing[-1][near:])
    )
    output = output_call(layout, counts, mixed_far, emb, packs, flat, (stem_send, coming[-1]))
    stem_parts = halve_stem(stem_send, stem_keep, group, output)
    second_leg(len(layout) - 1, (stem_parts[-1],))
    grad_w_stem, stem_total = sum_stem(stem_parts, dp, group)
    shares = [add_call(parts) for parts in landing[:-1]] + [add_call(landing[-1], (stem_total,))]

    total = shares[0]
    for f in range(1, fars):
        parts = [swap(s, "group", group, 2 * f) for s, where in zip(shares, layout) if where[0] == f]
        size = width // len(parts)
        pieces = [p[:, c * size : (c + 1) * size] for c in range(4) for p in parts]
        total = total + jnp.concatenate(pieces, axis=1)
    grad_w_qkv = total[:, : 3 * width].reshape(total.shape[0], 3, width)
    grad_w_out = total[:, 3 * width :].T
    return (output.reshape(scenes, GROUPS, CAP, D), grad_w_stem, grad_w_qkv, grad_w_out)


def solution(mesh):
    sizes = dict(mesh.shape)
    return jax.shard_map(
        functools.partial(on_device, sizes["dp"], sizes["group"]),
        mesh=mesh,
        in_specs=(
            P(("dp", "group"), None, None),
            P(("dp", "group"), None, None),
            P(("dp", "group"), None),
            P(),
            P(),
            P("dp", None, "group"),
            P("group", "dp"),
            P(("dp", "group"), None, None, None),
        ),
        out_specs=(
            P(("dp", "group"), None, None, None),
            P(),
            P("dp", None, "group"),
            P("group", "dp"),
        ),
        check_vma=False,
    )
```

```python
import functools

import jax
import jax.numpy as jnp
import ml_dtypes
import numpy as np
from jax import lax
from jax.experimental import pallas as pl
from jax.experimental.pallas import tpu as pltpu
from jax.sharding import PartitionSpec as P

D = 1024
HD = 64
GROUPS = 3
CAP = 48
GRID = 12
PIX = 64
TOK = GROUPS * CAP
PAIR = 128
GROUP_BANDS = ((0, 4), (4, 8), (8, 10))
NORM_EPS = 1e-06
F32 = jnp.float32
BF16 = jnp.bfloat16
VMEM_LIMIT = 48 * 1024 * 1024


def dot_nn(a, b):
    return lax.dot_general(a, b, (((1,), (0,)), ((), ())), preferred_element_type=F32)


def dot_nt(a, b):
    return lax.dot_general(a, b, (((1,), (1,)), ((), ())), preferred_element_type=F32)


def dot_tn(a, b):
    return lax.dot_general(a, b, (((0,), (0,)), ((), ())), preferred_element_type=F32)


def live_column(c0, c1, c2):
    row = lax.broadcasted_iota(jnp.int32, (TOK, 1), 0)
    return (
        (row < c0)
        | ((row >= CAP) & (row < CAP + c1))
        | ((row >= 2 * CAP) & (row < 2 * CAP + c2))
    )


def params():
    return pltpu.CompilerParams(vmem_limit_bytes=VMEM_LIMIT)


def cost(flops, nbytes):
    return pl.CostEstimate(flops=int(flops / 1000), bytes_accessed=int(nbytes / 1000), transcendentals=0)


def stem_kernel(
    cnt_ref, idx_ref, patch_ref, w_ref, gain_ref, parts, genc_ref, og_ref,
    emb_ref, normed_ref, gl_ref, cols_ref,
):
    step = pl.program_id(0)
    scenes = patch_ref.shape[0]
    patch_iota = lax.broadcasted_iota(jnp.int32, (TOK, parts.shape[1]), 1)
    picked, placed = [], []
    for s in range(scenes):
        onehot = (idx_ref[s] == patch_iota).astype(F32).astype(BF16)
        picked.append(dot_nn(onehot, patch_ref[s]).astype(BF16))
        placed.append(
            (dot_nn(onehot, parts[0]) + dot_nn(onehot, parts[1])) + dot_nn(onehot, parts[2])
        )
        live = live_column(
            cnt_ref[step * scenes + s, 0], cnt_ref[step * scenes + s, 1], cnt_ref[step * scenes + s, 2]
        )
        gl_ref[s] = jnp.where(live, og_ref[s].astype(F32), 0.0).astype(BF16)
    for g, (start, end) in enumerate(GROUP_BANDS):
        rows = slice(g * CAP, (g + 1) * CAP)
        columns = jnp.concatenate([p[rows, start * PIX : end * PIX] for p in picked], axis=0)
        summed = dot_nn(columns, w_ref[start * PIX : end * PIX, :])
        width = (end - start) * PIX
        for s in range(scenes):
            values = summed[s * CAP : (s + 1) * CAP] + (placed[s][rows] + genc_ref[g : g + 1, :])
            emb = values.astype(BF16)
            emb_ref[s, rows, :] = emb
            x = emb.astype(F32)
            centre = jnp.mean(x, axis=-1, keepdims=True)
            dev = x - centre
            spread = jnp.mean(dev * dev, axis=-1, keepdims=True)
            centred = dev * lax.rsqrt(spread + NORM_EPS)
            normed_ref[s, rows, :] = (centred * gain_ref[...]).astype(BF16)
            cols_ref[s, rows, :width] = columns[s * CAP : (s + 1) * CAP]
            if width < cols_ref.shape[2]:
                cols_ref[s, rows, width:] = jnp.zeros((CAP, cols_ref.shape[2] - width), BF16)


def stem_call(counts, index_col, patches, w_stem, gain, table, genc, out_grad):
    scenes, patch_count, width = patches.shape
    block = 3 if scenes % 3 == 0 else 1
    col_width = max(e - s for s, e in GROUP_BANDS) * PIX
    per = lambda shape: pl.BlockSpec((block,) + shape, lambda i: (i, 0, 0))
    whole = lambda a: pl.BlockSpec(a.shape, lambda i: (0,) * a.ndim)
    rows = jax.ShapeDtypeStruct((scenes, TOK, D), BF16)
    return pl.pallas_call(
        stem_kernel,
        grid=(scenes // block,),
        in_specs=[
            pl.BlockSpec(memory_space=pltpu.SMEM),
            per((TOK, 1)),
            per((patch_count, width)),
            whole(w_stem),
            whole(gain),
            whole(table),
            whole(genc),
            per((TOK, D)),
        ],
        out_specs=[per((TOK, D)), per((TOK, D)), per((TOK, D)), per((TOK, col_width))],
        out_shape=[rows, rows, rows, jax.ShapeDtypeStruct((scenes, TOK, col_width), BF16)],
        compiler_params=params(),
        cost_estimate=cost(8e9, 12e6),
        name="stem_norm",
    )(counts, index_col, patches, w_stem, gain, table, genc, out_grad)


def attention_kernel(
    deps, cnt_ref, na_ref, nb_ref, ga_ref, gb_ref, wq_ref, wk_ref, wv_ref, wo_ref, *refs
):
    out_ref, n_s, g_s, qkv = refs[deps:]
    half, step = pl.program_id(0), pl.program_id(1)
    rows = n_s.shape[0]
    scenes = rows // TOK
    width = wq_ref.shape[1]

    @pl.when(half == 0)
    def _():
        n_s[...] = na_ref[...]
        g_s[...] = ga_ref[...]

    @pl.when(half != 0)
    def _():
        n_s[...] = nb_ref[...]
        g_s[...] = gb_ref[...]

    into = jnp.concatenate([wq_ref[...], wk_ref[...], wv_ref[...]], axis=1)
    qkv[:, : 3 * width] = dot_nn(n_s[...], into).astype(BF16)
    qkv[:, 3 * width :] = dot_nn(g_s[...], wo_ref[...]).astype(BF16)
    heads = width // HD
    lane = lax.broadcasted_iota(jnp.int32, (1, width), 1)
    masks = [(lane // HD == h).astype(F32).astype(BF16) for h in range(heads)]
    scale = jnp.asarray(HD ** (-0.5), BF16)
    first_of_pair = lax.broadcasted_iota(jnp.int32, (1, PAIR), 1) < HD

    def own_lanes(tall):
        tiles = []
        for t in range(width // PAIR):
            at = slice(t * PAIR, (t + 1) * PAIR)
            one = tall[2 * t * TOK : (2 * t + 1) * TOK, at]
            two = tall[(2 * t + 1) * TOK : (2 * t + 2) * TOK, at]
            tiles.append(jnp.where(first_of_pair, one, two))
        return jnp.concatenate(tiles, axis=1)

    def scene_body(s, _):
        base = pl.multiple_of(s * TOK, 16)
        at = pl.ds(base, TOK)
        scene = step * scenes + s
        live = live_column(cnt_ref[half, scene, 0], cnt_ref[half, scene, 1], cnt_ref[half, scene, 2])
        bias = jnp.where(live, 0.0, -1e30)
        q, k, v, dc = [qkv[at, c * width : (c + 1) * width] for c in range(4)]
        tall_q = jnp.concatenate([q * (m * scale) for m in masks], axis=0)
        tall_dc = jnp.concatenate([dc * m for m in masks], axis=0)
        scores = dot_nt(k, tall_q)
        grad_probs = dot_nt(v, tall_dc)
        probs_parts, score_parts = [], []
        for start in range(0, heads * TOK, PAIR):
            cols = slice(start, min(start + PAIR, heads * TOK))
            part = scores[:, cols] + bias
            lifted = jnp.exp(part - jnp.max(part, axis=0, keepdims=True))
            probs = lifted * (1.0 / jnp.sum(lifted, axis=0, keepdims=True))
            weighted = probs * grad_probs[:, cols]
            inner = jnp.sum(weighted, axis=0, keepdims=True)
            probs_parts.append(probs.astype(BF16))
            score_parts.append((weighted - probs * inner).astype(BF16))
        half_probs = jnp.concatenate(probs_parts, axis=1)
        grad_score = jnp.concatenate(score_parts, axis=1)
        out_ref[at, :width] = (own_lanes(dot_tn(grad_score, k)) * HD ** (-0.5)).astype(BF16)
        out_ref[at, width : 2 * width] = dot_nn(grad_score, tall_q).astype(BF16)
        out_ref[at, 2 * width : 3 * width] = dot_nn(half_probs, tall_dc).astype(BF16)
        out_ref[at, 3 * width :] = own_lanes(dot_tn(half_probs, v)).astype(BF16)
        return 0

    lax.fori_loop(0, scenes, scene_body, 0)


def block_rows(tokens):
    return 3 * TOK if tokens % (3 * TOK) == 0 else TOK


def two_halves(rows, steps):
    first = pl.BlockSpec((rows, D), lambda h, i: (jnp.where(h == 0, i, steps - 1), 0))
    second = pl.BlockSpec((rows, D), lambda h, i: (jnp.where(h == 0, 0, i), 0))
    return [first, second, first, second]


ANYWHERE = pl.BlockSpec(memory_space=pl.ANY)
SCALARS = pl.BlockSpec(memory_space=pltpu.SMEM)


def section(weights, c):
    each = 4 // len(weights)
    return weights[c // each], c % each


def attention_call(counts, na, nb, ga, gb, weights, deps=()):
    tokens = na.shape[0]
    rows = block_rows(tokens)
    steps = tokens // rows
    sections = [section(weights, c) for c in range(4)]
    width = weights[0].shape[1] * len(weights) // 4
    weight = lambda at: pl.BlockSpec((D, width), lambda h, i: (0, at))
    return pl.pallas_call(
        functools.partial(attention_kernel, len(deps)),
        grid=(2, steps),
        in_specs=[SCALARS] + two_halves(rows, steps) + [weight(at) for _, at in sections] + [ANYWHERE] * len(deps),
        out_specs=pl.BlockSpec((rows, 4 * width), lambda h, i: (h * steps + i, 0)),
        out_shape=jax.ShapeDtypeStruct((2 * tokens, 4 * width), BF16),
        scratch_shapes=[
            pltpu.VMEM((rows, D), BF16),
            pltpu.VMEM((rows, D), BF16),
            pltpu.VMEM((rows, 4 * width), BF16),
        ],
        compiler_params=params(),
        cost_estimate=cost(20e9, 14e6),
        name="attention",
    )(counts, na, nb, ga, gb, *[a for a, _ in sections], *deps)


def transpose_kernel(*refs):
    count = len(refs) // 2
    for ref, out_ref in zip(refs[:count], refs[count:]):
        out_ref[...] = ref[...].T


def transpose_call(arrays):
    shapes = [jax.ShapeDtypeStruct(a.shape[::-1], a.dtype) for a in arrays]
    return pl.pallas_call(
        transpose_kernel,
        out_shape=shapes,
        compiler_params=params(),
        cost_estimate=cost(4e9, 8e6),
        name="transpose_rows",
    )(*arrays)


def weight_grad_kernel(deps, blocks, low_ref, na_ref, nb_ref, ga_ref, gb_ref, pack_ref, *refs):
    send_ref, keep_ref, total = refs[deps:]
    section_at = pl.program_id(0)
    tokens = na_ref.shape[1]

    def product(a_ref, b_ref):
        total[...] = dot_nn(a_ref[...], pack_ref[:tokens, :]) + dot_nn(b_ref[...], pack_ref[tokens:, :])

    pl.when(section_at < 3)(lambda: product(na_ref, nb_ref))
    pl.when(section_at == 3)(lambda: product(ga_ref, gb_ref))
    rows = total.shape[0] // blocks
    low = low_ref[0]
    for b in range(blocks // 2):
        at = slice(b * rows, (b + 1) * rows)
        mine = pl.multiple_of((2 * b + low) * rows, rows)
        other = pl.multiple_of((2 * b + 1 - low) * rows, rows)
        keep_ref[at, :] = total[pl.ds(mine, rows), :]
        send_ref[at, :] = total[pl.ds(other, rows), :].astype(BF16)


def weight_grad_call(low, na, nb, ga, gb, pack, blocks, deps=()):
    width = pack.shape[1] // 4
    whole = pl.BlockSpec(na.shape, lambda c: (0, 0))
    out = pl.BlockSpec((D // 2, width), lambda c: (0, c))
    return pl.pallas_call(
        functools.partial(weight_grad_kernel, len(deps), blocks),
        grid=(4,),
        in_specs=[SCALARS]
        + [whole] * 4
        + [pl.BlockSpec((pack.shape[0], width), lambda c: (0, c))]
        + [ANYWHERE] * len(deps),
        out_specs=[out, out],
        out_shape=[
            jax.ShapeDtypeStruct((D // 2, 4 * width), BF16),
            jax.ShapeDtypeStruct((D // 2, 4 * width), F32),
        ],
        scratch_shapes=[pltpu.VMEM((D, width), F32)],
        compiler_params=params(),
        cost_estimate=cost(6e9, 12e6),
        name="weight_grad",
    )(low, na, nb, ga, gb, pack, *deps)


def combine_kernel(deps, place_ref, keep_ref, recv_ref, *refs):
    refs = refs[deps:]
    rows = refs[0].shape[0]
    place = place_ref[0]
    for j, ref in enumerate(refs):
        at = pl.ds(pl.multiple_of((place ^ j) * rows, rows), rows)
        ref[...] = (keep_ref[at, :] + recv_ref[at, :].astype(F32)).astype(ref.dtype)


def combine_call(place, keep, recv, blocks, dtype, deps=()):
    rows, cols = keep.shape[0] // blocks, keep.shape[1]
    whole = lambda a: pl.BlockSpec(a.shape, lambda: (0, 0))
    shapes = [jax.ShapeDtypeStruct((rows, cols), F32 if j == 0 else dtype) for j in range(blocks)]
    return pl.pallas_call(
        functools.partial(combine_kernel, len(deps)),
        in_specs=[SCALARS, whole(keep), whole(recv)] + [ANYWHERE] * len(deps),
        out_specs=[pl.BlockSpec((rows, cols), lambda: (0, 0))] * blocks,
        out_shape=shapes,
        compiler_params=params(),
        cost_estimate=cost(1e6, 5e6),
        name="combine",
    )(place, keep, recv, *deps)


def add_kernel(count, *refs):
    total = refs[0][...]
    for ref in refs[1:count]:
        total = total + ref[...].astype(F32)
    refs[-1][...] = total


def add_call(parts, deps=()):
    spec = pl.BlockSpec(parts[0].shape, lambda: (0, 0))
    return pl.pallas_call(
        functools.partial(add_kernel, len(parts)),
        in_specs=[spec] * len(parts) + [ANYWHERE] * len(deps),
        out_specs=spec,
        out_shape=jax.ShapeDtypeStruct(parts[0].shape, F32),
        compiler_params=params(),
        cost_estimate=cost(1e6, 2e6),
        name="add_parts",
    )(*parts, *deps)


def split_weights(counts, refs):
    out = []
    for count in counts:
        out.append(refs[:count])
        refs = refs[count:]
    return out, refs


def back_product(pack_refs, weight_refs, start, first, count):
    total = None
    for pack_ref, refs in zip(pack_refs, weight_refs):
        width = refs[0].shape[1] * len(refs) // 4
        for c in range(first, first + count):
            ref, at = section(refs, c)
            columns = pack_ref[:, (c - start) * width : (c - start + 1) * width]
            new = dot_nt(columns, ref[:, at * width : (at + 1) * width])
            total = new if total is None else total + new
    return total


def weight_specs(weights):
    return [pl.BlockSpec(w.shape, lambda i: (0, 0)) for block in weights for w in block]


def back_kernel(counts, *refs):
    packs = refs[: len(counts)]
    weights, refs = split_weights(counts, refs[len(counts) :])
    grad_ref, mixed_ref = refs[-2:]
    grad_ref[...] = back_product(packs, weights, 0, 0, 3)
    mixed_ref[...] = back_product(packs, weights, 0, 3, 1).astype(BF16)


def back_call(packs, weights, half, deps=()):
    tokens = packs[0].shape[0] // 2
    rows = block_rows(tokens)
    steps = tokens // rows
    out = pl.BlockSpec((rows, D), lambda i: (i, 0))
    return pl.pallas_call(
        functools.partial(back_kernel, [len(w) for w in weights]),
        grid=(steps,),
        in_specs=[pl.BlockSpec((rows, p.shape[1]), lambda i: (half * steps + i, 0)) for p in packs]
        + weight_specs(weights)
        + [ANYWHERE] * len(deps),
        out_specs=[out, out],
        out_shape=[jax.ShapeDtypeStruct((tokens, D), F32), jax.ShapeDtypeStruct((tokens, D), BF16)],
        compiler_params=params(),
        cost_estimate=cost(10e9, 12e6),
        name="back",
    )(*packs, *[w for block in weights for w in block], *deps)


def tail_kernel(counts, core_ref, recv_ref, emb_ref, gl_ref, cols_ref, gain_ref, *refs):
    packs = refs[: len(counts)]
    weights, refs = split_weights(counts, refs[len(counts) :])
    send_ref, keep_ref, acc = refs[-3:]
    step = pl.program_id(0)
    rows = emb_ref.shape[0]
    scenes = rows // TOK

    @pl.when(step == 0)
    def _():
        acc[...] = jnp.zeros_like(acc)

    grad_normed = recv_ref[...] + back_product(packs, weights, 0, 0, 3)
    x = emb_ref[...].astype(F32)
    dev = x - jnp.mean(x, axis=-1, keepdims=True)
    inv_std = lax.rsqrt(jnp.mean(dev * dev, axis=-1, keepdims=True) + NORM_EPS)
    centred = dev * inv_std
    scaled = grad_normed * gain_ref[...]
    first_mean = jnp.mean(scaled, axis=-1, keepdims=True)
    second_mean = jnp.mean(scaled * centred, axis=-1, keepdims=True)
    back = inv_std * (scaled - first_mean - centred * second_mean)
    grad_in = (gl_ref[...].astype(F32) + back).astype(BF16)
    for g, (start, end) in enumerate(GROUP_BANDS):
        at = [slice(s * TOK + g * CAP, s * TOK + (g + 1) * CAP) for s in range(scenes)]
        columns = jnp.concatenate([cols_ref[a, : (end - start) * PIX] for a in at], axis=0)
        grads = jnp.concatenate([grad_in[a] for a in at], axis=0)
        acc[start * PIX : end * PIX, :] += dot_tn(columns, grads)

    @pl.when(step == pl.num_programs(0) - 1)
    def _():
        size = keep_ref.shape[0]
        core = core_ref[0]
        keep_ref[...] = acc[pl.ds(pl.multiple_of(core * size, size), size), :]
        send_ref[...] = acc[pl.ds(pl.multiple_of((1 - core) * size, size), size), :]


def tail_call(core, recv, emb, gl, cols, gain, packs, weights, deps=()):
    tokens = emb.shape[0]
    rows = block_rows(tokens)
    per = lambda a: pl.BlockSpec((rows, a.shape[1]), lambda i: (i, 0))
    stem_rows = GROUP_BANDS[-1][1] * PIX
    half = jax.ShapeDtypeStruct((stem_rows // 2, D), F32)
    return pl.pallas_call(
        functools.partial(tail_kernel, [len(w) for w in weights]),
        grid=(tokens // rows,),
        in_specs=[SCALARS, per(recv), per(emb), per(gl), per(cols)]
        + [pl.BlockSpec(gain.shape, lambda i: (0, 0))]
        + [pl.BlockSpec((rows, 3 * (p.shape[1] // 4)), lambda i: (i, 0)) for p in packs]
        + weight_specs(weights)
        + [ANYWHERE] * len(deps),
        out_specs=[pl.BlockSpec(half.shape, lambda i: (0, 0))] * 2,
        out_shape=[half, half],
        scratch_shapes=[pltpu.VMEM((stem_rows, D), F32)],
        compiler_params=params(),
        cost_estimate=cost(10e9, 12e6),
        name="tail",
    )(core, recv, emb, gl, cols, gain, *packs, *[w for block in weights for w in block], *deps)


def output_kernel(counts, cnt_ref, recv_ref, emb_ref, *refs):
    packs, out_ref = refs[: len(counts)], refs[-1]
    weights, _ = split_weights(counts, refs[len(counts) :])
    step = pl.program_id(0)
    scenes = emb_ref.shape[0] // TOK
    mixed = recv_ref[...].astype(F32) + back_product(packs, weights, 3, 3, 1)
    total = emb_ref[...].astype(F32) + mixed
    for s in range(scenes):
        scene = step * scenes + s
        live = live_column(cnt_ref[scene, 0], cnt_ref[scene, 1], cnt_ref[scene, 2])
        at = slice(s * TOK, (s + 1) * TOK)
        out_ref[at, :] = jnp.where(live, total[at], 0.0).astype(BF16)


def output_call(counts, recv, emb, packs, weights, deps=()):
    tokens = emb.shape[0]
    rows = block_rows(tokens)
    per = lambda a: pl.BlockSpec((rows, a.shape[1]), lambda i: (i, 0))
    return pl.pallas_call(
        functools.partial(output_kernel, [len(w) for w in weights]),
        grid=(tokens // rows,),
        in_specs=[SCALARS, per(recv), per(emb)]
        + [pl.BlockSpec((rows, p.shape[1] // 4), lambda i: (i, 3)) for p in packs]
        + weight_specs(weights)
        + [ANYWHERE] * len(deps),
        out_specs=per(emb),
        out_shape=jax.ShapeDtypeStruct(emb.shape, BF16),
        compiler_params=params(),
        cost_estimate=cost(5e9, 10e6),
        name="layer_output",
    )(counts, recv, emb, *packs, *[w for block in weights for w in block], *deps)


def swap(x, axis, size, bit):
    return lax.ppermute(x, axis, [(i, i ^ bit) for i in range(size)])


def together(*values):
    return lax.optimization_barrier(values)


class Ring:
    def __init__(self, x, axis, size):
        self.axis, self.size, self.rows = axis, size, x.shape[0]
        order = list(range(0, size, 2)) + list(range(size - 1, 0, -2))
        self.forward = [(order[i], order[(i + 1) % size]) for i in range(size)]
        self.backward = [(order[(i + 1) % size], order[i]) for i in range(size)]
        me = lax.axis_index(axis)
        self.here = jnp.where(me % 2 == 0, me // 2, size - 1 - me // 2)
        self.moving = [x, x]
        self.full = jnp.zeros((size * self.rows,) + x.shape[1:], x.dtype)
        self.steps = 0
        self.put(x, 0)

    def put(self, block, distance):
        size = self.size
        at = (self.here + distance + size) % size
        owner = jnp.where(at < size // 2, 2 * at, 2 * (size - 1 - at) + 1)
        self.full = lax.dynamic_update_slice_in_dim(self.full, block, owner * self.rows, 0)

    def step(self, *beside):
        self.steps += 1
        moved = [lax.ppermute(self.moving[0], self.axis, self.forward)]
        if self.steps <= (self.size - 1) // 2:
            moved.append(lax.ppermute(self.moving[1], self.axis, self.backward))
        moved, beside = together(moved, beside)
        self.moving = moved
        self.put(moved[0], -self.steps)
        if len(moved) > 1:
            self.put(moved[1], self.steps)
        return beside


def line_up(pair, arrived, high):
    rows = pair.shape[0]
    full = jnp.zeros(((len(arrived) + 1) * rows,) + pair.shape[1:], pair.dtype)
    for j, block in enumerate([pair] + list(arrived)):
        full = lax.dynamic_update_slice_in_dim(full, block, (high ^ j) * rows, 0)
    return full


def halve_stem(recv, keep, group):
    mine = lax.axis_index("group") // 2 * 2 + lax.axis_index("dp") % 2
    return combine_call(mine.reshape(1), keep, recv, group // 2 * 2, F32)


def sum_stem(parts, beside, dp, group):
    core = lax.axis_index("group") % 2
    far = lax.axis_index("group") // 2
    low = lax.axis_index("dp") % 2
    high = lax.axis_index("dp") // 2
    fars, highs = group // 2, dp // 2
    mine = far * 2 + low
    small, width = parts[0].shape
    rows = 2 * fars * small

    def hop(block, f, b):
        if f:
            pairs = [
                (d * group + g, (d ^ b) * group + (g ^ (2 * f))) for d in range(dp) for g in range(group)
            ]
            return lax.ppermute(block, ("dp", "group"), pairs)
        return swap(block, "dp", dp, b)

    hops = [(k // 2, k % 2) for k in range(1, 2 * fars)]
    arrived, beside = together([hop(part, f, b) for part, (f, b) in zip(parts[1:], hops)], beside)
    total = parts[0]
    for part in arrived:
        total = total + part
    cols = width // highs
    part = lax.dynamic_slice_in_dim(total, high * cols, cols, 1)
    for j in range(1, highs):
        away = lax.dynamic_slice_in_dim(total, (high ^ j) * cols, cols, 1)
        part = part + swap(away, "dp", dp, 2 * j)
    part = part.astype(BF16)
    line = jnp.zeros((small, width), BF16)
    line = lax.dynamic_update_slice_in_dim(line, part, high * cols, 1)
    for j in range(1, highs):
        line = lax.dynamic_update_slice_in_dim(
            line, swap(part, "dp", dp, 2 * j), (high ^ j) * cols, 1
        )
    block = jnp.zeros((rows, width), BF16)
    block = lax.dynamic_update_slice_in_dim(block, line, mine * small, 0)
    for f, b in hops:
        target = (far ^ f) * 2 + (low ^ b)
        block = lax.dynamic_update_slice_in_dim(block, hop(line, f, b), target * small, 0)
    partner = swap(block, "group", group, 1)
    first = jnp.where(core == 0, block, partner)
    second = jnp.where(core == 0, partner, block)
    return jnp.concatenate([first, second], axis=0).astype(F32), beside


def encoding_tables(patch_count):
    quarter = D // 4
    half_width = D // 2
    power = lambda n: np.power(np.float32(10000.0), -np.arange(n, dtype=np.float32) / np.float32(n))
    at = np.arange(GRID).astype(np.float32)[:, None] * power(quarter)
    both = np.concatenate([np.sin(at), np.cos(at)], axis=-1)
    patch = np.arange(patch_count)
    rest = np.concatenate([both[patch // GRID], both[patch % GRID]], axis=-1).astype(np.float32)
    parts = []
    for _ in range(3):
        parts.append(rest.astype(ml_dtypes.bfloat16))
        rest = rest - parts[-1].astype(np.float32)
    group_at = np.arange(GROUPS).astype(np.float32)[:, None] * power(half_width)
    return np.stack(parts), np.concatenate([np.sin(group_at), np.cos(group_at)], axis=-1).astype(np.float32)


def on_device(dp, group, patches, vis_index, vis_count, w_stem, ln_gain, w_qkv, w_out, out_grad):
    scenes = patches.shape[0]
    tokens = scenes * TOK
    width = w_qkv.shape[2]
    fars = range(1, group // 2)
    rests = range(1, dp // 2)
    dp_low, dp_high = lax.axis_index("dp") % 2, lax.axis_index("dp") // 2
    low, high = dp_low.reshape(1), dp_high.reshape(1)
    core = (lax.axis_index("group") % 2).reshape(1)

    shard = jnp.concatenate([w_qkv.reshape(w_qkv.shape[0], 3 * width), w_out.T], axis=1)
    ring = Ring(shard, "dp", dp)
    far_shards = [swap(shard[:, 2 * width :], "group", group, 2 * f) for f in fars]
    counts = vis_count.astype(jnp.int32)
    counts_far = swap(counts, "group", group, 1)
    table, genc = encoding_tables(patches.shape[1])
    gain = ln_gain.reshape(1, D)
    stem = stem_call(
        counts,
        vis_index.reshape(scenes, TOK, 1),
        patches,
        w_stem,
        gain,
        jnp.asarray(table),
        jnp.asarray(genc),
        out_grad.reshape(scenes, TOK, D),
    )
    stem, far_shards, counts_far = ring.step(stem, far_shards, counts_far)
    emb, normed, gl = [a.reshape(tokens, D) for a in stem[:3]]
    cols = stem[3].reshape(tokens, stem[3].shape[2])
    both_counts = jnp.stack([counts, counts_far])
    both = [normed, swap(normed, "group", group, 1), gl, swap(gl, "group", group, 1)]
    partners = [swap(x, "dp", dp, 1) for x in far_shards]
    both, partners = ring.step(both, partners)
    (turned,) = ring.step(transpose_call(both))
    while ring.steps < dp // 2:
        ring.step()
    own = ring.full
    pairs = [
        jnp.concatenate([jnp.where(dp_low == 0, x, y), jnp.where(dp_low == 0, y, x)], axis=0)
        for x, y in zip(far_shards, partners)
    ]
    own, pairs = together(own, pairs)
    weights = [[own]]
    far_own = [swap(own[:, : 2 * width], "group", group, 2 * f) for f in fars]
    far_rest = [[swap(pair, "dp", dp, 2 * j) for j in rests] for pair in pairs]

    packs, kept, coming, landing = [], [], [], []

    def first_to_rest(n):
        return combine_call(high, kept[n], coming[n], dp // 2, BF16)

    def rest_swaps(blocks):
        return [blocks[0]] + [swap(blocks[j], "dp", dp, 2 * j) for j in rests]

    packs.extend(together(attention_call(both_counts, *both, weights[0])))
    for n in fars:
        send, keep = weight_grad_call(low, *turned, packs[-1], dp)
        if n == 1:
            send, keep, far_own, far_rest = together(send, keep, far_own, far_rest)
            for f in fars:
                weights.append([far_own[f - 1], line_up(pairs[f - 1], far_rest[f - 1], dp_high)])
        else:
            send, keep = together(send, keep)
        kept.append(keep)
        coming.append(swap(send, "dp", dp, 1))
        pack, coming[-1] = together(attention_call(both_counts, *both, weights[n]), coming[-1])
        packs.append(pack)
        blocks, packs = together(first_to_rest(n - 1), packs)
        landing.append(rest_swaps(blocks))
    back, mixed = together(*back_call(packs, weights, 1))
    back = swap(back, "group", group, 1)
    mixed = swap(mixed, "group", group, 1)
    send, keep = weight_grad_call(low, *turned, packs[-1], dp)
    send, keep, landing[-1][1] = together(send, keep, landing[-1][1])
    kept.append(keep)
    coming.append(swap(send, "dp", dp, 1))
    back, landing = together(back, landing)
    stem_send, stem_keep, mixed, coming[-1] = together(
        *tail_call(core, back, emb, gl, cols, gain, packs, weights), mixed, coming[-1]
    )
    stem_recv = swap(stem_send, "group", group, 1)
    last = rest_swaps(first_to_rest(-1))
    near = dp // 2 * 3 // 4
    output, stem_recv, last[:near] = together(
        output_call(counts, mixed, emb, packs, weights), stem_recv, last[:near]
    )
    stem_parts = halve_stem(stem_recv, stem_keep, group)
    grad_w_stem, last[near:] = sum_stem(stem_parts, last[near:], dp, group)
    shares = [add_call(parts) for parts in landing + [last]]

    total = shares[0]
    for f in fars:
        total = total + swap(shares[f], "group", group, 2 * f)
    grad_w_qkv = total[:, : 3 * width].reshape(total.shape[0], 3, width)
    grad_w_out = total[:, 3 * width :].T
    return (output.reshape(scenes, GROUPS, CAP, D), grad_w_stem, grad_w_qkv, grad_w_out)


def solution(mesh):
    sizes = dict(mesh.shape)
    return jax.shard_map(
        functools.partial(on_device, sizes["dp"], sizes["group"]),
        mesh=mesh,
        in_specs=(
            P(("dp", "group"), None, None),
            P(("dp", "group"), None, None),
            P(("dp", "group"), None),
            P(),
            P(),
            P("dp", None, "group"),
            P("group", "dp"),
            P(("dp", "group"), None, None, None),
        ),
        out_specs=(
            P(("dp", "group"), None, None, None),
            P(),
            P("dp", None, "group"),
            P("group", "dp"),
        ),
        check_vma=False,
    )
```

```python
import functools

import jax
import jax.numpy as jnp
import ml_dtypes
import numpy as np
from jax import lax
from jax.experimental import pallas as pl
from jax.experimental.pallas import tpu as pltpu
from jax.sharding import PartitionSpec as P

D = 1024
HD = 64
GROUPS = 3
CAP = 48
GRID = 12
PIX = 64
TOK = GROUPS * CAP
PAIR = 128
GROUP_BANDS = ((0, 4), (4, 8), (8, 10))
NORM_EPS = 1e-06
F32 = jnp.float32
BF16 = jnp.bfloat16
VMEM_LIMIT = 60 * 1024 * 1024


def dot_nn(a, b):
    return lax.dot_general(a, b, (((1,), (0,)), ((), ())), preferred_element_type=F32)


def dot_nt(a, b):
    return lax.dot_general(a, b, (((1,), (1,)), ((), ())), preferred_element_type=F32)


def dot_tn(a, b):
    return lax.dot_general(a, b, (((0,), (0,)), ((), ())), preferred_element_type=F32)


def live_column(c0, c1, c2):
    row = lax.broadcasted_iota(jnp.int32, (TOK, 1), 0)
    return (
        (row < c0)
        | ((row >= CAP) & (row < CAP + c1))
        | ((row >= 2 * CAP) & (row < 2 * CAP + c2))
    )


def params():
    return pltpu.CompilerParams(vmem_limit_bytes=VMEM_LIMIT)


def cost(flops, nbytes):
    return pl.CostEstimate(flops=int(flops / 1000), bytes_accessed=int(nbytes / 1000), transcendentals=0)


def stem_kernel(
    cnt_ref, idx_ref, patch_ref, w_ref, gain_ref, parts, genc_ref, og_ref,
    emb_ref, normed_ref, gl_ref, cols_ref,
):
    step = pl.program_id(0)
    scenes = patch_ref.shape[0]
    patch_iota = lax.broadcasted_iota(jnp.int32, (TOK, parts.shape[1]), 1)
    picked, placed = [], []
    for s in range(scenes):
        onehot = (idx_ref[s] == patch_iota).astype(F32).astype(BF16)
        picked.append(dot_nn(onehot, patch_ref[s]).astype(BF16))
        placed.append(
            (dot_nn(onehot, parts[0]) + dot_nn(onehot, parts[1])) + dot_nn(onehot, parts[2])
        )
        live = live_column(
            cnt_ref[step * scenes + s, 0], cnt_ref[step * scenes + s, 1], cnt_ref[step * scenes + s, 2]
        )
        gl_ref[s] = jnp.where(live, og_ref[s].astype(F32), 0.0).astype(BF16)
    for g, (start, end) in enumerate(GROUP_BANDS):
        rows = slice(g * CAP, (g + 1) * CAP)
        columns = jnp.concatenate([p[rows, start * PIX : end * PIX] for p in picked], axis=0)
        summed = dot_nn(columns, w_ref[start * PIX : end * PIX, :])
        width = (end - start) * PIX
        for s in range(scenes):
            values = summed[s * CAP : (s + 1) * CAP] + (placed[s][rows] + genc_ref[g : g + 1, :])
            emb = values.astype(BF16)
            emb_ref[s, rows, :] = emb
            x = emb.astype(F32)
            centre = jnp.mean(x, axis=-1, keepdims=True)
            dev = x - centre
            spread = jnp.mean(dev * dev, axis=-1, keepdims=True)
            centred = dev * lax.rsqrt(spread + NORM_EPS)
            normed_ref[s, rows, :] = (centred * gain_ref[...]).astype(BF16)
            cols_ref[s, rows, :width] = columns[s * CAP : (s + 1) * CAP]
            if width < cols_ref.shape[2]:
                cols_ref[s, rows, width:] = jnp.zeros((CAP, cols_ref.shape[2] - width), BF16)


def stem_call(counts, index_col, patches, w_stem, gain, table, genc, out_grad):
    scenes, patch_count, width = patches.shape
    block = 3 if scenes % 3 == 0 else 1
    col_width = max(e - s for s, e in GROUP_BANDS) * PIX
    per = lambda shape: pl.BlockSpec((block,) + shape, lambda i: (i, 0, 0))
    whole = lambda a: pl.BlockSpec(a.shape, lambda i: (0,) * a.ndim)
    rows = jax.ShapeDtypeStruct((scenes, TOK, D), BF16)
    return pl.pallas_call(
        stem_kernel,
        grid=(scenes // block,),
        in_specs=[
            pl.BlockSpec(memory_space=pltpu.SMEM),
            per((TOK, 1)),
            per((patch_count, width)),
            whole(w_stem),
            whole(gain),
            whole(table),
            whole(genc),
            per((TOK, D)),
        ],
        out_specs=[per((TOK, D)), per((TOK, D)), per((TOK, D)), per((TOK, col_width))],
        out_shape=[rows, rows, rows, jax.ShapeDtypeStruct((scenes, TOK, col_width), BF16)],
        compiler_params=params(),
        cost_estimate=cost(8e9, 12e6),
        name="stem_norm",
    )(counts, index_col, patches, w_stem, gain, table, genc, out_grad)


def attention_kernel(
    cnt_ref, owner_ref, na_ref, nb_ref, ga_ref, gb_ref, *refs
):
    blocks, (out_ref, w_ref, n_s, g_s, qkv) = refs[:-5], refs[-5:]
    half, step = pl.program_id(0), pl.program_id(1)
    rows = n_s.shape[0]
    scenes = rows // TOK
    width = w_ref.shape[1] // 4

    @pl.when((half == 0) & (step == 0))
    def _():
        size = blocks[0].shape[0]
        for b, block in enumerate(blocks):
            w_ref[pl.ds(pl.multiple_of(owner_ref[b] * size, size), size), :] = block[...]

    @pl.when(half == 0)
    def _():
        n_s[...] = na_ref[...]
        g_s[...] = ga_ref[...]

    @pl.when(half != 0)
    def _():
        n_s[...] = nb_ref[...]
        g_s[...] = gb_ref[...]

    qkv[:, : 3 * width] = dot_nn(n_s[...], w_ref[:, : 3 * width]).astype(BF16)
    qkv[:, 3 * width :] = dot_nn(g_s[...], w_ref[:, 3 * width :]).astype(BF16)
    heads = width // HD
    lane = lax.broadcasted_iota(jnp.int32, (1, width), 1)
    masks = [(lane // HD == h).astype(F32).astype(BF16) for h in range(heads)]
    scale = jnp.asarray(HD ** (-0.5), BF16)
    first_of_pair = lax.broadcasted_iota(jnp.int32, (1, PAIR), 1) < HD

    def own_lanes(tall):
        tiles = []
        for t in range(width // PAIR):
            at = slice(t * PAIR, (t + 1) * PAIR)
            one = tall[2 * t * TOK : (2 * t + 1) * TOK, at]
            two = tall[(2 * t + 1) * TOK : (2 * t + 2) * TOK, at]
            tiles.append(jnp.where(first_of_pair, one, two))
        return jnp.concatenate(tiles, axis=1)

    def scene_body(s, _):
        base = pl.multiple_of(s * TOK, 16)
        at = pl.ds(base, TOK)
        scene = step * scenes + s
        live = live_column(cnt_ref[half, scene, 0], cnt_ref[half, scene, 1], cnt_ref[half, scene, 2])
        bias = jnp.where(live, 0.0, -1e30)
        q, k, v, dc = [qkv[at, c * width : (c + 1) * width] for c in range(4)]
        tall_q = jnp.concatenate([q * (m * scale) for m in masks], axis=0)
        tall_dc = jnp.concatenate([dc * m for m in masks], axis=0)
        scores = dot_nt(k, tall_q)
        grad_probs = dot_nt(v, tall_dc)
        probs_parts, score_parts = [], []
        for start in range(0, heads * TOK, PAIR):
            cols = slice(start, min(start + PAIR, heads * TOK))
            part = scores[:, cols] + bias
            lifted = jnp.exp(part - jnp.max(part, axis=0, keepdims=True))
            probs = lifted * (1.0 / jnp.sum(lifted, axis=0, keepdims=True))
            weighted = probs * grad_probs[:, cols]
            inner = jnp.sum(weighted, axis=0, keepdims=True)
            probs_parts.append(probs.astype(BF16))
            score_parts.append((weighted - probs * inner).astype(BF16))
        half_probs = jnp.concatenate(probs_parts, axis=1)
        grad_score = jnp.concatenate(score_parts, axis=1)
        out_ref[at, :width] = (own_lanes(dot_tn(grad_score, k)) * HD ** (-0.5)).astype(BF16)
        out_ref[at, width : 2 * width] = dot_nn(grad_score, tall_q).astype(BF16)
        out_ref[at, 2 * width : 3 * width] = dot_nn(half_probs, tall_dc).astype(BF16)
        out_ref[at, 3 * width :] = own_lanes(dot_tn(half_probs, v)).astype(BF16)
        return 0

    lax.fori_loop(0, scenes, scene_body, 0, unroll=True)


def block_rows(tokens):
    return 3 * TOK if tokens % (3 * TOK) == 0 else TOK


def two_halves(rows, steps):
    first = pl.BlockSpec((rows, D), lambda h, i: (jnp.where(h == 0, i, steps - 1), 0))
    second = pl.BlockSpec((rows, D), lambda h, i: (jnp.where(h == 0, 0, i), 0))
    return [first, second, first, second]


ANYWHERE = pl.BlockSpec(memory_space=pl.ANY)
SCALARS = pl.BlockSpec(memory_space=pltpu.SMEM)


def attention_call(counts, owners, na, nb, ga, gb, blocks):
    tokens = na.shape[0]
    rows = block_rows(tokens)
    steps = tokens // rows
    cols = blocks[0].shape[1]
    whole = lambda a: pl.BlockSpec(a.shape, lambda h, i: (0, 0))
    return pl.pallas_call(
        attention_kernel,
        grid=(2, steps),
        in_specs=[SCALARS, SCALARS] + two_halves(rows, steps) + [whole(b) for b in blocks],
        out_specs=[
            pl.BlockSpec((rows, cols), lambda h, i: (h * steps + i, 0)),
            pl.BlockSpec((D, cols), lambda h, i: (0, 0)),
        ],
        out_shape=[
            jax.ShapeDtypeStruct((2 * tokens, cols), BF16),
            jax.ShapeDtypeStruct((D, cols), BF16),
        ],
        scratch_shapes=[
            pltpu.VMEM((rows, D), BF16),
            pltpu.VMEM((rows, D), BF16),
            pltpu.VMEM((rows, cols), BF16),
        ],
        compiler_params=params(),
        cost_estimate=cost(20e9, 14e6),
        name="attention",
    )(counts, owners, na, nb, ga, gb, *blocks)


def transpose_kernel(*refs):
    count = len(refs) // 2
    for ref, out_ref in zip(refs[:count], refs[count:]):
        out_ref[...] = ref[...].T


def transpose_call(arrays):
    shapes = [jax.ShapeDtypeStruct(a.shape[::-1], a.dtype) for a in arrays]
    return pl.pallas_call(
        transpose_kernel,
        out_shape=shapes,
        compiler_params=params(),
        cost_estimate=cost(4e9, 8e6),
        name="transpose_rows",
    )(*arrays)


def weight_grad_kernel(deps, blocks, low_ref, na_ref, nb_ref, ga_ref, gb_ref, pack_ref, *refs):
    send_ref, keep_ref, total = refs[deps:]
    section_at = pl.program_id(0)
    tokens = na_ref.shape[1]

    def product(a_ref, b_ref):
        total[...] = dot_nn(a_ref[...], pack_ref[:tokens, :]) + dot_nn(b_ref[...], pack_ref[tokens:, :])

    pl.when(section_at < 3)(lambda: product(na_ref, nb_ref))
    pl.when(section_at == 3)(lambda: product(ga_ref, gb_ref))
    rows = total.shape[0] // blocks
    low = low_ref[0]
    for b in range(blocks // 2):
        at = slice(b * rows, (b + 1) * rows)
        mine = pl.multiple_of((2 * b + low) * rows, rows)
        other = pl.multiple_of((2 * b + 1 - low) * rows, rows)
        keep_ref[at, :] = total[pl.ds(mine, rows), :]
        send_ref[at, :] = total[pl.ds(other, rows), :].astype(BF16)


def weight_grad_call(low, na, nb, ga, gb, pack, blocks, deps=()):
    width = pack.shape[1] // 4
    whole = pl.BlockSpec(na.shape, lambda c: (0, 0))
    out = pl.BlockSpec((D // 2, width), lambda c: (0, c))
    return pl.pallas_call(
        functools.partial(weight_grad_kernel, len(deps), blocks),
        grid=(4,),
        in_specs=[SCALARS]
        + [whole] * 4
        + [pl.BlockSpec((pack.shape[0], width), lambda c: (0, c))]
        + [ANYWHERE] * len(deps),
        out_specs=[out, out],
        out_shape=[
            jax.ShapeDtypeStruct((D // 2, 4 * width), BF16),
            jax.ShapeDtypeStruct((D // 2, 4 * width), F32),
        ],
        scratch_shapes=[pltpu.VMEM((D, width), F32)],
        compiler_params=params(),
        cost_estimate=cost(6e9, 12e6),
        name="weight_grad",
    )(low, na, nb, ga, gb, pack, *deps)


def combine_kernel(deps, place_ref, keep_ref, recv_ref, *refs):
    refs = refs[deps:]
    rows = refs[0].shape[0]
    place = place_ref[0]
    for j, ref in enumerate(refs):
        at = pl.ds(pl.multiple_of((place ^ j) * rows, rows), rows)
        ref[...] = (keep_ref[at, :] + recv_ref[at, :].astype(F32)).astype(ref.dtype)


def combine_call(place, keep, recv, blocks, dtype, deps=()):
    rows, cols = keep.shape[0] // blocks, keep.shape[1]
    whole = lambda a: pl.BlockSpec(a.shape, lambda: (0, 0))
    shapes = [jax.ShapeDtypeStruct((rows, cols), F32 if j == 0 else dtype) for j in range(blocks)]
    return pl.pallas_call(
        functools.partial(combine_kernel, len(deps)),
        in_specs=[SCALARS, whole(keep), whole(recv)] + [ANYWHERE] * len(deps),
        out_specs=[pl.BlockSpec((rows, cols), lambda: (0, 0))] * blocks,
        out_shape=shapes,
        compiler_params=params(),
        cost_estimate=cost(1e6, 5e6),
        name="combine",
    )(place, keep, recv, *deps)


def add_kernel(count, *refs):
    total = refs[0][...]
    for ref in refs[1:count]:
        total = total + ref[...].astype(F32)
    refs[-1][...] = total


def add_call(parts, deps=()):
    spec = pl.BlockSpec(parts[0].shape, lambda: (0, 0))
    return pl.pallas_call(
        functools.partial(add_kernel, len(parts)),
        in_specs=[spec] * len(parts) + [ANYWHERE] * len(deps),
        out_specs=spec,
        out_shape=jax.ShapeDtypeStruct(parts[0].shape, F32),
        compiler_params=params(),
        cost_estimate=cost(1e6, 2e6),
        name="add_parts",
    )(*parts, *deps)


def back_product(pack_refs, weight_refs, start, first, count):
    total = None
    for pack_ref, w_ref in zip(pack_refs, weight_refs):
        width = w_ref.shape[1] // 4
        columns = pack_ref[:, (first - start) * width : (first - start + count) * width]
        new = dot_nt(columns, w_ref[:, first * width : (first + count) * width])
        total = new if total is None else total + new
    return total


def weight_specs(weights):
    return [pl.BlockSpec(w.shape, lambda i: (0, 0)) for w in weights]


def back_kernel(count, *refs):
    packs, weights = refs[:count], refs[count : 2 * count]
    grad_ref, mixed_ref = refs[-2:]
    grad_ref[...] = back_product(packs, weights, 0, 0, 3)
    mixed_ref[...] = back_product(packs, weights, 0, 3, 1).astype(BF16)


def back_call(packs, weights, half, deps=()):
    tokens = packs[0].shape[0] // 2
    rows = block_rows(tokens)
    steps = tokens // rows
    out = pl.BlockSpec((rows, D), lambda i: (i, 0))
    return pl.pallas_call(
        functools.partial(back_kernel, len(packs)),
        grid=(steps,),
        in_specs=[pl.BlockSpec((rows, p.shape[1]), lambda i: (half * steps + i, 0)) for p in packs]
        + weight_specs(weights)
        + [ANYWHERE] * len(deps),
        out_specs=[out, out],
        out_shape=[jax.ShapeDtypeStruct((tokens, D), F32), jax.ShapeDtypeStruct((tokens, D), BF16)],
        compiler_params=params(),
        cost_estimate=cost(10e9, 12e6),
        name="back",
    )(*packs, *weights, *deps)


def tail_kernel(count, core_ref, recv_ref, emb_ref, gl_ref, cols_ref, gain_ref, *refs):
    packs, weights = refs[:count], refs[count : 2 * count]
    send_ref, keep_ref, acc = refs[-3:]
    step = pl.program_id(0)
    rows = emb_ref.shape[0]
    scenes = rows // TOK

    @pl.when(step == 0)
    def _():
        acc[...] = jnp.zeros_like(acc)

    grad_normed = recv_ref[...] + back_product(packs, weights, 0, 0, 3)
    x = emb_ref[...].astype(F32)
    dev = x - jnp.mean(x, axis=-1, keepdims=True)
    inv_std = lax.rsqrt(jnp.mean(dev * dev, axis=-1, keepdims=True) + NORM_EPS)
    centred = dev * inv_std
    scaled = grad_normed * gain_ref[...]
    first_mean = jnp.mean(scaled, axis=-1, keepdims=True)
    second_mean = jnp.mean(scaled * centred, axis=-1, keepdims=True)
    back = inv_std * (scaled - first_mean - centred * second_mean)
    grad_in = (gl_ref[...].astype(F32) + back).astype(BF16)
    for g, (start, end) in enumerate(GROUP_BANDS):
        at = [slice(s * TOK + g * CAP, s * TOK + (g + 1) * CAP) for s in range(scenes)]
        columns = jnp.concatenate([cols_ref[a, : (end - start) * PIX] for a in at], axis=0)
        grads = jnp.concatenate([grad_in[a] for a in at], axis=0)
        acc[start * PIX : end * PIX, :] += dot_tn(columns, grads)

    @pl.when(step == pl.num_programs(0) - 1)
    def _():
        size = keep_ref.shape[0]
        core = core_ref[0]
        keep_ref[...] = acc[pl.ds(pl.multiple_of(core * size, size), size), :]
        send_ref[...] = acc[pl.ds(pl.multiple_of((1 - core) * size, size), size), :]


def tail_call(core, recv, emb, gl, cols, gain, packs, weights, deps=()):
    tokens = emb.shape[0]
    rows = block_rows(tokens)
    per = lambda a: pl.BlockSpec((rows, a.shape[1]), lambda i: (i, 0))
    stem_rows = GROUP_BANDS[-1][1] * PIX
    half = jax.ShapeDtypeStruct((stem_rows // 2, D), F32)
    return pl.pallas_call(
        functools.partial(tail_kernel, len(packs)),
        grid=(tokens // rows,),
        in_specs=[SCALARS, per(recv), per(emb), per(gl), per(cols)]
        + [pl.BlockSpec(gain.shape, lambda i: (0, 0))]
        + [pl.BlockSpec((rows, 3 * (p.shape[1] // 4)), lambda i: (i, 0)) for p in packs]
        + weight_specs(weights)
        + [ANYWHERE] * len(deps),
        out_specs=[pl.BlockSpec(half.shape, lambda i: (0, 0))] * 2,
        out_shape=[half, half],
        scratch_shapes=[pltpu.VMEM((stem_rows, D), F32)],
        compiler_params=params(),
        cost_estimate=cost(10e9, 12e6),
        name="tail",
    )(core, recv, emb, gl, cols, gain, *packs, *weights, *deps)


def output_kernel(count, cnt_ref, recv_ref, emb_ref, *refs):
    packs, weights, out_ref = refs[:count], refs[count : 2 * count], refs[-1]
    step = pl.program_id(0)
    scenes = emb_ref.shape[0] // TOK
    mixed = recv_ref[...].astype(F32) + back_product(packs, weights, 3, 3, 1)
    total = emb_ref[...].astype(F32) + mixed
    for s in range(scenes):
        scene = step * scenes + s
        live = live_column(cnt_ref[scene, 0], cnt_ref[scene, 1], cnt_ref[scene, 2])
        at = slice(s * TOK, (s + 1) * TOK)
        out_ref[at, :] = jnp.where(live, total[at], 0.0).astype(BF16)


def output_call(counts, recv, emb, packs, weights, deps=()):
    tokens = emb.shape[0]
    rows = block_rows(tokens)
    per = lambda a: pl.BlockSpec((rows, a.shape[1]), lambda i: (i, 0))
    return pl.pallas_call(
        functools.partial(output_kernel, len(packs)),
        grid=(tokens // rows,),
        in_specs=[SCALARS, per(recv), per(emb)]
        + [pl.BlockSpec((rows, p.shape[1] // 4), lambda i: (i, 3)) for p in packs]
        + weight_specs(weights)
        + [ANYWHERE] * len(deps),
        out_specs=per(emb),
        out_shape=jax.ShapeDtypeStruct(emb.shape, BF16),
        compiler_params=params(),
        cost_estimate=cost(5e9, 10e6),
        name="layer_output",
    )(counts, recv, emb, *packs, *weights, *deps)


def swap(x, axis, size, bit):
    return lax.ppermute(x, axis, [(i, i ^ bit) for i in range(size)])


def together(*values):
    return lax.optimization_barrier(values)


class Ring:
    def __init__(self, x, axis, size):
        self.axis, self.size = axis, size
        order = list(range(0, size, 2)) + list(range(size - 1, 0, -2))
        self.forward = [(order[i], order[(i + 1) % size]) for i in range(size)]
        self.backward = [(order[(i + 1) % size], order[i]) for i in range(size)]
        self.ahead, self.behind = [x], [x]

    def step(self, *beside):
        ahead = lax.ppermute(self.ahead[-1], self.axis, self.forward)
        if len(self.behind) <= (self.size - 1) // 2:
            behind = lax.ppermute(self.behind[-1], self.axis, self.backward)
            ahead, behind, beside = together(ahead, behind, beside)
            self.behind.append(behind)
        else:
            ahead, beside = together(ahead, beside)
        self.ahead.append(ahead)
        return beside

    def owners(self):
        size = self.size
        me = lax.axis_index(self.axis)
        here = jnp.where(me % 2 == 0, me // 2, size - 1 - me // 2)
        distances = [-s for s in range(len(self.ahead))] + list(range(1, len(self.behind)))
        at = (here + size + jnp.array(distances, jnp.int32)) % size
        return jnp.where(at < size // 2, 2 * at, 2 * (size - 1 - at) + 1)


def halve_stem(recv, keep, group):
    mine = lax.axis_index("group") // 2 * 2 + lax.axis_index("dp") % 2
    return combine_call(mine.reshape(1), keep, recv, group // 2 * 2, F32)


def sum_stem(parts, beside, dp, group):
    core = lax.axis_index("group") % 2
    far = lax.axis_index("group") // 2
    low = lax.axis_index("dp") % 2
    high = lax.axis_index("dp") // 2
    fars, highs = group // 2, dp // 2
    mine = far * 2 + low
    small, width = parts[0].shape
    rows = 2 * fars * small

    def hop(block, f, b):
        if f:
            pairs = [
                (d * group + g, (d ^ b) * group + (g ^ (2 * f))) for d in range(dp) for g in range(group)
            ]
            return lax.ppermute(block, ("dp", "group"), pairs)
        return swap(block, "dp", dp, b)

    hops = [(k // 2, k % 2) for k in range(1, 2 * fars)]
    arrived = [hop(part, f, b) for part, (f, b) in zip(parts[1:], hops)]
    beside = beside()
    arrived, beside[:2] = together(arrived, beside[:2])
    near = (len(beside) + 2) // 2
    total = parts[0]
    for part in arrived:
        total = total + part
    cols = width // highs
    part = lax.dynamic_slice_in_dim(total, high * cols, cols, 1)
    away = [lax.dynamic_slice_in_dim(total, (high ^ j) * cols, cols, 1) for j in range(1, highs)]
    arrived = [swap(a, "dp", dp, 2 * (j + 1)) for j, a in enumerate(away)]
    arrived, beside[:near] = together(arrived, beside[:near])
    for block in arrived:
        part = part + block
    part = part.astype(BF16)
    line = jnp.zeros((small, width), BF16)
    line = lax.dynamic_update_slice_in_dim(line, part, high * cols, 1)
    arrived = [swap(part, "dp", dp, 2 * j) for j in range(1, highs)]
    arrived, beside = together(arrived, beside)
    for j, block in enumerate(arrived):
        line = lax.dynamic_update_slice_in_dim(line, block, (high ^ (j + 1)) * cols, 1)
    block = jnp.zeros((rows, width), BF16)
    block = lax.dynamic_update_slice_in_dim(block, line, mine * small, 0)
    for f, b in hops:
        target = (far ^ f) * 2 + (low ^ b)
        block = lax.dynamic_update_slice_in_dim(block, hop(line, f, b), target * small, 0)
    partner = swap(block, "group", group, 1)
    first = jnp.where(core == 0, block, partner)
    second = jnp.where(core == 0, partner, block)
    return jnp.concatenate([first, second], axis=0).astype(F32), beside


def encoding_tables(patch_count):
    quarter = D // 4
    half_width = D // 2
    power = lambda n: np.power(np.float32(10000.0), -np.arange(n, dtype=np.float32) / np.float32(n))
    at = np.arange(GRID).astype(np.float32)[:, None] * power(quarter)
    both = np.concatenate([np.sin(at), np.cos(at)], axis=-1)
    patch = np.arange(patch_count)
    rest = np.concatenate([both[patch // GRID], both[patch % GRID]], axis=-1).astype(np.float32)
    parts = []
    for _ in range(3):
        parts.append(rest.astype(ml_dtypes.bfloat16))
        rest = rest - parts[-1].astype(np.float32)
    group_at = np.arange(GROUPS).astype(np.float32)[:, None] * power(half_width)
    return np.stack(parts), np.concatenate([np.sin(group_at), np.cos(group_at)], axis=-1).astype(np.float32)


def on_device(dp, group, patches, vis_index, vis_count, w_stem, ln_gain, w_qkv, w_out, out_grad):
    scenes = patches.shape[0]
    tokens = scenes * TOK
    width = w_qkv.shape[2]
    fars = range(1, group // 2)
    rests = range(1, dp // 2)
    dp_low, dp_high = lax.axis_index("dp") % 2, lax.axis_index("dp") // 2
    low, high = dp_low.reshape(1), dp_high.reshape(1)
    core = (lax.axis_index("group") % 2).reshape(1)

    shard = jnp.concatenate([w_qkv.reshape(w_qkv.shape[0], 3 * width), w_out.T], axis=1)
    ring = Ring(shard, "dp", dp)
    cross = lambda x: [swap(x, "group", group, 2 * f) for f in fars]
    far = [cross(shard)]
    counts = vis_count.astype(jnp.int32)
    counts_far = swap(counts, "group", group, 1)
    table, genc = encoding_tables(patches.shape[1])
    gain = ln_gain.reshape(1, D)
    stem = stem_call(
        counts,
        vis_index.reshape(scenes, TOK, 1),
        patches,
        w_stem,
        gain,
        jnp.asarray(table),
        jnp.asarray(genc),
        out_grad.reshape(scenes, TOK, D),
    )
    stem, counts_far = ring.step(stem, counts_far)
    emb, normed, gl = [a.reshape(tokens, D) for a in stem[:3]]
    cols = stem[3].reshape(tokens, stem[3].shape[2])
    both_counts = jnp.stack([counts, counts_far])
    both = [normed, swap(normed, "group", group, 1), gl, swap(gl, "group", group, 1)]
    far.append(cross(ring.ahead[-1]))
    both, far[0] = ring.step(both, far[0])
    while len(ring.ahead) < dp // 2:
        far.append(cross(ring.ahead[-1]))
        (far[-2],) = ring.step(far[-2])
    far.append(cross(ring.ahead[-1]))
    turned, far[-2:] = ring.step(transpose_call(both), far[-2:])
    far.append(cross(ring.ahead[-1]))
    behind = ring.behind[1:]
    far.append(cross(jnp.concatenate(behind, axis=0)))
    owners = ring.owners()

    packs, kept, coming, landing = [], [], [], []

    def first_to_rest(n):
        return combine_call(high, kept[n], coming[n], dp // 2, BF16)

    def rest_swaps(blocks):
        return [blocks[0]] + [swap(blocks[j], "dp", dp, 2 * j) for j in rests]

    weights = []
    for n in range(group // 2):
        if n == 0:
            blocks = ring.ahead + behind
        else:
            rows = shard.shape[0]
            last = [far[-1][n - 1][b * rows : (b + 1) * rows] for b in range(len(behind))]
            blocks = [f[n - 1] for f in far[:-1]] + last
        made = attention_call(both_counts, owners, *both, blocks)
        if n == 0:
            pack, weight = together(*made)
        else:
            pack, weight, coming[-1] = together(*made, coming[-1])
        packs.append(pack)
        weights.append(weight)
        if n == len(fars):
            break
        send, keep = weight_grad_call(low, *turned, pack, dp)
        if n == 0:
            send, keep, far[-2:] = together(send, keep, far[-2:])
        else:
            send, keep = together(send, keep)
        kept.append(keep)
        coming.append(swap(send, "dp", dp, 1))
    back, mixed = together(*back_call(packs, weights, 1))
    back = swap(back, "group", group, 1)
    mixed = swap(mixed, "group", group, 1)
    near = dp // 2 * 3 // 4
    for n in range(len(fars)):
        landing.append(rest_swaps(first_to_rest(n)))
    send, keep = weight_grad_call(low, *turned, packs[-1], dp)
    send, keep, back, landing[-1][:near] = together(send, keep, back, landing[-1][:near])
    kept.append(keep)
    coming.append(swap(send, "dp", dp, 1))
    stem_send, stem_keep, mixed, landing = together(
        *tail_call(core, back, emb, gl, cols, gain, packs, weights), mixed, landing
    )
    cols = stem_send.shape[1] // 2
    stem_recv = [swap(stem_send[:, c * cols : (c + 1) * cols], "group", group, 1) for c in range(2)]
    output, stem_recv, coming[-1] = together(
        output_call(counts, mixed, emb, packs, weights), stem_recv, coming[-1]
    )
    stem_parts = halve_stem(jnp.concatenate(stem_recv, axis=1), stem_keep, group)
    grad_w_stem, last = sum_stem(stem_parts, lambda: rest_swaps(first_to_rest(-1)), dp, group)
    shares = [add_call(parts) for parts in landing + [last]]

    total = shares[0]
    for f in fars:
        total = total + swap(shares[f], "group", group, 2 * f)
    grad_w_qkv = total[:, : 3 * width].reshape(total.shape[0], 3, width)
    grad_w_out = total[:, 3 * width :].T
    return (output.reshape(scenes, GROUPS, CAP, D), grad_w_stem, grad_w_qkv, grad_w_out)


def solution(mesh):
    sizes = dict(mesh.shape)
    return jax.shard_map(
        functools.partial(on_device, sizes["dp"], sizes["group"]),
        mesh=mesh,
        in_specs=(
            P(("dp", "group"), None, None),
            P(("dp", "group"), None, None),
            P(("dp", "group"), None),
            P(),
            P(),
            P("dp", None, "group"),
            P("group", "dp"),
            P(("dp", "group"), None, None, None),
        ),
        out_specs=(
            P(("dp", "group"), None, None, None),
            P(),
            P("dp", None, "group"),
            P("group", "dp"),
        ),
        check_vma=False,
    )
```

```python
import functools

import jax
import jax.numpy as jnp
import ml_dtypes
import numpy as np
from jax import lax
from jax.experimental import pallas as pl
from jax.experimental.pallas import tpu as pltpu
from jax.sharding import PartitionSpec as P

D = 1024
HD = 64
GROUPS = 3
CAP = 48
GRID = 12
PIX = 64
TOK = GROUPS * CAP
PAIR = 128
GROUP_BANDS = ((0, 4), (4, 8), (8, 10))
NORM_EPS = 1e-06
F32 = jnp.float32
BF16 = jnp.bfloat16
VMEM_LIMIT = 36 * 1024 * 1024


def dot_nn(a, b):
    return lax.dot_general(a, b, (((1,), (0,)), ((), ())), preferred_element_type=F32)


def dot_nt(a, b):
    return lax.dot_general(a, b, (((1,), (1,)), ((), ())), preferred_element_type=F32)


def dot_tn(a, b):
    return lax.dot_general(a, b, (((0,), (0,)), ((), ())), preferred_element_type=F32)


def live_column(c0, c1, c2):
    row = lax.broadcasted_iota(jnp.int32, (TOK, 1), 0)
    return (
        (row < c0)
        | ((row >= CAP) & (row < CAP + c1))
        | ((row >= 2 * CAP) & (row < 2 * CAP + c2))
    )


def params():
    return pltpu.CompilerParams(vmem_limit_bytes=VMEM_LIMIT)


def cost(flops, nbytes):
    return pl.CostEstimate(flops=int(flops / 1000), bytes_accessed=int(nbytes / 1000), transcendentals=0)


def stem_kernel(
    cnt_ref, idx_ref, patch_ref, w_ref, gain_ref, parts, genc_ref, og_ref,
    emb_ref, normed_ref, gl_ref, cols_ref,
):
    step = pl.program_id(0)
    scenes = patch_ref.shape[0]
    patch_iota = lax.broadcasted_iota(jnp.int32, (parts.shape[1], CAP), 0)
    slot = lax.broadcasted_iota(jnp.int32, (CAP, 1), 0)
    for g, (start, end) in enumerate(GROUP_BANDS):
        rows = slice(g * CAP, (g + 1) * CAP)
        width = (end - start) * PIX
        picked, placed = [], []
        for s in range(scenes):
            onehot = (idx_ref[s, g : g + 1, :] == patch_iota).astype(F32).astype(BF16).T
            picked.append(dot_nn(onehot, patch_ref[s, :, start * PIX : end * PIX]).astype(BF16))
            placed.append(
                (dot_nn(onehot, parts[0]) + dot_nn(onehot, parts[1])) + dot_nn(onehot, parts[2])
            )
            live = slot < cnt_ref[step * scenes + s, g]
            gl_ref[s, rows, :] = jnp.where(live, og_ref[s, rows, :].astype(F32), 0.0).astype(BF16)
        summed = dot_nn(jnp.concatenate(picked, axis=0), w_ref[start * PIX : end * PIX, :])
        for s in range(scenes):
            values = summed[s * CAP : (s + 1) * CAP] + (placed[s] + genc_ref[g : g + 1, :])
            emb = values.astype(BF16)
            emb_ref[s, rows, :] = emb
            x = emb.astype(F32)
            centre = jnp.mean(x, axis=-1, keepdims=True)
            dev = x - centre
            spread = jnp.mean(dev * dev, axis=-1, keepdims=True)
            centred = dev * lax.rsqrt(spread + NORM_EPS)
            normed_ref[s, rows, :] = (centred * gain_ref[...]).astype(BF16)
            cols_ref[s, rows, :width] = picked[s]
            if width < cols_ref.shape[2]:
                cols_ref[s, rows, width:] = jnp.zeros((CAP, cols_ref.shape[2] - width), BF16)


def stem_call(counts, index, patches, w_stem, gain, table, genc, out_grad):
    scenes, patch_count, width = patches.shape
    block = 3 if scenes % 3 == 0 else 1
    col_width = max(e - s for s, e in GROUP_BANDS) * PIX
    per = lambda shape: pl.BlockSpec((block,) + shape, lambda i: (i, 0, 0))
    whole = lambda a: pl.BlockSpec(a.shape, lambda i: (0,) * a.ndim)
    rows = jax.ShapeDtypeStruct((scenes, TOK, D), BF16)
    return pl.pallas_call(
        stem_kernel,
        grid=(scenes // block,),
        in_specs=[
            pl.BlockSpec(memory_space=pltpu.SMEM),
            per((GROUPS, CAP)),
            per((patch_count, width)),
            whole(w_stem),
            whole(gain),
            whole(table),
            whole(genc),
            per((TOK, D)),
        ],
        out_specs=[per((TOK, D)), per((TOK, D)), per((TOK, D)), per((TOK, col_width))],
        out_shape=[rows, rows, rows, jax.ShapeDtypeStruct((scenes, TOK, col_width), BF16)],
        compiler_params=params(),
        cost_estimate=cost(8e9, 12e6),
        name="stem_norm",
    )(counts, index, patches, w_stem, gain, table, genc, out_grad)


def attention_kernel(first, cnt_ref, owner_ref, na_ref, nb_ref, ga_ref, gb_ref, *refs):
    before, refs = refs[: 0 if first else 2], refs[0 if first else 2 :]
    blocks, (out_ref, w_ref, back_own_ref, back_far_ref, n_s, g_s, qkv) = refs[:-7], refs[-7:]
    half, step = pl.program_id(0), pl.program_id(1)
    rows = n_s.shape[0]
    scenes = rows // TOK
    width = w_ref.shape[1] // 4

    @pl.when((half == 0) & (step == 0))
    def _():
        size = blocks[0].shape[0]
        for b, block in enumerate(blocks):
            w_ref[pl.ds(pl.multiple_of(owner_ref[b] * size, size), size), :] = block[...]

    @pl.when(half == 0)
    def _():
        n_s[...] = na_ref[...]
        g_s[...] = ga_ref[...]

    @pl.when(half != 0)
    def _():
        n_s[...] = nb_ref[...]
        g_s[...] = gb_ref[...]

    qkv[:, : 3 * width] = dot_nn(n_s[...], w_ref[:, : 3 * width]).astype(BF16)
    qkv[:, 3 * width :] = dot_nn(g_s[...], w_ref[:, 3 * width :]).astype(BF16)
    heads = width // HD
    lane = lax.broadcasted_iota(jnp.int32, (1, width), 1)
    masks = [(lane // HD == h).astype(F32).astype(BF16) for h in range(heads)]
    scale = jnp.asarray(HD ** (-0.5), BF16)
    first_of_pair = lax.broadcasted_iota(jnp.int32, (1, PAIR), 1) < HD

    def own_lanes(tall):
        tiles = []
        for t in range(width // PAIR):
            at = slice(t * PAIR, (t + 1) * PAIR)
            one = tall[2 * t * TOK : (2 * t + 1) * TOK, at]
            two = tall[(2 * t + 1) * TOK : (2 * t + 2) * TOK, at]
            tiles.append(jnp.where(first_of_pair, one, two))
        return jnp.concatenate(tiles, axis=1)

    def scene_body(s, _):
        base = pl.multiple_of(s * TOK, 16)
        at = pl.ds(base, TOK)
        scene = step * scenes + s
        live = live_column(cnt_ref[half, scene, 0], cnt_ref[half, scene, 1], cnt_ref[half, scene, 2])
        bias = jnp.where(live, 0.0, -1e30)
        q, k, v, dc = [qkv[at, c * width : (c + 1) * width] for c in range(4)]
        tall_q = jnp.concatenate([q * (m * scale) for m in masks], axis=0)
        tall_dc = jnp.concatenate([dc * m for m in masks], axis=0)
        scores = dot_nt(k, tall_q)
        grad_probs = dot_nt(v, tall_dc)
        probs_parts, score_parts = [], []
        for start in range(0, heads * TOK, PAIR):
            cols = slice(start, min(start + PAIR, heads * TOK))
            part = scores[:, cols] + bias
            lifted = jnp.exp(part - jnp.max(part, axis=0, keepdims=True))
            probs = lifted * (1.0 / jnp.sum(lifted, axis=0, keepdims=True))
            weighted = probs * grad_probs[:, cols]
            inner = jnp.sum(weighted, axis=0, keepdims=True)
            probs_parts.append(probs.astype(BF16))
            score_parts.append((weighted - probs * inner).astype(BF16))
        half_probs = jnp.concatenate(probs_parts, axis=1)
        grad_score = jnp.concatenate(score_parts, axis=1)
        out_ref[at, :width] = (own_lanes(dot_tn(grad_score, k)) * HD ** (-0.5)).astype(BF16)
        out_ref[at, width : 2 * width] = dot_nn(grad_score, tall_q).astype(BF16)
        out_ref[at, 2 * width : 3 * width] = dot_nn(half_probs, tall_dc).astype(BF16)
        out_ref[at, 3 * width :] = own_lanes(dot_tn(half_probs, v)).astype(BF16)
        return 0

    lax.fori_loop(0, scenes, scene_body, 0, unroll=True)
    back = dot_nt(out_ref[:, : 3 * width], w_ref[:, : 3 * width])

    @pl.when(half == 0)
    def _():
        back_own_ref[...] = back if first else before[0][...] + back

    @pl.when(half != 0)
    def _():
        back_far_ref[...] = back if first else before[1][...] + back


def block_rows(tokens):
    return 3 * TOK if tokens % (3 * TOK) == 0 else TOK


def two_halves(rows, steps):
    first = pl.BlockSpec((rows, D), lambda h, i: (jnp.where(h == 0, i, steps - 1), 0))
    second = pl.BlockSpec((rows, D), lambda h, i: (jnp.where(h == 0, 0, i), 0))
    return [first, second, first, second]


SCALARS = pl.BlockSpec(memory_space=pltpu.SMEM)


def attention_call(counts, owners, na, nb, ga, gb, before, blocks):
    tokens = na.shape[0]
    rows = block_rows(tokens)
    steps = tokens // rows
    cols = blocks[0].shape[1]
    whole = lambda a: pl.BlockSpec(a.shape, lambda h, i: (0, 0))
    halves = two_halves(rows, steps)
    return pl.pallas_call(
        functools.partial(attention_kernel, not before),
        grid=(2, steps),
        in_specs=[SCALARS, SCALARS] + halves + halves[: len(before)] + [whole(b) for b in blocks],
        out_specs=[
            pl.BlockSpec((rows, cols), lambda h, i: (h * steps + i, 0)),
            pl.BlockSpec((D, cols), lambda h, i: (0, 0)),
        ]
        + halves[:2],
        out_shape=[
            jax.ShapeDtypeStruct((2 * tokens, cols), BF16),
            jax.ShapeDtypeStruct((D, cols), BF16),
            jax.ShapeDtypeStruct((tokens, D), F32),
            jax.ShapeDtypeStruct((tokens, D), F32),
        ],
        scratch_shapes=[
            pltpu.VMEM((rows, D), BF16),
            pltpu.VMEM((rows, D), BF16),
            pltpu.VMEM((rows, cols), BF16),
        ],
        compiler_params=params(),
        cost_estimate=cost(20e9, 14e6),
        name="attention",
    )(counts, owners, na, nb, ga, gb, *before, *blocks)


def transpose_kernel(*refs):
    out_ref = refs[-1]
    for k, ref in enumerate(refs[:-1]):

        @pl.when(pl.program_id(0) == k)
        def _():
            out_ref[0] = ref[...].T


def transpose_call(arrays):
    rows, cols = arrays[0].shape
    return pl.pallas_call(
        transpose_kernel,
        grid=(len(arrays),),
        in_specs=[pl.BlockSpec((rows, cols), lambda i: (0, 0))] * len(arrays),
        out_specs=pl.BlockSpec((1, cols, rows), lambda i: (i, 0, 0)),
        out_shape=jax.ShapeDtypeStruct((len(arrays), cols, rows), BF16),
        compiler_params=params(),
        cost_estimate=cost(4e9, 8e6),
        name="transpose_rows",
    )(*arrays)


def weight_grad_kernel(blocks, low_ref, turned_ref, pack_ref, keep_ref, *refs):
    sends, total = refs[:-1], refs[-1]
    step = pl.program_id(0)
    width = pack_ref.shape[1] // 4
    parts = [slice(0, 3 * width), slice(3 * width, 4 * width)]
    for k in range(4):

        @pl.when(step == k)
        def _():
            new = dot_nn(turned_ref[0], pack_ref[:, parts[k % 2]])
            total[:, parts[k % 2]] = new if k < 2 else total[:, parts[k % 2]] + new

    @pl.when(step == 3)
    def _():
        rows = total.shape[0] // blocks
        low = low_ref[0]
        for b in range(blocks // 2):
            at = slice(b * rows, (b + 1) * rows)
            mine = pl.multiple_of((2 * b + low) * rows, rows)
            other = pl.multiple_of((2 * b + 1 - low) * rows, rows)
            keep_ref[at, :] = total[pl.ds(mine, rows), :]
            for c, send_ref in enumerate(sends):
                cols = send_ref.shape[1]
                send_ref[at, :] = total[pl.ds(other, rows), c * cols : (c + 1) * cols].astype(BF16)


def weight_grad_call(low, turned, pack, blocks):
    tokens, cols = pack.shape
    out = lambda cols: pl.BlockSpec((D // 2, cols), lambda i: (0, 0))
    send = jax.ShapeDtypeStruct((D // 2, cols // 2), BF16)
    return pl.pallas_call(
        functools.partial(weight_grad_kernel, blocks),
        grid=(4,),
        in_specs=[
            SCALARS,
            pl.BlockSpec((1,) + turned.shape[1:], lambda i: (i, 0, 0)),
            pl.BlockSpec((tokens // 2, cols), lambda i: (i // 2, 0)),
        ],
        out_specs=[out(cols), out(cols // 2), out(cols // 2)],
        out_shape=[jax.ShapeDtypeStruct((D // 2, cols), F32), send, send],
        scratch_shapes=[pltpu.VMEM((D, cols), F32)],
        compiler_params=params(),
        cost_estimate=cost(6e9, 12e6),
        name="weight_grad",
    )(low, turned, pack)


def combine_kernel(pieces, place_ref, keep_ref, *refs):
    recvs, refs = refs[:pieces], refs[pieces:]
    rows = refs[0].shape[0]
    place = place_ref[0]
    for j, ref in enumerate(refs):
        at = pl.ds(pl.multiple_of((place ^ j) * rows, rows), rows)
        start = 0
        for recv_ref in recvs:
            cols = slice(start, start + recv_ref.shape[1])
            ref[:, cols] = (keep_ref[at, cols] + recv_ref[at, :].astype(F32)).astype(ref.dtype)
            start = cols.stop


def combine_call(place, keep, recvs, blocks, dtype):
    rows, cols = keep.shape[0] // blocks, keep.shape[1]
    whole = lambda a: pl.BlockSpec(a.shape, lambda: (0, 0))
    shapes = [jax.ShapeDtypeStruct((rows, cols), F32 if j == 0 else dtype) for j in range(blocks)]
    return pl.pallas_call(
        functools.partial(combine_kernel, len(recvs)),
        in_specs=[SCALARS, whole(keep)] + [whole(r) for r in recvs],
        out_specs=[pl.BlockSpec((rows, cols), lambda: (0, 0))] * blocks,
        out_shape=shapes,
        compiler_params=params(),
        cost_estimate=cost(1e6, 5e6),
        name="combine",
    )(place, keep, *recvs)


def add_kernel(count, *refs):
    total = refs[0][...]
    for ref in refs[1:count]:
        total = total + ref[...].astype(F32)
    refs[-1][...] = total


def add_call(parts):
    spec = pl.BlockSpec(parts[0].shape, lambda: (0, 0))
    return pl.pallas_call(
        functools.partial(add_kernel, len(parts)),
        in_specs=[spec] * len(parts),
        out_specs=spec,
        out_shape=jax.ShapeDtypeStruct(parts[0].shape, F32),
        compiler_params=params(),
        cost_estimate=cost(1e6, 2e6),
        name="add_parts",
    )(*parts)


def mixed_product(context_refs, weight_refs):
    total = None
    for context_ref, w_ref in zip(context_refs, weight_refs):
        new = dot_nt(context_ref[...], w_ref[...])
        total = new if total is None else total + new
    return total


def context_specs(rows, packs, weights, first):
    width = packs[0].shape[1] // 4
    return [pl.BlockSpec((rows, width), lambda i: (first + i, 3))] * len(packs) + [
        pl.BlockSpec((D, width), lambda i: (0, 3))
    ] * len(weights)


def mixed_kernel(count, *refs):
    refs[-1][...] = mixed_product(refs[:count], refs[count : 2 * count]).astype(BF16)


def mixed_call(packs, weights):
    tokens = packs[0].shape[0] // 2
    rows = block_rows(tokens)
    return pl.pallas_call(
        functools.partial(mixed_kernel, len(packs)),
        grid=(tokens // rows,),
        in_specs=context_specs(rows, packs, weights, tokens // rows),
        out_specs=pl.BlockSpec((rows, D), lambda i: (i, 0)),
        out_shape=jax.ShapeDtypeStruct((tokens, D), BF16),
        compiler_params=params(),
        cost_estimate=cost(2e9, 5e6),
        name="mixed",
    )(*packs, *weights)


def tail_kernel(core_ref, own_ref, recv_ref, emb_ref, gl_ref, cols_ref, gain_ref, send_ref, keep_ref, acc):
    step = pl.program_id(0)
    rows = emb_ref.shape[0]
    scenes = rows // TOK

    @pl.when(step == 0)
    def _():
        acc[...] = jnp.zeros_like(acc)

    grad_normed = own_ref[...] + recv_ref[...]
    x = emb_ref[...].astype(F32)
    dev = x - jnp.mean(x, axis=-1, keepdims=True)
    inv_std = lax.rsqrt(jnp.mean(dev * dev, axis=-1, keepdims=True) + NORM_EPS)
    centred = dev * inv_std
    scaled = grad_normed * gain_ref[...]
    first_mean = jnp.mean(scaled, axis=-1, keepdims=True)
    second_mean = jnp.mean(scaled * centred, axis=-1, keepdims=True)
    back = inv_std * (scaled - first_mean - centred * second_mean)
    grad_in = (gl_ref[...].astype(F32) + back).astype(BF16)
    for g, (start, end) in enumerate(GROUP_BANDS):
        at = [slice(s * TOK + g * CAP, s * TOK + (g + 1) * CAP) for s in range(scenes)]
        columns = jnp.concatenate([cols_ref[a, : (end - start) * PIX] for a in at], axis=0)
        grads = jnp.concatenate([grad_in[a] for a in at], axis=0)
        acc[start * PIX : end * PIX, :] += dot_tn(columns, grads)

    @pl.when(step == pl.num_programs(0) - 1)
    def _():
        size = keep_ref.shape[0]
        core = core_ref[0]
        keep_ref[...] = acc[pl.ds(pl.multiple_of(core * size, size), size), :]
        send_ref[...] = acc[pl.ds(pl.multiple_of((1 - core) * size, size), size), :]


def tail_call(core, own, recv, emb, gl, cols, gain):
    tokens = emb.shape[0]
    rows = 2 * TOK if tokens % (2 * TOK) == 0 else TOK
    per = lambda a: pl.BlockSpec((rows, a.shape[1]), lambda i: (i, 0))
    stem_rows = GROUP_BANDS[-1][1] * PIX
    half = jax.ShapeDtypeStruct((stem_rows // 2, D), F32)
    return pl.pallas_call(
        tail_kernel,
        grid=(tokens // rows,),
        in_specs=[SCALARS, per(own), per(recv), per(emb), per(gl), per(cols)]
        + [pl.BlockSpec(gain.shape, lambda i: (0, 0))],
        out_specs=[pl.BlockSpec(half.shape, lambda i: (0, 0))] * 2,
        out_shape=[half, half],
        scratch_shapes=[pltpu.VMEM((stem_rows, D), F32)],
        compiler_params=params(),
        cost_estimate=cost(10e9, 12e6),
        name="tail",
    )(core, own, recv, emb, gl, cols, gain)


def output_kernel(count, cnt_ref, recv_ref, emb_ref, *refs):
    out_ref = refs[-1]
    step = pl.program_id(0)
    scenes = emb_ref.shape[0] // TOK
    mixed = recv_ref[...].astype(F32) + mixed_product(refs[:count], refs[count : 2 * count])
    total = emb_ref[...].astype(F32) + mixed
    for s in range(scenes):
        scene = step * scenes + s
        live = live_column(cnt_ref[scene, 0], cnt_ref[scene, 1], cnt_ref[scene, 2])
        at = slice(s * TOK, (s + 1) * TOK)
        out_ref[at, :] = jnp.where(live, total[at], 0.0).astype(BF16)


def output_call(counts, recv, emb, packs, weights):
    tokens = emb.shape[0]
    rows = block_rows(tokens)
    per = lambda a: pl.BlockSpec((rows, a.shape[1]), lambda i: (i, 0))
    return pl.pallas_call(
        functools.partial(output_kernel, len(packs)),
        grid=(tokens // rows,),
        in_specs=[SCALARS, per(recv), per(emb)]
        + context_specs(rows, packs, weights, 0),
        out_specs=per(emb),
        out_shape=jax.ShapeDtypeStruct(emb.shape, BF16),
        compiler_params=params(),
        cost_estimate=cost(5e9, 10e6),
        name="layer_output",
    )(counts, recv, emb, *packs, *weights)


def swap(x, axis, size, bit):
    return lax.ppermute(x, axis, [(i, i ^ bit) for i in range(size)])


def together(*values):
    return lax.optimization_barrier(values)


class Ring:
    def __init__(self, x, axis, size):
        self.axis, self.size = axis, size
        order = list(range(0, size, 2)) + list(range(size - 1, 0, -2))
        self.forward = [(order[i], order[(i + 1) % size]) for i in range(size)]
        self.backward = [(order[(i + 1) % size], order[i]) for i in range(size)]
        self.ahead, self.behind = [x], [x]

    def step(self, *beside):
        ahead = lax.ppermute(self.ahead[-1], self.axis, self.forward)
        if len(self.behind) <= (self.size - 1) // 2:
            behind = lax.ppermute(self.behind[-1], self.axis, self.backward)
            ahead, behind, beside = together(ahead, behind, beside)
            self.behind.append(behind)
        else:
            ahead, beside = together(ahead, beside)
        self.ahead.append(ahead)
        return beside

    def owners(self):
        size = self.size
        me = lax.axis_index(self.axis)
        here = jnp.where(me % 2 == 0, me // 2, size - 1 - me // 2)
        distances = [-s for s in range(len(self.ahead))] + list(range(1, len(self.behind)))
        at = (here + size + jnp.array(distances, jnp.int32)) % size
        return jnp.where(at < size // 2, 2 * at, 2 * (size - 1 - at) + 1)


def halve_stem(recv, keep, group):
    mine = lax.axis_index("group") // 2 * 2 + lax.axis_index("dp") % 2
    return combine_call(mine.reshape(1), keep, recv, group // 2 * 2, F32)


def sum_stem(parts, beside, dp, group):
    core = lax.axis_index("group") % 2
    far = lax.axis_index("group") // 2
    low = lax.axis_index("dp") % 2
    high = lax.axis_index("dp") // 2
    fars, highs = group // 2, dp // 2
    mine = far * 2 + low
    small, width = parts[0].shape
    rows = 2 * fars * small

    def hop(block, f, b):
        if f:
            pairs = [
                (d * group + g, (d ^ b) * group + (g ^ (2 * f))) for d in range(dp) for g in range(group)
            ]
            return lax.ppermute(block, ("dp", "group"), pairs)
        return swap(block, "dp", dp, b)

    hops = [(k // 2, k % 2) for k in range(1, 2 * fars)]
    arrived = [hop(part, f, b) for part, (f, b) in zip(parts[1:], hops)]
    beside = beside()
    arrived, beside[:3] = together(arrived, beside[:3])
    near = (len(beside) + 3) // 2
    total = parts[0]
    for part in arrived:
        total = total + part
    cols = width // highs
    part = lax.dynamic_slice_in_dim(total, high * cols, cols, 1)
    away = [lax.dynamic_slice_in_dim(total, (high ^ j) * cols, cols, 1) for j in range(1, highs)]
    arrived = [swap(a, "dp", dp, 2 * (j + 1)) for j, a in enumerate(away)]
    arrived, beside[:near] = together(arrived, beside[:near])
    for block in arrived:
        part = part + block
    part = part.astype(BF16)
    line = jnp.zeros((small, width), BF16)
    line = lax.dynamic_update_slice_in_dim(line, part, high * cols, 1)
    arrived = [swap(part, "dp", dp, 2 * j) for j in range(1, highs)]
    arrived, beside = together(arrived, beside)
    for j, block in enumerate(arrived):
        line = lax.dynamic_update_slice_in_dim(line, block, (high ^ (j + 1)) * cols, 1)
    block = jnp.zeros((rows, width), BF16)
    block = lax.dynamic_update_slice_in_dim(block, line, mine * small, 0)
    for f, b in hops:
        target = (far ^ f) * 2 + (low ^ b)
        block = lax.dynamic_update_slice_in_dim(block, hop(line, f, b), target * small, 0)
    partner = swap(block, "group", group, 1)
    first = jnp.where(core == 0, block, partner)
    second = jnp.where(core == 0, partner, block)
    return jnp.concatenate([first, second], axis=0).astype(F32), beside


def encoding_tables(patch_count):
    quarter = D // 4
    half_width = D // 2
    power = lambda n: np.power(np.float32(10000.0), -np.arange(n, dtype=np.float32) / np.float32(n))
    at = np.arange(GRID).astype(np.float32)[:, None] * power(quarter)
    both = np.concatenate([np.sin(at), np.cos(at)], axis=-1)
    patch = np.arange(patch_count)
    rest = np.concatenate([both[patch // GRID], both[patch % GRID]], axis=-1).astype(np.float32)
    parts = []
    for _ in range(3):
        parts.append(rest.astype(ml_dtypes.bfloat16))
        rest = rest - parts[-1].astype(np.float32)
    group_at = np.arange(GROUPS).astype(np.float32)[:, None] * power(half_width)
    return np.stack(parts), np.concatenate([np.sin(group_at), np.cos(group_at)], axis=-1).astype(np.float32)


def on_device(dp, group, patches, vis_index, vis_count, w_stem, ln_gain, w_qkv, w_out, out_grad):
    scenes = patches.shape[0]
    tokens = scenes * TOK
    width = w_qkv.shape[2]
    fars = range(1, group // 2)
    rests = range(1, dp // 2)
    dp_low, dp_high = lax.axis_index("dp") % 2, lax.axis_index("dp") // 2
    low, high = dp_low.reshape(1), dp_high.reshape(1)
    core = (lax.axis_index("group") % 2).reshape(1)

    shard = jnp.concatenate([w_qkv.reshape(w_qkv.shape[0], 3 * width), w_out.T], axis=1)
    ring = Ring(shard, "dp", dp)
    cross = lambda x: [swap(x, "group", group, 2 * f) for f in fars]
    far = [cross(shard)]
    counts = vis_count.astype(jnp.int32)
    counts_far = swap(counts, "group", group, 1)
    table, genc = encoding_tables(patches.shape[1])
    gain = ln_gain.reshape(1, D)
    stem = stem_call(
        counts,
        vis_index,
        patches,
        w_stem,
        gain,
        jnp.asarray(table),
        jnp.asarray(genc),
        out_grad.reshape(scenes, TOK, D),
    )
    stem, counts_far = ring.step(stem, counts_far)
    emb, normed, gl = [a.reshape(tokens, D) for a in stem[:3]]
    cols = stem[3].reshape(tokens, stem[3].shape[2])
    both_counts = jnp.stack([counts, counts_far])
    both = [normed, swap(normed, "group", group, 1), gl, swap(gl, "group", group, 1)]
    far.append(cross(ring.ahead[-1]))
    both, far[0] = ring.step(both, far[0])
    while len(ring.ahead) < dp // 2:
        far.append(cross(ring.ahead[-1]))
        (far[-2],) = ring.step(far[-2])
    far.append(cross(ring.ahead[-1]))
    turned, far[-2] = ring.step(transpose_call([both[0], both[2], both[1], both[3]]), far[-2])
    ring.ahead, ring.behind = together(ring.ahead, ring.behind)
    far.append(cross(ring.ahead[-1]))
    behind = ring.behind[1:]
    far.append(cross(jnp.concatenate(behind, axis=0)))
    owners = ring.owners()

    packs, kept, coming, landing = [], [], [], []

    def first_to_rest(n):
        return combine_call(high, kept[n], coming[n], dp // 2, BF16)

    def rest_swaps(blocks):
        return [blocks[0]] + [swap(blocks[j], "dp", dp, 2 * j) for j in rests]

    weights, back = [], []
    for n in range(group // 2):
        if n == 0:
            blocks = ring.ahead + behind
        else:
            rows = shard.shape[0]
            last = [far[-1][n - 1][b * rows : (b + 1) * rows] for b in range(len(behind))]
            blocks = [f[n - 1] for f in far[:-1]] + last
        made = attention_call(both_counts, owners, *both, back, blocks)
        if n == 0:
            pack, weight, *back = together(*made)
        else:
            pack, weight, *back, coming[-1] = together(*made, coming[-1])
        packs.append(pack)
        weights.append(weight)
        if n == len(fars):
            back_far = swap(back[1], "group", group, 1)
        keep, *send = weight_grad_call(low, turned, pack, dp)
        if n == 0:
            send, keep, far[-3:] = together(send, keep, far[-3:])
        if n == len(fars):
            send, keep, back_far, kept, coming = together(send, keep, back_far, kept, coming)
        kept.append(keep)
        coming.append([swap(x, "dp", dp, 1) for x in send])
    blocks, back_far = together([first_to_rest(n) for n in range(len(fars))], back_far)
    landing = [rest_swaps(b) for b in blocks]
    near = dp // 2 * 3 // 4
    stem_send, stem_keep, landing[-1][:near], coming[-1][0] = together(
        *tail_call(core, back[0], back_far, emb, gl, cols, gain), landing[-1][:near], coming[-1][0]
    )
    half = stem_send.shape[1] // 2
    stem_recv = [swap(stem_send[:, c * half : (c + 1) * half], "group", group, 1) for c in range(2)]
    mixed, stem_recv, landing, coming = together(mixed_call(packs, weights), stem_recv, landing, coming)
    mixed = swap(mixed, "group", group, 1)
    stem_parts = halve_stem(stem_recv, stem_keep, group)

    def beside():
        last = rest_swaps(first_to_rest(-1))
        output = output_call(counts, mixed, emb, packs, weights)
        return [output] + last

    grad_w_stem, (output, *last) = sum_stem(stem_parts, beside, dp, group)
    shares = [add_call(parts) for parts in landing + [last]]

    total = shares[0]
    for f in fars:
        total = total + swap(shares[f], "group", group, 2 * f)
    grad_w_qkv = total[:, : 3 * width].reshape(total.shape[0], 3, width)
    grad_w_out = total[:, 3 * width :].T
    return (output.reshape(scenes, GROUPS, CAP, D), grad_w_stem, grad_w_qkv, grad_w_out)


def solution(mesh):
    sizes = dict(mesh.shape)
    return jax.shard_map(
        functools.partial(on_device, sizes["dp"], sizes["group"]),
        mesh=mesh,
        in_specs=(
            P(("dp", "group"), None, None),
            P(("dp", "group"), None, None),
            P(("dp", "group"), None),
            P(),
            P(),
            P("dp", None, "group"),
            P("group", "dp"),
            P(("dp", "group"), None, None, None),
        ),
        out_specs=(
            P(("dp", "group"), None, None, None),
            P(),
            P("dp", None, "group"),
            P("group", "dp"),
        ),
        check_vma=False,
    )
```

```python
import functools

import jax
import jax.numpy as jnp
import ml_dtypes
import numpy as np
from jax import lax
from jax.experimental import pallas as pl
from jax.experimental.pallas import tpu as pltpu
from jax.sharding import PartitionSpec as P

D = 1024
HD = 64
GROUPS = 3
CAP = 48
GRID = 12
PIX = 64
TOK = GROUPS * CAP
PAIR = 128
GROUP_BANDS = ((0, 4), (4, 8), (8, 10))
NORM_EPS = 1e-06
F32 = jnp.float32
BF16 = jnp.bfloat16
VMEM_LIMIT = 60 * 1024 * 1024


def dot_nn(a, b):
    return lax.dot_general(a, b, (((1,), (0,)), ((), ())), preferred_element_type=F32)


def dot_nt(a, b):
    return lax.dot_general(a, b, (((1,), (1,)), ((), ())), preferred_element_type=F32)


def dot_tn(a, b):
    return lax.dot_general(a, b, (((0,), (0,)), ((), ())), preferred_element_type=F32)


def live_column(c0, c1, c2):
    row = lax.broadcasted_iota(jnp.int32, (TOK, 1), 0)
    return (
        (row < c0)
        | ((row >= CAP) & (row < CAP + c1))
        | ((row >= 2 * CAP) & (row < 2 * CAP + c2))
    )


def params():
    return pltpu.CompilerParams(vmem_limit_bytes=VMEM_LIMIT)


def cost(flops, nbytes):
    return pl.CostEstimate(flops=int(flops / 1000), bytes_accessed=int(nbytes / 1000), transcendentals=0)


def stem_kernel(
    cnt_ref, idx_ref, patch_ref, w_ref, gain_ref, parts, genc_ref, og_ref,
    emb_ref, normed_ref, gl_ref, cols_ref,
):
    step = pl.program_id(0)
    scenes = patch_ref.shape[0]
    patch_iota = lax.broadcasted_iota(jnp.int32, (parts.shape[1], CAP), 0)
    slot = lax.broadcasted_iota(jnp.int32, (CAP, 1), 0)
    for g, (start, end) in enumerate(GROUP_BANDS):
        rows = slice(g * CAP, (g + 1) * CAP)
        width = (end - start) * PIX
        picked, placed = [], []
        for s in range(scenes):
            onehot = (idx_ref[s, g : g + 1, :] == patch_iota).astype(F32).astype(BF16).T
            picked.append(dot_nn(onehot, patch_ref[s, :, start * PIX : end * PIX]).astype(BF16))
            placed.append(
                (dot_nn(onehot, parts[0]) + dot_nn(onehot, parts[1])) + dot_nn(onehot, parts[2])
            )
            live = slot < cnt_ref[step * scenes + s, g]
            gl_ref[s, rows, :] = jnp.where(live, og_ref[s, rows, :].astype(F32), 0.0).astype(BF16)
        summed = dot_nn(jnp.concatenate(picked, axis=0), w_ref[start * PIX : end * PIX, :])
        for s in range(scenes):
            values = summed[s * CAP : (s + 1) * CAP] + (placed[s] + genc_ref[g : g + 1, :])
            emb = values.astype(BF16)
            emb_ref[s, rows, :] = emb
            x = emb.astype(F32)
            centre = jnp.mean(x, axis=-1, keepdims=True)
            dev = x - centre
            spread = jnp.mean(dev * dev, axis=-1, keepdims=True)
            centred = dev * lax.rsqrt(spread + NORM_EPS)
            normed_ref[s, rows, :] = (centred * gain_ref[...]).astype(BF16)
            cols_ref[s, rows, :width] = picked[s]
            if width < cols_ref.shape[2]:
                cols_ref[s, rows, width:] = jnp.zeros((CAP, cols_ref.shape[2] - width), BF16)


def stem_call(counts, index, patches, w_stem, gain, table, genc, out_grad):
    scenes, patch_count, width = patches.shape
    block = 2 if scenes % 2 == 0 else 1
    col_width = max(e - s for s, e in GROUP_BANDS) * PIX
    per = lambda shape: pl.BlockSpec((block,) + shape, lambda i: (i, 0, 0))
    whole = lambda a: pl.BlockSpec(a.shape, lambda i: (0,) * a.ndim)
    rows = jax.ShapeDtypeStruct((scenes, TOK, D), BF16)
    return pl.pallas_call(
        stem_kernel,
        grid=(scenes // block,),
        in_specs=[
            pl.BlockSpec(memory_space=pltpu.SMEM),
            per((GROUPS, CAP)),
            per((patch_count, width)),
            whole(w_stem),
            whole(gain),
            whole(table),
            whole(genc),
            per((TOK, D)),
        ],
        out_specs=[per((TOK, D)), per((TOK, D)), per((TOK, D)), per((TOK, col_width))],
        out_shape=[rows, rows, rows, jax.ShapeDtypeStruct((scenes, TOK, col_width), BF16)],
        compiler_params=params(),
        cost_estimate=cost(8e9, 12e6),
        name="stem_norm",
    )(counts, index, patches, w_stem, gain, table, genc, out_grad)


def attention_kernel(first, cnt_ref, owner_ref, na_ref, nb_ref, ga_ref, gb_ref, *refs):
    before, refs = refs[: 0 if first else 2], refs[0 if first else 2 :]
    blocks, (out_ref, w_ref, back_own_ref, back_far_ref, n_s, g_s, qkv) = refs[:-7], refs[-7:]
    half, step = pl.program_id(0), pl.program_id(1)
    rows = n_s.shape[0]
    scenes = rows // TOK
    width = w_ref.shape[1] // 4

    @pl.when((half == 0) & (step == 0))
    def _():
        size = blocks[0].shape[0]
        for b, block in enumerate(blocks):
            w_ref[pl.ds(pl.multiple_of(owner_ref[b] * size, size), size), :] = block[...]

    @pl.when(half == 0)
    def _():
        n_s[...] = na_ref[...]
        g_s[...] = ga_ref[...]

    @pl.when(half != 0)
    def _():
        n_s[...] = nb_ref[...]
        g_s[...] = gb_ref[...]

    qkv[:, : 3 * width] = dot_nn(n_s[...], w_ref[:, : 3 * width]).astype(BF16)
    qkv[:, 3 * width :] = dot_nn(g_s[...], w_ref[:, 3 * width :]).astype(BF16)
    heads = width // HD
    lane = lax.broadcasted_iota(jnp.int32, (1, width), 1)
    masks = [(lane // HD == h).astype(F32).astype(BF16) for h in range(heads)]
    scale = jnp.asarray(HD ** (-0.5), BF16)
    first_of_pair = lax.broadcasted_iota(jnp.int32, (1, PAIR), 1) < HD

    def own_lanes(tall):
        tiles = []
        for t in range(width // PAIR):
            at = slice(t * PAIR, (t + 1) * PAIR)
            one = tall[2 * t * TOK : (2 * t + 1) * TOK, at]
            two = tall[(2 * t + 1) * TOK : (2 * t + 2) * TOK, at]
            tiles.append(jnp.where(first_of_pair, one, two))
        return jnp.concatenate(tiles, axis=1)

    def scene_body(s, _):
        base = pl.multiple_of(s * TOK, 16)
        at = pl.ds(base, TOK)
        scene = step * scenes + s
        live = live_column(cnt_ref[half, scene, 0], cnt_ref[half, scene, 1], cnt_ref[half, scene, 2])
        bias = jnp.where(live, 0.0, -1e30)
        q, k, v, dc = [qkv[at, c * width : (c + 1) * width] for c in range(4)]
        tall_q = jnp.concatenate([q * (m * scale) for m in masks], axis=0)
        tall_dc = jnp.concatenate([dc * m for m in masks], axis=0)
        scores = dot_nt(k, tall_q)
        grad_probs = dot_nt(v, tall_dc)
        probs_parts, score_parts = [], []
        for start in range(0, heads * TOK, PAIR):
            cols = slice(start, min(start + PAIR, heads * TOK))
            part = scores[:, cols] + bias
            lifted = jnp.exp(part - jnp.max(part, axis=0, keepdims=True))
            probs = lifted * (1.0 / jnp.sum(lifted, axis=0, keepdims=True))
            weighted = probs * grad_probs[:, cols]
            inner = jnp.sum(weighted, axis=0, keepdims=True)
            probs_parts.append(probs.astype(BF16))
            score_parts.append((weighted - probs * inner).astype(BF16))
        half_probs = jnp.concatenate(probs_parts, axis=1)
        grad_score = jnp.concatenate(score_parts, axis=1)
        out_ref[at, :width] = (own_lanes(dot_tn(grad_score, k)) * HD ** (-0.5)).astype(BF16)
        out_ref[at, width : 2 * width] = dot_nn(grad_score, tall_q).astype(BF16)
        out_ref[at, 2 * width : 3 * width] = dot_nn(half_probs, tall_dc).astype(BF16)
        out_ref[at, 3 * width :] = own_lanes(dot_tn(half_probs, v)).astype(BF16)
        return 0

    lax.fori_loop(0, scenes, scene_body, 0, unroll=True)
    back = dot_nt(out_ref[:, : 3 * width], w_ref[:, : 3 * width])

    @pl.when(half == 0)
    def _():
        back_own_ref[...] = back if first else before[0][...] + back

    @pl.when(half != 0)
    def _():
        back_far_ref[...] = back if first else before[1][...] + back


def block_rows(tokens):
    return 3 * TOK if tokens % (3 * TOK) == 0 else TOK


def two_halves(rows, steps):
    first = pl.BlockSpec((rows, D), lambda h, i: (jnp.where(h == 0, i, steps - 1), 0))
    second = pl.BlockSpec((rows, D), lambda h, i: (jnp.where(h == 0, 0, i), 0))
    return [first, second, first, second]


SCALARS = pl.BlockSpec(memory_space=pltpu.SMEM)


def attention_call(counts, owners, na, nb, ga, gb, before, blocks):
    tokens = na.shape[0]
    rows = block_rows(tokens)
    steps = tokens // rows
    cols = blocks[0].shape[1]
    whole = lambda a: pl.BlockSpec(a.shape, lambda h, i: (0, 0))
    halves = two_halves(rows, steps)
    return pl.pallas_call(
        functools.partial(attention_kernel, not before),
        grid=(2, steps),
        in_specs=[SCALARS, SCALARS] + halves + halves[: len(before)] + [whole(b) for b in blocks],
        out_specs=[
            pl.BlockSpec((rows, cols), lambda h, i: (h * steps + i, 0)),
            pl.BlockSpec((D, cols), lambda h, i: (0, 0)),
        ]
        + halves[:2],
        out_shape=[
            jax.ShapeDtypeStruct((2 * tokens, cols), BF16),
            jax.ShapeDtypeStruct((D, cols), BF16),
            jax.ShapeDtypeStruct((tokens, D), F32),
            jax.ShapeDtypeStruct((tokens, D), F32),
        ],
        scratch_shapes=[
            pltpu.VMEM((rows, D), BF16),
            pltpu.VMEM((rows, D), BF16),
            pltpu.VMEM((rows, cols), BF16),
        ],
        compiler_params=params(),
        cost_estimate=cost(20e9, 14e6),
        name="attention",
    )(counts, owners, na, nb, ga, gb, *before, *blocks)


def transpose_kernel(*refs):
    for k, ref in enumerate(refs[:-1]):
        refs[-1][k] = ref[...].T


def transpose_call(arrays):
    rows, cols = arrays[0].shape
    block = cols // 4
    return pl.pallas_call(
        transpose_kernel,
        grid=(4,),
        in_specs=[pl.BlockSpec((rows, block), lambda i: (0, i))] * len(arrays),
        out_specs=pl.BlockSpec((len(arrays), block, rows), lambda i: (0, i, 0)),
        out_shape=jax.ShapeDtypeStruct((len(arrays), cols, rows), BF16),
        compiler_params=params(),
        cost_estimate=cost(4e9, 8e6),
        name="transpose_rows",
    )(*arrays)


def weight_grad_kernel(blocks, low_ref, turned_ref, pack_ref, keep_ref, *refs):
    sends, total = refs[:-1], refs[-1]
    step = pl.program_id(0)
    width = pack_ref.shape[1] // 4
    parts = [slice(0, 3 * width), slice(3 * width, 4 * width)]
    for k in range(4):

        @pl.when(step == k)
        def _():
            new = dot_nn(turned_ref[0], pack_ref[:, parts[k % 2]])
            total[:, parts[k % 2]] = new if k < 2 else total[:, parts[k % 2]] + new

    @pl.when(step == 3)
    def _():
        rows = total.shape[0] // blocks
        low = low_ref[0]
        for b in range(blocks // 2):
            at = slice(b * rows, (b + 1) * rows)
            mine = pl.multiple_of((2 * b + low) * rows, rows)
            other = pl.multiple_of((2 * b + 1 - low) * rows, rows)
            keep_ref[at, :] = total[pl.ds(mine, rows), :]
            for c, send_ref in enumerate(sends):
                cols = send_ref.shape[1]
                send_ref[at, :] = total[pl.ds(other, rows), c * cols : (c + 1) * cols].astype(BF16)


def weight_grad_call(low, turned, pack, blocks):
    tokens, cols = pack.shape
    out = lambda cols: pl.BlockSpec((D // 2, cols), lambda i: (0, 0))
    send = jax.ShapeDtypeStruct((D // 2, cols // 2), BF16)
    return pl.pallas_call(
        functools.partial(weight_grad_kernel, blocks),
        grid=(4,),
        in_specs=[
            SCALARS,
            pl.BlockSpec((1,) + turned.shape[1:], lambda i: (i, 0, 0)),
            pl.BlockSpec((tokens // 2, cols), lambda i: (i // 2, 0)),
        ],
        out_specs=[out(cols), out(cols // 2), out(cols // 2)],
        out_shape=[jax.ShapeDtypeStruct((D // 2, cols), F32), send, send],
        scratch_shapes=[pltpu.VMEM((D, cols), F32)],
        compiler_params=params(),
        cost_estimate=cost(6e9, 12e6),
        name="weight_grad",
    )(low, turned, pack)


def combine_kernel(place_ref, keep_ref, first_ref, second_ref, *refs):
    rows = refs[0].shape[0]
    place = place_ref[0]

    def add(recv_ref):
        for j, ref in enumerate(refs):
            at = pl.ds(pl.multiple_of((place ^ j) * rows, rows), rows)
            ref[...] = (keep_ref[at, :] + recv_ref[at, :].astype(F32)).astype(ref.dtype)

    pl.when(pl.program_id(0) < 2)(lambda: add(first_ref))
    pl.when(pl.program_id(0) >= 2)(lambda: add(second_ref))


def combine_call(place, keep, recvs, blocks, dtype):
    rows, cols = keep.shape[0] // blocks, keep.shape[1]
    step = cols // 4
    whole = lambda at: pl.BlockSpec((keep.shape[0], step), lambda c: (0, at(c)))
    shapes = [jax.ShapeDtypeStruct((rows, cols), F32 if j == 0 else dtype) for j in range(blocks)]
    return pl.pallas_call(
        combine_kernel,
        grid=(4,),
        in_specs=[SCALARS, whole(lambda c: c), whole(lambda c: jnp.minimum(c, 1)), whole(lambda c: jnp.maximum(c - 2, 0))],
        out_specs=[pl.BlockSpec((rows, step), lambda c: (0, c))] * blocks,
        out_shape=shapes,
        compiler_params=params(),
        cost_estimate=cost(1e6, 5e6),
        name="combine",
    )(place, keep, *recvs)


def add_kernel(*refs):
    total = refs[0][...]
    for ref in refs[1:-1]:
        total = total + ref[...].astype(F32)
    refs[-1][...] = total


def add_call(parts):
    rows, cols = parts[0].shape
    spec = pl.BlockSpec((rows, cols // 4), lambda c: (0, c))
    return pl.pallas_call(
        add_kernel,
        grid=(4,),
        in_specs=[spec] * len(parts),
        out_specs=spec,
        out_shape=jax.ShapeDtypeStruct(parts[0].shape, F32),
        compiler_params=params(),
        cost_estimate=cost(1e6, 2e6),
        name="add_parts",
    )(*parts)


def mixed_product(context_refs, weight_refs):
    total = None
    for context_ref, w_ref in zip(context_refs, weight_refs):
        new = dot_nt(context_ref[...], w_ref[...])
        total = new if total is None else total + new
    return total


def context_specs(rows, packs, weights, first):
    width = packs[0].shape[1] // 4
    return [pl.BlockSpec((rows, width), lambda i: (first + i, 3))] * len(packs) + [
        pl.BlockSpec((D, width), lambda i: (0, 3))
    ] * len(weights)


def mixed_kernel(count, *refs):
    refs[-1][...] = mixed_product(refs[:count], refs[count : 2 * count]).astype(BF16)


def mixed_call(packs, weights):
    tokens = packs[0].shape[0] // 2
    rows = block_rows(tokens)
    return pl.pallas_call(
        functools.partial(mixed_kernel, len(packs)),
        grid=(tokens // rows,),
        in_specs=context_specs(rows, packs, weights, tokens // rows),
        out_specs=pl.BlockSpec((rows, D), lambda i: (i, 0)),
        out_shape=jax.ShapeDtypeStruct((tokens, D), BF16),
        compiler_params=params(),
        cost_estimate=cost(2e9, 5e6),
        name="mixed",
    )(*packs, *weights)


def tail_kernel(core_ref, own_ref, recv_ref, emb_ref, gl_ref, cols_ref, gain_ref, send_ref, keep_ref, acc):
    step = pl.program_id(0)
    rows = emb_ref.shape[0]
    scenes = rows // TOK

    @pl.when(step == 0)
    def _():
        acc[...] = jnp.zeros_like(acc)

    grad_normed = own_ref[...] + recv_ref[...]
    x = emb_ref[...].astype(F32)
    dev = x - jnp.mean(x, axis=-1, keepdims=True)
    inv_std = lax.rsqrt(jnp.mean(dev * dev, axis=-1, keepdims=True) + NORM_EPS)
    centred = dev * inv_std
    scaled = grad_normed * gain_ref[...]
    first_mean = jnp.mean(scaled, axis=-1, keepdims=True)
    second_mean = jnp.mean(scaled * centred, axis=-1, keepdims=True)
    back = inv_std * (scaled - first_mean - centred * second_mean)
    grad_in = (gl_ref[...].astype(F32) + back).astype(BF16)
    for g, (start, end) in enumerate(GROUP_BANDS):
        at = [slice(s * TOK + g * CAP, s * TOK + (g + 1) * CAP) for s in range(scenes)]
        columns = jnp.concatenate([cols_ref[a, : (end - start) * PIX] for a in at], axis=0)
        grads = jnp.concatenate([grad_in[a] for a in at], axis=0)
        acc[start * PIX : end * PIX, :] += dot_tn(columns, grads)

    @pl.when(step == pl.num_programs(0) - 1)
    def _():
        size = keep_ref.shape[0]
        core = core_ref[0]
        keep_ref[...] = acc[pl.ds(pl.multiple_of(core * size, size), size), :]
        send_ref[...] = acc[pl.ds(pl.multiple_of((1 - core) * size, size), size), :]


def tail_call(core, own, recv, emb, gl, cols, gain):
    tokens = emb.shape[0]
    rows = 2 * TOK if tokens % (2 * TOK) == 0 else TOK
    per = lambda a: pl.BlockSpec((rows, a.shape[1]), lambda i: (i, 0))
    stem_rows = GROUP_BANDS[-1][1] * PIX
    half = jax.ShapeDtypeStruct((stem_rows // 2, D), F32)
    return pl.pallas_call(
        tail_kernel,
        grid=(tokens // rows,),
        in_specs=[SCALARS, per(own), per(recv), per(emb), per(gl), per(cols)]
        + [pl.BlockSpec(gain.shape, lambda i: (0, 0))],
        out_specs=[pl.BlockSpec(half.shape, lambda i: (0, 0))] * 2,
        out_shape=[half, half],
        scratch_shapes=[pltpu.VMEM((stem_rows, D), F32)],
        compiler_params=params(),
        cost_estimate=cost(10e9, 12e6),
        name="tail",
    )(core, own, recv, emb, gl, cols, gain)


def output_kernel(count, cnt_ref, recv_ref, emb_ref, *refs):
    out_ref = refs[-1]
    step = pl.program_id(0)
    scenes = emb_ref.shape[0] // TOK
    mixed = recv_ref[...].astype(F32) + mixed_product(refs[:count], refs[count : 2 * count])
    total = emb_ref[...].astype(F32) + mixed
    for s in range(scenes):
        scene = step * scenes + s
        live = live_column(cnt_ref[scene, 0], cnt_ref[scene, 1], cnt_ref[scene, 2])
        at = slice(s * TOK, (s + 1) * TOK)
        out_ref[at, :] = jnp.where(live, total[at], 0.0).astype(BF16)


def output_call(counts, recv, emb, packs, weights):
    tokens = emb.shape[0]
    rows = 2 * TOK if tokens % (2 * TOK) == 0 else TOK
    per = lambda a: pl.BlockSpec((rows, a.shape[1]), lambda i: (i, 0))
    return pl.pallas_call(
        functools.partial(output_kernel, len(packs)),
        grid=(tokens // rows,),
        in_specs=[SCALARS, per(recv), per(emb)]
        + context_specs(rows, packs, weights, 0),
        out_specs=per(emb),
        out_shape=jax.ShapeDtypeStruct(emb.shape, BF16),
        compiler_params=params(),
        cost_estimate=cost(5e9, 10e6),
        name="layer_output",
    )(counts, recv, emb, *packs, *weights)


def swap(x, axis, size, bit):
    return lax.ppermute(x, axis, [(i, i ^ bit) for i in range(size)])


def together(*values):
    return lax.optimization_barrier(values)


class Ring:
    def __init__(self, x, axis, size):
        self.axis, self.size = axis, size
        order = list(range(0, size, 2)) + list(range(size - 1, 0, -2))
        self.forward = [(order[i], order[(i + 1) % size]) for i in range(size)]
        self.backward = [(order[(i + 1) % size], order[i]) for i in range(size)]
        self.ahead, self.behind = [x], [x]

    def step(self, *beside):
        ahead = lax.ppermute(self.ahead[-1], self.axis, self.forward)
        if len(self.behind) <= (self.size - 1) // 2:
            behind = lax.ppermute(self.behind[-1], self.axis, self.backward)
            ahead, behind, beside = together(ahead, behind, beside)
            self.behind.append(behind)
        else:
            ahead, beside = together(ahead, beside)
        self.ahead.append(ahead)
        return beside

    def owners(self):
        size = self.size
        me = lax.axis_index(self.axis)
        here = jnp.where(me % 2 == 0, me // 2, size - 1 - me // 2)
        distances = [-s for s in range(len(self.ahead))] + list(range(1, len(self.behind)))
        at = (here + size + jnp.array(distances, jnp.int32)) % size
        return jnp.where(at < size // 2, 2 * at, 2 * (size - 1 - at) + 1)


def halve_stem(recv, keep, group):
    mine = lax.axis_index("group") // 2 * 2 + lax.axis_index("dp") % 2
    return combine_call(mine.reshape(1), keep, recv, group // 2 * 2, F32)


def sum_stem(parts, beside, dp, group):
    core = lax.axis_index("group") % 2
    far = lax.axis_index("group") // 2
    low = lax.axis_index("dp") % 2
    high = lax.axis_index("dp") // 2
    fars, highs = group // 2, dp // 2
    mine = far * 2 + low
    small, width = parts[0].shape
    rows = 2 * fars * small

    def hop(block, f, b):
        if f:
            pairs = [
                (d * group + g, (d ^ b) * group + (g ^ (2 * f))) for d in range(dp) for g in range(group)
            ]
            return lax.ppermute(block, ("dp", "group"), pairs)
        return swap(block, "dp", dp, b)

    hops = [(k // 2, k % 2) for k in range(1, 2 * fars)]
    arrived = [hop(part, f, b) for part, (f, b) in zip(parts[1:], hops)]
    beside = beside()
    arrived, beside[:3] = together(arrived, beside[:3])
    near = (len(beside) + 3) // 2
    total = parts[0]
    for part in arrived:
        total = total + part
    cols = width // highs
    part = lax.dynamic_slice_in_dim(total, high * cols, cols, 1)
    away = [lax.dynamic_slice_in_dim(total, (high ^ j) * cols, cols, 1) for j in range(1, highs)]
    arrived = [swap(a, "dp", dp, 2 * (j + 1)) for j, a in enumerate(away)]
    arrived, beside[:near] = together(arrived, beside[:near])
    for block in arrived:
        part = part + block
    part = part.astype(BF16)
    line = jnp.zeros((small, width), BF16)
    line = lax.dynamic_update_slice_in_dim(line, part, high * cols, 1)
    arrived = [swap(part, "dp", dp, 2 * j) for j in range(1, highs)]
    arrived, beside = together(arrived, beside)
    for j, block in enumerate(arrived):
        line = lax.dynamic_update_slice_in_dim(line, block, (high ^ (j + 1)) * cols, 1)
    block = jnp.zeros((rows, width), BF16)
    block = lax.dynamic_update_slice_in_dim(block, line, mine * small, 0)
    for f, b in hops:
        target = (far ^ f) * 2 + (low ^ b)
        block = lax.dynamic_update_slice_in_dim(block, hop(line, f, b), target * small, 0)
    partner = swap(block, "group", group, 1)
    first = jnp.where(core == 0, block, partner)
    second = jnp.where(core == 0, partner, block)
    return jnp.concatenate([first, second], axis=0).astype(F32), beside


def encoding_tables(patch_count):
    quarter = D // 4
    half_width = D // 2
    power = lambda n: np.power(np.float32(10000.0), -np.arange(n, dtype=np.float32) / np.float32(n))
    at = np.arange(GRID).astype(np.float32)[:, None] * power(quarter)
    both = np.concatenate([np.sin(at), np.cos(at)], axis=-1)
    patch = np.arange(patch_count)
    rest = np.concatenate([both[patch // GRID], both[patch % GRID]], axis=-1).astype(np.float32)
    parts = []
    for _ in range(3):
        parts.append(rest.astype(ml_dtypes.bfloat16))
        rest = rest - parts[-1].astype(np.float32)
    group_at = np.arange(GROUPS).astype(np.float32)[:, None] * power(half_width)
    return np.stack(parts), np.concatenate([np.sin(group_at), np.cos(group_at)], axis=-1).astype(np.float32)


def on_device(dp, group, patches, vis_index, vis_count, w_stem, ln_gain, w_qkv, w_out, out_grad):
    scenes = patches.shape[0]
    tokens = scenes * TOK
    width = w_qkv.shape[2]
    fars = range(1, group // 2)
    rests = range(1, dp // 2)
    dp_low, dp_high = lax.axis_index("dp") % 2, lax.axis_index("dp") // 2
    low, high = dp_low.reshape(1), dp_high.reshape(1)
    core = (lax.axis_index("group") % 2).reshape(1)

    shard = jnp.concatenate([w_qkv.reshape(w_qkv.shape[0], 3 * width), w_out.T], axis=1)
    ring = Ring(shard, "dp", dp)
    cross = lambda x: [swap(x, "group", group, 2 * f) for f in fars]
    far = [cross(shard)]
    counts = vis_count.astype(jnp.int32)
    counts_far = swap(counts, "group", group, 1)
    table, genc = encoding_tables(patches.shape[1])
    gain = ln_gain.reshape(1, D)
    stem = stem_call(
        counts,
        vis_index,
        patches,
        w_stem,
        gain,
        jnp.asarray(table),
        jnp.asarray(genc),
        out_grad.reshape(scenes, TOK, D),
    )
    stem, counts_far = ring.step(stem, counts_far)
    emb, normed, gl = [a.reshape(tokens, D) for a in stem[:3]]
    cols = stem[3].reshape(tokens, stem[3].shape[2])
    both_counts = jnp.stack([counts, counts_far])
    both = [normed, swap(normed, "group", group, 1), gl, swap(gl, "group", group, 1)]
    far.append(cross(ring.ahead[-1]))
    both, far[0] = ring.step(both, far[0])
    while len(ring.ahead) < dp // 2:
        far.append(cross(ring.ahead[-1]))
        (far[-2],) = ring.step(far[-2])
    far.append(cross(ring.ahead[-1]))
    turned, far[-2] = ring.step(transpose_call([both[0], both[2], both[1], both[3]]), far[-2])
    ring.ahead, ring.behind = together(ring.ahead, ring.behind)
    far.append(cross(ring.ahead[-1]))
    behind = ring.behind[1:]
    far.append(cross(jnp.concatenate(behind, axis=0)))
    owners = ring.owners()

    packs, kept, coming, landing = [], [], [], []

    def first_to_rest(n):
        return combine_call(high, kept[n], coming[n], dp // 2, BF16)

    def rest_swaps(blocks):
        return [blocks[0]] + [swap(blocks[j], "dp", dp, 2 * j) for j in rests]

    weights, back = [], []
    for n in range(group // 2):
        if n == 0:
            blocks = ring.ahead + behind
        else:
            rows = shard.shape[0]
            last = [far[-1][n - 1][b * rows : (b + 1) * rows] for b in range(len(behind))]
            blocks = [f[n - 1] for f in far[:-1]] + last
        made = attention_call(both_counts, owners, *both, back, blocks)
        if n == 0:
            pack, weight, *back = together(*made)
        else:
            pack, weight, *back, coming[-1] = together(*made, coming[-1])
        packs.append(pack)
        weights.append(weight)
        if n == len(fars):
            back_far = swap(back[1], "group", group, 1)
        keep, *send = weight_grad_call(low, turned, pack, dp)
        if n == 0:
            send, keep, far[-3:] = together(send, keep, far[-3:])
        if n == len(fars):
            send, keep, back_far, kept, coming = together(send, keep, back_far, kept, coming)
        kept.append(keep)
        coming.append([swap(x, "dp", dp, 1) for x in send])
    blocks, back_far = together([first_to_rest(n) for n in range(len(fars))], back_far)
    landing = [rest_swaps(b) for b in blocks]
    near = dp // 2 * 3 // 4
    stem_send, stem_keep, landing[-1][:near], coming[-1][0] = together(
        *tail_call(core, back[0], back_far, emb, gl, cols, gain), landing[-1][:near], coming[-1][0]
    )
    half = stem_send.shape[1] // 2
    stem_recv = [swap(stem_send[:, c * half : (c + 1) * half], "group", group, 1) for c in range(2)]
    mixed, stem_recv, landing, coming = together(mixed_call(packs, weights), stem_recv, landing, coming)
    mixed = swap(mixed, "group", group, 1)
    stem_parts = halve_stem(stem_recv, stem_keep, group)

    def beside():
        last = rest_swaps(first_to_rest(-1))
        output = output_call(counts, mixed, emb, packs, weights)
        return [output] + last

    grad_w_stem, (output, *last) = sum_stem(stem_parts, beside, dp, group)
    shares = [add_call(parts) for parts in landing + [last]]

    total = shares[0]
    for f in fars:
        total = total + swap(shares[f], "group", group, 2 * f)
    grad_w_qkv = total[:, : 3 * width].reshape(total.shape[0], 3, width)
    grad_w_out = total[:, 3 * width :].T
    return (output.reshape(scenes, GROUPS, CAP, D), grad_w_stem, grad_w_qkv, grad_w_out)


def solution(mesh):
    sizes = dict(mesh.shape)
    return jax.shard_map(
        functools.partial(on_device, sizes["dp"], sizes["group"]),
        mesh=mesh,
        in_specs=(
            P(("dp", "group"), None, None),
            P(("dp", "group"), None, None),
            P(("dp", "group"), None),
            P(),
            P(),
            P("dp", None, "group"),
            P("group", "dp"),
            P(("dp", "group"), None, None, None),
        ),
        out_specs=(
            P(("dp", "group"), None, None, None),
            P(),
            P("dp", None, "group"),
            P("group", "dp"),
        ),
        check_vma=False,
    )
```

```python
import functools

import jax
import jax.numpy as jnp
import ml_dtypes
import numpy as np
from jax import lax
from jax.experimental import pallas as pl
from jax.experimental.pallas import tpu as pltpu
from jax.sharding import PartitionSpec as P

D = 1024
HD = 64
GROUPS = 3
CAP = 48
GRID = 12
PIX = 64
TOK = GROUPS * CAP
PAIR = 128
GROUP_BANDS = ((0, 4), (4, 8), (8, 10))
NORM_EPS = 1e-06
F32 = jnp.float32
BF16 = jnp.bfloat16
VMEM_LIMIT = 60 * 1024 * 1024


def dot_nn(a, b):
    return lax.dot_general(a, b, (((1,), (0,)), ((), ())), preferred_element_type=F32)


def dot_nt(a, b):
    return lax.dot_general(a, b, (((1,), (1,)), ((), ())), preferred_element_type=F32)


def dot_tn(a, b):
    return lax.dot_general(a, b, (((0,), (0,)), ((), ())), preferred_element_type=F32)


def live_column(c0, c1, c2):
    row = lax.broadcasted_iota(jnp.int32, (TOK, 1), 0)
    return (
        (row < c0)
        | ((row >= CAP) & (row < CAP + c1))
        | ((row >= 2 * CAP) & (row < 2 * CAP + c2))
    )


def params():
    return pltpu.CompilerParams(vmem_limit_bytes=VMEM_LIMIT)


def cost(flops, nbytes):
    return pl.CostEstimate(flops=int(flops / 1000), bytes_accessed=int(nbytes / 1000), transcendentals=0)


def stem_kernel(
    cnt_ref, idx_ref, patch_ref, w_ref, gain_ref, parts, genc_ref, og_ref,
    emb_ref, rows_ref, cols_ref,
):
    scenes = patch_ref.shape[0]
    patch_iota = lax.broadcasted_iota(jnp.int32, (parts.shape[1], CAP), 0)
    slot = lax.broadcasted_iota(jnp.int32, (CAP, 1), 0)
    for g, (start, end) in enumerate(GROUP_BANDS):
        rows = slice(g * CAP, (g + 1) * CAP)
        width = (end - start) * PIX
        picked, placed = [], []
        for s in range(scenes):
            onehot = (idx_ref[s, g : g + 1, :] == patch_iota).astype(F32).astype(BF16).T
            picked.append(dot_nn(onehot, patch_ref[s, :, start * PIX : end * PIX]).astype(BF16))
            placed.append(
                (dot_nn(onehot, parts[0]) + dot_nn(onehot, parts[1])) + dot_nn(onehot, parts[2])
            )
            live = slot < cnt_ref[s, :, g : g + 1]
            rows_ref[1, s, rows, :] = jnp.where(live, og_ref[s, rows, :].astype(F32), 0.0).astype(BF16)
        summed = dot_nn(jnp.concatenate(picked, axis=0), w_ref[start * PIX : end * PIX, :])
        for s in range(scenes):
            values = summed[s * CAP : (s + 1) * CAP] + (placed[s] + genc_ref[g : g + 1, :])
            emb = values.astype(BF16)
            emb_ref[s, rows, :] = emb
            x = emb.astype(F32)
            centre = jnp.mean(x, axis=-1, keepdims=True)
            dev = x - centre
            spread = jnp.mean(dev * dev, axis=-1, keepdims=True)
            centred = dev * lax.rsqrt(spread + NORM_EPS)
            rows_ref[0, s, rows, :] = (centred * gain_ref[...]).astype(BF16)
            cols_ref[s, rows, :width] = picked[s]
            if width < cols_ref.shape[2]:
                cols_ref[s, rows, width:] = jnp.zeros((CAP, cols_ref.shape[2] - width), BF16)


def stem_call(counts, index, patches, w_stem, gain, table, genc, out_grad):
    scenes, patch_count, width = patches.shape
    block = 3 if scenes % 3 == 0 else 1
    col_width = max(e - s for s, e in GROUP_BANDS) * PIX
    per = lambda shape: pl.BlockSpec((block,) + shape, lambda i: (i, 0, 0))
    whole = lambda a: pl.BlockSpec(a.shape, lambda i: (0,) * a.ndim)
    return pl.pallas_call(
        stem_kernel,
        grid=(scenes // block,),
        in_specs=[
            per((1, GROUPS)),
            per((GROUPS, CAP)),
            per((patch_count, width)),
            whole(w_stem),
            whole(gain),
            whole(table),
            whole(genc),
            per((TOK, D)),
        ],
        out_specs=[
            per((TOK, D)),
            pl.BlockSpec((2, block, TOK, D), lambda i: (0, i, 0, 0)),
            per((TOK, col_width)),
        ],
        out_shape=[
            jax.ShapeDtypeStruct((scenes, TOK, D), BF16),
            jax.ShapeDtypeStruct((2, scenes, TOK, D), BF16),
            jax.ShapeDtypeStruct((scenes, TOK, col_width), BF16),
        ],
        compiler_params=params(),
        cost_estimate=cost(8e9, 12e6),
        name="stem_norm",
    )(counts.reshape(scenes, 1, GROUPS), index, patches, w_stem, gain, table, genc, out_grad)


def attention_kernel(
    packs, blocks, dp, cnt_ref, owner_ref, low_ref, na_ref, nb_ref, ga_ref, gb_ref, *refs
):
    earlier, refs = refs[: 2 * (packs or 0)], refs[2 * (packs or 0) :]
    blocks, refs = refs[:blocks], refs[blocks:]
    out_ref, w_ref, keep_ref, *refs = refs
    sends, refs = refs[:2], refs[2:]
    n_s, g_s, qkv, total = refs[-4:]
    half, step = pl.program_id(0), pl.program_id(1)
    rows = n_s.shape[0]
    scenes = rows // TOK
    width = w_ref.shape[1] // 4

    @pl.when((half == 0) & (step == 0))
    def _():
        size = blocks[0].shape[0]
        for b, block in enumerate(blocks):
            w_ref[pl.ds(pl.multiple_of(owner_ref[b] * size, size), size), :] = block[...]
        total[...] = jnp.zeros_like(total)

    @pl.when(half == 0)
    def _():
        n_s[...] = na_ref[0]
        g_s[...] = ga_ref[0]

    @pl.when(half != 0)
    def _():
        n_s[...] = nb_ref[0]
        g_s[...] = gb_ref[0]

    qkv[:, : 3 * width] = dot_nn(n_s[...], w_ref[:, : 3 * width]).astype(BF16)
    qkv[:, 3 * width :] = dot_nn(g_s[...], w_ref[:, 3 * width :]).astype(BF16)
    heads = width // HD
    lane = lax.broadcasted_iota(jnp.int32, (1, width), 1)
    masks = [(lane // HD == h).astype(F32).astype(BF16) for h in range(heads)]
    scale = jnp.asarray(HD ** (-0.5), BF16)
    first_of_pair = lax.broadcasted_iota(jnp.int32, (1, PAIR), 1) < HD

    def own_lanes(tall):
        tiles = []
        for t in range(width // PAIR):
            at = slice(t * PAIR, (t + 1) * PAIR)
            one = tall[2 * t * TOK : (2 * t + 1) * TOK, at]
            two = tall[(2 * t + 1) * TOK : (2 * t + 2) * TOK, at]
            tiles.append(jnp.where(first_of_pair, one, two))
        return jnp.concatenate(tiles, axis=1)

    def scene_body(s, _):
        base = pl.multiple_of(s * TOK, 16)
        at = pl.ds(base, TOK)
        scene = step * scenes + s
        live = live_column(cnt_ref[half, scene, 0], cnt_ref[half, scene, 1], cnt_ref[half, scene, 2])
        bias = jnp.where(live, 0.0, -1e30)
        q, k, v, dc = [qkv[at, c * width : (c + 1) * width] for c in range(4)]
        tall_q = jnp.concatenate([q * (m * scale) for m in masks], axis=0)
        tall_dc = jnp.concatenate([dc * m for m in masks], axis=0)
        scores = dot_nt(k, tall_q)
        grad_probs = dot_nt(v, tall_dc)
        probs_parts, score_parts = [], []
        for start in range(0, heads * TOK, PAIR):
            cols = slice(start, min(start + PAIR, heads * TOK))
            part = scores[:, cols] + bias
            lifted = jnp.exp(part - jnp.max(part, axis=0, keepdims=True))
            probs = lifted * (1.0 / jnp.sum(lifted, axis=0, keepdims=True))
            weighted = probs * grad_probs[:, cols]
            inner = jnp.sum(weighted, axis=0, keepdims=True)
            probs_parts.append(probs.astype(BF16))
            score_parts.append((weighted - probs * inner).astype(BF16))
        half_probs = jnp.concatenate(probs_parts, axis=1)
        grad_score = jnp.concatenate(score_parts, axis=1)
        out_ref[at, :width] = (own_lanes(dot_tn(grad_score, k)) * HD ** (-0.5)).astype(BF16)
        out_ref[at, width : 2 * width] = dot_nn(grad_score, tall_q).astype(BF16)
        out_ref[at, 2 * width : 3 * width] = dot_nn(half_probs, tall_dc).astype(BF16)
        out_ref[at, 3 * width :] = own_lanes(dot_tn(half_probs, v)).astype(BF16)
        return 0

    lax.fori_loop(0, scenes, scene_body, 0, unroll=True)
    total[:, : 3 * width] += dot_tn(n_s[...], out_ref[:, : 3 * width])
    total[:, 3 * width :] += dot_tn(g_s[...], out_ref[:, 3 * width :])

    @pl.when((half == pl.num_programs(0) - 1) & (step == pl.num_programs(1) - 1))
    def _():
        size = total.shape[0] // dp
        low = low_ref[0]
        for b in range(dp // 2):
            at = slice(b * size, (b + 1) * size)
            mine = pl.multiple_of((2 * b + low) * size, size)
            other = pl.multiple_of((2 * b + 1 - low) * size, size)
            keep_ref[at, :] = total[pl.ds(mine, size), :]
            for c, send_ref in enumerate(sends):
                cols = send_ref.shape[1]
                send_ref[at, :] = total[pl.ds(other, size), c * cols : (c + 1) * cols].astype(BF16)

    if packs is not None:
        back = dot_nt(out_ref[:, : 3 * width], w_ref[:, : 3 * width])
        for pack_ref, weight_ref in zip(earlier[:packs], earlier[packs:]):
            back = back + dot_nt(pack_ref[...], weight_ref[...])

        @pl.when(half == 0)
        def _():
            refs[0][...] = back

        @pl.when(half != 0)
        def _():
            refs[1][...] = back


def block_rows(tokens):
    return 3 * TOK if tokens % (3 * TOK) == 0 else TOK


def two_halves(rows, steps, lead):
    shape = (1,) * len(lead) + (rows, D)
    first = pl.BlockSpec(shape, lambda h, i: lead + (jnp.where(h == 0, i, steps - 1), 0))
    second = pl.BlockSpec(shape, lambda h, i: lead + (jnp.where(h == 0, 0, i), 0))
    return [first, second]


SCALARS = pl.BlockSpec(memory_space=pltpu.SMEM)


def attention_call(counts, owners, low, own, far, earlier, blocks, dp):
    tokens = own.shape[1]
    rows = block_rows(tokens)
    steps = tokens // rows
    cols = blocks[0].shape[1]
    whole = lambda shape: pl.BlockSpec(shape, lambda h, i: (0, 0))
    at = lambda h, i: (h * steps + i, 0)
    packs = None if earlier is None else len(earlier[0])
    back = [] if earlier is None else two_halves(rows, steps, ())
    send = jax.ShapeDtypeStruct((D // 2, cols // 2), BF16)
    back_shape = jax.ShapeDtypeStruct((tokens, D), F32)
    return pl.pallas_call(
        functools.partial(attention_kernel, packs, len(blocks), dp),
        grid=(2, steps),
        in_specs=[SCALARS] * 3
        + two_halves(rows, steps, (0,))
        + two_halves(rows, steps, (1,))
        + [pl.BlockSpec((rows, cols // 4 * 3), at)] * (packs or 0)
        + [whole((D, cols // 4 * 3))] * (packs or 0)
        + [whole(b.shape) for b in blocks],
        out_specs=[pl.BlockSpec((rows, cols), at), whole((D, cols)), whole((D // 2, cols))]
        + [whole(send.shape)] * 2
        + back,
        out_shape=[
            jax.ShapeDtypeStruct((2 * tokens, cols), BF16),
            jax.ShapeDtypeStruct((D, cols), BF16),
            jax.ShapeDtypeStruct((D // 2, cols), F32),
            send,
            send,
        ]
        + [back_shape] * len(back),
        scratch_shapes=[
            pltpu.VMEM((rows, D), BF16),
            pltpu.VMEM((rows, D), BF16),
            pltpu.VMEM((rows, cols), BF16),
            pltpu.VMEM((D, cols), F32),
        ],
        compiler_params=params(),
        cost_estimate=cost(20e9, 14e6),
        name="attention",
    )(counts, owners, low, own, far, own, far, *[x for group in earlier or () for x in group], *blocks)


def combine_kernel(place_ref, keep_ref, first_ref, second_ref, *refs):
    rows, cols = refs[0].shape
    place = place_ref[0]
    for c, recv_ref in enumerate((first_ref, second_ref)):
        half = slice(c * cols // 2, (c + 1) * cols // 2)
        for j, ref in enumerate(refs):
            at = pl.ds(pl.multiple_of((place ^ j) * rows, rows), rows)
            ref[:, half] = (keep_ref[at, half] + recv_ref[at, :].astype(F32)).astype(ref.dtype)


def combine_call(place, keep, recvs, blocks, dtype):
    rows, cols = keep.shape[0] // blocks, keep.shape[1]
    whole = lambda a: pl.BlockSpec(a.shape, lambda: (0, 0))
    shapes = [jax.ShapeDtypeStruct((rows, cols), F32 if j == 0 else dtype) for j in range(blocks)]
    return pl.pallas_call(
        combine_kernel,
        in_specs=[SCALARS, whole(keep)] + [whole(r) for r in recvs],
        out_specs=[pl.BlockSpec((rows, cols), lambda: (0, 0))] * blocks,
        out_shape=shapes,
        compiler_params=params(),
        cost_estimate=cost(1e6, 5e6),
        name="combine",
    )(place, keep, *recvs)


def add_kernel(*refs):
    total = refs[0][...]
    for ref in refs[1:-1]:
        total = total + ref[...].astype(F32)
    refs[-1][...] = total


def add_call(parts):
    spec = pl.BlockSpec(parts[0].shape, lambda: (0, 0))
    return pl.pallas_call(
        add_kernel,
        in_specs=[spec] * len(parts),
        out_specs=spec,
        out_shape=jax.ShapeDtypeStruct(parts[0].shape, F32),
        compiler_params=params(),
        cost_estimate=cost(1e6, 2e6),
        name="add_parts",
    )(*parts)


def mixed_product(context_refs, weight_refs):
    total = None
    for context_ref, w_ref in zip(context_refs, weight_refs):
        new = dot_nt(context_ref[...], w_ref[...])
        total = new if total is None else total + new
    return total


def context_specs(rows, packs, weights, first):
    width = packs[0].shape[1] // 4
    return [pl.BlockSpec((rows, width), lambda i: (first + i, 3))] * len(packs) + [
        pl.BlockSpec((D, width), lambda i: (0, 3))
    ] * len(weights)


def mixed_kernel(count, *refs):
    refs[-1][...] = mixed_product(refs[:count], refs[count : 2 * count]).astype(BF16)


def mixed_call(packs, weights):
    tokens = packs[0].shape[0] // 2
    rows = block_rows(tokens)
    return pl.pallas_call(
        functools.partial(mixed_kernel, len(packs)),
        grid=(tokens // rows,),
        in_specs=context_specs(rows, packs, weights, tokens // rows),
        out_specs=pl.BlockSpec((rows, D), lambda i: (i, 0)),
        out_shape=jax.ShapeDtypeStruct((tokens, D), BF16),
        compiler_params=params(),
        cost_estimate=cost(2e9, 5e6),
        name="mixed",
    )(*packs, *weights)


def tail_kernel(core_ref, own_ref, recv_ref, emb_ref, gl_ref, cols_ref, gain_ref, keep_ref, first_ref, second_ref, acc):
    step = pl.program_id(0)
    rows = emb_ref.shape[0]
    scenes = rows // TOK

    @pl.when(step == 0)
    def _():
        acc[...] = jnp.zeros_like(acc)

    grad_normed = own_ref[...] + recv_ref[...]
    x = emb_ref[...].astype(F32)
    dev = x - jnp.mean(x, axis=-1, keepdims=True)
    inv_std = lax.rsqrt(jnp.mean(dev * dev, axis=-1, keepdims=True) + NORM_EPS)
    centred = dev * inv_std
    scaled = grad_normed * gain_ref[...]
    first_mean = jnp.mean(scaled, axis=-1, keepdims=True)
    second_mean = jnp.mean(scaled * centred, axis=-1, keepdims=True)
    back = inv_std * (scaled - first_mean - centred * second_mean)
    grad_in = (gl_ref[0].astype(F32) + back).astype(BF16)
    for g, (start, end) in enumerate(GROUP_BANDS):
        at = [slice(s * TOK + g * CAP, s * TOK + (g + 1) * CAP) for s in range(scenes)]
        columns = jnp.concatenate([cols_ref[a, : (end - start) * PIX] for a in at], axis=0)
        grads = jnp.concatenate([grad_in[a] for a in at], axis=0)
        acc[start * PIX : end * PIX, :] += dot_tn(columns, grads)

    @pl.when(step == pl.num_programs(0) - 1)
    def _():
        size = keep_ref.shape[0]
        core = core_ref[0]
        keep_ref[...] = acc[pl.ds(pl.multiple_of(core * size, size), size), :]
        other = pl.ds(pl.multiple_of((1 - core) * size, size), size)
        first_ref[...] = acc[other, : D // 2]
        second_ref[...] = acc[other, D // 2 :]


def tail_call(core, own, recv, emb, rows_own, cols, gain):
    tokens = emb.shape[0]
    rows = 2 * TOK if tokens % (2 * TOK) == 0 else TOK
    per = lambda a: pl.BlockSpec((rows, a.shape[1]), lambda i: (i, 0))
    stem_rows = GROUP_BANDS[-1][1] * PIX
    keep = jax.ShapeDtypeStruct((stem_rows // 2, D), F32)
    send = jax.ShapeDtypeStruct((stem_rows // 2, D // 2), F32)
    return pl.pallas_call(
        tail_kernel,
        grid=(tokens // rows,),
        in_specs=[SCALARS, per(own), per(recv), per(emb), pl.BlockSpec((1, rows, D), lambda i: (1, i, 0)), per(cols)]
        + [pl.BlockSpec(gain.shape, lambda i: (0, 0))],
        out_specs=[pl.BlockSpec(a.shape, lambda i: (0, 0)) for a in (keep, send, send)],
        out_shape=[keep, send, send],
        scratch_shapes=[pltpu.VMEM((stem_rows, D), F32)],
        compiler_params=params(),
        cost_estimate=cost(10e9, 12e6),
        name="tail",
    )(core, own, recv, emb, rows_own, cols, gain)


def output_kernel(count, cnt_ref, recv_ref, emb_ref, *refs):
    out_ref = refs[-1]
    step = pl.program_id(0)
    scenes = emb_ref.shape[0] // TOK
    mixed = recv_ref[...].astype(F32) + mixed_product(refs[:count], refs[count : 2 * count])
    total = emb_ref[...].astype(F32) + mixed
    for s in range(scenes):
        scene = step * scenes + s
        live = live_column(cnt_ref[scene, 0], cnt_ref[scene, 1], cnt_ref[scene, 2])
        at = slice(s * TOK, (s + 1) * TOK)
        out_ref[at, :] = jnp.where(live, total[at], 0.0).astype(BF16)


def output_call(counts, recv, emb, packs, weights):
    tokens = emb.shape[0]
    rows = 2 * TOK if tokens % (2 * TOK) == 0 else TOK
    per = lambda a: pl.BlockSpec((rows, a.shape[1]), lambda i: (i, 0))
    return pl.pallas_call(
        functools.partial(output_kernel, len(packs)),
        grid=(tokens // rows,),
        in_specs=[SCALARS, per(recv), per(emb)]
        + context_specs(rows, packs, weights, 0),
        out_specs=per(emb),
        out_shape=jax.ShapeDtypeStruct(emb.shape, BF16),
        compiler_params=params(),
        cost_estimate=cost(5e9, 10e6),
        name="layer_output",
    )(counts, recv, emb, *packs, *weights)


def swap(x, axis, size, bit):
    return lax.ppermute(x, axis, [(i, i ^ bit) for i in range(size)])


def together(*values):
    return lax.optimization_barrier(values)


class Ring:
    def __init__(self, x, axis, size):
        self.axis, self.size = axis, size
        order = list(range(0, size, 2)) + list(range(size - 1, 0, -2))
        self.forward = [(order[i], order[(i + 1) % size]) for i in range(size)]
        self.backward = [(order[(i + 1) % size], order[i]) for i in range(size)]
        self.ahead, self.behind = [x], [x]

    def step(self, *beside):
        ahead = lax.ppermute(self.ahead[-1], self.axis, self.forward)
        if len(self.behind) <= (self.size - 1) // 2:
            behind = lax.ppermute(self.behind[-1], self.axis, self.backward)
            ahead, behind, beside = together(ahead, behind, beside)
            self.behind.append(behind)
        else:
            ahead, beside = together(ahead, beside)
        self.ahead.append(ahead)
        return beside

    def owners(self):
        size = self.size
        me = lax.axis_index(self.axis)
        here = jnp.where(me % 2 == 0, me // 2, size - 1 - me // 2)
        distances = [-s for s in range(len(self.ahead))] + list(range(1, len(self.behind)))
        at = (here + size + jnp.array(distances, jnp.int32)) % size
        return jnp.where(at < size // 2, 2 * at, 2 * (size - 1 - at) + 1)


def halve_stem(recv, keep, group):
    mine = lax.axis_index("group") // 2 * 2 + lax.axis_index("dp") % 2
    return combine_call(mine.reshape(1), keep, recv, group // 2 * 2, F32)


def sum_stem(parts, beside, after, dp, group):
    core = lax.axis_index("group") % 2
    far = lax.axis_index("group") // 2
    low = lax.axis_index("dp") % 2
    high = lax.axis_index("dp") // 2
    fars, highs = group // 2, dp // 2
    mine = far * 2 + low
    small, width = parts[0].shape
    rows = 2 * fars * small

    def hop(block, f, b):
        if f:
            pairs = [
                (d * group + g, (d ^ b) * group + (g ^ (2 * f))) for d in range(dp) for g in range(group)
            ]
            return lax.ppermute(block, ("dp", "group"), pairs)
        return swap(block, "dp", dp, b)

    hops = [(k // 2, k % 2) for k in range(1, 2 * fars)]
    arrived = [hop(part, f, b) for part, (f, b) in zip(parts[1:], hops)]
    arrived, beside = together(arrived, beside)
    beside = after(*beside)
    total = parts[0]
    for part in arrived:
        total = total + part
    cols = width // highs
    part = lax.dynamic_slice_in_dim(total, high * cols, cols, 1)
    away = [lax.dynamic_slice_in_dim(total, (high ^ j) * cols, cols, 1) for j in range(1, highs)]
    arrived = [swap(a, "dp", dp, 2 * (j + 1)) for j, a in enumerate(away)]
    arrived, beside = together(arrived, beside)
    for block in arrived:
        part = part + block
    part = part.astype(BF16)
    line = jnp.zeros((small, width), BF16)
    line = lax.dynamic_update_slice_in_dim(line, part, high * cols, 1)
    arrived = [swap(part, "dp", dp, 2 * j) for j in range(1, highs)]
    for j, block in enumerate(arrived):
        line = lax.dynamic_update_slice_in_dim(line, block, (high ^ (j + 1)) * cols, 1)
    block = jnp.zeros((rows, width), BF16)
    block = lax.dynamic_update_slice_in_dim(block, line, mine * small, 0)
    for f, b in hops:
        target = (far ^ f) * 2 + (low ^ b)
        block = lax.dynamic_update_slice_in_dim(block, hop(line, f, b), target * small, 0)
    partner = swap(block, "group", group, 1)
    first = jnp.where(core == 0, block, partner)
    second = jnp.where(core == 0, partner, block)
    return jnp.concatenate([first, second], axis=0).astype(F32), beside


def encoding_tables(patch_count):
    quarter = D // 4
    half_width = D // 2
    power = lambda n: np.power(np.float32(10000.0), -np.arange(n, dtype=np.float32) / np.float32(n))
    at = np.arange(GRID).astype(np.float32)[:, None] * power(quarter)
    both = np.concatenate([np.sin(at), np.cos(at)], axis=-1)
    patch = np.arange(patch_count)
    rest = np.concatenate([both[patch // GRID], both[patch % GRID]], axis=-1).astype(np.float32)
    parts = []
    for _ in range(3):
        parts.append(rest.astype(ml_dtypes.bfloat16))
        rest = rest - parts[-1].astype(np.float32)
    group_at = np.arange(GROUPS).astype(np.float32)[:, None] * power(half_width)
    return np.stack(parts), np.concatenate([np.sin(group_at), np.cos(group_at)], axis=-1).astype(np.float32)


def on_device(dp, group, patches, vis_index, vis_count, w_stem, ln_gain, w_qkv, w_out, out_grad):
    scenes = patches.shape[0]
    tokens = scenes * TOK
    width = w_qkv.shape[2]
    fars = range(1, group // 2)
    rests = range(1, dp // 2)
    dp_low, dp_high = lax.axis_index("dp") % 2, lax.axis_index("dp") // 2
    low, high = dp_low.reshape(1), dp_high.reshape(1)
    core = (lax.axis_index("group") % 2).reshape(1)

    shard = jnp.concatenate([w_qkv.reshape(w_qkv.shape[0], 3 * width), w_out.T], axis=1)
    ring = Ring(shard, "dp", dp)
    cross = lambda x: [swap(x, "group", group, 2 * f) for f in fars]
    far = [cross(shard)]
    counts = vis_count.astype(jnp.int32)
    counts_far = swap(counts, "group", group, 1)
    table, genc = encoding_tables(patches.shape[1])
    gain = ln_gain.reshape(1, D)
    stem = stem_call(
        counts,
        vis_index,
        patches,
        w_stem,
        gain,
        jnp.asarray(table),
        jnp.asarray(genc),
        out_grad.reshape(scenes, TOK, D),
    )
    stem, counts_far = ring.step(stem, counts_far)
    emb = stem[0].reshape(tokens, D)
    both = [stem[1].reshape(2, tokens, D)]
    cols = stem[2].reshape(tokens, stem[2].shape[2])
    both_counts = jnp.stack([counts, counts_far])
    both.append(swap(both[0], "group", group, 1))
    far.append(cross(ring.ahead[-1]))
    both, far[0] = ring.step(both, far[0])
    while len(ring.ahead) < dp // 2:
        far.append(cross(ring.ahead[-1]))
        (far[-2],) = ring.step(far[-2])
    far.append(cross(ring.ahead[-1]))
    (far[-2],) = ring.step(far[-2])
    ring.ahead, ring.behind = together(ring.ahead, ring.behind)
    far.append(cross(ring.ahead[-1]))
    behind = ring.behind[1:]
    far.append(cross(jnp.concatenate(behind, axis=0)))
    owners = ring.owners()

    packs, kept, coming, landing = [], [], [], []

    def first_to_rest(n):
        return combine_call(high, kept[n], coming[n], dp // 2, BF16)

    def rest_swaps(blocks):
        return [blocks[0]] + [swap(blocks[j], "dp", dp, 2 * j) for j in rests]

    weights = []
    for n in range(group // 2):
        if n == 0:
            blocks = ring.ahead + behind
        else:
            rows = shard.shape[0]
            last = [far[-1][n - 1][b * rows : (b + 1) * rows] for b in range(len(behind))]
            blocks = [f[n - 1] for f in far[:-1]] + last
        earlier = (packs, weights) if n == len(fars) else None
        made = attention_call(both_counts, owners, low, *both, earlier, blocks, dp)
        if n == 0:
            made, far[-3:] = together(made, far[-3:])
        else:
            made, coming[-1] = together(made, coming[-1])
        pack, weight, keep, first, second, *back = made
        packs.append(pack)
        weights.append(weight)
        kept.append(keep)
        coming.append([swap(x, "dp", dp, 1) for x in (first, second)])
    back_far = swap(back[1], "group", group, 1)
    blocks, back_far = together([first_to_rest(n) for n in range(len(fars))], back_far)
    landing = [rest_swaps(b) for b in blocks]
    near = dp // 2 * 3 // 4
    stem_made, landing[-1][:near], coming[-1] = together(
        tail_call(core, back[0], back_far, emb, both[0], cols, gain), landing[-1][:near], coming[-1]
    )
    stem_keep, *stem_recv = stem_made
    stem_recv = [swap(x, "group", group, 1) for x in stem_recv]
    blocks = list(first_to_rest(-1))
    stem_recv, blocks[0], landing = together(stem_recv, blocks[0], landing)
    last = rest_swaps(blocks)

    def after(mixed, *near_last):
        mixed = swap(mixed, "group", group, 1)
        return [output_call(counts, mixed, emb, packs, weights)] + list(near_last) + last[near:]

    grad_w_stem, (output, *last) = sum_stem(
        halve_stem(stem_recv, stem_keep, group), [mixed_call(packs, weights)] + last[:near], after, dp, group
    )
    shares = [add_call(parts) for parts in landing + [last]]

    total = shares[0]
    for f in fars:
        total = total + swap(shares[f], "group", group, 2 * f)
    grad_w_qkv = total[:, : 3 * width].reshape(total.shape[0], 3, width)
    grad_w_out = total[:, 3 * width :].T
    return (output.reshape(scenes, GROUPS, CAP, D), grad_w_stem, grad_w_qkv, grad_w_out)


def solution(mesh):
    sizes = dict(mesh.shape)
    return jax.shard_map(
        functools.partial(on_device, sizes["dp"], sizes["group"]),
        mesh=mesh,
        in_specs=(
            P(("dp", "group"), None, None),
            P(("dp", "group"), None, None),
            P(("dp", "group"), None),
            P(),
            P(),
            P("dp", None, "group"),
            P("group", "dp"),
            P(("dp", "group"), None, None, None),
        ),
        out_specs=(
            P(("dp", "group"), None, None, None),
            P(),
            P("dp", None, "group"),
            P("group", "dp"),
        ),
        check_vma=False,
    )
```

```python
import functools

import jax
import jax.numpy as jnp
import ml_dtypes
import numpy as np
from jax import lax
from jax.experimental import pallas as pl
from jax.experimental.pallas import tpu as pltpu
from jax.sharding import PartitionSpec as P

D = 1024
HD = 64
GROUPS = 3
CAP = 48
GRID = 12
PIX = 64
TOK = GROUPS * CAP
PAIR = 128
GROUP_BANDS = ((0, 4), (4, 8), (8, 10))
NORM_EPS = 1e-06
F32 = jnp.float32
BF16 = jnp.bfloat16
VMEM_LIMIT = 60 * 1024 * 1024


def dot_nn(a, b):
    return lax.dot_general(a, b, (((1,), (0,)), ((), ())), preferred_element_type=F32)


def dot_nt(a, b):
    return lax.dot_general(a, b, (((1,), (1,)), ((), ())), preferred_element_type=F32)


def dot_tn(a, b):
    return lax.dot_general(a, b, (((0,), (0,)), ((), ())), preferred_element_type=F32)


def live_column(c0, c1, c2):
    row = lax.broadcasted_iota(jnp.int32, (TOK, 1), 0)
    return (
        (row < c0)
        | ((row >= CAP) & (row < CAP + c1))
        | ((row >= 2 * CAP) & (row < 2 * CAP + c2))
    )


def params():
    return pltpu.CompilerParams(vmem_limit_bytes=VMEM_LIMIT)


def cost(flops, nbytes):
    return pl.CostEstimate(flops=int(flops / 1000), bytes_accessed=int(nbytes / 1000), transcendentals=0)


def stem_kernel(
    cnt_ref, idx_ref, patch_ref, w_ref, gain_ref, parts, genc_ref, og_ref,
    emb_ref, rows_ref, cols_ref,
):
    scenes = patch_ref.shape[0]
    patch_iota = lax.broadcasted_iota(jnp.int32, (parts.shape[1], CAP), 0)
    slot = lax.broadcasted_iota(jnp.int32, (CAP, 1), 0)
    for g, (start, end) in enumerate(GROUP_BANDS):
        rows = slice(g * CAP, (g + 1) * CAP)
        width = (end - start) * PIX
        picked, placed = [], []
        for s in range(scenes):
            onehot = (idx_ref[s, g : g + 1, :] == patch_iota).astype(F32).astype(BF16).T
            picked.append(dot_nn(onehot, patch_ref[s, :, start * PIX : end * PIX]).astype(BF16))
            placed.append(
                (dot_nn(onehot, parts[0]) + dot_nn(onehot, parts[1])) + dot_nn(onehot, parts[2])
            )
            live = slot < cnt_ref[s, :, g : g + 1]
            rows_ref[1, s, rows, :] = jnp.where(live, og_ref[s, rows, :].astype(F32), 0.0).astype(BF16)
        summed = dot_nn(jnp.concatenate(picked, axis=0), w_ref[start * PIX : end * PIX, :])
        for s in range(scenes):
            values = summed[s * CAP : (s + 1) * CAP] + (placed[s] + genc_ref[g : g + 1, :])
            emb = values.astype(BF16)
            emb_ref[s, rows, :] = emb
            x = emb.astype(F32)
            centre = jnp.mean(x, axis=-1, keepdims=True)
            dev = x - centre
            spread = jnp.mean(dev * dev, axis=-1, keepdims=True)
            centred = dev * lax.rsqrt(spread + NORM_EPS)
            rows_ref[0, s, rows, :] = (centred * gain_ref[...]).astype(BF16)
            cols_ref[s, rows, :width] = picked[s]
            if width < cols_ref.shape[2]:
                cols_ref[s, rows, width:] = jnp.zeros((CAP, cols_ref.shape[2] - width), BF16)


def stem_call(counts, index, patches, w_stem, gain, table, genc, out_grad):
    scenes, patch_count, width = patches.shape
    block = 3 if scenes % 3 == 0 else 1
    col_width = max(e - s for s, e in GROUP_BANDS) * PIX
    per = lambda shape: pl.BlockSpec((block,) + shape, lambda i: (i, 0, 0))
    whole = lambda a: pl.BlockSpec(a.shape, lambda i: (0,) * a.ndim)
    return pl.pallas_call(
        stem_kernel,
        grid=(scenes // block,),
        in_specs=[
            per((1, GROUPS)),
            per((GROUPS, CAP)),
            per((patch_count, width)),
            whole(w_stem),
            whole(gain),
            whole(table),
            whole(genc),
            per((TOK, D)),
        ],
        out_specs=[
            per((TOK, D)),
            pl.BlockSpec((2, block, TOK, D), lambda i: (0, i, 0, 0)),
            per((TOK, col_width)),
        ],
        out_shape=[
            jax.ShapeDtypeStruct((scenes, TOK, D), BF16),
            jax.ShapeDtypeStruct((2, scenes, TOK, D), BF16),
            jax.ShapeDtypeStruct((scenes, TOK, col_width), BF16),
        ],
        compiler_params=params(),
        cost_estimate=cost(8e9, 12e6),
        name="stem_norm",
    )(counts.reshape(scenes, 1, GROUPS), index, patches, w_stem, gain, table, genc, out_grad)


def attention_kernel(
    packs, blocks, dp, cnt_ref, owner_ref, low_ref, na_ref, nb_ref, ga_ref, gb_ref, *refs
):
    earlier, refs = refs[: 2 * (packs or 0)], refs[2 * (packs or 0) :]
    blocks, refs = refs[:blocks], refs[blocks:]
    out_ref, w_ref, keep_ref, other_ref, *refs = refs
    n_s, g_s, qkv, total = refs[-4:]
    half, step = pl.program_id(0), pl.program_id(1)
    rows = n_s.shape[0]
    scenes = rows // TOK
    width = w_ref.shape[1] // 4

    @pl.when((half == 0) & (step == 0))
    def _():
        size = blocks[0].shape[0]
        for b, block in enumerate(blocks):
            w_ref[pl.ds(pl.multiple_of(owner_ref[b] * size, size), size), :] = block[...]
        total[...] = jnp.zeros_like(total)

    @pl.when(half == 0)
    def _():
        n_s[...] = na_ref[0]
        g_s[...] = ga_ref[0]

    @pl.when(half != 0)
    def _():
        n_s[...] = nb_ref[0]
        g_s[...] = gb_ref[0]

    qkv[:, : 3 * width] = dot_nn(n_s[...], w_ref[:, : 3 * width]).astype(BF16)
    qkv[:, 3 * width :] = dot_nn(g_s[...], w_ref[:, 3 * width :]).astype(BF16)
    heads = width // HD
    lane = lax.broadcasted_iota(jnp.int32, (1, width), 1)
    masks = [(lane // HD == h).astype(F32).astype(BF16) for h in range(heads)]
    scale = jnp.asarray(HD ** (-0.5), BF16)
    first_of_pair = lax.broadcasted_iota(jnp.int32, (1, PAIR), 1) < HD

    def own_lanes(tall):
        tiles = []
        for t in range(width // PAIR):
            at = slice(t * PAIR, (t + 1) * PAIR)
            one = tall[2 * t * TOK : (2 * t + 1) * TOK, at]
            two = tall[(2 * t + 1) * TOK : (2 * t + 2) * TOK, at]
            tiles.append(jnp.where(first_of_pair, one, two))
        return jnp.concatenate(tiles, axis=1)

    def scene_body(s, _):
        base = pl.multiple_of(s * TOK, 16)
        at = pl.ds(base, TOK)
        scene = step * scenes + s
        live = live_column(cnt_ref[half, scene, 0], cnt_ref[half, scene, 1], cnt_ref[half, scene, 2])
        bias = jnp.where(live, 0.0, -1e30)
        q, k, v, dc = [qkv[at, c * width : (c + 1) * width] for c in range(4)]
        tall_q = jnp.concatenate([q * (m * scale) for m in masks], axis=0)
        tall_dc = jnp.concatenate([dc * m for m in masks], axis=0)
        scores = dot_nt(k, tall_q)
        grad_probs = dot_nt(v, tall_dc)
        probs_parts, score_parts = [], []
        for start in range(0, heads * TOK, PAIR):
            cols = slice(start, min(start + PAIR, heads * TOK))
            part = scores[:, cols] + bias
            lifted = jnp.exp(part - jnp.max(part, axis=0, keepdims=True))
            probs = lifted * (1.0 / jnp.sum(lifted, axis=0, keepdims=True))
            weighted = probs * grad_probs[:, cols]
            inner = jnp.sum(weighted, axis=0, keepdims=True)
            probs_parts.append(probs.astype(BF16))
            score_parts.append((weighted - probs * inner).astype(BF16))
        half_probs = jnp.concatenate(probs_parts, axis=1)
        grad_score = jnp.concatenate(score_parts, axis=1)
        out_ref[at, :width] = (own_lanes(dot_tn(grad_score, k)) * HD ** (-0.5)).astype(BF16)
        out_ref[at, width : 2 * width] = dot_nn(grad_score, tall_q).astype(BF16)
        out_ref[at, 2 * width : 3 * width] = dot_nn(half_probs, tall_dc).astype(BF16)
        out_ref[at, 3 * width :] = own_lanes(dot_tn(half_probs, v)).astype(BF16)
        return 0

    lax.fori_loop(0, scenes, scene_body, 0, unroll=True)
    total[:, : 3 * width] += dot_tn(n_s[...], out_ref[:, : 3 * width])
    total[:, 3 * width :] += dot_tn(g_s[...], out_ref[:, 3 * width :])

    @pl.when((half == pl.num_programs(0) - 1) & (step == pl.num_programs(1) - 1))
    def _():
        size = total.shape[0] // dp
        low = low_ref[0]
        for b in range(dp // 2):
            at = slice(b * size, (b + 1) * size)
            mine = pl.multiple_of((2 * b + low) * size, size)
            other = pl.multiple_of((2 * b + 1 - low) * size, size)
            keep_ref[at, :] = total[pl.ds(mine, size), :].astype(keep_ref.dtype)
            other_ref[at, :] = total[pl.ds(other, size), :].astype(other_ref.dtype)

    if packs is not None:
        back = dot_nt(out_ref[:, : 3 * width], w_ref[:, : 3 * width])
        for pack_ref, weight_ref in zip(earlier[:packs], earlier[packs:]):
            back = back + dot_nt(pack_ref[...], weight_ref[...])

        @pl.when(half == 0)
        def _():
            refs[0][...] = back

        @pl.when(half != 0)
        def _():
            refs[1][...] = back


def block_rows(tokens):
    return 3 * TOK if tokens % (3 * TOK) == 0 else TOK


def two_halves(rows, steps, lead):
    shape = (1,) * len(lead) + (rows, D)
    first = pl.BlockSpec(shape, lambda h, i: lead + (jnp.where(h == 0, i, steps - 1), 0))
    second = pl.BlockSpec(shape, lambda h, i: lead + (jnp.where(h == 0, 0, i), 0))
    return [first, second]


SCALARS = pl.BlockSpec(memory_space=pltpu.SMEM)


def attention_call(counts, owners, low, own, far, earlier, blocks, dp):
    tokens = own.shape[1]
    rows = block_rows(tokens)
    steps = tokens // rows
    cols = blocks[0].shape[1]
    whole = lambda shape: pl.BlockSpec(shape, lambda h, i: (0, 0))
    at = lambda h, i: (h * steps + i, 0)
    packs = None if earlier is None else len(earlier[0])
    back = [] if earlier is None else two_halves(rows, steps, ())
    grads = jax.ShapeDtypeStruct((D // 2, cols), BF16 if earlier is None else F32)
    back_shape = jax.ShapeDtypeStruct((tokens, D), F32)
    return pl.pallas_call(
        functools.partial(attention_kernel, packs, len(blocks), dp),
        grid=(2, steps),
        in_specs=[SCALARS] * 3
        + two_halves(rows, steps, (0,))
        + two_halves(rows, steps, (1,))
        + [pl.BlockSpec((rows, cols // 4 * 3), at)] * (packs or 0)
        + [whole((D, cols // 4 * 3))] * (packs or 0)
        + [whole(b.shape) for b in blocks],
        out_specs=[pl.BlockSpec((rows, cols), at), whole((D, cols))] + [whole(grads.shape)] * 2 + back,
        out_shape=[
            jax.ShapeDtypeStruct((2 * tokens, cols), BF16),
            jax.ShapeDtypeStruct((D, cols), BF16),
            grads,
            grads,
        ]
        + [back_shape] * len(back),
        scratch_shapes=[
            pltpu.VMEM((rows, D), BF16),
            pltpu.VMEM((rows, D), BF16),
            pltpu.VMEM((rows, cols), BF16),
            pltpu.VMEM((D, cols), F32),
        ],
        compiler_params=params(),
        cost_estimate=cost(20e9, 14e6),
        name="attention",
    )(counts, owners, low, own, far, own, far, *[x for group in earlier or () for x in group], *blocks)


def combine_kernel(counts, place_ref, keep_ref, *refs):
    recvs, refs = refs[: sum(counts)], refs[sum(counts) :]
    rows = refs[0].shape[0]
    place = place_ref[0]
    for j, ref in enumerate(refs):
        at = pl.ds(pl.multiple_of((place ^ j) * rows, rows), rows)
        total = keep_ref[at, :]
        first = 0
        for count in counts:
            pieces = [r[at, :].astype(F32) for r in recvs[first : first + count]]
            total = total + (pieces[0] if count == 1 else jnp.concatenate(pieces, axis=1))
            first += count
        ref[...] = total.astype(ref.dtype)


def combine_call(place, keep, arrived, dtypes):
    rows, cols = keep.shape[0] // len(dtypes), keep.shape[1]
    recvs = [r for pieces in arrived for r in pieces]
    whole = lambda a: pl.BlockSpec(a.shape, lambda: (0, 0))
    return pl.pallas_call(
        functools.partial(combine_kernel, [len(pieces) for pieces in arrived]),
        in_specs=[SCALARS, whole(keep)] + [whole(r) for r in recvs],
        out_specs=[pl.BlockSpec((rows, cols), lambda: (0, 0))] * len(dtypes),
        out_shape=[jax.ShapeDtypeStruct((rows, cols), d) for d in dtypes],
        compiler_params=params(),
        cost_estimate=cost(1e6, 5e6),
        name="combine",
    )(place, keep, *recvs)


def add_kernel(*refs):
    total = refs[0][...]
    for ref in refs[1:-1]:
        total = total + ref[...].astype(F32)
    refs[-1][...] = total


def add_call(parts):
    spec = pl.BlockSpec(parts[0].shape, lambda: (0, 0))
    return pl.pallas_call(
        add_kernel,
        in_specs=[spec] * len(parts),
        out_specs=spec,
        out_shape=jax.ShapeDtypeStruct(parts[0].shape, F32),
        compiler_params=params(),
        cost_estimate=cost(1e6, 2e6),
        name="add_parts",
    )(*parts)


def mixed_product(context_refs, weight_refs):
    total = None
    for context_ref, w_ref in zip(context_refs, weight_refs):
        new = dot_nt(context_ref[...], w_ref[...])
        total = new if total is None else total + new
    return total


def context_specs(rows, packs, weights, first):
    width = packs[0].shape[1] // 4
    return [pl.BlockSpec((rows, width), lambda i: (first + i, 3))] * len(packs) + [
        pl.BlockSpec((D, width), lambda i: (0, 3))
    ] * len(weights)


def mixed_kernel(count, *refs):
    refs[-1][...] = mixed_product(refs[:count], refs[count : 2 * count]).astype(BF16)


def mixed_call(packs, weights):
    tokens = packs[0].shape[0] // 2
    rows = block_rows(tokens)
    return pl.pallas_call(
        functools.partial(mixed_kernel, len(packs)),
        grid=(tokens // rows,),
        in_specs=context_specs(rows, packs, weights, tokens // rows),
        out_specs=pl.BlockSpec((rows, D), lambda i: (i, 0)),
        out_shape=jax.ShapeDtypeStruct((tokens, D), BF16),
        compiler_params=params(),
        cost_estimate=cost(2e9, 5e6),
        name="mixed",
    )(*packs, *weights)


def tail_kernel(core_ref, own_ref, recv_ref, emb_ref, gl_ref, cols_ref, gain_ref, keep_ref, first_ref, second_ref, acc):
    step = pl.program_id(0)
    rows = emb_ref.shape[0]
    scenes = rows // TOK

    @pl.when(step == 0)
    def _():
        acc[...] = jnp.zeros_like(acc)

    grad_normed = own_ref[...] + recv_ref[...]
    x = emb_ref[...].astype(F32)
    dev = x - jnp.mean(x, axis=-1, keepdims=True)
    inv_std = lax.rsqrt(jnp.mean(dev * dev, axis=-1, keepdims=True) + NORM_EPS)
    centred = dev * inv_std
    scaled = grad_normed * gain_ref[...]
    first_mean = jnp.mean(scaled, axis=-1, keepdims=True)
    second_mean = jnp.mean(scaled * centred, axis=-1, keepdims=True)
    back = inv_std * (scaled - first_mean - centred * second_mean)
    grad_in = (gl_ref[0].astype(F32) + back).astype(BF16)
    for g, (start, end) in enumerate(GROUP_BANDS):
        at = [slice(s * TOK + g * CAP, s * TOK + (g + 1) * CAP) for s in range(scenes)]
        columns = jnp.concatenate([cols_ref[a, : (end - start) * PIX] for a in at], axis=0)
        grads = jnp.concatenate([grad_in[a] for a in at], axis=0)
        acc[start * PIX : end * PIX, :] += dot_tn(columns, grads)

    @pl.when(step == pl.num_programs(0) - 1)
    def _():
        size = keep_ref.shape[0]
        core = core_ref[0]
        keep_ref[...] = acc[pl.ds(pl.multiple_of(core * size, size), size), :]
        other = pl.ds(pl.multiple_of((1 - core) * size, size), size)
        first_ref[...] = acc[other, : D // 2]
        second_ref[...] = acc[other, D // 2 :]


def tail_call(core, own, recv, emb, rows_own, cols, gain):
    tokens = emb.shape[0]
    rows = 2 * TOK if tokens % (2 * TOK) == 0 else TOK
    per = lambda a: pl.BlockSpec((rows, a.shape[1]), lambda i: (i, 0))
    stem_rows = GROUP_BANDS[-1][1] * PIX
    keep = jax.ShapeDtypeStruct((stem_rows // 2, D), F32)
    send = jax.ShapeDtypeStruct((stem_rows // 2, D // 2), F32)
    return pl.pallas_call(
        tail_kernel,
        grid=(tokens // rows,),
        in_specs=[SCALARS, per(own), per(recv), per(emb), pl.BlockSpec((1, rows, D), lambda i: (1, i, 0)), per(cols)]
        + [pl.BlockSpec(gain.shape, lambda i: (0, 0))],
        out_specs=[pl.BlockSpec(a.shape, lambda i: (0, 0)) for a in (keep, send, send)],
        out_shape=[keep, send, send],
        scratch_shapes=[pltpu.VMEM((stem_rows, D), F32)],
        compiler_params=params(),
        cost_estimate=cost(10e9, 12e6),
        name="tail",
    )(core, own, recv, emb, rows_own, cols, gain)


def output_kernel(count, cnt_ref, recv_ref, emb_ref, *refs):
    out_ref = refs[-1]
    step = pl.program_id(0)
    scenes = emb_ref.shape[0] // TOK
    mixed = recv_ref[...].astype(F32) + mixed_product(refs[:count], refs[count : 2 * count])
    total = emb_ref[...].astype(F32) + mixed
    for s in range(scenes):
        scene = step * scenes + s
        live = live_column(cnt_ref[scene, 0], cnt_ref[scene, 1], cnt_ref[scene, 2])
        at = slice(s * TOK, (s + 1) * TOK)
        out_ref[at, :] = jnp.where(live, total[at], 0.0).astype(BF16)


def output_call(counts, recv, emb, packs, weights):
    tokens = emb.shape[0]
    rows = 2 * TOK if tokens % (2 * TOK) == 0 else TOK
    per = lambda a: pl.BlockSpec((rows, a.shape[1]), lambda i: (i, 0))
    return pl.pallas_call(
        functools.partial(output_kernel, len(packs)),
        grid=(tokens // rows,),
        in_specs=[SCALARS, per(recv), per(emb)]
        + context_specs(rows, packs, weights, 0),
        out_specs=per(emb),
        out_shape=jax.ShapeDtypeStruct(emb.shape, BF16),
        compiler_params=params(),
        cost_estimate=cost(5e9, 10e6),
        name="layer_output",
    )(counts, recv, emb, *packs, *weights)


def swap(x, axis, size, bit):
    return lax.ppermute(x, axis, [(i, i ^ bit) for i in range(size)])


def together(*values):
    return lax.optimization_barrier(values)


class Ring:
    def __init__(self, x, axis, size):
        self.axis, self.size = axis, size
        order = list(range(0, size, 2)) + list(range(size - 1, 0, -2))
        self.forward = [(order[i], order[(i + 1) % size]) for i in range(size)]
        self.backward = [(order[(i + 1) % size], order[i]) for i in range(size)]
        self.ahead, self.behind = [x], [x]

    def send(self):
        moved = [lax.ppermute(self.ahead[-1], self.axis, self.forward)]
        if len(self.behind) <= (self.size - 1) // 2:
            moved.append(lax.ppermute(self.behind[-1], self.axis, self.backward))
        return moved

    def receive(self, moved):
        self.ahead.append(moved[0])
        self.behind.extend(moved[1:])

    @property
    def steps(self):
        return len(self.ahead) - 1

    def owners(self):
        size = self.size
        me = lax.axis_index(self.axis)
        here = jnp.where(me % 2 == 0, me // 2, size - 1 - me // 2)
        distances = [-s for s in range(len(self.ahead))] + list(range(1, len(self.behind)))
        at = (here + size + jnp.array(distances, jnp.int32)) % size
        return jnp.where(at < size // 2, 2 * at, 2 * (size - 1 - at) + 1)


def step_all(rings, *beside):
    moved, beside = together([ring.send() for ring in rings], beside)
    for ring, blocks in zip(rings, moved):
        ring.receive(blocks)
    return beside


def halve_stem(recv, keep, group):
    mine = lax.axis_index("group") // 2 * 2 + lax.axis_index("dp") % 2
    return combine_call(mine.reshape(1), keep, [recv], [F32] * (group // 2 * 2))


def sum_stem(parts, beside, after, dp, group):
    core = lax.axis_index("group") % 2
    far = lax.axis_index("group") // 2
    low = lax.axis_index("dp") % 2
    high = lax.axis_index("dp") // 2
    fars, highs = group // 2, dp // 2
    mine = far * 2 + low
    small, width = parts[0].shape
    rows = 2 * fars * small

    def hop(block, f, b):
        if f:
            pairs = [
                (d * group + g, (d ^ b) * group + (g ^ (2 * f))) for d in range(dp) for g in range(group)
            ]
            return lax.ppermute(block, ("dp", "group"), pairs)
        return swap(block, "dp", dp, b)

    hops = [(k // 2, k % 2) for k in range(1, 2 * fars)]
    arrived = [hop(part, f, b) for part, (f, b) in zip(parts[1:], hops)]
    arrived, beside = together(arrived, beside)
    beside = after(*beside)
    total = parts[0]
    for part in arrived:
        total = total + part
    cols = width // highs
    part = lax.dynamic_slice_in_dim(total, high * cols, cols, 1)
    away = [lax.dynamic_slice_in_dim(total, (high ^ j) * cols, cols, 1) for j in range(1, highs)]
    arrived = [swap(a, "dp", dp, 2 * (j + 1)) for j, a in enumerate(away)]
    arrived, beside = together(arrived, beside)
    for block in arrived:
        part = part + block
    part = part.astype(BF16)
    line = jnp.zeros((small, width), BF16)
    line = lax.dynamic_update_slice_in_dim(line, part, high * cols, 1)
    arrived = [swap(part, "dp", dp, 2 * j) for j in range(1, highs)]
    for j, block in enumerate(arrived):
        line = lax.dynamic_update_slice_in_dim(line, block, (high ^ (j + 1)) * cols, 1)
    block = jnp.zeros((rows, width), BF16)
    block = lax.dynamic_update_slice_in_dim(block, line, mine * small, 0)
    for f, b in hops:
        target = (far ^ f) * 2 + (low ^ b)
        block = lax.dynamic_update_slice_in_dim(block, hop(line, f, b), target * small, 0)
    partner = swap(block, "group", group, 1)
    first = jnp.where(core == 0, block, partner)
    second = jnp.where(core == 0, partner, block)
    return jnp.concatenate([first, second], axis=0).astype(F32), beside


def encoding_tables(patch_count):
    quarter = D // 4
    half_width = D // 2
    power = lambda n: np.power(np.float32(10000.0), -np.arange(n, dtype=np.float32) / np.float32(n))
    at = np.arange(GRID).astype(np.float32)[:, None] * power(quarter)
    both = np.concatenate([np.sin(at), np.cos(at)], axis=-1)
    patch = np.arange(patch_count)
    rest = np.concatenate([both[patch // GRID], both[patch % GRID]], axis=-1).astype(np.float32)
    parts = []
    for _ in range(3):
        parts.append(rest.astype(ml_dtypes.bfloat16))
        rest = rest - parts[-1].astype(np.float32)
    group_at = np.arange(GROUPS).astype(np.float32)[:, None] * power(half_width)
    return np.stack(parts), np.concatenate([np.sin(group_at), np.cos(group_at)], axis=-1).astype(np.float32)


def on_device(dp, group, patches, vis_index, vis_count, w_stem, ln_gain, w_qkv, w_out, out_grad):
    scenes = patches.shape[0]
    tokens = scenes * TOK
    width = w_qkv.shape[2]
    fars = range(1, group // 2)
    rests = range(1, dp // 2)
    dp_low, dp_high = lax.axis_index("dp") % 2, lax.axis_index("dp") // 2
    low, high = dp_low.reshape(1), dp_high.reshape(1)
    core = (lax.axis_index("group") % 2).reshape(1)

    shard = jnp.concatenate([w_qkv.reshape(w_qkv.shape[0], 3 * width), w_out.T], axis=1)
    cross = lambda x, f: swap(x, "group", group, 2 * f)
    far_shards = [cross(shard, f) for f in fars]
    counts = vis_count.astype(jnp.int32)
    counts_far = swap(counts, "group", group, 1)
    table, genc = encoding_tables(patches.shape[1])
    gain = ln_gain.reshape(1, D)
    stem = stem_call(
        counts,
        vis_index,
        patches,
        w_stem,
        gain,
        jnp.asarray(table),
        jnp.asarray(genc),
        out_grad.reshape(scenes, TOK, D),
    )
    stem, counts_far, far_shards = together(stem, counts_far, far_shards)
    emb = stem[0].reshape(tokens, D)
    both = [stem[1].reshape(2, tokens, D)]
    cols = stem[2].reshape(tokens, stem[2].shape[2])
    both_counts = jnp.stack([counts, counts_far])
    both.append(swap(both[0], "group", group, 1))
    rings = [Ring(x, "dp", dp) for x in far_shards]
    passed = []
    (both,) = step_all(rings, both)
    while rings[0].steps < dp // 2:
        passed.append(cross(rings[0].ahead[-1], 1))
        if len(passed) > 1:
            (passed[-2],) = step_all(rings, passed[-2])
        else:
            step_all(rings)
    ring = rings[0]
    ring.ahead, ring.behind = together(ring.ahead, ring.behind)
    passed.append(cross(ring.ahead[-1], 1))
    behind = ring.behind[1:]
    passed.append(cross(jnp.concatenate(behind, axis=0), 1))
    owners = ring.owners()

    packs, weights, crossing = [], [], []
    for f in list(fars) + [0]:
        if f:
            blocks = rings[f - 1].ahead + rings[f - 1].behind[1:]
        else:
            rows = shard.shape[0]
            blocks = [shard] + passed[:-1] + [passed[-1][b * rows : (b + 1) * rows] for b in range(len(behind))]
        made = attention_call(both_counts, owners, low, *both, None if f else (packs, weights), blocks, dp)
        if f == 1:
            made, passed[-3:] = together(made, passed[-3:])
        elif f:
            made = together(*made)
        else:
            made, others = together(made, [c[1] for c in crossing])
        pack, weight, keep, other, *back = made
        packs.append(pack)
        weights.append(weight)
        if f:
            crossing.append([cross(keep, f), cross(other, f)])
    back_far = swap(back[1], "group", group, 1)
    for x in others:
        other = other + x.astype(F32)
    coming = swap(other.astype(BF16), "dp", dp, 1)
    stem_made, keeps = together(
        tail_call(core, back[0], back_far, emb, both[0], cols, gain), [c[0] for c in crossing]
    )
    stem_keep, *stem_recv = stem_made
    stem_recv = [swap(x, "group", group, 1) for x in stem_recv]
    stem_recv, coming = together(stem_recv, coming)
    stem_parts = halve_stem(stem_recv, stem_keep, group)
    kinds = [F32 if j < 2 else BF16 for j in range(dp // 2)]
    blocks = combine_call(high, keep, [[k] for k in keeps] + [[coming]], kinds)
    landing = [blocks[0]] + [swap(blocks[j], "dp", dp, 2 * j) for j in rests]
    near = dp // 2 * 3 // 4

    def after(mixed, *arrived):
        mixed = swap(mixed, "group", group, 1)
        return [output_call(counts, mixed, emb, packs, weights)] + list(arrived) + landing[near:]

    grad_w_stem, (output, *landing) = sum_stem(
        stem_parts, [mixed_call(packs, weights)] + landing[:near], after, dp, group
    )
    total = add_call(landing)
    grad_w_qkv = total[:, : 3 * width].reshape(total.shape[0], 3, width)
    grad_w_out = total[:, 3 * width :].T
    return (output.reshape(scenes, GROUPS, CAP, D), grad_w_stem, grad_w_qkv, grad_w_out)


def solution(mesh):
    sizes = dict(mesh.shape)
    return jax.shard_map(
        functools.partial(on_device, sizes["dp"], sizes["group"]),
        mesh=mesh,
        in_specs=(
            P(("dp", "group"), None, None),
            P(("dp", "group"), None, None),
            P(("dp", "group"), None),
            P(),
            P(),
            P("dp", None, "group"),
            P("group", "dp"),
            P(("dp", "group"), None, None, None),
        ),
        out_specs=(
            P(("dp", "group"), None, None, None),
            P(),
            P("dp", None, "group"),
            P("group", "dp"),
        ),
        check_vma=False,
    )
```

```python
import functools

import jax
import jax.numpy as jnp
import ml_dtypes
import numpy as np
from jax import lax
from jax.experimental import pallas as pl
from jax.experimental.pallas import tpu as pltpu
from jax.sharding import PartitionSpec as P

D = 1024
HD = 64
GROUPS = 3
CAP = 48
GRID = 12
PIX = 64
TOK = GROUPS * CAP
PAIR = 128
GROUP_BANDS = ((0, 4), (4, 8), (8, 10))
NORM_EPS = 1e-06
F32 = jnp.float32
BF16 = jnp.bfloat16
VMEM_LIMIT = 60 * 1024 * 1024


def dot_nn(a, b):
    return lax.dot_general(a, b, (((1,), (0,)), ((), ())), preferred_element_type=F32)


def dot_nt(a, b):
    return lax.dot_general(a, b, (((1,), (1,)), ((), ())), preferred_element_type=F32)


def dot_tn(a, b):
    return lax.dot_general(a, b, (((0,), (0,)), ((), ())), preferred_element_type=F32)


def live_column(c0, c1, c2):
    row = lax.broadcasted_iota(jnp.int32, (TOK, 1), 0)
    return (
        (row < c0)
        | ((row >= CAP) & (row < CAP + c1))
        | ((row >= 2 * CAP) & (row < 2 * CAP + c2))
    )


def params():
    return pltpu.CompilerParams(vmem_limit_bytes=VMEM_LIMIT)


def cost(flops, nbytes):
    return pl.CostEstimate(flops=int(flops / 1000), bytes_accessed=int(nbytes / 1000), transcendentals=0)


def stem_kernel(
    cnt_ref, idx_ref, patch_ref, w_ref, gain_ref, parts, genc_ref, og_ref,
    emb_ref, rows_ref, cols_ref,
):
    step = pl.program_id(0)
    scenes = patch_ref.shape[0]
    patch_iota = lax.broadcasted_iota(jnp.int32, (parts.shape[1], CAP), 0)
    slot = lax.broadcasted_iota(jnp.int32, (CAP, 1), 0)
    for g, (start, end) in enumerate(GROUP_BANDS):
        rows = slice(g * CAP, (g + 1) * CAP)
        width = (end - start) * PIX
        picked, placed = [], []
        for s in range(scenes):
            onehot = (idx_ref[s, g : g + 1, :] == patch_iota).astype(F32).astype(BF16).T
            picked.append(dot_nn(onehot, patch_ref[s, :, start * PIX : end * PIX]).astype(BF16))
            placed.append(
                (dot_nn(onehot, parts[0]) + dot_nn(onehot, parts[1])) + dot_nn(onehot, parts[2])
            )
            live = slot < cnt_ref[pl.ds(step * scenes + s, 1), g : g + 1]
            rows_ref[1, s, rows, :] = jnp.where(live, og_ref[s, rows, :].astype(F32), 0.0).astype(BF16)
        summed = dot_nn(jnp.concatenate(picked, axis=0), w_ref[start * PIX : end * PIX, :])
        for s in range(scenes):
            values = summed[s * CAP : (s + 1) * CAP] + (placed[s] + genc_ref[g : g + 1, :])
            emb = values.astype(BF16)
            emb_ref[s, rows, :] = emb
            x = emb.astype(F32)
            centre = jnp.mean(x, axis=-1, keepdims=True)
            dev = x - centre
            spread = jnp.mean(dev * dev, axis=-1, keepdims=True)
            centred = dev * lax.rsqrt(spread + NORM_EPS)
            rows_ref[0, s, rows, :] = (centred * gain_ref[...]).astype(BF16)
            cols_ref[s, rows, :width] = picked[s]
            if width < cols_ref.shape[2]:
                cols_ref[s, rows, width:] = jnp.zeros((CAP, cols_ref.shape[2] - width), BF16)


def stem_call(counts, index, patches, w_stem, gain, table, genc, out_grad):
    scenes, patch_count, width = patches.shape
    block = 3 if scenes % 3 == 0 else 1
    col_width = max(e - s for s, e in GROUP_BANDS) * PIX
    per = lambda shape: pl.BlockSpec((block,) + shape, lambda i: (i, 0, 0))
    whole = lambda a: pl.BlockSpec(a.shape, lambda i: (0,) * a.ndim)
    return pl.pallas_call(
        stem_kernel,
        grid=(scenes // block,),
        in_specs=[
            whole(counts),
            per((GROUPS, CAP)),
            per((patch_count, width)),
            whole(w_stem),
            whole(gain),
            whole(table),
            whole(genc),
            per((TOK, D)),
        ],
        out_specs=[
            per((TOK, D)),
            pl.BlockSpec((2, block, TOK, D), lambda i: (0, i, 0, 0)),
            per((TOK, col_width)),
        ],
        out_shape=[
            jax.ShapeDtypeStruct((scenes, TOK, D), BF16),
            jax.ShapeDtypeStruct((2, scenes, TOK, D), BF16),
            jax.ShapeDtypeStruct((scenes, TOK, col_width), BF16),
        ],
        compiler_params=params(),
        cost_estimate=cost(8e9, 12e6),
        name="stem_norm",
    )(counts, index, patches, w_stem, gain, table, genc, out_grad)


def attention_kernel(
    packs, blocks, dp, cnt_ref, owner_ref, low_ref, na_ref, nb_ref, ga_ref, gb_ref, *refs
):
    earlier, refs = refs[: 2 * (packs or 0)], refs[2 * (packs or 0) :]
    blocks, refs = refs[:blocks], refs[blocks:]
    out_ref, w_ref, *refs = refs
    keeps, other_ref, refs = refs[:2], refs[2], refs[3:]
    n_s, g_s, qkv, total = refs[-4:]
    half, step = pl.program_id(0), pl.program_id(1)
    rows = n_s.shape[0]
    scenes = rows // TOK
    width = w_ref.shape[1] // 4

    @pl.when((half == 0) & (step == 0))
    def _():
        size = blocks[0].shape[0]
        for b, block in enumerate(blocks):
            w_ref[pl.ds(pl.multiple_of(owner_ref[b] * size, size), size), :] = block[...]
        total[...] = jnp.zeros_like(total)

    @pl.when(half == 0)
    def _():
        n_s[...] = na_ref[0]
        g_s[...] = ga_ref[0]

    @pl.when(half != 0)
    def _():
        n_s[...] = nb_ref[0]
        g_s[...] = gb_ref[0]

    qkv[:, : 3 * width] = dot_nn(n_s[...], w_ref[:, : 3 * width]).astype(BF16)
    qkv[:, 3 * width :] = dot_nn(g_s[...], w_ref[:, 3 * width :]).astype(BF16)
    heads = width // HD
    lane = lax.broadcasted_iota(jnp.int32, (1, width), 1)
    masks = [(lane // HD == h).astype(F32).astype(BF16) for h in range(heads)]
    scale = jnp.asarray(HD ** (-0.5), BF16)
    first_of_pair = lax.broadcasted_iota(jnp.int32, (1, PAIR), 1) < HD

    def own_lanes(tall):
        tiles = []
        for t in range(width // PAIR):
            at = slice(t * PAIR, (t + 1) * PAIR)
            one = tall[2 * t * TOK : (2 * t + 1) * TOK, at]
            two = tall[(2 * t + 1) * TOK : (2 * t + 2) * TOK, at]
            tiles.append(jnp.where(first_of_pair, one, two))
        return jnp.concatenate(tiles, axis=1)

    def scene_body(s, _):
        base = pl.multiple_of(s * TOK, 16)
        at = pl.ds(base, TOK)
        scene = step * scenes + s
        live = live_column(cnt_ref[half, scene, 0], cnt_ref[half, scene, 1], cnt_ref[half, scene, 2])
        bias = jnp.where(live, 0.0, -1e30)
        q, k, v, dc = [qkv[at, c * width : (c + 1) * width] for c in range(4)]
        tall_q = jnp.concatenate([q * (m * scale) for m in masks], axis=0)
        tall_dc = jnp.concatenate([dc * m for m in masks], axis=0)
        scores = dot_nt(k, tall_q)
        grad_probs = dot_nt(v, tall_dc)
        probs_parts, score_parts = [], []
        for start in range(0, heads * TOK, PAIR):
            cols = slice(start, min(start + PAIR, heads * TOK))
            part = scores[:, cols] + bias
            lifted = jnp.exp(part - jnp.max(part, axis=0, keepdims=True))
            probs = lifted * (1.0 / jnp.sum(lifted, axis=0, keepdims=True))
            weighted = probs * grad_probs[:, cols]
            inner = jnp.sum(weighted, axis=0, keepdims=True)
            probs_parts.append(probs.astype(BF16))
            score_parts.append((weighted - probs * inner).astype(BF16))
        half_probs = jnp.concatenate(probs_parts, axis=1)
        grad_score = jnp.concatenate(score_parts, axis=1)
        out_ref[at, :width] = (own_lanes(dot_tn(grad_score, k)) * HD ** (-0.5)).astype(BF16)
        out_ref[at, width : 2 * width] = dot_nn(grad_score, tall_q).astype(BF16)
        out_ref[at, 2 * width : 3 * width] = dot_nn(half_probs, tall_dc).astype(BF16)
        out_ref[at, 3 * width :] = own_lanes(dot_tn(half_probs, v)).astype(BF16)
        return 0

    lax.fori_loop(0, scenes, scene_body, 0, unroll=True)
    total[:, : 3 * width] += dot_tn(n_s[...], out_ref[:, : 3 * width])
    total[:, 3 * width :] += dot_tn(g_s[...], out_ref[:, 3 * width :])

    @pl.when((half == pl.num_programs(0) - 1) & (step == pl.num_programs(1) - 1))
    def _():
        size = total.shape[0] // dp
        low = low_ref[0]
        for b in range(dp // 2):
            at = slice(b * size, (b + 1) * size)
            mine = pl.multiple_of((2 * b + low) * size, size)
            other = pl.multiple_of((2 * b + 1 - low) * size, size)
            for c in range(2):
                cols = slice(c * 2 * width, (c + 1) * 2 * width)
                keeps[c][at, :] = total[pl.ds(mine, size), cols].astype(keeps[c].dtype)
            other_ref[at, :] = total[pl.ds(other, size), :].astype(other_ref.dtype)

    if packs is not None:
        back = dot_nt(out_ref[:, : 3 * width], w_ref[:, : 3 * width])
        for pack_ref, weight_ref in zip(earlier[:packs], earlier[packs:]):
            back = back + dot_nt(pack_ref[...], weight_ref[...])

        @pl.when(half == 0)
        def _():
            refs[0][...] = back

        @pl.when(half != 0)
        def _():
            refs[1][...] = back


def block_rows(tokens):
    return 3 * TOK if tokens % (3 * TOK) == 0 else TOK


def two_halves(rows, steps, lead):
    shape = (1,) * len(lead) + (rows, D)
    first = pl.BlockSpec(shape, lambda h, i: lead + (jnp.where(h == 0, i, steps - 1), 0))
    second = pl.BlockSpec(shape, lambda h, i: lead + (jnp.where(h == 0, 0, i), 0))
    return [first, second]


SCALARS = pl.BlockSpec(memory_space=pltpu.SMEM)


def attention_call(counts, owners, low, own, far, earlier, blocks, dp):
    tokens = own.shape[1]
    rows = block_rows(tokens)
    steps = tokens // rows
    cols = blocks[0].shape[1]
    whole = lambda shape: pl.BlockSpec(shape, lambda h, i: (0, 0))
    at = lambda h, i: (h * steps + i, 0)
    packs = None if earlier is None else len(earlier[0])
    back = [] if earlier is None else two_halves(rows, steps, ())
    kind = BF16 if earlier is None else F32
    grads = [jax.ShapeDtypeStruct((D // 2, c), kind) for c in (cols // 2, cols // 2, cols)]
    back_shape = jax.ShapeDtypeStruct((tokens, D), F32)
    return pl.pallas_call(
        functools.partial(attention_kernel, packs, len(blocks), dp),
        grid=(2, steps),
        in_specs=[SCALARS] * 3
        + two_halves(rows, steps, (0,))
        + two_halves(rows, steps, (1,))
        + [pl.BlockSpec((rows, cols // 4 * 3), at)] * (packs or 0)
        + [whole((D, cols // 4 * 3))] * (packs or 0)
        + [whole(b.shape) for b in blocks],
        out_specs=[pl.BlockSpec((rows, cols), at), whole((D, cols))] + [whole(g.shape) for g in grads] + back,
        out_shape=[
            jax.ShapeDtypeStruct((2 * tokens, cols), BF16),
            jax.ShapeDtypeStruct((D, cols), BF16),
            *grads,
        ]
        + [back_shape] * len(back),
        scratch_shapes=[
            pltpu.VMEM((rows, D), BF16),
            pltpu.VMEM((rows, D), BF16),
            pltpu.VMEM((rows, cols), BF16),
            pltpu.VMEM((D, cols), F32),
        ],
        compiler_params=params(),
        cost_estimate=cost(20e9, 14e6),
        name="attention",
    )(counts, owners, low, own, far, own, far, *[x for group in earlier or () for x in group], *blocks)


def combine_kernel(counts, place_ref, *refs):
    ins, refs = refs[: sum(counts)], refs[sum(counts) :]
    rows = refs[0].shape[0]
    place = place_ref[0]
    for j, ref in enumerate(refs):
        at = pl.ds(pl.multiple_of((place ^ j) * rows, rows), rows)
        total = None
        first = 0
        for count in counts:
            pieces = [r[at, :].astype(F32) for r in ins[first : first + count]]
            new = pieces[0] if count == 1 else jnp.concatenate(pieces, axis=1)
            total = new if total is None else total + new
            first += count
        ref[...] = total.astype(ref.dtype)


def combine_call(place, parts, dtypes):
    ins = [piece for part in parts for piece in part]
    rows, cols = ins[0].shape[0] // len(dtypes), sum(piece.shape[1] for piece in parts[0])
    whole = lambda a: pl.BlockSpec(a.shape, lambda: (0, 0))
    return pl.pallas_call(
        functools.partial(combine_kernel, [len(part) for part in parts]),
        in_specs=[SCALARS] + [whole(a) for a in ins],
        out_specs=[pl.BlockSpec((rows, cols), lambda: (0, 0))] * len(dtypes),
        out_shape=[jax.ShapeDtypeStruct((rows, cols), d) for d in dtypes],
        compiler_params=params(),
        cost_estimate=cost(1e6, 5e6),
        name="combine",
    )(place, *ins)


def add_kernel(*refs):
    total = refs[0][...]
    for ref in refs[1:-1]:
        total = total + ref[...].astype(F32)
    refs[-1][...] = total


def add_call(parts):
    spec = pl.BlockSpec(parts[0].shape, lambda: (0, 0))
    return pl.pallas_call(
        add_kernel,
        in_specs=[spec] * len(parts),
        out_specs=spec,
        out_shape=jax.ShapeDtypeStruct(parts[0].shape, F32),
        compiler_params=params(),
        cost_estimate=cost(1e6, 2e6),
        name="add_parts",
    )(*parts)


def mixed_product(context_refs, weight_refs):
    total = None
    for context_ref, w_ref in zip(context_refs, weight_refs):
        new = dot_nt(context_ref[...], w_ref[...])
        total = new if total is None else total + new
    return total


def context_specs(rows, packs, weights, first):
    width = packs[0].shape[1] // 4
    return [pl.BlockSpec((rows, width), lambda i: (first + i, 3))] * len(packs) + [
        pl.BlockSpec((D, width), lambda i: (0, 3))
    ] * len(weights)


def mixed_kernel(count, *refs):
    refs[-1][...] = mixed_product(refs[:count], refs[count : 2 * count]).astype(BF16)


def mixed_call(packs, weights):
    tokens = packs[0].shape[0] // 2
    rows = block_rows(tokens)
    return pl.pallas_call(
        functools.partial(mixed_kernel, len(packs)),
        grid=(tokens // rows,),
        in_specs=context_specs(rows, packs, weights, tokens // rows),
        out_specs=pl.BlockSpec((rows, D), lambda i: (i, 0)),
        out_shape=jax.ShapeDtypeStruct((tokens, D), BF16),
        compiler_params=params(),
        cost_estimate=cost(2e9, 5e6),
        name="mixed",
    )(*packs, *weights)


def tail_kernel(core_ref, own_ref, recv_ref, emb_ref, gl_ref, cols_ref, gain_ref, keep_ref, first_ref, second_ref, acc):
    step = pl.program_id(0)
    rows = emb_ref.shape[0]
    scenes = rows // TOK

    @pl.when(step == 0)
    def _():
        acc[...] = jnp.zeros_like(acc)

    grad_normed = own_ref[...] + recv_ref[...]
    x = emb_ref[...].astype(F32)
    dev = x - jnp.mean(x, axis=-1, keepdims=True)
    inv_std = lax.rsqrt(jnp.mean(dev * dev, axis=-1, keepdims=True) + NORM_EPS)
    centred = dev * inv_std
    scaled = grad_normed * gain_ref[...]
    first_mean = jnp.mean(scaled, axis=-1, keepdims=True)
    second_mean = jnp.mean(scaled * centred, axis=-1, keepdims=True)
    back = inv_std * (scaled - first_mean - centred * second_mean)
    grad_in = (gl_ref[0].astype(F32) + back).astype(BF16)
    for g, (start, end) in enumerate(GROUP_BANDS):
        at = [slice(s * TOK + g * CAP, s * TOK + (g + 1) * CAP) for s in range(scenes)]
        columns = jnp.concatenate([cols_ref[a, : (end - start) * PIX] for a in at], axis=0)
        grads = jnp.concatenate([grad_in[a] for a in at], axis=0)
        acc[start * PIX : end * PIX, :] += dot_tn(columns, grads)

    @pl.when(step == pl.num_programs(0) - 1)
    def _():
        size = keep_ref.shape[0]
        core = core_ref[0]
        keep_ref[...] = acc[pl.ds(pl.multiple_of(core * size, size), size), :]
        other = pl.ds(pl.multiple_of((1 - core) * size, size), size)
        first_ref[...] = acc[other, : D // 2]
        second_ref[...] = acc[other, D // 2 :]


def tail_call(core, own, recv, emb, rows_own, cols, gain):
    tokens = emb.shape[0]
    rows = 2 * TOK if tokens % (2 * TOK) == 0 else TOK
    per = lambda a: pl.BlockSpec((rows, a.shape[1]), lambda i: (i, 0))
    stem_rows = GROUP_BANDS[-1][1] * PIX
    keep = jax.ShapeDtypeStruct((stem_rows // 2, D), F32)
    send = jax.ShapeDtypeStruct((stem_rows // 2, D // 2), F32)
    return pl.pallas_call(
        tail_kernel,
        grid=(tokens // rows,),
        in_specs=[SCALARS, per(own), per(recv), per(emb), pl.BlockSpec((1, rows, D), lambda i: (1, i, 0)), per(cols)]
        + [pl.BlockSpec(gain.shape, lambda i: (0, 0))],
        out_specs=[pl.BlockSpec(a.shape, lambda i: (0, 0)) for a in (keep, send, send)],
        out_shape=[keep, send, send],
        scratch_shapes=[pltpu.VMEM((stem_rows, D), F32)],
        compiler_params=params(),
        cost_estimate=cost(10e9, 12e6),
        name="tail",
    )(core, own, recv, emb, rows_own, cols, gain)


def output_kernel(count, cnt_ref, recv_ref, emb_ref, *refs):
    out_ref = refs[-1]
    step = pl.program_id(0)
    scenes = emb_ref.shape[0] // TOK
    mixed = recv_ref[...].astype(F32) + mixed_product(refs[:count], refs[count : 2 * count])
    total = emb_ref[...].astype(F32) + mixed
    for s in range(scenes):
        scene = step * scenes + s
        live = live_column(cnt_ref[scene, 0], cnt_ref[scene, 1], cnt_ref[scene, 2])
        at = slice(s * TOK, (s + 1) * TOK)
        out_ref[at, :] = jnp.where(live, total[at], 0.0).astype(BF16)


def output_call(counts, recv, emb, packs, weights):
    tokens = emb.shape[0]
    rows = 2 * TOK if tokens % (2 * TOK) == 0 else TOK
    per = lambda a: pl.BlockSpec((rows, a.shape[1]), lambda i: (i, 0))
    return pl.pallas_call(
        functools.partial(output_kernel, len(packs)),
        grid=(tokens // rows,),
        in_specs=[SCALARS, per(recv), per(emb)]
        + context_specs(rows, packs, weights, 0),
        out_specs=per(emb),
        out_shape=jax.ShapeDtypeStruct(emb.shape, BF16),
        compiler_params=params(),
        cost_estimate=cost(5e9, 10e6),
        name="layer_output",
    )(counts, recv, emb, *packs, *weights)


def swap(x, axis, size, bit):
    return lax.ppermute(x, axis, [(i, i ^ bit) for i in range(size)])


def together(*values):
    return lax.optimization_barrier(values)


class Ring:
    def __init__(self, x, axis, size):
        self.axis, self.size = axis, size
        order = list(range(0, size, 2)) + list(range(size - 1, 0, -2))
        self.forward = [(order[i], order[(i + 1) % size]) for i in range(size)]
        self.backward = [(order[(i + 1) % size], order[i]) for i in range(size)]
        self.ahead, self.behind = [x], [x]

    def send(self):
        moved = [lax.ppermute(self.ahead[-1], self.axis, self.forward)]
        if len(self.behind) <= (self.size - 1) // 2:
            moved.append(lax.ppermute(self.behind[-1], self.axis, self.backward))
        return moved

    def receive(self, moved):
        self.ahead.append(moved[0])
        self.behind.extend(moved[1:])

    @property
    def steps(self):
        return len(self.ahead) - 1

    def owners(self, ahead, behind):
        size = self.size
        me = lax.axis_index(self.axis)
        here = jnp.where(me % 2 == 0, me // 2, size - 1 - me // 2)
        distances = [-s for s in range(ahead)] + list(range(1, behind))
        at = (here + size + jnp.array(distances, jnp.int32)) % size
        return jnp.where(at < size // 2, 2 * at, 2 * (size - 1 - at) + 1)


def step_all(rings, *beside):
    moved, beside = together([ring.send() for ring in rings], beside)
    for ring, blocks in zip(rings, moved):
        ring.receive(blocks)
    return beside


def halve_stem(recv, keep, group):
    mine = lax.axis_index("group") // 2 * 2 + lax.axis_index("dp") % 2
    return combine_call(mine.reshape(1), [[keep], recv], [F32] * (group // 2 * 2))


def sum_stem(parts, beside, after, last, dp, group):
    core = lax.axis_index("group") % 2
    far = lax.axis_index("group") // 2
    low = lax.axis_index("dp") % 2
    high = lax.axis_index("dp") // 2
    fars, highs = group // 2, dp // 2
    mine = far * 2 + low
    small, width = parts[0].shape
    rows = 2 * fars * small

    def hop(block, f, b):
        if f:
            pairs = [
                (d * group + g, (d ^ b) * group + (g ^ (2 * f))) for d in range(dp) for g in range(group)
            ]
            return lax.ppermute(block, ("dp", "group"), pairs)
        return swap(block, "dp", dp, b)

    hops = [(k // 2, k % 2) for k in range(1, 2 * fars)]
    arrived = [hop(part, f, b) for part, (f, b) in zip(parts[1:], hops)]
    arrived, beside = together(arrived, beside)
    beside = after(*beside)
    total = parts[0]
    for part in arrived:
        total = total + part
    cols = width // highs
    part = lax.dynamic_slice_in_dim(total, high * cols, cols, 1)
    away = [lax.dynamic_slice_in_dim(total, (high ^ j) * cols, cols, 1) for j in range(1, highs)]
    arrived = [swap(a, "dp", dp, 2 * (j + 1)) for j, a in enumerate(away)]
    arrived, beside = together(arrived, beside)
    for block in arrived:
        part = part + block
    part = part.astype(BF16)
    line = jnp.zeros((small, width), BF16)
    line = lax.dynamic_update_slice_in_dim(line, part, high * cols, 1)
    arrived = [swap(part, "dp", dp, 2 * j) for j in range(1, highs)]
    for j, block in enumerate(arrived):
        line = lax.dynamic_update_slice_in_dim(line, block, (high ^ (j + 1)) * cols, 1)
    block = jnp.zeros((rows, width), BF16)
    block = lax.dynamic_update_slice_in_dim(block, line, mine * small, 0)
    arrived, beside = together([hop(line, f, b) for f, b in hops], last(*beside))
    for (f, b), piece in zip(hops, arrived):
        target = (far ^ f) * 2 + (low ^ b)
        block = lax.dynamic_update_slice_in_dim(block, piece, target * small, 0)
    partner = swap(block, "group", group, 1)
    first = jnp.where(core == 0, block, partner)
    second = jnp.where(core == 0, partner, block)
    return jnp.concatenate([first, second], axis=0).astype(F32), beside


def encoding_tables(patch_count):
    quarter = D // 4
    half_width = D // 2
    power = lambda n: np.power(np.float32(10000.0), -np.arange(n, dtype=np.float32) / np.float32(n))
    at = np.arange(GRID).astype(np.float32)[:, None] * power(quarter)
    both = np.concatenate([np.sin(at), np.cos(at)], axis=-1)
    patch = np.arange(patch_count)
    rest = np.concatenate([both[patch // GRID], both[patch % GRID]], axis=-1).astype(np.float32)
    parts = []
    for _ in range(3):
        parts.append(rest.astype(ml_dtypes.bfloat16))
        rest = rest - parts[-1].astype(np.float32)
    group_at = np.arange(GROUPS).astype(np.float32)[:, None] * power(half_width)
    return np.stack(parts), np.concatenate([np.sin(group_at), np.cos(group_at)], axis=-1).astype(np.float32)


def on_device(dp, group, patches, vis_index, vis_count, w_stem, ln_gain, w_qkv, w_out, out_grad):
    scenes = patches.shape[0]
    tokens = scenes * TOK
    width = w_qkv.shape[2]
    fars = range(1, group // 2)
    rests = range(1, dp // 2)
    dp_low, dp_high = lax.axis_index("dp") % 2, lax.axis_index("dp") // 2
    low, high = dp_low.reshape(1), dp_high.reshape(1)
    core = (lax.axis_index("group") % 2).reshape(1)

    shard = jnp.concatenate([w_qkv.reshape(w_qkv.shape[0], 3 * width), w_out.T], axis=1)
    cross = lambda x, f: swap(x, "group", group, 2 * f)
    far_shards = [cross(shard, f) for f in fars]
    counts = vis_count.astype(jnp.int32)
    counts_far = swap(counts, "group", group, 1)
    table, genc = encoding_tables(patches.shape[1])
    gain = ln_gain.reshape(1, D)
    counts_far, far_shards = together(counts_far, far_shards)
    far_shards, gain = together(far_shards, gain)
    stem = stem_call(
        counts,
        vis_index,
        patches,
        w_stem,
        gain,
        jnp.asarray(table),
        jnp.asarray(genc),
        out_grad.reshape(scenes, TOK, D),
    )
    rings = [Ring(x, "dp", dp) for x in far_shards]
    ring = rings[0]
    stem, both_counts, owners = step_all(rings, stem, jnp.stack([counts, counts_far]), ring.owners(dp // 2 + 1, dp // 2))
    emb = stem[0].reshape(tokens, D)
    both = [stem[1].reshape(2, tokens, D)]
    cols = stem[2].reshape(tokens, stem[2].shape[2])
    both.append(swap(both[0], "group", group, 1))
    passed = [cross(ring.ahead[-1], 1)]
    (both,) = step_all(rings, both)
    while ring.steps < dp // 2:
        passed.append(cross(ring.ahead[-1], 1))
        (passed[-2],) = step_all(rings, passed[-2])
    ring.ahead, ring.behind = together(ring.ahead, ring.behind)
    passed.append(cross(ring.ahead[-1], 1))
    behind = ring.behind[1:]
    passed.append(cross(jnp.concatenate(behind, axis=0), 1))

    packs, weights, crossing = [], [], []
    for f in list(fars) + [0]:
        if f:
            blocks = rings[f - 1].ahead + rings[f - 1].behind[1:]
        else:
            rows = shard.shape[0]
            blocks = [shard] + passed[:-1] + [passed[-1][b * rows : (b + 1) * rows] for b in range(len(behind))]
        made = attention_call(both_counts, owners, low, *both, None if f else (packs, weights), blocks, dp)
        if f == 1:
            made, passed[-3:] = together(made, passed[-3:])
        elif f:
            made = together(*made)
        else:
            made, arrived = together(made, [x[:2] for x in crossing])
        pack, weight, keep, other, back = made[0], made[1], made[2:4], made[4], made[5:]
        packs.append(pack)
        weights.append(weight)
        if f:
            crossing.append([cross(x, f) for x in (other, *keep)])
    back_far = swap(back[1], "group", group, 1)
    for x in arrived:
        other = other + x[0].astype(F32)
    coming = swap(other.astype(BF16), "dp", dp, 1)
    stem_made, last_keeps = together(
        tail_call(core, back[0], back_far, emb, both[0], cols, gain), [x[2] for x in crossing]
    )
    keeps = [list(keep)] + [[x[1], y] for x, y in zip(arrived, last_keeps)]
    stem_keep, *stem_recv = stem_made
    stem_recv = [swap(x, "group", group, 1) for x in stem_recv]
    stem_parts = halve_stem(stem_recv, stem_keep, group)
    _, coming, keeps = together(stem_parts, coming, keeps)
    kinds = [F32 if j < 2 else BF16 for j in range(dp // 2)]
    blocks = combine_call(high, keeps + [[coming]], kinds)
    landing = [blocks[0]] + [swap(blocks[j], "dp", dp, 2 * j) for j in rests]
    near = dp // 2 * 3 // 4

    def after(mixed, share):
        mixed = swap(mixed, "group", group, 1)
        return [output_call(counts, mixed, emb, packs, weights), share] + landing[1:near]

    def last(output, *arrived):
        total = add_call(list(arrived) + landing[near:])
        return output, total[:, : 3 * width].reshape(total.shape[0], 3, width), total[:, 3 * width :].T

    grad_w_stem, (output, grad_w_qkv, grad_w_out) = sum_stem(
        stem_parts, [mixed_call(packs, weights), landing[0]], after, last, dp, group
    )
    return (output.reshape(scenes, GROUPS, CAP, D), grad_w_stem, grad_w_qkv, grad_w_out)


def solution(mesh):
    sizes = dict(mesh.shape)
    return jax.shard_map(
        functools.partial(on_device, sizes["dp"], sizes["group"]),
        mesh=mesh,
        in_specs=(
            P(("dp", "group"), None, None),
            P(("dp", "group"), None, None),
            P(("dp", "group"), None),
            P(),
            P(),
            P("dp", None, "group"),
            P("group", "dp"),
            P(("dp", "group"), None, None, None),
        ),
        out_specs=(
            P(("dp", "group"), None, None, None),
            P(),
            P("dp", None, "group"),
            P("group", "dp"),
        ),
        check_vma=False,
    )
```

```python
import functools

import jax
import jax.numpy as jnp
import ml_dtypes
import numpy as np
from jax import lax
from jax.experimental import pallas as pl
from jax.experimental.pallas import tpu as pltpu
from jax.sharding import PartitionSpec as P

D = 1024
HD = 64
GROUPS = 3
CAP = 48
GRID = 12
PIX = 64
TOK = GROUPS * CAP
PAIR = 128
GROUP_BANDS = ((0, 4), (4, 8), (8, 10))
NORM_EPS = 1e-06
F32 = jnp.float32
BF16 = jnp.bfloat16
VMEM_LIMIT = 60 * 1024 * 1024


def dot_nn(a, b):
    return lax.dot_general(a, b, (((1,), (0,)), ((), ())), preferred_element_type=F32)


def dot_nt(a, b):
    return lax.dot_general(a, b, (((1,), (1,)), ((), ())), preferred_element_type=F32)


def dot_tn(a, b):
    return lax.dot_general(a, b, (((0,), (0,)), ((), ())), preferred_element_type=F32)


def live_column(c0, c1, c2):
    row = lax.broadcasted_iota(jnp.int32, (TOK, 1), 0)
    return (
        (row < c0)
        | ((row >= CAP) & (row < CAP + c1))
        | ((row >= 2 * CAP) & (row < 2 * CAP + c2))
    )


def params():
    return pltpu.CompilerParams(vmem_limit_bytes=VMEM_LIMIT)


def cost(flops, nbytes):
    return pl.CostEstimate(flops=int(flops / 1000), bytes_accessed=int(nbytes / 1000), transcendentals=0)


def stem_kernel(
    cnt_ref, idx_ref, patch_ref, w_ref, gain_ref, parts, genc_ref, og_ref,
    emb_ref, rows_ref, cols_ref,
):
    step = pl.program_id(0)
    scenes = patch_ref.shape[0]
    patch_iota = lax.broadcasted_iota(jnp.int32, (parts.shape[1], CAP), 0)
    slot = lax.broadcasted_iota(jnp.int32, (CAP, 1), 0)
    for g, (start, end) in enumerate(GROUP_BANDS):
        rows = slice(g * CAP, (g + 1) * CAP)
        width = (end - start) * PIX
        picked, placed = [], []
        for s in range(scenes):
            onehot = (idx_ref[s, g : g + 1, :] == patch_iota).astype(F32).astype(BF16).T
            picked.append(dot_nn(onehot, patch_ref[s, :, start * PIX : end * PIX]).astype(BF16))
            placed.append(
                (dot_nn(onehot, parts[0]) + dot_nn(onehot, parts[1])) + dot_nn(onehot, parts[2])
            )
            live = slot < cnt_ref[pl.ds(step * scenes + s, 1), g : g + 1]
            rows_ref[1, s, rows, :] = jnp.where(live, og_ref[s, rows, :].astype(F32), 0.0).astype(BF16)
        summed = dot_nn(jnp.concatenate(picked, axis=0), w_ref[start * PIX : end * PIX, :])
        for s in range(scenes):
            values = summed[s * CAP : (s + 1) * CAP] + (placed[s] + genc_ref[g : g + 1, :])
            emb = values.astype(BF16)
            emb_ref[s, rows, :] = emb
            x = emb.astype(F32)
            centre = jnp.mean(x, axis=-1, keepdims=True)
            dev = x - centre
            spread = jnp.mean(dev * dev, axis=-1, keepdims=True)
            centred = dev * lax.rsqrt(spread + NORM_EPS)
            rows_ref[0, s, rows, :] = (centred * gain_ref[...]).astype(BF16)
            cols_ref[s, rows, :width] = picked[s]
            if width < cols_ref.shape[2]:
                cols_ref[s, rows, width:] = jnp.zeros((CAP, cols_ref.shape[2] - width), BF16)


def stem_call(counts, index, patches, w_stem, gain, table, genc, out_grad):
    scenes, patch_count, width = patches.shape
    block = 3 if scenes % 3 == 0 else 1
    col_width = max(e - s for s, e in GROUP_BANDS) * PIX
    per = lambda shape: pl.BlockSpec((block,) + shape, lambda i: (i, 0, 0))
    whole = lambda a: pl.BlockSpec(a.shape, lambda i: (0,) * a.ndim)
    return pl.pallas_call(
        stem_kernel,
        grid=(scenes // block,),
        in_specs=[
            whole(counts),
            per((GROUPS, CAP)),
            per((patch_count, width)),
            whole(w_stem),
            whole(gain),
            whole(table),
            whole(genc),
            per((TOK, D)),
        ],
        out_specs=[
            per((TOK, D)),
            pl.BlockSpec((2, block, TOK, D), lambda i: (0, i, 0, 0)),
            per((TOK, col_width)),
        ],
        out_shape=[
            jax.ShapeDtypeStruct((scenes, TOK, D), BF16),
            jax.ShapeDtypeStruct((2, scenes, TOK, D), BF16),
            jax.ShapeDtypeStruct((scenes, TOK, col_width), BF16),
        ],
        compiler_params=params(),
        cost_estimate=cost(8e9, 12e6),
        name="stem_norm",
    )(counts, index, patches, w_stem, gain, table, genc, out_grad)


def attention_kernel(
    packs, blocks, dp, cnt_ref, owner_ref, low_ref, na_ref, nb_ref, ga_ref, gb_ref, *refs
):
    earlier, refs = refs[: 2 * (packs or 0)], refs[2 * (packs or 0) :]
    blocks, refs = refs[:blocks], refs[blocks:]
    out_ref, w_ref, *refs = refs
    keeps, other_ref, refs = refs[:2], refs[2], refs[3:]
    n_s, g_s, qkv, total = refs[-4:]
    half, step = pl.program_id(0), pl.program_id(1)
    rows = n_s.shape[0]
    scenes = rows // TOK
    width = w_ref.shape[1] // 4

    @pl.when((half == 0) & (step == 0))
    def _():
        size = blocks[0].shape[0]
        for b, block in enumerate(blocks):
            w_ref[pl.ds(pl.multiple_of(owner_ref[b] * size, size), size), :] = block[...]
        total[...] = jnp.zeros_like(total)

    @pl.when(half == 0)
    def _():
        n_s[...] = na_ref[0]
        g_s[...] = ga_ref[0]

    @pl.when(half != 0)
    def _():
        n_s[...] = nb_ref[0]
        g_s[...] = gb_ref[0]

    qkv[:, : 3 * width] = dot_nn(n_s[...], w_ref[:, : 3 * width]).astype(BF16)
    qkv[:, 3 * width :] = dot_nn(g_s[...], w_ref[:, 3 * width :]).astype(BF16)
    heads = width // HD
    lane = lax.broadcasted_iota(jnp.int32, (1, width), 1)
    masks = [(lane // HD == h).astype(F32).astype(BF16) for h in range(heads)]
    scale = jnp.asarray(HD ** (-0.5), BF16)
    first_of_pair = lax.broadcasted_iota(jnp.int32, (1, PAIR), 1) < HD

    def own_lanes(tall):
        tiles = []
        for t in range(width // PAIR):
            at = slice(t * PAIR, (t + 1) * PAIR)
            one = tall[2 * t * TOK : (2 * t + 1) * TOK, at]
            two = tall[(2 * t + 1) * TOK : (2 * t + 2) * TOK, at]
            tiles.append(jnp.where(first_of_pair, one, two))
        return jnp.concatenate(tiles, axis=1)

    def scene_body(s, _):
        base = pl.multiple_of(s * TOK, 16)
        at = pl.ds(base, TOK)
        scene = step * scenes + s
        live = live_column(cnt_ref[half, scene, 0], cnt_ref[half, scene, 1], cnt_ref[half, scene, 2])
        bias = jnp.where(live, 0.0, -1e30)
        q, k, v, dc = [qkv[at, c * width : (c + 1) * width] for c in range(4)]
        tall_q = jnp.concatenate([q * (m * scale) for m in masks], axis=0)
        tall_dc = jnp.concatenate([dc * m for m in masks], axis=0)
        scores = dot_nt(k, tall_q)
        grad_probs = dot_nt(v, tall_dc)
        probs_parts, score_parts = [], []
        for start in range(0, heads * TOK, PAIR):
            cols = slice(start, min(start + PAIR, heads * TOK))
            part = scores[:, cols] + bias
            lifted = jnp.exp(part - jnp.max(part, axis=0, keepdims=True))
            probs = lifted * (1.0 / jnp.sum(lifted, axis=0, keepdims=True))
            weighted = probs * grad_probs[:, cols]
            inner = jnp.sum(weighted, axis=0, keepdims=True)
            probs_parts.append(probs.astype(BF16))
            score_parts.append((weighted - probs * inner).astype(BF16))
        half_probs = jnp.concatenate(probs_parts, axis=1)
        grad_score = jnp.concatenate(score_parts, axis=1)
        out_ref[at, :width] = (own_lanes(dot_tn(grad_score, k)) * HD ** (-0.5)).astype(BF16)
        out_ref[at, width : 2 * width] = dot_nn(grad_score, tall_q).astype(BF16)
        out_ref[at, 2 * width : 3 * width] = dot_nn(half_probs, tall_dc).astype(BF16)
        out_ref[at, 3 * width :] = own_lanes(dot_tn(half_probs, v)).astype(BF16)
        return 0

    lax.fori_loop(0, scenes, scene_body, 0, unroll=True)
    total[:, : 3 * width] += dot_tn(n_s[...], out_ref[:, : 3 * width])
    total[:, 3 * width :] += dot_tn(g_s[...], out_ref[:, 3 * width :])

    @pl.when((half == pl.num_programs(0) - 1) & (step == pl.num_programs(1) - 1))
    def _():
        size = total.shape[0] // dp
        low = low_ref[0]
        for b in range(dp // 2):
            at = slice(b * size, (b + 1) * size)
            mine = pl.multiple_of((2 * b + low) * size, size)
            other = pl.multiple_of((2 * b + 1 - low) * size, size)
            for c in range(2):
                cols = slice(c * 2 * width, (c + 1) * 2 * width)
                keeps[c][at, :] = total[pl.ds(mine, size), cols].astype(keeps[c].dtype)
            other_ref[at, :] = total[pl.ds(other, size), :].astype(other_ref.dtype)

    if packs is not None:
        back = dot_nt(out_ref[:, : 3 * width], w_ref[:, : 3 * width])
        for pack_ref, weight_ref in zip(earlier[:packs], earlier[packs:]):
            back = back + dot_nt(pack_ref[...], weight_ref[...])

        @pl.when(half == 0)
        def _():
            refs[0][...] = back

        @pl.when(half != 0)
        def _():
            refs[1][...] = back.astype(BF16)


def block_rows(tokens):
    return 3 * TOK if tokens % (3 * TOK) == 0 else TOK


def two_halves(rows, steps, lead):
    shape = (1,) * len(lead) + (rows, D)
    first = pl.BlockSpec(shape, lambda h, i: lead + (jnp.where(h == 0, i, steps - 1), 0))
    second = pl.BlockSpec(shape, lambda h, i: lead + (jnp.where(h == 0, 0, i), 0))
    return [first, second]


SCALARS = pl.BlockSpec(memory_space=pltpu.SMEM)


def attention_call(counts, owners, low, own, far, earlier, blocks, dp):
    tokens = own.shape[1]
    rows = block_rows(tokens)
    steps = tokens // rows
    cols = blocks[0].shape[1]
    whole = lambda shape: pl.BlockSpec(shape, lambda h, i: (0, 0))
    at = lambda h, i: (h * steps + i, 0)
    packs = None if earlier is None else len(earlier[0])
    back = [] if earlier is None else two_halves(rows, steps, ())
    kind = BF16 if earlier is None else F32
    grads = [jax.ShapeDtypeStruct((D // 2, c), kind) for c in (cols // 2, cols // 2, cols)]
    return pl.pallas_call(
        functools.partial(attention_kernel, packs, len(blocks), dp),
        grid=(2, steps),
        in_specs=[SCALARS] * 3
        + two_halves(rows, steps, (0,))
        + two_halves(rows, steps, (1,))
        + [pl.BlockSpec((rows, cols // 4 * 3), at)] * (packs or 0)
        + [whole((D, cols // 4 * 3))] * (packs or 0)
        + [whole(b.shape) for b in blocks],
        out_specs=[pl.BlockSpec((rows, cols), at), whole((D, cols))] + [whole(g.shape) for g in grads] + back,
        out_shape=[
            jax.ShapeDtypeStruct((2 * tokens, cols), BF16),
            jax.ShapeDtypeStruct((D, cols), BF16),
            *grads,
        ]
        + [jax.ShapeDtypeStruct((tokens, D), kind) for kind in (F32, BF16)[: len(back)]],
        scratch_shapes=[
            pltpu.VMEM((rows, D), BF16),
            pltpu.VMEM((rows, D), BF16),
            pltpu.VMEM((rows, cols), BF16),
            pltpu.VMEM((D, cols), F32),
        ],
        compiler_params=params(),
        cost_estimate=cost(20e9, 14e6),
        name="attention",
    )(counts, owners, low, own, far, own, far, *[x for group in earlier or () for x in group], *blocks)


def combine_kernel(counts, place_ref, *refs):
    ins, refs = refs[: sum(counts)], refs[sum(counts) :]
    rows = refs[0].shape[0]
    place = place_ref[0]
    for j, ref in enumerate(refs):
        at = pl.ds(pl.multiple_of((place ^ j) * rows, rows), rows)
        total = None
        first = 0
        for count in counts:
            pieces = [r[at, :].astype(F32) for r in ins[first : first + count]]
            new = pieces[0] if count == 1 else jnp.concatenate(pieces, axis=1)
            total = new if total is None else total + new
            first += count
        ref[...] = total.astype(ref.dtype)


def combine_call(place, parts, dtypes):
    ins = [piece for part in parts for piece in part]
    rows, cols = ins[0].shape[0] // len(dtypes), sum(piece.shape[1] for piece in parts[0])
    whole = lambda a: pl.BlockSpec(a.shape, lambda: (0, 0))
    return pl.pallas_call(
        functools.partial(combine_kernel, [len(part) for part in parts]),
        in_specs=[SCALARS] + [whole(a) for a in ins],
        out_specs=[pl.BlockSpec((rows, cols), lambda: (0, 0))] * len(dtypes),
        out_shape=[jax.ShapeDtypeStruct((rows, cols), d) for d in dtypes],
        compiler_params=params(),
        cost_estimate=cost(1e6, 5e6),
        name="combine",
    )(place, *ins)


def add_kernel(*refs):
    total = refs[0][...]
    for ref in refs[1:-1]:
        total = total + ref[...].astype(F32)
    refs[-1][...] = total


def add_call(parts):
    spec = pl.BlockSpec(parts[0].shape, lambda: (0, 0))
    return pl.pallas_call(
        add_kernel,
        in_specs=[spec] * len(parts),
        out_specs=spec,
        out_shape=jax.ShapeDtypeStruct(parts[0].shape, F32),
        compiler_params=params(),
        cost_estimate=cost(1e6, 2e6),
        name="add_parts",
    )(*parts)


def mixed_product(context_refs, weight_refs):
    total = None
    for context_ref, w_ref in zip(context_refs, weight_refs):
        new = dot_nt(context_ref[...], w_ref[...])
        total = new if total is None else total + new
    return total


def context_specs(rows, packs, weights, first):
    width = packs[0].shape[1] // 4
    return [pl.BlockSpec((rows, width), lambda i: (first + i, 3))] * len(packs) + [
        pl.BlockSpec((D, width), lambda i: (0, 3))
    ] * len(weights)


def mixed_kernel(count, *refs):
    refs[-1][...] = mixed_product(refs[:count], refs[count : 2 * count]).astype(BF16)


def mixed_call(packs, weights):
    tokens = packs[0].shape[0] // 2
    rows = block_rows(tokens)
    return pl.pallas_call(
        functools.partial(mixed_kernel, len(packs)),
        grid=(tokens // rows,),
        in_specs=context_specs(rows, packs, weights, tokens // rows),
        out_specs=pl.BlockSpec((rows, D), lambda i: (i, 0)),
        out_shape=jax.ShapeDtypeStruct((tokens, D), BF16),
        compiler_params=params(),
        cost_estimate=cost(2e9, 5e6),
        name="mixed",
    )(*packs, *weights)


def tail_kernel(core_ref, own_ref, recv_ref, emb_ref, gl_ref, cols_ref, gain_ref, keep_ref, first_ref, second_ref, acc):
    step = pl.program_id(0)
    rows = emb_ref.shape[0]
    scenes = rows // TOK

    @pl.when(step == 0)
    def _():
        acc[...] = jnp.zeros_like(acc)

    grad_normed = own_ref[...] + recv_ref[...].astype(F32)
    x = emb_ref[...].astype(F32)
    dev = x - jnp.mean(x, axis=-1, keepdims=True)
    inv_std = lax.rsqrt(jnp.mean(dev * dev, axis=-1, keepdims=True) + NORM_EPS)
    centred = dev * inv_std
    scaled = grad_normed * gain_ref[...]
    first_mean = jnp.mean(scaled, axis=-1, keepdims=True)
    second_mean = jnp.mean(scaled * centred, axis=-1, keepdims=True)
    back = inv_std * (scaled - first_mean - centred * second_mean)
    grad_in = (gl_ref[0].astype(F32) + back).astype(BF16)
    for g, (start, end) in enumerate(GROUP_BANDS):
        at = [slice(s * TOK + g * CAP, s * TOK + (g + 1) * CAP) for s in range(scenes)]
        columns = jnp.concatenate([cols_ref[a, : (end - start) * PIX] for a in at], axis=0)
        grads = jnp.concatenate([grad_in[a] for a in at], axis=0)
        acc[start * PIX : end * PIX, :] += dot_tn(columns, grads)

    @pl.when(step == pl.num_programs(0) - 1)
    def _():
        size = keep_ref.shape[0]
        core = core_ref[0]
        keep_ref[...] = acc[pl.ds(pl.multiple_of(core * size, size), size), :]
        other = pl.ds(pl.multiple_of((1 - core) * size, size), size)
        first_ref[...] = acc[other, : D // 2]
        second_ref[...] = acc[other, D // 2 :]


def tail_call(core, own, recv, emb, rows_own, cols, gain):
    tokens = emb.shape[0]
    rows = 2 * TOK if tokens % (2 * TOK) == 0 else TOK
    per = lambda a: pl.BlockSpec((rows, a.shape[1]), lambda i: (i, 0))
    stem_rows = GROUP_BANDS[-1][1] * PIX
    keep = jax.ShapeDtypeStruct((stem_rows // 2, D), F32)
    send = jax.ShapeDtypeStruct((stem_rows // 2, D // 2), F32)
    return pl.pallas_call(
        tail_kernel,
        grid=(tokens // rows,),
        in_specs=[SCALARS, per(own), per(recv), per(emb), pl.BlockSpec((1, rows, D), lambda i: (1, i, 0)), per(cols)]
        + [pl.BlockSpec(gain.shape, lambda i: (0, 0))],
        out_specs=[pl.BlockSpec(a.shape, lambda i: (0, 0)) for a in (keep, send, send)],
        out_shape=[keep, send, send],
        scratch_shapes=[pltpu.VMEM((stem_rows, D), F32)],
        compiler_params=params(),
        cost_estimate=cost(10e9, 12e6),
        name="tail",
    )(core, own, recv, emb, rows_own, cols, gain)


def output_kernel(count, cnt_ref, recv_ref, emb_ref, *refs):
    out_ref = refs[-1]
    step = pl.program_id(0)
    scenes = emb_ref.shape[0] // TOK
    mixed = recv_ref[...].astype(F32) + mixed_product(refs[:count], refs[count : 2 * count])
    total = emb_ref[...].astype(F32) + mixed
    for s in range(scenes):
        scene = step * scenes + s
        live = live_column(cnt_ref[scene, 0], cnt_ref[scene, 1], cnt_ref[scene, 2])
        at = slice(s * TOK, (s + 1) * TOK)
        out_ref[at, :] = jnp.where(live, total[at], 0.0).astype(BF16)


def output_call(counts, recv, emb, packs, weights):
    tokens = emb.shape[0]
    rows = 2 * TOK if tokens % (2 * TOK) == 0 else TOK
    per = lambda a: pl.BlockSpec((rows, a.shape[1]), lambda i: (i, 0))
    return pl.pallas_call(
        functools.partial(output_kernel, len(packs)),
        grid=(tokens // rows,),
        in_specs=[SCALARS, per(recv), per(emb)]
        + context_specs(rows, packs, weights, 0),
        out_specs=per(emb),
        out_shape=jax.ShapeDtypeStruct(emb.shape, BF16),
        compiler_params=params(),
        cost_estimate=cost(5e9, 10e6),
        name="layer_output",
    )(counts, recv, emb, *packs, *weights)


def swap(x, axis, size, bit):
    return lax.ppermute(x, axis, [(i, i ^ bit) for i in range(size)])


def together(*values):
    return lax.optimization_barrier(values)


class Ring:
    def __init__(self, x, axis, size):
        self.axis, self.size = axis, size
        order = list(range(0, size, 2)) + list(range(size - 1, 0, -2))
        self.forward = [(order[i], order[(i + 1) % size]) for i in range(size)]
        self.backward = [(order[(i + 1) % size], order[i]) for i in range(size)]
        self.ahead, self.behind = [x], [x]

    @classmethod
    def across(cls, x, axis, size, other, other_size, bit):
        ring = cls(swap(x, other, other_size, bit), axis, size)
        for pairs, blocks in ((ring.forward, ring.ahead), (ring.backward, ring.behind)):
            both = [(s * other_size + g, t * other_size + (g ^ bit)) for s, t in pairs for g in range(other_size)]
            blocks.append(lax.ppermute(x, (axis, other), both))
        return ring

    def send(self):
        moved = [lax.ppermute(self.ahead[-1], self.axis, self.forward)]
        if len(self.behind) <= (self.size - 1) // 2:
            moved.append(lax.ppermute(self.behind[-1], self.axis, self.backward))
        return moved

    def receive(self, moved):
        self.ahead.append(moved[0])
        self.behind.extend(moved[1:])

    @property
    def steps(self):
        return len(self.ahead) - 1

    def owners(self, ahead, behind):
        size = self.size
        me = lax.axis_index(self.axis)
        here = jnp.where(me % 2 == 0, me // 2, size - 1 - me // 2)
        distances = [-s for s in range(ahead)] + list(range(1, behind))
        at = (here + size + jnp.array(distances, jnp.int32)) % size
        return jnp.where(at < size // 2, 2 * at, 2 * (size - 1 - at) + 1)


def step_all(rings, *beside):
    moved, beside = together([ring.send() for ring in rings], beside)
    for ring, blocks in zip(rings, moved):
        ring.receive(blocks)
    return beside


def halve_stem(recv, keep, group):
    mine = lax.axis_index("group") // 2 * 2 + lax.axis_index("dp") % 2
    return combine_call(mine.reshape(1), [[keep], recv], [F32] * (group // 2 * 2))


def sum_stem(parts, beside, after, last, dp, group):
    core = lax.axis_index("group") % 2
    far = lax.axis_index("group") // 2
    low = lax.axis_index("dp") % 2
    high = lax.axis_index("dp") // 2
    fars, highs = group // 2, dp // 2
    mine = far * 2 + low
    small, width = parts[0].shape
    rows = 2 * fars * small

    def hop(block, f, b):
        if f:
            pairs = [
                (d * group + g, (d ^ b) * group + (g ^ (2 * f))) for d in range(dp) for g in range(group)
            ]
            return lax.ppermute(block, ("dp", "group"), pairs)
        return swap(block, "dp", dp, b)

    hops = [(k // 2, k % 2) for k in range(1, 2 * fars)]
    arrived = [hop(part, f, b) for part, (f, b) in zip(parts[1:], hops)]
    arrived, beside = together(arrived, beside)
    beside = after(*beside)
    total = parts[0]
    for part in arrived:
        total = total + part
    cols = width // highs
    part = lax.dynamic_slice_in_dim(total, high * cols, cols, 1)
    away = [lax.dynamic_slice_in_dim(total, (high ^ j) * cols, cols, 1) for j in range(1, highs)]
    arrived = [swap(a, "dp", dp, 2 * (j + 1)) for j, a in enumerate(away)]
    arrived, beside = together(arrived, beside)
    for block in arrived:
        part = part + block
    part = part.astype(BF16)
    line = jnp.zeros((small, width), BF16)
    line = lax.dynamic_update_slice_in_dim(line, part, high * cols, 1)
    arrived = [swap(part, "dp", dp, 2 * j) for j in range(1, highs)]
    for j, block in enumerate(arrived):
        line = lax.dynamic_update_slice_in_dim(line, block, (high ^ (j + 1)) * cols, 1)
    block = jnp.zeros((rows, width), BF16)
    block = lax.dynamic_update_slice_in_dim(block, line, mine * small, 0)
    arrived, beside = together([hop(line, f, b) for f, b in hops], last(*beside))
    for (f, b), piece in zip(hops, arrived):
        target = (far ^ f) * 2 + (low ^ b)
        block = lax.dynamic_update_slice_in_dim(block, piece, target * small, 0)
    partner = swap(block, "group", group, 1)
    first = jnp.where(core == 0, block, partner)
    second = jnp.where(core == 0, partner, block)
    return jnp.concatenate([first, second], axis=0).astype(F32), beside


def encoding_tables(patch_count):
    quarter = D // 4
    half_width = D // 2
    power = lambda n: np.power(np.float32(10000.0), -np.arange(n, dtype=np.float32) / np.float32(n))
    at = np.arange(GRID).astype(np.float32)[:, None] * power(quarter)
    both = np.concatenate([np.sin(at), np.cos(at)], axis=-1)
    patch = np.arange(patch_count)
    rest = np.concatenate([both[patch // GRID], both[patch % GRID]], axis=-1).astype(np.float32)
    parts = []
    for _ in range(3):
        parts.append(rest.astype(ml_dtypes.bfloat16))
        rest = rest - parts[-1].astype(np.float32)
    group_at = np.arange(GROUPS).astype(np.float32)[:, None] * power(half_width)
    return np.stack(parts), np.concatenate([np.sin(group_at), np.cos(group_at)], axis=-1).astype(np.float32)


def on_device(dp, group, patches, vis_index, vis_count, w_stem, ln_gain, w_qkv, w_out, out_grad):
    scenes = patches.shape[0]
    tokens = scenes * TOK
    width = w_qkv.shape[2]
    fars = range(1, group // 2)
    rests = range(1, dp // 2)
    dp_low, dp_high = lax.axis_index("dp") % 2, lax.axis_index("dp") // 2
    low, high = dp_low.reshape(1), dp_high.reshape(1)
    core = (lax.axis_index("group") % 2).reshape(1)

    shard = jnp.concatenate([w_qkv.reshape(w_qkv.shape[0], 3 * width), w_out.T], axis=1)
    cross = lambda x, f: swap(x, "group", group, 2 * f)
    rings = [Ring.across(shard, "dp", dp, "group", group, 2 * f) for f in fars]
    ring = rings[0]
    counts = vis_count.astype(jnp.int32)
    counts_far = swap(counts, "group", group, 1)
    table, genc = encoding_tables(patches.shape[1])
    gain = ln_gain.reshape(1, D)
    stem = stem_call(
        counts,
        vis_index,
        patches,
        w_stem,
        gain,
        jnp.asarray(table),
        jnp.asarray(genc),
        out_grad.reshape(scenes, TOK, D),
    )
    moved = [(r.ahead, r.behind) for r in rings]
    owners = ring.owners(dp // 2 + 1, dp // 2)
    stem, both_counts, owners, moved = together(stem, jnp.stack([counts, counts_far]), owners, moved)
    for r, (ahead, behind) in zip(rings, moved):
        r.ahead, r.behind = list(ahead), list(behind)
    emb = stem[0].reshape(tokens, D)
    both = [stem[1].reshape(2, tokens, D)]
    cols = stem[2].reshape(tokens, stem[2].shape[2])
    both.append(swap(both[0], "group", group, 1))
    passed = [cross(ring.ahead[-1], 1)]
    (both,) = step_all(rings, both)
    while ring.steps < dp // 2:
        passed.append(cross(ring.ahead[-1], 1))
        if ring.steps == dp // 2 - 1:
            behind = jnp.concatenate(ring.behind[1:], axis=0)
            passed[-2], behind = step_all(rings, passed[-2], behind)
        else:
            (passed[-2],) = step_all(rings, passed[-2])
    ring.ahead, behind = together(ring.ahead, behind)
    passed.append(cross(ring.ahead[-1], 1))
    passed.append(cross(behind, 1))

    packs, weights, crossing = [], [], []
    for f in list(fars) + [0]:
        if f:
            blocks = rings[f - 1].ahead + rings[f - 1].behind[1:]
        else:
            rows = shard.shape[0]
            blocks = [shard] + passed[:-1] + [passed[-1][b * rows : (b + 1) * rows] for b in range(dp // 2 - 1)]
        made = attention_call(both_counts, owners, low, *both, None if f else (packs, weights), blocks, dp)
        if f == 1:
            made, passed[-3:] = together(made, passed[-3:])
        elif f:
            made = together(*made)
        else:
            made, arrived = together(made, [x[:2] for x in crossing])
        pack, weight, keep, other, back = made[0], made[1], made[2:4], made[4], made[5:]
        packs.append(pack)
        weights.append(weight)
        if f:
            crossing.append([cross(x, f) for x in (other, *keep)])
    back_far = swap(back[1], "group", group, 1)
    for x in arrived:
        other = other + x[0].astype(F32)
    coming = swap(other.astype(BF16), "dp", dp, 1)
    stem_made, last_keeps = together(
        tail_call(core, back[0], back_far, emb, both[0], cols, gain), [x[2] for x in crossing]
    )
    keeps = [list(keep)] + [[x[1], y] for x, y in zip(arrived, last_keeps)]
    stem_keep, *stem_recv = stem_made
    stem_recv = [swap(x, "group", group, 1) for x in stem_recv]
    stem_parts = halve_stem(stem_recv, stem_keep, group)
    _, coming, keeps = together(stem_parts, coming, keeps)
    kinds = [F32 if j < 2 else BF16 for j in range(dp // 2)]
    blocks = combine_call(high, keeps + [[coming]], kinds)
    landing = [blocks[0]] + [swap(blocks[j], "dp", dp, 2 * j) for j in rests]
    near = dp // 2 * 3 // 4

    def after(mixed, *arrived):
        return [mixed] + list(arrived) + [landing[1]] + landing[near:]

    def last(mixed, *arrived):
        output = output_call(counts, swap(mixed, "group", group, 1), emb, packs, weights)
        total = add_call(list(arrived))
        return output, total[:, : 3 * width].reshape(total.shape[0], 3, width), total[:, 3 * width :].T

    grad_w_stem, (output, grad_w_qkv, grad_w_out) = sum_stem(
        stem_parts, [mixed_call(packs, weights), landing[0]] + landing[2:near], after, last, dp, group
    )
    return (output.reshape(scenes, GROUPS, CAP, D), grad_w_stem, grad_w_qkv, grad_w_out)


def solution(mesh):
    sizes = dict(mesh.shape)
    return jax.shard_map(
        functools.partial(on_device, sizes["dp"], sizes["group"]),
        mesh=mesh,
        in_specs=(
            P(("dp", "group"), None, None),
            P(("dp", "group"), None, None),
            P(("dp", "group"), None),
            P(),
            P(),
            P("dp", None, "group"),
            P("group", "dp"),
            P(("dp", "group"), None, None, None),
        ),
        out_specs=(
            P(("dp", "group"), None, None, None),
            P(),
            P("dp", None, "group"),
            P("group", "dp"),
        ),
        check_vma=False,
    )
```

```python
import functools

import jax
import jax.numpy as jnp
import ml_dtypes
import numpy as np
from jax import lax
from jax.experimental import pallas as pl
from jax.experimental.pallas import tpu as pltpu
from jax.sharding import PartitionSpec as P

D = 1024
HD = 64
GROUPS = 3
CAP = 48
GRID = 12
PIX = 64
TOK = GROUPS * CAP
PAIR = 128
GROUP_BANDS = ((0, 4), (4, 8), (8, 10))
NORM_EPS = 1e-06
F32 = jnp.float32
BF16 = jnp.bfloat16
VMEM_LIMIT = 60 * 1024 * 1024


def dot_nn(a, b):
    return lax.dot_general(a, b, (((1,), (0,)), ((), ())), preferred_element_type=F32)


def dot_nt(a, b):
    return lax.dot_general(a, b, (((1,), (1,)), ((), ())), preferred_element_type=F32)


def dot_tn(a, b):
    return lax.dot_general(a, b, (((0,), (0,)), ((), ())), preferred_element_type=F32)


def live_column(c0, c1, c2):
    row = lax.broadcasted_iota(jnp.int32, (TOK, 1), 0)
    return (
        (row < c0)
        | ((row >= CAP) & (row < CAP + c1))
        | ((row >= 2 * CAP) & (row < 2 * CAP + c2))
    )


def params():
    return pltpu.CompilerParams(vmem_limit_bytes=VMEM_LIMIT)


def cost(flops, nbytes):
    return pl.CostEstimate(flops=int(flops / 1000), bytes_accessed=int(nbytes / 1000), transcendentals=0)


def stem_kernel(
    cnt_ref, idx_ref, patch_ref, w_ref, gain_ref, parts, genc_ref, og_ref,
    emb_ref, rows_ref, cols_ref,
):
    step = pl.program_id(0)
    scenes = patch_ref.shape[0]
    patch_iota = lax.broadcasted_iota(jnp.int32, (parts.shape[1], CAP), 0)
    slot = lax.broadcasted_iota(jnp.int32, (CAP, 1), 0)
    for g, (start, end) in enumerate(GROUP_BANDS):
        rows = slice(g * CAP, (g + 1) * CAP)
        width = (end - start) * PIX
        picked, placed = [], []
        for s in range(scenes):
            onehot = (idx_ref[s, g : g + 1, :] == patch_iota).astype(F32).astype(BF16).T
            picked.append(dot_nn(onehot, patch_ref[s, :, start * PIX : end * PIX]).astype(BF16))
            placed.append(
                (dot_nn(onehot, parts[0]) + dot_nn(onehot, parts[1])) + dot_nn(onehot, parts[2])
            )
            live = slot < cnt_ref[pl.ds(step * scenes + s, 1), g : g + 1]
            rows_ref[1, s, rows, :] = jnp.where(live, og_ref[s, rows, :].astype(F32), 0.0).astype(BF16)
        summed = dot_nn(jnp.concatenate(picked, axis=0), w_ref[start * PIX : end * PIX, :])
        for s in range(scenes):
            values = summed[s * CAP : (s + 1) * CAP] + (placed[s] + genc_ref[g : g + 1, :])
            emb = values.astype(BF16)
            emb_ref[s, rows, :] = emb
            x = emb.astype(F32)
            centre = jnp.mean(x, axis=-1, keepdims=True)
            dev = x - centre
            spread = jnp.mean(dev * dev, axis=-1, keepdims=True)
            centred = dev * lax.rsqrt(spread + NORM_EPS)
            rows_ref[0, s, rows, :] = (centred * gain_ref[...]).astype(BF16)
            cols_ref[s, rows, :width] = picked[s]
            if width < cols_ref.shape[2]:
                cols_ref[s, rows, width:] = jnp.zeros((CAP, cols_ref.shape[2] - width), BF16)


def stem_call(counts, index, patches, w_stem, gain, table, genc, out_grad):
    scenes, patch_count, width = patches.shape
    block = 3 if scenes % 3 == 0 else 1
    col_width = max(e - s for s, e in GROUP_BANDS) * PIX
    per = lambda shape: pl.BlockSpec((block,) + shape, lambda i: (i, 0, 0))
    whole = lambda a: pl.BlockSpec(a.shape, lambda i: (0,) * a.ndim)
    return pl.pallas_call(
        stem_kernel,
        grid=(scenes // block,),
        in_specs=[
            whole(counts),
            per((GROUPS, CAP)),
            per((patch_count, width)),
            whole(w_stem),
            whole(gain),
            whole(table),
            whole(genc),
            per((TOK, D)),
        ],
        out_specs=[
            per((TOK, D)),
            pl.BlockSpec((2, block, TOK, D), lambda i: (0, i, 0, 0)),
            per((TOK, col_width)),
        ],
        out_shape=[
            jax.ShapeDtypeStruct((scenes, TOK, D), BF16),
            jax.ShapeDtypeStruct((2, scenes, TOK, D), BF16),
            jax.ShapeDtypeStruct((scenes, TOK, col_width), BF16),
        ],
        compiler_params=params(),
        cost_estimate=cost(8e9, 12e6),
        name="stem_norm",
    )(counts, index, patches, w_stem, gain, table, genc, out_grad)


def attention_kernel(
    packs, blocks, dp, cnt_ref, owner_ref, low_ref, na_ref, nb_ref, ga_ref, gb_ref, *refs
):
    earlier, refs = refs[: 2 * (packs or 0)], refs[2 * (packs or 0) :]
    blocks, refs = refs[:blocks], refs[blocks:]
    out_ref, w_ref, *refs = refs
    keeps, other_ref, refs = refs[:2], refs[2], refs[3:]
    n_s, g_s, qkv, total = refs[-4:]
    half, step = pl.program_id(0), pl.program_id(1)
    rows = n_s.shape[0]
    scenes = rows // TOK
    width = w_ref.shape[1] // 4

    @pl.when((half == 0) & (step == 0))
    def _():
        size = blocks[0].shape[0]
        for b, block in enumerate(blocks):
            w_ref[pl.ds(pl.multiple_of(owner_ref[b] * size, size), size), :] = block[...]
        total[...] = jnp.zeros_like(total)

    @pl.when(half == 0)
    def _():
        n_s[...] = na_ref[0]
        g_s[...] = ga_ref[0]

    @pl.when(half != 0)
    def _():
        n_s[...] = nb_ref[0]
        g_s[...] = gb_ref[0]

    qkv[:, : 3 * width] = dot_nn(n_s[...], w_ref[:, : 3 * width]).astype(BF16)
    qkv[:, 3 * width :] = dot_nn(g_s[...], w_ref[:, 3 * width :]).astype(BF16)
    heads = width // HD
    lane = lax.broadcasted_iota(jnp.int32, (1, width), 1)
    masks = [(lane // HD == h).astype(F32).astype(BF16) for h in range(heads)]
    scale = jnp.asarray(HD ** (-0.5), BF16)
    first_of_pair = lax.broadcasted_iota(jnp.int32, (1, PAIR), 1) < HD

    def own_lanes(tall):
        tiles = []
        for t in range(width // PAIR):
            at = slice(t * PAIR, (t + 1) * PAIR)
            one = tall[2 * t * TOK : (2 * t + 1) * TOK, at]
            two = tall[(2 * t + 1) * TOK : (2 * t + 2) * TOK, at]
            tiles.append(jnp.where(first_of_pair, one, two))
        return jnp.concatenate(tiles, axis=1)

    def scene_body(s, _):
        base = pl.multiple_of(s * TOK, 16)
        at = pl.ds(base, TOK)
        scene = step * scenes + s
        live = live_column(cnt_ref[half, scene, 0], cnt_ref[half, scene, 1], cnt_ref[half, scene, 2])
        bias = jnp.where(live, 0.0, -1e30)
        q, k, v, dc = [qkv[at, c * width : (c + 1) * width] for c in range(4)]
        tall_q = jnp.concatenate([q * (m * scale) for m in masks], axis=0)
        tall_dc = jnp.concatenate([dc * m for m in masks], axis=0)
        scores = dot_nt(k, tall_q)
        grad_probs = dot_nt(v, tall_dc)
        probs_parts, score_parts = [], []
        for start in range(0, heads * TOK, PAIR):
            cols = slice(start, min(start + PAIR, heads * TOK))
            part = scores[:, cols] + bias
            lifted = jnp.exp(part - jnp.max(part, axis=0, keepdims=True))
            probs = lifted * (1.0 / jnp.sum(lifted, axis=0, keepdims=True))
            weighted = probs * grad_probs[:, cols]
            inner = jnp.sum(weighted, axis=0, keepdims=True)
            probs_parts.append(probs.astype(BF16))
            score_parts.append((weighted - probs * inner).astype(BF16))
        half_probs = jnp.concatenate(probs_parts, axis=1)
        grad_score = jnp.concatenate(score_parts, axis=1)
        out_ref[at, :width] = (own_lanes(dot_tn(grad_score, k)) * HD ** (-0.5)).astype(BF16)
        out_ref[at, width : 2 * width] = dot_nn(grad_score, tall_q).astype(BF16)
        out_ref[at, 2 * width : 3 * width] = dot_nn(half_probs, tall_dc).astype(BF16)
        out_ref[at, 3 * width :] = own_lanes(dot_tn(half_probs, v)).astype(BF16)
        return 0

    lax.fori_loop(0, scenes, scene_body, 0, unroll=True)
    total[:, : 3 * width] += dot_tn(n_s[...], out_ref[:, : 3 * width])
    total[:, 3 * width :] += dot_tn(g_s[...], out_ref[:, 3 * width :])

    @pl.when((half == pl.num_programs(0) - 1) & (step == pl.num_programs(1) - 1))
    def _():
        size = total.shape[0] // dp
        low = low_ref[0]
        for b in range(dp // 2):
            at = slice(b * size, (b + 1) * size)
            mine = pl.multiple_of((2 * b + low) * size, size)
            other = pl.multiple_of((2 * b + 1 - low) * size, size)
            for c in range(2):
                cols = slice(c * 2 * width, (c + 1) * 2 * width)
                keeps[c][at, :] = total[pl.ds(mine, size), cols].astype(keeps[c].dtype)
            other_ref[at, :] = total[pl.ds(other, size), :].astype(other_ref.dtype)

    if packs is not None:
        back = dot_nt(out_ref[:, : 3 * width], w_ref[:, : 3 * width])
        for pack_ref, weight_ref in zip(earlier[:packs], earlier[packs:]):
            back = back + dot_nt(pack_ref[...], weight_ref[...])

        @pl.when(half == 0)
        def _():
            refs[0][...] = back

        @pl.when(half != 0)
        def _():
            refs[1][...] = back.astype(BF16)


def block_rows(tokens):
    return 3 * TOK if tokens % (3 * TOK) == 0 else TOK


def two_halves(rows, steps, lead):
    shape = (1,) * len(lead) + (rows, D)
    first = pl.BlockSpec(shape, lambda h, i: lead + (jnp.where(h == 0, i, steps - 1), 0))
    second = pl.BlockSpec(shape, lambda h, i: lead + (jnp.where(h == 0, 0, i), 0))
    return [first, second]


SCALARS = pl.BlockSpec(memory_space=pltpu.SMEM)


def attention_call(counts, owners, low, own, far, earlier, blocks, dp):
    tokens = own.shape[1]
    rows = block_rows(tokens)
    steps = tokens // rows
    cols = blocks[0][0].shape[1]
    whole = lambda shape: pl.BlockSpec(shape, lambda h, i: (0, 0))
    at = lambda h, i: (h * steps + i, 0)
    packs = None if earlier is None else len(earlier[0])
    back = [] if earlier is None else two_halves(rows, steps, ())
    kind = BF16 if earlier is None else F32
    grads = [jax.ShapeDtypeStruct((D // 2, c), kind) for c in (cols // 2, cols // 2, cols)]
    return pl.pallas_call(
        functools.partial(attention_kernel, packs, len(blocks), dp),
        grid=(2, steps),
        in_specs=[SCALARS] * 3
        + two_halves(rows, steps, (0,))
        + two_halves(rows, steps, (1,))
        + [pl.BlockSpec((rows, cols // 4 * 3), at)] * (packs or 0)
        + [whole((D, cols // 4 * 3))] * (packs or 0)
        + [pl.BlockSpec((D // dp, cols), functools.partial(lambda at, h, i: (at, 0), at)) for _, at in blocks],
        out_specs=[pl.BlockSpec((rows, cols), at), whole((D, cols))] + [whole(g.shape) for g in grads] + back,
        out_shape=[
            jax.ShapeDtypeStruct((2 * tokens, cols), BF16),
            jax.ShapeDtypeStruct((D, cols), BF16),
            *grads,
        ]
        + [jax.ShapeDtypeStruct((tokens, D), kind) for kind in (F32, BF16)[: len(back)]],
        scratch_shapes=[
            pltpu.VMEM((rows, D), BF16),
            pltpu.VMEM((rows, D), BF16),
            pltpu.VMEM((rows, cols), BF16),
            pltpu.VMEM((D, cols), F32),
        ],
        compiler_params=params(),
        cost_estimate=cost(20e9, 14e6),
        name="attention",
    )(counts, owners, low, own, far, own, far, *[x for group in earlier or () for x in group], *[b for b, _ in blocks])


def combine_kernel(counts, place_ref, *refs):
    ins, refs = refs[: sum(counts)], refs[sum(counts) :]
    rows = refs[0].shape[0]
    place = place_ref[0]
    for j, ref in enumerate(refs):
        at = pl.ds(pl.multiple_of((place ^ j) * rows, rows), rows)
        total = None
        first = 0
        for count in counts:
            pieces = [r[at, :].astype(F32) for r in ins[first : first + count]]
            new = pieces[0] if count == 1 else jnp.concatenate(pieces, axis=1)
            total = new if total is None else total + new
            first += count
        ref[...] = total.astype(ref.dtype)


def combine_call(place, parts, dtypes):
    ins = [piece for part in parts for piece in part]
    rows, cols = ins[0].shape[0] // len(dtypes), sum(piece.shape[1] for piece in parts[0])
    whole = lambda a: pl.BlockSpec(a.shape, lambda: (0, 0))
    return pl.pallas_call(
        functools.partial(combine_kernel, [len(part) for part in parts]),
        in_specs=[SCALARS] + [whole(a) for a in ins],
        out_specs=[pl.BlockSpec((rows, cols), lambda: (0, 0))] * len(dtypes),
        out_shape=[jax.ShapeDtypeStruct((rows, cols), d) for d in dtypes],
        compiler_params=params(),
        cost_estimate=cost(1e6, 5e6),
        name="combine",
    )(place, *ins)


def add_kernel(*refs):
    total = refs[0][...]
    for ref in refs[1:-1]:
        total = total + ref[...].astype(F32)
    refs[-1][...] = total


def add_call(parts):
    spec = pl.BlockSpec(parts[0].shape, lambda: (0, 0))
    return pl.pallas_call(
        add_kernel,
        in_specs=[spec] * len(parts),
        out_specs=spec,
        out_shape=jax.ShapeDtypeStruct(parts[0].shape, F32),
        compiler_params=params(),
        cost_estimate=cost(1e6, 2e6),
        name="add_parts",
    )(*parts)


def mixed_product(context_refs, weight_refs):
    total = None
    for context_ref, w_ref in zip(context_refs, weight_refs):
        new = dot_nt(context_ref[...], w_ref[...])
        total = new if total is None else total + new
    return total


def context_specs(rows, packs, weights, first):
    width = packs[0].shape[1] // 4
    return [pl.BlockSpec((rows, width), lambda i: (first + i, 3))] * len(packs) + [
        pl.BlockSpec((D, width), lambda i: (0, 3))
    ] * len(weights)


def mixed_kernel(count, *refs):
    refs[-1][...] = mixed_product(refs[:count], refs[count : 2 * count]).astype(BF16)


def mixed_call(packs, weights):
    tokens = packs[0].shape[0] // 2
    rows = block_rows(tokens)
    return pl.pallas_call(
        functools.partial(mixed_kernel, len(packs)),
        grid=(tokens // rows,),
        in_specs=context_specs(rows, packs, weights, tokens // rows),
        out_specs=pl.BlockSpec((rows, D), lambda i: (i, 0)),
        out_shape=jax.ShapeDtypeStruct((tokens, D), BF16),
        compiler_params=params(),
        cost_estimate=cost(2e9, 5e6),
        name="mixed",
    )(*packs, *weights)


def tail_kernel(core_ref, own_ref, recv_ref, emb_ref, gl_ref, cols_ref, gain_ref, keep_ref, first_ref, second_ref, acc):
    step = pl.program_id(0)
    rows = emb_ref.shape[0]
    scenes = rows // TOK

    @pl.when(step == 0)
    def _():
        acc[...] = jnp.zeros_like(acc)

    grad_normed = own_ref[...] + recv_ref[...].astype(F32)
    x = emb_ref[...].astype(F32)
    dev = x - jnp.mean(x, axis=-1, keepdims=True)
    inv_std = lax.rsqrt(jnp.mean(dev * dev, axis=-1, keepdims=True) + NORM_EPS)
    centred = dev * inv_std
    scaled = grad_normed * gain_ref[...]
    first_mean = jnp.mean(scaled, axis=-1, keepdims=True)
    second_mean = jnp.mean(scaled * centred, axis=-1, keepdims=True)
    back = inv_std * (scaled - first_mean - centred * second_mean)
    grad_in = (gl_ref[0].astype(F32) + back).astype(BF16)
    for g, (start, end) in enumerate(GROUP_BANDS):
        at = [slice(s * TOK + g * CAP, s * TOK + (g + 1) * CAP) for s in range(scenes)]
        columns = jnp.concatenate([cols_ref[a, : (end - start) * PIX] for a in at], axis=0)
        grads = jnp.concatenate([grad_in[a] for a in at], axis=0)
        acc[start * PIX : end * PIX, :] += dot_tn(columns, grads)

    @pl.when(step == pl.num_programs(0) - 1)
    def _():
        size = keep_ref.shape[0]
        core = core_ref[0]
        keep_ref[...] = acc[pl.ds(pl.multiple_of(core * size, size), size), :]
        other = pl.ds(pl.multiple_of((1 - core) * size, size), size)
        first_ref[...] = acc[other, : D // 2]
        second_ref[...] = acc[other, D // 2 :]


def tail_call(core, own, recv, emb, rows_own, cols, gain):
    tokens = emb.shape[0]
    rows = 2 * TOK if tokens % (2 * TOK) == 0 else TOK
    per = lambda a: pl.BlockSpec((rows, a.shape[1]), lambda i: (i, 0))
    stem_rows = GROUP_BANDS[-1][1] * PIX
    keep = jax.ShapeDtypeStruct((stem_rows // 2, D), F32)
    send = jax.ShapeDtypeStruct((stem_rows // 2, D // 2), F32)
    return pl.pallas_call(
        tail_kernel,
        grid=(tokens // rows,),
        in_specs=[SCALARS, per(own), per(recv), per(emb), pl.BlockSpec((1, rows, D), lambda i: (1, i, 0)), per(cols)]
        + [pl.BlockSpec(gain.shape, lambda i: (0, 0))],
        out_specs=[pl.BlockSpec(a.shape, lambda i: (0, 0)) for a in (keep, send, send)],
        out_shape=[keep, send, send],
        scratch_shapes=[pltpu.VMEM((stem_rows, D), F32)],
        compiler_params=params(),
        cost_estimate=cost(10e9, 12e6),
        name="tail",
    )(core, own, recv, emb, rows_own, cols, gain)


def output_kernel(count, cnt_ref, recv_ref, emb_ref, *refs):
    out_ref = refs[-1]
    step = pl.program_id(0)
    scenes = emb_ref.shape[0] // TOK
    mixed = recv_ref[...].astype(F32) + mixed_product(refs[:count], refs[count : 2 * count])
    total = emb_ref[...].astype(F32) + mixed
    for s in range(scenes):
        scene = step * scenes + s
        live = live_column(cnt_ref[scene, 0], cnt_ref[scene, 1], cnt_ref[scene, 2])
        at = slice(s * TOK, (s + 1) * TOK)
        out_ref[at, :] = jnp.where(live, total[at], 0.0).astype(BF16)


def output_call(counts, recv, emb, packs, weights):
    tokens = emb.shape[0]
    rows = 2 * TOK if tokens % (2 * TOK) == 0 else TOK
    per = lambda a: pl.BlockSpec((rows, a.shape[1]), lambda i: (i, 0))
    return pl.pallas_call(
        functools.partial(output_kernel, len(packs)),
        grid=(tokens // rows,),
        in_specs=[SCALARS, per(recv), per(emb)]
        + context_specs(rows, packs, weights, 0),
        out_specs=per(emb),
        out_shape=jax.ShapeDtypeStruct(emb.shape, BF16),
        compiler_params=params(),
        cost_estimate=cost(5e9, 10e6),
        name="layer_output",
    )(counts, recv, emb, *packs, *weights)


def swap(x, axis, size, bit):
    return lax.ppermute(x, axis, [(i, i ^ bit) for i in range(size)])


def together(*values):
    return lax.optimization_barrier(values)


class Ring:
    def __init__(self, x, axis, size):
        self.axis, self.size = axis, size
        order = list(range(0, size, 2)) + list(range(size - 1, 0, -2))
        self.forward = [(order[i], order[(i + 1) % size]) for i in range(size)]
        self.backward = [(order[(i + 1) % size], order[i]) for i in range(size)]
        self.ahead, self.behind = [x], [x]

    @classmethod
    def across(cls, x, axis, size, other, other_size, bit):
        ring = cls(swap(x, other, other_size, bit), axis, size)
        both = [(s * other_size + g, t * other_size + (g ^ bit)) for s, t in ring.forward for g in range(other_size)]
        ring.ahead.append(lax.ppermute(x, (axis, other), both))
        return ring

    def send(self):
        moved = [lax.ppermute(self.ahead[-1], self.axis, self.forward)]
        if len(self.behind) <= (self.size - 1) // 2:
            moved.append(lax.ppermute(self.behind[-1], self.axis, self.backward))
        return moved

    def receive(self, moved):
        self.ahead.append(moved[0])
        self.behind.extend(moved[1:])

    @property
    def steps(self):
        return len(self.ahead) - 1

    def owners(self, ahead, behind):
        size = self.size
        me = lax.axis_index(self.axis)
        here = jnp.where(me % 2 == 0, me // 2, size - 1 - me // 2)
        distances = [-s for s in range(ahead)] + list(range(1, behind))
        at = (here + size + jnp.array(distances, jnp.int32)) % size
        return jnp.where(at < size // 2, 2 * at, 2 * (size - 1 - at) + 1)


def step_all(rings, *beside):
    moved, beside = together([ring.send() for ring in rings], beside)
    for ring, blocks in zip(rings, moved):
        ring.receive(blocks)
    return beside


def halve_stem(recv, keep, group):
    mine = lax.axis_index("group") // 2 * 2 + lax.axis_index("dp") % 2
    return combine_call(mine.reshape(1), [[keep], recv], [F32] * (group // 2 * 2))


def sum_stem(parts, beside, after, last, dp, group):
    core = lax.axis_index("group") % 2
    far = lax.axis_index("group") // 2
    low = lax.axis_index("dp") % 2
    high = lax.axis_index("dp") // 2
    fars, highs = group // 2, dp // 2
    mine = far * 2 + low
    small, width = parts[0].shape
    rows = 2 * fars * small

    def hop(block, f, b):
        if f:
            pairs = [
                (d * group + g, (d ^ b) * group + (g ^ (2 * f))) for d in range(dp) for g in range(group)
            ]
            return lax.ppermute(block, ("dp", "group"), pairs)
        return swap(block, "dp", dp, b)

    hops = [(k // 2, k % 2) for k in range(1, 2 * fars)]
    arrived = [hop(part, f, b) for part, (f, b) in zip(parts[1:], hops)]
    arrived, beside = together(arrived, beside)
    beside = after(*beside)
    total = parts[0]
    for part in arrived:
        total = total + part
    cols = width // highs
    part = lax.dynamic_slice_in_dim(total, high * cols, cols, 1)
    away = [lax.dynamic_slice_in_dim(total, (high ^ j) * cols, cols, 1) for j in range(1, highs)]
    arrived = [swap(a, "dp", dp, 2 * (j + 1)) for j, a in enumerate(away)]
    arrived, beside = together(arrived, beside)
    for block in arrived:
        part = part + block
    part = part.astype(BF16)
    line = jnp.zeros((small, width), BF16)
    line = lax.dynamic_update_slice_in_dim(line, part, high * cols, 1)
    arrived = [swap(part, "dp", dp, 2 * j) for j in range(1, highs)]
    for j, block in enumerate(arrived):
        line = lax.dynamic_update_slice_in_dim(line, block, (high ^ (j + 1)) * cols, 1)
    block = jnp.zeros((rows, width), BF16)
    block = lax.dynamic_update_slice_in_dim(block, line, mine * small, 0)
    arrived, beside = together([hop(line, f, b) for f, b in hops], last(*beside))
    for (f, b), piece in zip(hops, arrived):
        target = (far ^ f) * 2 + (low ^ b)
        block = lax.dynamic_update_slice_in_dim(block, piece, target * small, 0)
    partner = swap(block, "group", group, 1)
    first = jnp.where(core == 0, block, partner)
    second = jnp.where(core == 0, partner, block)
    return jnp.concatenate([first, second], axis=0).astype(F32), beside


def encoding_tables(patch_count):
    quarter = D // 4
    half_width = D // 2
    power = lambda n: np.power(np.float32(10000.0), -np.arange(n, dtype=np.float32) / np.float32(n))
    at = np.arange(GRID).astype(np.float32)[:, None] * power(quarter)
    both = np.concatenate([np.sin(at), np.cos(at)], axis=-1)
    patch = np.arange(patch_count)
    rest = np.concatenate([both[patch // GRID], both[patch % GRID]], axis=-1).astype(np.float32)
    parts = []
    for _ in range(3):
        parts.append(rest.astype(ml_dtypes.bfloat16))
        rest = rest - parts[-1].astype(np.float32)
    group_at = np.arange(GROUPS).astype(np.float32)[:, None] * power(half_width)
    return np.stack(parts), np.concatenate([np.sin(group_at), np.cos(group_at)], axis=-1).astype(np.float32)


def on_device(dp, group, patches, vis_index, vis_count, w_stem, ln_gain, w_qkv, w_out, out_grad):
    scenes = patches.shape[0]
    tokens = scenes * TOK
    width = w_qkv.shape[2]
    fars = range(1, group // 2)
    rests = range(1, dp // 2)
    dp_low, dp_high = lax.axis_index("dp") % 2, lax.axis_index("dp") // 2
    low, high = dp_low.reshape(1), dp_high.reshape(1)
    core = (lax.axis_index("group") % 2).reshape(1)

    shard = jnp.concatenate([w_qkv.reshape(w_qkv.shape[0], 3 * width), w_out.T], axis=1)
    cross = lambda x, f: swap(x, "group", group, 2 * f)
    rings = [Ring.across(shard, "dp", dp, "group", group, 2 * f) for f in fars]
    ring = rings[0]
    counts = vis_count.astype(jnp.int32)
    counts_far = swap(counts, "group", group, 1)
    table, genc = encoding_tables(patches.shape[1])
    gain = ln_gain.reshape(1, D)
    stem = stem_call(
        counts,
        vis_index,
        patches,
        w_stem,
        gain,
        jnp.asarray(table),
        jnp.asarray(genc),
        out_grad.reshape(scenes, TOK, D),
    )
    moved = [(r.ahead, r.behind) for r in rings]
    owners = ring.owners(dp // 2 + 1, dp // 2)
    stem, both_counts, owners, moved = together(stem, jnp.stack([counts, counts_far]), owners, moved)
    for r, (ahead, behind) in zip(rings, moved):
        r.ahead, r.behind = list(ahead), list(behind)
    emb = stem[0].reshape(tokens, D)
    both = [stem[1].reshape(2, tokens, D)]
    cols = stem[2].reshape(tokens, stem[2].shape[2])
    both.append(swap(both[0], "group", group, 1))
    passed = [cross(ring.ahead[-1], 1)]
    (both,) = step_all(rings, both)
    while ring.steps < dp // 2:
        passed.append(cross(ring.ahead[-1], 1))
        (passed[-2],) = step_all(rings, passed[-2])
    ring.ahead, ring.behind = together(ring.ahead, ring.behind)
    passed.append(cross(ring.ahead[-1], 1))
    passed.append(cross(jnp.concatenate(ring.behind[1:], axis=0), 1))

    packs, weights, crossing = [], [], []
    for f in list(fars) + [0]:
        if f:
            blocks = [(x, 0) for x in rings[f - 1].ahead + rings[f - 1].behind[1:]]
        else:
            blocks = [(x, 0) for x in [shard] + passed[:-1]] + [(passed[-1], b) for b in range(dp // 2 - 1)]
        made = attention_call(both_counts, owners, low, *both, None if f else (packs, weights), blocks, dp)
        if f == 1:
            made, passed[-3:] = together(made, passed[-3:])
        elif f:
            made = together(*made)
        else:
            made, arrived = together(made, [x[:2] for x in crossing])
        pack, weight, keep, other, back = made[0], made[1], made[2:4], made[4], made[5:]
        packs.append(pack)
        weights.append(weight)
        if f:
            crossing.append([cross(x, f) for x in (other, *keep)])
    back_far = swap(back[1], "group", group, 1)
    for x in arrived:
        other = other + x[0].astype(F32)
    coming = swap(other.astype(BF16), "dp", dp, 1)
    stem_made, last_keeps = together(
        tail_call(core, back[0], back_far, emb, both[0], cols, gain), [x[2] for x in crossing]
    )
    keeps = [list(keep)] + [[x[1], y] for x, y in zip(arrived, last_keeps)]
    stem_keep, *stem_recv = stem_made
    stem_recv = [swap(x, "group", group, 1) for x in stem_recv]
    stem_parts = halve_stem(stem_recv, stem_keep, group)
    _, coming, keeps = together(stem_parts, coming, keeps)
    kinds = [F32 if j < 2 else BF16 for j in range(dp // 2)]
    blocks = combine_call(high, keeps + [[coming]], kinds)
    landing = [blocks[0]] + [swap(blocks[j], "dp", dp, 2 * j) for j in rests]
    near = dp // 2 * 3 // 4

    def after(mixed, share):
        return [swap(mixed, "group", group, 1), share] + landing[2:near]

    def last(mixed, *arrived):
        output = output_call(counts, mixed, emb, packs, weights)
        total = add_call(list(arrived) + [landing[1]] + landing[near:])
        return output, total[:, : 3 * width].reshape(total.shape[0], 3, width), total[:, 3 * width :].T

    grad_w_stem, (output, grad_w_qkv, grad_w_out) = sum_stem(
        stem_parts, [mixed_call(packs, weights), landing[0]], after, last, dp, group
    )
    return (output.reshape(scenes, GROUPS, CAP, D), grad_w_stem, grad_w_qkv, grad_w_out)


def solution(mesh):
    sizes = dict(mesh.shape)
    return jax.shard_map(
        functools.partial(on_device, sizes["dp"], sizes["group"]),
        mesh=mesh,
        in_specs=(
            P(("dp", "group"), None, None),
            P(("dp", "group"), None, None),
            P(("dp", "group"), None),
            P(),
            P(),
            P("dp", None, "group"),
            P("group", "dp"),
            P(("dp", "group"), None, None, None),
        ),
        out_specs=(
            P(("dp", "group"), None, None, None),
            P(),
            P("dp", None, "group"),
            P("group", "dp"),
        ),
        check_vma=False,
    )
```

```python
import functools

import jax
import jax.numpy as jnp
import ml_dtypes
import numpy as np
from jax import lax
from jax.experimental import pallas as pl
from jax.experimental.pallas import tpu as pltpu
from jax.sharding import PartitionSpec as P

D = 1024
HD = 64
GROUPS = 3
CAP = 48
GRID = 12
PIX = 64
TOK = GROUPS * CAP
PAIR = 128
GROUP_BANDS = ((0, 4), (4, 8), (8, 10))
NORM_EPS = 1e-06
F32 = jnp.float32
BF16 = jnp.bfloat16
VMEM_LIMIT = 60 * 1024 * 1024


def dot_nn(a, b):
    return lax.dot_general(a, b, (((1,), (0,)), ((), ())), preferred_element_type=F32)


def dot_nt(a, b):
    return lax.dot_general(a, b, (((1,), (1,)), ((), ())), preferred_element_type=F32)


def dot_tn(a, b):
    return lax.dot_general(a, b, (((0,), (0,)), ((), ())), preferred_element_type=F32)


def live_column(c0, c1, c2):
    row = lax.broadcasted_iota(jnp.int32, (TOK, 1), 0)
    return (
        (row < c0)
        | ((row >= CAP) & (row < CAP + c1))
        | ((row >= 2 * CAP) & (row < 2 * CAP + c2))
    )


def params():
    return pltpu.CompilerParams(vmem_limit_bytes=VMEM_LIMIT)


def cost(flops, nbytes):
    return pl.CostEstimate(flops=int(flops / 1000), bytes_accessed=int(nbytes / 1000), transcendentals=0)


def stem_kernel(
    cnt_ref, idx_ref, patch_ref, w_ref, gain_ref, parts, genc_ref, og_ref,
    emb_ref, rows_ref, cols_ref,
):
    step = pl.program_id(0)
    scenes = patch_ref.shape[0]
    patch_iota = lax.broadcasted_iota(jnp.int32, (parts.shape[1], CAP), 0)
    slot = lax.broadcasted_iota(jnp.int32, (CAP, 1), 0)
    for g, (start, end) in enumerate(GROUP_BANDS):
        rows = slice(g * CAP, (g + 1) * CAP)
        width = (end - start) * PIX
        picked, placed = [], []
        for s in range(scenes):
            onehot = (idx_ref[s, g : g + 1, :] == patch_iota).astype(F32).astype(BF16).T
            picked.append(dot_nn(onehot, patch_ref[s, :, start * PIX : end * PIX]).astype(BF16))
            placed.append(
                (dot_nn(onehot, parts[0]) + dot_nn(onehot, parts[1])) + dot_nn(onehot, parts[2])
            )
            live = slot < cnt_ref[pl.ds(step * scenes + s, 1), g : g + 1]
            rows_ref[1, s, rows, :] = jnp.where(live, og_ref[s, rows, :].astype(F32), 0.0).astype(BF16)
        summed = dot_nn(jnp.concatenate(picked, axis=0), w_ref[start * PIX : end * PIX, :])
        for s in range(scenes):
            values = summed[s * CAP : (s + 1) * CAP] + (placed[s] + genc_ref[g : g + 1, :])
            emb = values.astype(BF16)
            emb_ref[s, rows, :] = emb
            x = emb.astype(F32)
            centre = jnp.mean(x, axis=-1, keepdims=True)
            dev = x - centre
            spread = jnp.mean(dev * dev, axis=-1, keepdims=True)
            centred = dev * lax.rsqrt(spread + NORM_EPS)
            rows_ref[0, s, rows, :] = (centred * gain_ref[...]).astype(BF16)
            cols_ref[s, rows, :width] = picked[s]
            if width < cols_ref.shape[2]:
                cols_ref[s, rows, width:] = jnp.zeros((CAP, cols_ref.shape[2] - width), BF16)


def stem_call(counts, index, patches, w_stem, gain, table, genc, out_grad):
    scenes, patch_count, width = patches.shape
    block = 3 if scenes % 3 == 0 else 1
    col_width = max(e - s for s, e in GROUP_BANDS) * PIX
    per = lambda shape: pl.BlockSpec((block,) + shape, lambda i: (i, 0, 0))
    whole = lambda a: pl.BlockSpec(a.shape, lambda i: (0,) * a.ndim)
    return pl.pallas_call(
        stem_kernel,
        grid=(scenes // block,),
        in_specs=[
            whole(counts),
            per((GROUPS, CAP)),
            per((patch_count, width)),
            whole(w_stem),
            whole(gain),
            whole(table),
            whole(genc),
            per((TOK, D)),
        ],
        out_specs=[
            per((TOK, D)),
            pl.BlockSpec((2, block, TOK, D), lambda i: (0, i, 0, 0)),
            per((TOK, col_width)),
        ],
        out_shape=[
            jax.ShapeDtypeStruct((scenes, TOK, D), BF16),
            jax.ShapeDtypeStruct((2, scenes, TOK, D), BF16),
            jax.ShapeDtypeStruct((scenes, TOK, col_width), BF16),
        ],
        compiler_params=params(),
        cost_estimate=cost(8e9, 12e6),
        name="stem_norm",
    )(counts, index, patches, w_stem, gain, table, genc, out_grad)


def attention_kernel(
    packs, blocks, dp, cnt_ref, owner_ref, low_ref, na_ref, nb_ref, ga_ref, gb_ref, *refs
):
    earlier, refs = refs[: 2 * (packs or 0)], refs[2 * (packs or 0) :]
    blocks, refs = refs[:blocks], refs[blocks:]
    out_ref, w_ref, *refs = refs
    keeps, others, refs = refs[:2], refs[2:4], refs[4:]
    n_s, g_s, qkv, total = refs[-4:]
    half, step = pl.program_id(0), pl.program_id(1)
    rows = n_s.shape[0]
    scenes = rows // TOK
    width = w_ref.shape[1] // 4

    @pl.when((half == 0) & (step == 0))
    def _():
        size = blocks[0].shape[0]
        for b, block in enumerate(blocks):
            w_ref[pl.ds(pl.multiple_of(owner_ref[b] * size, size), size), :] = block[...]
        total[...] = jnp.zeros_like(total)

    @pl.when(half == 0)
    def _():
        n_s[...] = na_ref[0]
        g_s[...] = ga_ref[0]

    @pl.when(half != 0)
    def _():
        n_s[...] = nb_ref[0]
        g_s[...] = gb_ref[0]

    qkv[:, : 3 * width] = dot_nn(n_s[...], w_ref[:, : 3 * width]).astype(BF16)
    qkv[:, 3 * width :] = dot_nn(g_s[...], w_ref[:, 3 * width :]).astype(BF16)
    heads = width // HD
    lane = lax.broadcasted_iota(jnp.int32, (1, width), 1)
    masks = [(lane // HD == h).astype(F32).astype(BF16) for h in range(heads)]
    scale = jnp.asarray(HD ** (-0.5), BF16)
    first_of_pair = lax.broadcasted_iota(jnp.int32, (1, PAIR), 1) < HD

    def own_lanes(tall):
        tiles = []
        for t in range(width // PAIR):
            at = slice(t * PAIR, (t + 1) * PAIR)
            one = tall[2 * t * TOK : (2 * t + 1) * TOK, at]
            two = tall[(2 * t + 1) * TOK : (2 * t + 2) * TOK, at]
            tiles.append(jnp.where(first_of_pair, one, two))
        return jnp.concatenate(tiles, axis=1)

    def scene_body(s, _):
        base = pl.multiple_of(s * TOK, 16)
        at = pl.ds(base, TOK)
        scene = step * scenes + s
        live = live_column(cnt_ref[half, scene, 0], cnt_ref[half, scene, 1], cnt_ref[half, scene, 2])
        bias = jnp.where(live, 0.0, -1e30)
        q, k, v, dc = [qkv[at, c * width : (c + 1) * width] for c in range(4)]
        tall_q = jnp.concatenate([q * (m * scale) for m in masks], axis=0)
        tall_dc = jnp.concatenate([dc * m for m in masks], axis=0)
        scores = dot_nt(k, tall_q)
        grad_probs = dot_nt(v, tall_dc)
        probs_parts, score_parts = [], []
        for start in range(0, heads * TOK, PAIR):
            cols = slice(start, min(start + PAIR, heads * TOK))
            part = scores[:, cols] + bias
            lifted = jnp.exp(part - jnp.max(part, axis=0, keepdims=True))
            probs = lifted * (1.0 / jnp.sum(lifted, axis=0, keepdims=True))
            weighted = probs * grad_probs[:, cols]
            inner = jnp.sum(weighted, axis=0, keepdims=True)
            probs_parts.append(probs.astype(BF16))
            score_parts.append((weighted - probs * inner).astype(BF16))
        half_probs = jnp.concatenate(probs_parts, axis=1)
        grad_score = jnp.concatenate(score_parts, axis=1)
        out_ref[at, :width] = (own_lanes(dot_tn(grad_score, k)) * HD ** (-0.5)).astype(BF16)
        out_ref[at, width : 2 * width] = dot_nn(grad_score, tall_q).astype(BF16)
        out_ref[at, 2 * width : 3 * width] = dot_nn(half_probs, tall_dc).astype(BF16)
        out_ref[at, 3 * width :] = own_lanes(dot_tn(half_probs, v)).astype(BF16)
        return 0

    lax.fori_loop(0, scenes, scene_body, 0, unroll=True)
    total[:, : 3 * width] += dot_tn(n_s[...], out_ref[:, : 3 * width])
    total[:, 3 * width :] += dot_tn(g_s[...], out_ref[:, 3 * width :])

    @pl.when((half == pl.num_programs(0) - 1) & (step == pl.num_programs(1) - 1))
    def _():
        size = total.shape[0] // dp
        low = low_ref[0]
        for b in range(dp // 2):
            at = slice(b * size, (b + 1) * size)
            mine = pl.multiple_of((2 * b + low) * size, size)
            other = pl.multiple_of((2 * b + 1 - low) * size, size)
            for c in range(2):
                cols = slice(c * 2 * width, (c + 1) * 2 * width)
                keeps[c][at, :] = total[pl.ds(mine, size), cols].astype(keeps[c].dtype)
                others[c][at, :] = total[pl.ds(other, size), cols].astype(others[c].dtype)

    if packs is not None:
        back = dot_nt(out_ref[:, : 3 * width], w_ref[:, : 3 * width])
        for pack_ref, weight_ref in zip(earlier[:packs], earlier[packs:]):
            back = back + dot_nt(pack_ref[...], weight_ref[...])

        @pl.when(half == 0)
        def _():
            refs[0][...] = back

        @pl.when(half != 0)
        def _():
            refs[1][...] = back.astype(BF16)


def block_rows(tokens):
    return 3 * TOK if tokens % (3 * TOK) == 0 else TOK


def two_halves(rows, steps, lead):
    shape = (1,) * len(lead) + (rows, D)
    first = pl.BlockSpec(shape, lambda h, i: lead + (jnp.where(h == 0, i, steps - 1), 0))
    second = pl.BlockSpec(shape, lambda h, i: lead + (jnp.where(h == 0, 0, i), 0))
    return [first, second]


SCALARS = pl.BlockSpec(memory_space=pltpu.SMEM)


def attention_call(counts, owners, low, own, far, earlier, blocks, dp):
    tokens = own.shape[1]
    rows = block_rows(tokens)
    steps = tokens // rows
    cols = blocks[0][0].shape[1]
    whole = lambda shape: pl.BlockSpec(shape, lambda h, i: (0, 0))
    at = lambda h, i: (h * steps + i, 0)
    packs = None if earlier is None else len(earlier[0])
    back = [] if earlier is None else two_halves(rows, steps, ())
    kind = BF16 if earlier is None else F32
    grads = [jax.ShapeDtypeStruct((D // 2, c), kind) for c in [cols // 2] * 4]
    return pl.pallas_call(
        functools.partial(attention_kernel, packs, len(blocks), dp),
        grid=(2, steps),
        in_specs=[SCALARS] * 3
        + two_halves(rows, steps, (0,))
        + two_halves(rows, steps, (1,))
        + [pl.BlockSpec((rows, cols // 4 * 3), at)] * (packs or 0)
        + [whole((D, cols // 4 * 3))] * (packs or 0)
        + [pl.BlockSpec((D // dp, cols), functools.partial(lambda at, h, i: (at, 0), at)) for _, at in blocks],
        out_specs=[pl.BlockSpec((rows, cols), at), whole((D, cols))] + [whole(g.shape) for g in grads] + back,
        out_shape=[
            jax.ShapeDtypeStruct((2 * tokens, cols), BF16),
            jax.ShapeDtypeStruct((D, cols), BF16),
            *grads,
        ]
        + [jax.ShapeDtypeStruct((tokens, D), kind) for kind in (F32, BF16)[: len(back)]],
        scratch_shapes=[
            pltpu.VMEM((rows, D), BF16),
            pltpu.VMEM((rows, D), BF16),
            pltpu.VMEM((rows, cols), BF16),
            pltpu.VMEM((D, cols), F32),
        ],
        compiler_params=params(),
        cost_estimate=cost(20e9, 14e6),
        name="attention",
    )(counts, owners, low, own, far, own, far, *[x for group in earlier or () for x in group], *[b for b, _ in blocks])


def combine_kernel(counts, place_ref, *refs):
    ins, refs = refs[: sum(counts)], refs[sum(counts) :]
    rows = refs[0].shape[0]
    place = place_ref[0]
    for j, ref in enumerate(refs):
        at = pl.ds(pl.multiple_of((place ^ j) * rows, rows), rows)
        total = None
        first = 0
        for count in counts:
            pieces = [r[at, :].astype(F32) for r in ins[first : first + count]]
            new = pieces[0] if count == 1 else jnp.concatenate(pieces, axis=1)
            total = new if total is None else total + new
            first += count
        ref[...] = total.astype(ref.dtype)


def combine_call(place, parts, dtypes):
    ins = [piece for part in parts for piece in part]
    rows, cols = ins[0].shape[0] // len(dtypes), sum(piece.shape[1] for piece in parts[0])
    whole = lambda a: pl.BlockSpec(a.shape, lambda: (0, 0))
    return pl.pallas_call(
        functools.partial(combine_kernel, [len(part) for part in parts]),
        in_specs=[SCALARS] + [whole(a) for a in ins],
        out_specs=[pl.BlockSpec((rows, cols), lambda: (0, 0))] * len(dtypes),
        out_shape=[jax.ShapeDtypeStruct((rows, cols), d) for d in dtypes],
        compiler_params=params(),
        cost_estimate=cost(1e6, 5e6),
        name="combine",
    )(place, *ins)


def add_kernel(*refs):
    total = refs[0][...]
    for ref in refs[1:-1]:
        total = total + ref[...].astype(F32)
    refs[-1][...] = total


def add_call(parts):
    spec = pl.BlockSpec(parts[0].shape, lambda: (0, 0))
    return pl.pallas_call(
        add_kernel,
        in_specs=[spec] * len(parts),
        out_specs=spec,
        out_shape=jax.ShapeDtypeStruct(parts[0].shape, F32),
        compiler_params=params(),
        cost_estimate=cost(1e6, 2e6),
        name="add_parts",
    )(*parts)


def mixed_product(context_refs, weight_refs):
    total = None
    for context_ref, w_ref in zip(context_refs, weight_refs):
        new = dot_nt(context_ref[...], w_ref[...])
        total = new if total is None else total + new
    return total


def context_specs(rows, packs, weights, first):
    width = packs[0].shape[1] // 4
    return [pl.BlockSpec((rows, width), lambda i: (first + i, 3))] * len(packs) + [
        pl.BlockSpec((D, width), lambda i: (0, 3))
    ] * len(weights)


def mixed_kernel(count, *refs):
    refs[-1][...] = mixed_product(refs[:count], refs[count : 2 * count]).astype(BF16)


def mixed_call(packs, weights):
    tokens = packs[0].shape[0] // 2
    rows = block_rows(tokens)
    return pl.pallas_call(
        functools.partial(mixed_kernel, len(packs)),
        grid=(tokens // rows,),
        in_specs=context_specs(rows, packs, weights, tokens // rows),
        out_specs=pl.BlockSpec((rows, D), lambda i: (i, 0)),
        out_shape=jax.ShapeDtypeStruct((tokens, D), BF16),
        compiler_params=params(),
        cost_estimate=cost(2e9, 5e6),
        name="mixed",
    )(*packs, *weights)


def tail_kernel(core_ref, own_ref, recv_ref, emb_ref, gl_ref, cols_ref, gain_ref, keep_ref, first_ref, second_ref, acc):
    step = pl.program_id(0)
    rows = emb_ref.shape[0]
    scenes = rows // TOK

    @pl.when(step == 0)
    def _():
        acc[...] = jnp.zeros_like(acc)

    grad_normed = own_ref[...] + recv_ref[...].astype(F32)
    x = emb_ref[...].astype(F32)
    dev = x - jnp.mean(x, axis=-1, keepdims=True)
    inv_std = lax.rsqrt(jnp.mean(dev * dev, axis=-1, keepdims=True) + NORM_EPS)
    centred = dev * inv_std
    scaled = grad_normed * gain_ref[...]
    first_mean = jnp.mean(scaled, axis=-1, keepdims=True)
    second_mean = jnp.mean(scaled * centred, axis=-1, keepdims=True)
    back = inv_std * (scaled - first_mean - centred * second_mean)
    grad_in = (gl_ref[0].astype(F32) + back).astype(BF16)
    for g, (start, end) in enumerate(GROUP_BANDS):
        at = [slice(s * TOK + g * CAP, s * TOK + (g + 1) * CAP) for s in range(scenes)]
        columns = jnp.concatenate([cols_ref[a, : (end - start) * PIX] for a in at], axis=0)
        grads = jnp.concatenate([grad_in[a] for a in at], axis=0)
        acc[start * PIX : end * PIX, :] += dot_tn(columns, grads)

    @pl.when(step == pl.num_programs(0) - 1)
    def _():
        size = keep_ref.shape[0]
        core = core_ref[0]
        keep_ref[...] = acc[pl.ds(pl.multiple_of(core * size, size), size), :]
        other = pl.ds(pl.multiple_of((1 - core) * size, size), size)
        first_ref[...] = acc[other, : D // 2]
        second_ref[...] = acc[other, D // 2 :]


def tail_call(core, own, recv, emb, rows_own, cols, gain):
    tokens = emb.shape[0]
    rows = 2 * TOK if tokens % (2 * TOK) == 0 else TOK
    per = lambda a: pl.BlockSpec((rows, a.shape[1]), lambda i: (i, 0))
    stem_rows = GROUP_BANDS[-1][1] * PIX
    keep = jax.ShapeDtypeStruct((stem_rows // 2, D), F32)
    send = jax.ShapeDtypeStruct((stem_rows // 2, D // 2), F32)
    return pl.pallas_call(
        tail_kernel,
        grid=(tokens // rows,),
        in_specs=[SCALARS, per(own), per(recv), per(emb), pl.BlockSpec((1, rows, D), lambda i: (1, i, 0)), per(cols)]
        + [pl.BlockSpec(gain.shape, lambda i: (0, 0))],
        out_specs=[pl.BlockSpec(a.shape, lambda i: (0, 0)) for a in (keep, send, send)],
        out_shape=[keep, send, send],
        scratch_shapes=[pltpu.VMEM((stem_rows, D), F32)],
        compiler_params=params(),
        cost_estimate=cost(10e9, 12e6),
        name="tail",
    )(core, own, recv, emb, rows_own, cols, gain)


def output_kernel(count, cnt_ref, recv_ref, emb_ref, *refs):
    out_ref = refs[-1]
    step = pl.program_id(0)
    scenes = emb_ref.shape[0] // TOK
    mixed = recv_ref[...].astype(F32) + mixed_product(refs[:count], refs[count : 2 * count])
    total = emb_ref[...].astype(F32) + mixed
    for s in range(scenes):
        scene = step * scenes + s
        live = live_column(cnt_ref[scene, 0], cnt_ref[scene, 1], cnt_ref[scene, 2])
        at = slice(s * TOK, (s + 1) * TOK)
        out_ref[at, :] = jnp.where(live, total[at], 0.0).astype(BF16)


def output_call(counts, recv, emb, packs, weights):
    tokens = emb.shape[0]
    rows = 2 * TOK if tokens % (2 * TOK) == 0 else TOK
    per = lambda a: pl.BlockSpec((rows, a.shape[1]), lambda i: (i, 0))
    return pl.pallas_call(
        functools.partial(output_kernel, len(packs)),
        grid=(tokens // rows,),
        in_specs=[SCALARS, per(recv), per(emb)]
        + context_specs(rows, packs, weights, 0),
        out_specs=per(emb),
        out_shape=jax.ShapeDtypeStruct(emb.shape, BF16),
        compiler_params=params(),
        cost_estimate=cost(5e9, 10e6),
        name="layer_output",
    )(counts, recv, emb, *packs, *weights)


def swap(x, axis, size, bit):
    return lax.ppermute(x, axis, [(i, i ^ bit) for i in range(size)])


def together(*values):
    return lax.optimization_barrier(values)


class Ring:
    def __init__(self, x, axis, size):
        self.axis, self.size = axis, size
        order = list(range(0, size, 2)) + list(range(size - 1, 0, -2))
        self.forward = [(order[i], order[(i + 1) % size]) for i in range(size)]
        self.backward = [(order[(i + 1) % size], order[i]) for i in range(size)]
        self.ahead, self.behind = [x], [x]

    def send(self):
        moved = [lax.ppermute(self.ahead[-1], self.axis, self.forward)]
        if len(self.behind) <= (self.size - 1) // 2:
            moved.append(lax.ppermute(self.behind[-1], self.axis, self.backward))
        return moved

    def receive(self, moved):
        self.ahead.append(moved[0])
        self.behind.extend(moved[1:])

    @property
    def steps(self):
        return len(self.ahead) - 1

    def owners(self, ahead, behind):
        size = self.size
        me = lax.axis_index(self.axis)
        here = jnp.where(me % 2 == 0, me // 2, size - 1 - me // 2)
        distances = [-s for s in range(ahead)] + list(range(1, behind))
        at = (here + size + jnp.array(distances, jnp.int32)) % size
        return jnp.where(at < size // 2, 2 * at, 2 * (size - 1 - at) + 1)


def step_all(rings, *beside):
    moved, beside = together([ring.send() for ring in rings], beside)
    for ring, blocks in zip(rings, moved):
        ring.receive(blocks)
    return beside


def halve_stem(recv, keep, group):
    mine = lax.axis_index("group") // 2 * 2 + lax.axis_index("dp") % 2
    return combine_call(mine.reshape(1), [[keep], recv], [F32] * (group // 2 * 2))


def sum_stem(parts, beside, after, last, dp, group):
    core = lax.axis_index("group") % 2
    far = lax.axis_index("group") // 2
    low = lax.axis_index("dp") % 2
    high = lax.axis_index("dp") // 2
    fars, highs = group // 2, dp // 2
    mine = far * 2 + low
    small, width = parts[0].shape
    rows = 2 * fars * small

    def hop(block, f, b):
        if f:
            pairs = [
                (d * group + g, (d ^ b) * group + (g ^ (2 * f))) for d in range(dp) for g in range(group)
            ]
            return lax.ppermute(block, ("dp", "group"), pairs)
        return swap(block, "dp", dp, b)

    hops = [(k // 2, k % 2) for k in range(1, 2 * fars)]
    arrived = [hop(part, f, b) for part, (f, b) in zip(parts[1:], hops)]
    arrived, beside = together(arrived, beside)
    beside = after(*beside)
    total = parts[0]
    for part in arrived:
        total = total + part
    cols = width // highs
    part = lax.dynamic_slice_in_dim(total, high * cols, cols, 1)
    away = [lax.dynamic_slice_in_dim(total, (high ^ j) * cols, cols, 1) for j in range(1, highs)]
    arrived = [swap(a, "dp", dp, 2 * (j + 1)) for j, a in enumerate(away)]
    arrived, beside = together(arrived, beside)
    for block in arrived:
        part = part + block
    part = part.astype(BF16)
    line = jnp.zeros((small, width), BF16)
    line = lax.dynamic_update_slice_in_dim(line, part, high * cols, 1)
    arrived = [swap(part, "dp", dp, 2 * j) for j in range(1, highs)]
    for j, block in enumerate(arrived):
        line = lax.dynamic_update_slice_in_dim(line, block, (high ^ (j + 1)) * cols, 1)
    block = jnp.zeros((rows, width), BF16)
    block = lax.dynamic_update_slice_in_dim(block, line, mine * small, 0)
    arrived, beside = together([hop(line, f, b) for f, b in hops], last(*beside))
    for (f, b), piece in zip(hops, arrived):
        target = (far ^ f) * 2 + (low ^ b)
        block = lax.dynamic_update_slice_in_dim(block, piece, target * small, 0)
    partner = swap(block, "group", group, 1)
    first = jnp.where(core == 0, block, partner)
    second = jnp.where(core == 0, partner, block)
    return jnp.concatenate([first, second], axis=0).astype(F32), beside


def encoding_tables(patch_count):
    quarter = D // 4
    half_width = D // 2
    power = lambda n: np.power(np.float32(10000.0), -np.arange(n, dtype=np.float32) / np.float32(n))
    at = np.arange(GRID).astype(np.float32)[:, None] * power(quarter)
    both = np.concatenate([np.sin(at), np.cos(at)], axis=-1)
    patch = np.arange(patch_count)
    rest = np.concatenate([both[patch // GRID], both[patch % GRID]], axis=-1).astype(np.float32)
    parts = []
    for _ in range(3):
        parts.append(rest.astype(ml_dtypes.bfloat16))
        rest = rest - parts[-1].astype(np.float32)
    group_at = np.arange(GROUPS).astype(np.float32)[:, None] * power(half_width)
    return np.stack(parts), np.concatenate([np.sin(group_at), np.cos(group_at)], axis=-1).astype(np.float32)


def on_device(dp, group, patches, vis_index, vis_count, w_stem, ln_gain, w_qkv, w_out, out_grad):
    scenes = patches.shape[0]
    tokens = scenes * TOK
    width = w_qkv.shape[2]
    fars = range(1, group // 2)
    rests = range(1, dp // 2)
    dp_low, dp_high = lax.axis_index("dp") % 2, lax.axis_index("dp") // 2
    low, high = dp_low.reshape(1), dp_high.reshape(1)
    core = (lax.axis_index("group") % 2).reshape(1)

    shard = jnp.concatenate([w_qkv.reshape(w_qkv.shape[0], 3 * width), w_out.T], axis=1)
    cross = lambda x, f: swap(x, "group", group, 2 * f)
    far_shards = [cross(shard, f) for f in fars]
    counts = vis_count.astype(jnp.int32)
    counts_far = swap(counts, "group", group, 1)
    table, genc = encoding_tables(patches.shape[1])
    gain = ln_gain.reshape(1, D)
    stem = stem_call(
        counts,
        vis_index,
        patches,
        w_stem,
        gain,
        jnp.asarray(table),
        jnp.asarray(genc),
        out_grad.reshape(scenes, TOK, D),
    )
    stem, both_counts, far_shards = together(stem, jnp.stack([counts, counts_far]), far_shards)
    rings = [Ring(x, "dp", dp) for x in far_shards]
    ring = rings[0]
    owners = ring.owners(dp // 2 + 1, dp // 2)
    emb = stem[0].reshape(tokens, D)
    both = [stem[1].reshape(2, tokens, D)]
    cols = stem[2].reshape(tokens, stem[2].shape[2])
    both.append(swap(both[0], "group", group, 1))
    passed = []
    both, owners = step_all(rings, both, owners)
    while ring.steps < dp // 2:
        passed.append(cross(ring.ahead[-1], 1))
        if len(passed) > 1:
            (passed[-2],) = step_all(rings, passed[-2])
        else:
            step_all(rings)
    ring.ahead, ring.behind = together(ring.ahead, ring.behind)
    passed.append(cross(ring.ahead[-1], 1))
    passed.append(cross(jnp.concatenate(ring.behind[1:], axis=0), 1))

    packs, weights, crossing = [], [], []
    for f in list(fars) + [0]:
        if f:
            blocks = [(x, 0) for x in rings[f - 1].ahead + rings[f - 1].behind[1:]]
        else:
            blocks = [(x, 0) for x in [shard] + passed[:-1]] + [(passed[-1], b) for b in range(dp // 2 - 1)]
        made = attention_call(both_counts, owners, low, *both, None if f else (packs, weights), blocks, dp)
        if f == 1:
            made, passed[-3:] = together(made, passed[-3:])
        elif f:
            made = together(*made)
        else:
            made, arrived = together(made, [x[:3] for x in crossing])
        pack, weight, keep, other, back = made[0], made[1], made[2:4], made[4:6], made[6:]
        packs.append(pack)
        weights.append(weight)
        if f:
            crossing.append([cross(x, f) for x in (*other, *keep)])
    back_far = swap(back[1], "group", group, 1)
    coming = []
    for c in range(2):
        send = other[c]
        for x in arrived:
            send = send + x[c].astype(F32)
        coming.append(swap(send.astype(BF16), "dp", dp, 1))
    stem_made, coming[0], last_keeps = together(
        tail_call(core, back[0], back_far, emb, both[0], cols, gain), coming[0], [x[3] for x in crossing]
    )
    keeps = [[keep[0]] + [x[2] for x in arrived], [keep[1]] + list(last_keeps)]
    stem_keep, *stem_recv = stem_made
    stem_recv = [swap(x, "group", group, 1) for x in stem_recv]
    kinds = [F32 if j < 2 else BF16 for j in range(dp // 2)]
    second_leg = lambda c: combine_call(high, [[x] for x in keeps[c] + [coming[c]]], kinds)
    spread = lambda blocks, js: [swap(blocks[j], "dp", dp, 2 * j) for j in js]
    first = second_leg(0)
    stem_recv, share = together(stem_recv, first[0])
    first_rest = spread(first, rests[1:])
    stem_parts = halve_stem(stem_recv, stem_keep, group)
    _, coming[1], keeps[1] = together(stem_parts, coming[1], keeps[1])
    second = second_leg(1)
    near = dp // 2 * 3 // 4
    beside = [
        mixed_call(packs, weights),
        [share, *first_rest],
        [second[0], *spread(second, range(2, near))],
    ]

    def after(mixed, first, second):
        return [swap(mixed, "group", group, 1), first, [*second, *spread(blocks[1], range(near, dp // 2))]]

    def last(mixed, first, second):
        output = output_call(counts, mixed, emb, packs, weights)
        first, second = [add_call([*x, *spread(b, [1])]) for x, b in zip((first, second), blocks)]
        qkv = jnp.concatenate([first, second[:, :width]], axis=1)
        return output, qkv.reshape(qkv.shape[0], 3, width), second[:, width:].T

    blocks = (first, second)
    grad_w_stem, (output, grad_w_qkv, grad_w_out) = sum_stem(
        stem_parts, beside, after, last, dp, group
    )
    return (output.reshape(scenes, GROUPS, CAP, D), grad_w_stem, grad_w_qkv, grad_w_out)


def solution(mesh):
    sizes = dict(mesh.shape)
    return jax.shard_map(
        functools.partial(on_device, sizes["dp"], sizes["group"]),
        mesh=mesh,
        in_specs=(
            P(("dp", "group"), None, None),
            P(("dp", "group"), None, None),
            P(("dp", "group"), None),
            P(),
            P(),
            P("dp", None, "group"),
            P("group", "dp"),
            P(("dp", "group"), None, None, None),
        ),
        out_specs=(
            P(("dp", "group"), None, None, None),
            P(),
            P("dp", None, "group"),
            P("group", "dp"),
        ),
        check_vma=False,
    )
```

```python
import functools

import jax
import jax.numpy as jnp
import ml_dtypes
import numpy as np
from jax import lax
from jax.experimental import pallas as pl
from jax.experimental.pallas import tpu as pltpu
from jax.sharding import PartitionSpec as P

D = 1024
HD = 64
GROUPS = 3
CAP = 48
GRID = 12
PIX = 64
TOK = GROUPS * CAP
PAIR = 128
GROUP_BANDS = ((0, 4), (4, 8), (8, 10))
NORM_EPS = 1e-06
F32 = jnp.float32
BF16 = jnp.bfloat16
VMEM_LIMIT = 60 * 1024 * 1024


def dot_nn(a, b):
    return lax.dot_general(a, b, (((1,), (0,)), ((), ())), preferred_element_type=F32)


def dot_nt(a, b):
    return lax.dot_general(a, b, (((1,), (1,)), ((), ())), preferred_element_type=F32)


def dot_tn(a, b):
    return lax.dot_general(a, b, (((0,), (0,)), ((), ())), preferred_element_type=F32)


def live_column(c0, c1, c2):
    row = lax.broadcasted_iota(jnp.int32, (TOK, 1), 0)
    return (
        (row < c0)
        | ((row >= CAP) & (row < CAP + c1))
        | ((row >= 2 * CAP) & (row < 2 * CAP + c2))
    )


def params():
    return pltpu.CompilerParams(vmem_limit_bytes=VMEM_LIMIT)


def cost(flops, nbytes):
    return pl.CostEstimate(flops=int(flops / 1000), bytes_accessed=int(nbytes / 1000), transcendentals=0)


def stem_kernel(
    cnt_ref, idx_ref, patch_ref, w_ref, gain_ref, parts, genc_ref, og_ref,
    emb_ref, rows_ref, cols_ref,
):
    step = pl.program_id(0)
    scenes = patch_ref.shape[0]
    patch_iota = lax.broadcasted_iota(jnp.int32, (parts.shape[1], CAP), 0)
    slot = lax.broadcasted_iota(jnp.int32, (CAP, 1), 0)
    for g, (start, end) in enumerate(GROUP_BANDS):
        rows = slice(g * CAP, (g + 1) * CAP)
        width = (end - start) * PIX
        picked, placed = [], []
        for s in range(scenes):
            onehot = (idx_ref[s, g : g + 1, :] == patch_iota).astype(F32).astype(BF16).T
            picked.append(dot_nn(onehot, patch_ref[s, :, start * PIX : end * PIX]).astype(BF16))
            placed.append(
                (dot_nn(onehot, parts[0]) + dot_nn(onehot, parts[1])) + dot_nn(onehot, parts[2])
            )
            live = slot < cnt_ref[g, step * scenes + s]
            rows_ref[1, s, rows, :] = jnp.where(live, og_ref[s, rows, :].astype(F32), 0.0).astype(BF16)
        summed = dot_nn(jnp.concatenate(picked, axis=0), w_ref[start * PIX : end * PIX, :])
        for s in range(scenes):
            values = summed[s * CAP : (s + 1) * CAP] + (placed[s] + genc_ref[g : g + 1, :])
            emb = values.astype(BF16)
            emb_ref[s, rows, :] = emb
            x = emb.astype(F32)
            centre = jnp.mean(x, axis=-1, keepdims=True)
            dev = x - centre
            spread = jnp.mean(dev * dev, axis=-1, keepdims=True)
            centred = dev * lax.rsqrt(spread + NORM_EPS)
            rows_ref[0, s, rows, :] = (centred * gain_ref[...]).astype(BF16)
            cols_ref[s, rows, :width] = picked[s]
            if width < cols_ref.shape[2]:
                cols_ref[s, rows, width:] = jnp.zeros((CAP, cols_ref.shape[2] - width), BF16)


def stem_call(counts, index, patches, w_stem, gain, table, genc, out_grad):
    scenes, patch_count, width = patches.shape
    block = 3 if scenes % 3 == 0 else 1
    col_width = max(e - s for s, e in GROUP_BANDS) * PIX
    per = lambda shape: pl.BlockSpec((block,) + shape, lambda i: (i, 0, 0))
    whole = lambda a: pl.BlockSpec(a.shape, lambda i: (0,) * a.ndim)
    return pl.pallas_call(
        stem_kernel,
        grid=(scenes // block,),
        in_specs=[
            pl.BlockSpec(memory_space=pltpu.SMEM),
            per((GROUPS, CAP)),
            per((patch_count, width)),
            whole(w_stem),
            whole(gain),
            whole(table),
            whole(genc),
            per((TOK, D)),
        ],
        out_specs=[
            per((TOK, D)),
            pl.BlockSpec((2, block, TOK, D), lambda i: (0, i, 0, 0)),
            per((TOK, col_width)),
        ],
        out_shape=[
            jax.ShapeDtypeStruct((scenes, TOK, D), BF16),
            jax.ShapeDtypeStruct((2, scenes, TOK, D), BF16),
            jax.ShapeDtypeStruct((scenes, TOK, col_width), BF16),
        ],
        compiler_params=params(),
        cost_estimate=cost(8e9, 12e6),
        name="stem_norm",
    )(counts, index, patches, w_stem, gain, table, genc, out_grad)


def pack_kernel(qkv_ref, out_w_ref, pack_ref):
    count, _, width = qkv_ref.shape
    for c in range(count):
        pack_ref[:, c * width : (c + 1) * width] = qkv_ref[c]
    pack_ref[:, count * width :] = out_w_ref[...].T


def pack_call(w_qkv, w_out):
    parts = jnp.transpose(w_qkv, (1, 0, 2))
    return pl.pallas_call(
        pack_kernel,
        out_shape=jax.ShapeDtypeStruct((w_qkv.shape[0], 3 * w_qkv.shape[2] + w_out.shape[0]), BF16),
        compiler_params=params(),
        cost_estimate=cost(1e6, 5e5),
        name="pack_weights",
    )(parts, w_out)


def attention_kernel(
    packs, blocks, dp, cnt_ref, owner_ref, low_ref, na_ref, nb_ref, ga_ref, gb_ref, *refs
):
    earlier, refs = refs[: 2 * (packs or 0)], refs[2 * (packs or 0) :]
    blocks, refs = refs[:blocks], refs[blocks:]
    out_ref, w_ref, *refs = refs
    keeps, others, refs = refs[:2], refs[2:4], refs[4:]
    n_s, g_s, qkv, total = refs[-4:]
    half, step = pl.program_id(0), pl.program_id(1)
    rows = n_s.shape[0]
    scenes = rows // TOK
    width = w_ref.shape[1] // 4

    @pl.when((half == 0) & (step == 0))
    def _():
        size = blocks[0].shape[0]
        for b, block in enumerate(blocks):
            w_ref[pl.ds(pl.multiple_of(owner_ref[b] * size, size), size), :] = block[...]
        total[...] = jnp.zeros_like(total)

    @pl.when(half == 0)
    def _():
        n_s[...] = na_ref[0]
        g_s[...] = ga_ref[0]

    @pl.when(half != 0)
    def _():
        n_s[...] = nb_ref[0]
        g_s[...] = gb_ref[0]

    qkv[:, : 3 * width] = dot_nn(n_s[...], w_ref[:, : 3 * width]).astype(BF16)
    qkv[:, 3 * width :] = dot_nn(g_s[...], w_ref[:, 3 * width :]).astype(BF16)
    heads = width // HD
    lane = lax.broadcasted_iota(jnp.int32, (1, width), 1)
    masks = [(lane // HD == h).astype(F32).astype(BF16) for h in range(heads)]
    scale = jnp.asarray(HD ** (-0.5), BF16)
    first_of_pair = lax.broadcasted_iota(jnp.int32, (1, PAIR), 1) < HD

    def own_lanes(tall):
        tiles = []
        for t in range(width // PAIR):
            at = slice(t * PAIR, (t + 1) * PAIR)
            one = tall[2 * t * TOK : (2 * t + 1) * TOK, at]
            two = tall[(2 * t + 1) * TOK : (2 * t + 2) * TOK, at]
            tiles.append(jnp.where(first_of_pair, one, two))
        return jnp.concatenate(tiles, axis=1)

    def scene_body(s, _):
        base = pl.multiple_of(s * TOK, 16)
        at = pl.ds(base, TOK)
        scene = step * scenes + s
        live = live_column(*[cnt_ref[half, g, scene] for g in range(GROUPS)])
        bias = jnp.where(live, 0.0, -1e30)
        q, k, v, dc = [qkv[at, c * width : (c + 1) * width] for c in range(4)]
        tall_q = jnp.concatenate([q * (m * scale) for m in masks], axis=0)
        tall_dc = jnp.concatenate([dc * m for m in masks], axis=0)
        scores = dot_nt(k, tall_q)
        grad_probs = dot_nt(v, tall_dc)
        probs_parts, score_parts = [], []
        for start in range(0, heads * TOK, PAIR):
            cols = slice(start, min(start + PAIR, heads * TOK))
            part = scores[:, cols] + bias
            lifted = jnp.exp(part - jnp.max(part, axis=0, keepdims=True))
            probs = lifted * (1.0 / jnp.sum(lifted, axis=0, keepdims=True))
            weighted = probs * grad_probs[:, cols]
            inner = jnp.sum(weighted, axis=0, keepdims=True)
            probs_parts.append(probs.astype(BF16))
            score_parts.append((weighted - probs * inner).astype(BF16))
        half_probs = jnp.concatenate(probs_parts, axis=1)
        grad_score = jnp.concatenate(score_parts, axis=1)
        out_ref[at, :width] = (own_lanes(dot_tn(grad_score, k)) * HD ** (-0.5)).astype(BF16)
        out_ref[at, width : 2 * width] = dot_nn(grad_score, tall_q).astype(BF16)
        out_ref[at, 2 * width : 3 * width] = dot_nn(half_probs, tall_dc).astype(BF16)
        out_ref[at, 3 * width :] = own_lanes(dot_tn(half_probs, v)).astype(BF16)
        return 0

    lax.fori_loop(0, scenes, scene_body, 0, unroll=True)
    total[:, : 3 * width] += dot_tn(n_s[...], out_ref[:, : 3 * width])
    total[:, 3 * width :] += dot_tn(g_s[...], out_ref[:, 3 * width :])

    @pl.when((half == pl.num_programs(0) - 1) & (step == pl.num_programs(1) - 1))
    def _():
        size = total.shape[0] // dp
        low = low_ref[0]
        for b in range(dp // 2):
            at = slice(b * size, (b + 1) * size)
            mine = pl.multiple_of((2 * b + low) * size, size)
            other = pl.multiple_of((2 * b + 1 - low) * size, size)
            for c in range(2):
                cols = slice(c * 2 * width, (c + 1) * 2 * width)
                keeps[c][at, :] = total[pl.ds(mine, size), cols].astype(keeps[c].dtype)
                others[c][at, :] = total[pl.ds(other, size), cols].astype(others[c].dtype)

    if packs is not None:
        back = dot_nt(out_ref[:, : 3 * width], w_ref[:, : 3 * width])
        for pack_ref, weight_ref in zip(earlier[:packs], earlier[packs:]):
            back = back + dot_nt(pack_ref[...], weight_ref[...])

        @pl.when(half == 0)
        def _():
            refs[0][...] = back

        @pl.when(half != 0)
        def _():
            refs[1][...] = back.astype(BF16)


def block_rows(tokens):
    return 3 * TOK if tokens % (3 * TOK) == 0 else TOK


def two_halves(rows, steps, lead):
    shape = (1,) * len(lead) + (rows, D)
    first = pl.BlockSpec(shape, lambda h, i: lead + (jnp.where(h == 0, i, steps - 1), 0))
    second = pl.BlockSpec(shape, lambda h, i: lead + (jnp.where(h == 0, 0, i), 0))
    return [first, second]


SCALARS = pl.BlockSpec(memory_space=pltpu.SMEM)


def attention_call(counts, owners, low, own, far, earlier, blocks, dp):
    tokens = own.shape[1]
    rows = block_rows(tokens)
    steps = tokens // rows
    cols = blocks[0][0].shape[1]
    whole = lambda shape: pl.BlockSpec(shape, lambda h, i: (0, 0))
    at = lambda h, i: (h * steps + i, 0)
    packs = None if earlier is None else len(earlier[0])
    back = [] if earlier is None else two_halves(rows, steps, ())
    kind = BF16 if earlier is None else F32
    grads = [jax.ShapeDtypeStruct((D // 2, c), kind) for c in [cols // 2] * 4]
    return pl.pallas_call(
        functools.partial(attention_kernel, packs, len(blocks), dp),
        grid=(2, steps),
        in_specs=[SCALARS] * 3
        + two_halves(rows, steps, (0,))
        + two_halves(rows, steps, (1,))
        + [pl.BlockSpec((rows, cols // 4 * 3), at)] * (packs or 0)
        + [whole((D, cols // 4 * 3))] * (packs or 0)
        + [pl.BlockSpec((D // dp, cols), functools.partial(lambda at, h, i: (at, 0), at)) for _, at in blocks],
        out_specs=[pl.BlockSpec((rows, cols), at), whole((D, cols))] + [whole(g.shape) for g in grads] + back,
        out_shape=[
            jax.ShapeDtypeStruct((2 * tokens, cols), BF16),
            jax.ShapeDtypeStruct((D, cols), BF16),
            *grads,
        ]
        + [jax.ShapeDtypeStruct((tokens, D), kind) for kind in (F32, BF16)[: len(back)]],
        scratch_shapes=[
            pltpu.VMEM((rows, D), BF16),
            pltpu.VMEM((rows, D), BF16),
            pltpu.VMEM((rows, cols), BF16),
            pltpu.VMEM((D, cols), F32),
        ],
        compiler_params=params(),
        cost_estimate=cost(20e9, 14e6),
        name="attention",
    )(counts, owners, low, own, far, own, far, *[x for group in earlier or () for x in group], *[b for b, _ in blocks])


def combine_kernel(counts, place_ref, *refs):
    ins, refs = refs[: sum(counts)], refs[sum(counts) :]
    rows = refs[0].shape[0]
    place = place_ref[0]
    for j, ref in enumerate(refs):
        at = pl.ds(pl.multiple_of((place ^ j) * rows, rows), rows)
        total = None
        first = 0
        for count in counts:
            pieces = [r[at, :].astype(F32) for r in ins[first : first + count]]
            new = pieces[0] if count == 1 else jnp.concatenate(pieces, axis=1)
            total = new if total is None else total + new
            first += count
        ref[...] = total.astype(ref.dtype)


def combine_call(place, parts, dtypes):
    ins = [piece for part in parts for piece in part]
    rows, cols = ins[0].shape[0] // len(dtypes), sum(piece.shape[1] for piece in parts[0])
    whole = lambda a: pl.BlockSpec(a.shape, lambda: (0, 0))
    return pl.pallas_call(
        functools.partial(combine_kernel, [len(part) for part in parts]),
        in_specs=[SCALARS] + [whole(a) for a in ins],
        out_specs=[pl.BlockSpec((rows, cols), lambda: (0, 0))] * len(dtypes),
        out_shape=[jax.ShapeDtypeStruct((rows, cols), d) for d in dtypes],
        compiler_params=params(),
        cost_estimate=cost(1e6, 5e6),
        name="combine",
    )(place, *ins)


def result_kernel(count, *refs):
    halves, qkv_ref, out_ref = (refs[:count], refs[count:-2]), refs[-2], refs[-1]
    first, second = [functools.reduce(lambda a, b: a + b, [r[...].astype(F32) for r in half]) for half in halves]
    width = first.shape[1] // 2
    qkv_ref[0] = first[:, :width]
    qkv_ref[1] = first[:, width:]
    qkv_ref[2] = second[:, :width]
    out_ref[...] = second[:, width:].T


def result_call(first, second):
    rows, cols = first[0].shape
    qkv, out = pl.pallas_call(
        functools.partial(result_kernel, len(first)),
        out_shape=[
            jax.ShapeDtypeStruct((3, rows, cols // 2), F32),
            jax.ShapeDtypeStruct((cols // 2, rows), F32),
        ],
        compiler_params=params(),
        cost_estimate=cost(1e6, 2e6),
        name="weight_results",
    )(*first, *second)
    return jnp.transpose(qkv, (1, 0, 2)), out


def mixed_product(context_refs, weight_refs):
    total = None
    for context_ref, w_ref in zip(context_refs, weight_refs):
        new = dot_nt(context_ref[...], w_ref[...])
        total = new if total is None else total + new
    return total


def context_specs(rows, packs, weights, first):
    width = packs[0].shape[1] // 4
    return [pl.BlockSpec((rows, width), lambda i: (first + i, 3))] * len(packs) + [
        pl.BlockSpec((D, width), lambda i: (0, 3))
    ] * len(weights)


def mixed_kernel(count, *refs):
    refs[-1][...] = mixed_product(refs[:count], refs[count : 2 * count]).astype(BF16)


def mixed_call(packs, weights):
    tokens = packs[0].shape[0] // 2
    rows = block_rows(tokens)
    return pl.pallas_call(
        functools.partial(mixed_kernel, len(packs)),
        grid=(tokens // rows,),
        in_specs=context_specs(rows, packs, weights, tokens // rows),
        out_specs=pl.BlockSpec((rows, D), lambda i: (i, 0)),
        out_shape=jax.ShapeDtypeStruct((tokens, D), BF16),
        compiler_params=params(),
        cost_estimate=cost(2e9, 5e6),
        name="mixed",
    )(*packs, *weights)


def tail_kernel(core_ref, own_ref, recv_ref, emb_ref, gl_ref, cols_ref, gain_ref, keep_ref, first_ref, second_ref, acc):
    step = pl.program_id(0)
    rows = emb_ref.shape[0]
    scenes = rows // TOK

    @pl.when(step == 0)
    def _():
        acc[...] = jnp.zeros_like(acc)

    grad_normed = own_ref[...] + recv_ref[...].astype(F32)
    x = emb_ref[...].astype(F32)
    dev = x - jnp.mean(x, axis=-1, keepdims=True)
    inv_std = lax.rsqrt(jnp.mean(dev * dev, axis=-1, keepdims=True) + NORM_EPS)
    centred = dev * inv_std
    scaled = grad_normed * gain_ref[...]
    first_mean = jnp.mean(scaled, axis=-1, keepdims=True)
    second_mean = jnp.mean(scaled * centred, axis=-1, keepdims=True)
    back = inv_std * (scaled - first_mean - centred * second_mean)
    grad_in = (gl_ref[0].astype(F32) + back).astype(BF16)
    for g, (start, end) in enumerate(GROUP_BANDS):
        at = [slice(s * TOK + g * CAP, s * TOK + (g + 1) * CAP) for s in range(scenes)]
        columns = jnp.concatenate([cols_ref[a, : (end - start) * PIX] for a in at], axis=0)
        grads = jnp.concatenate([grad_in[a] for a in at], axis=0)
        acc[start * PIX : end * PIX, :] += dot_tn(columns, grads)

    @pl.when(step == pl.num_programs(0) - 1)
    def _():
        size = keep_ref.shape[0]
        core = core_ref[0]
        keep_ref[...] = acc[pl.ds(pl.multiple_of(core * size, size), size), :]
        other = pl.ds(pl.multiple_of((1 - core) * size, size), size)
        first_ref[...] = acc[other, : D // 2]
        second_ref[...] = acc[other, D // 2 :]


def tail_call(core, own, recv, emb, rows_own, cols, gain):
    tokens = emb.shape[0]
    rows = 2 * TOK if tokens % (2 * TOK) == 0 else TOK
    per = lambda a: pl.BlockSpec((rows, a.shape[1]), lambda i: (i, 0))
    stem_rows = GROUP_BANDS[-1][1] * PIX
    keep = jax.ShapeDtypeStruct((stem_rows // 2, D), F32)
    send = jax.ShapeDtypeStruct((stem_rows // 2, D // 2), F32)
    return pl.pallas_call(
        tail_kernel,
        grid=(tokens // rows,),
        in_specs=[SCALARS, per(own), per(recv), per(emb), pl.BlockSpec((1, rows, D), lambda i: (1, i, 0)), per(cols)]
        + [pl.BlockSpec(gain.shape, lambda i: (0, 0))],
        out_specs=[pl.BlockSpec(a.shape, lambda i: (0, 0)) for a in (keep, send, send)],
        out_shape=[keep, send, send],
        scratch_shapes=[pltpu.VMEM((stem_rows, D), F32)],
        compiler_params=params(),
        cost_estimate=cost(10e9, 12e6),
        name="tail",
    )(core, own, recv, emb, rows_own, cols, gain)


def output_kernel(count, cnt_ref, recv_ref, emb_ref, *refs):
    out_ref = refs[-1]
    step = pl.program_id(0)
    scenes = emb_ref.shape[0] // TOK
    mixed = recv_ref[...].astype(F32) + mixed_product(refs[:count], refs[count : 2 * count])
    total = emb_ref[...].astype(F32) + mixed
    for s in range(scenes):
        scene = step * scenes + s
        live = live_column(*[cnt_ref[g, scene] for g in range(GROUPS)])
        at = slice(s * TOK, (s + 1) * TOK)
        out_ref[at, :] = jnp.where(live, total[at], 0.0).astype(BF16)


def output_call(counts, recv, emb, packs, weights):
    tokens = emb.shape[0]
    rows = 2 * TOK if tokens % (2 * TOK) == 0 else TOK
    per = lambda a: pl.BlockSpec((rows, a.shape[1]), lambda i: (i, 0))
    return pl.pallas_call(
        functools.partial(output_kernel, len(packs)),
        grid=(tokens // rows,),
        in_specs=[SCALARS, per(recv), per(emb)]
        + context_specs(rows, packs, weights, 0),
        out_specs=per(emb),
        out_shape=jax.ShapeDtypeStruct(emb.shape, BF16),
        compiler_params=params(),
        cost_estimate=cost(5e9, 10e6),
        name="layer_output",
    )(counts, recv, emb, *packs, *weights)


def swap(x, axis, size, bit):
    return lax.ppermute(x, axis, [(i, i ^ bit) for i in range(size)])


def together(*values):
    return lax.optimization_barrier(values)


class Ring:
    def __init__(self, x, axis, size):
        self.axis, self.size = axis, size
        order = list(range(0, size, 2)) + list(range(size - 1, 0, -2))
        self.forward = [(order[i], order[(i + 1) % size]) for i in range(size)]
        self.backward = [(order[(i + 1) % size], order[i]) for i in range(size)]
        self.ahead, self.behind = [x], [x]

    def send(self):
        moved = [lax.ppermute(self.ahead[-1], self.axis, self.forward)]
        if len(self.behind) <= (self.size - 1) // 2:
            moved.append(lax.ppermute(self.behind[-1], self.axis, self.backward))
        return moved

    def receive(self, moved):
        self.ahead.append(moved[0])
        self.behind.extend(moved[1:])

    @property
    def steps(self):
        return len(self.ahead) - 1

    def owners(self, ahead, behind):
        size = self.size
        me = lax.axis_index(self.axis)
        here = jnp.where(me % 2 == 0, me // 2, size - 1 - me // 2)
        distances = [-s for s in range(ahead)] + list(range(1, behind))
        at = (here + size + jnp.array(distances, jnp.int32)) % size
        return jnp.where(at < size // 2, 2 * at, 2 * (size - 1 - at) + 1)


def step_all(rings, *beside):
    moved, beside = together([ring.send() for ring in rings], beside)
    for ring, blocks in zip(rings, moved):
        ring.receive(blocks)
    return beside


def halve_stem(recv, keep, group):
    mine = lax.axis_index("group") // 2 * 2 + lax.axis_index("dp") % 2
    return combine_call(mine.reshape(1), [[keep], recv], [F32] * (group // 2 * 2))


def sum_stem(parts, beside, after, last, dp, group):
    core = lax.axis_index("group") % 2
    far = lax.axis_index("group") // 2
    low = lax.axis_index("dp") % 2
    high = lax.axis_index("dp") // 2
    fars, highs = group // 2, dp // 2
    mine = far * 2 + low
    small, width = parts[0].shape
    rows = 2 * fars * small

    def hop(block, f, b):
        if f:
            pairs = [
                (d * group + g, (d ^ b) * group + (g ^ (2 * f))) for d in range(dp) for g in range(group)
            ]
            return lax.ppermute(block, ("dp", "group"), pairs)
        return swap(block, "dp", dp, b)

    hops = [(k // 2, k % 2) for k in range(1, 2 * fars)]
    arrived = [hop(part, f, b) for part, (f, b) in zip(parts[1:], hops)]
    arrived, beside = together(arrived, beside)
    beside = after[0](*beside)
    total = parts[0]
    for part in arrived:
        total = total + part
    cols = width // highs
    part = lax.dynamic_slice_in_dim(total, high * cols, cols, 1)
    away = [lax.dynamic_slice_in_dim(total, (high ^ j) * cols, cols, 1) for j in range(1, highs)]
    arrived = [swap(a, "dp", dp, 2 * (j + 1)) for j, a in enumerate(away)]
    arrived, beside = together(arrived, beside)
    for block in arrived:
        part = part + block
    part = part.astype(BF16)
    line = jnp.zeros((small, width), BF16)
    line = lax.dynamic_update_slice_in_dim(line, part, high * cols, 1)
    arrived = [swap(part, "dp", dp, 2 * j) for j in range(1, highs)]
    arrived, beside = together(arrived, after[1](*beside))
    for j, block in enumerate(arrived):
        line = lax.dynamic_update_slice_in_dim(line, block, (high ^ (j + 1)) * cols, 1)
    block = jnp.zeros((rows, width), BF16)
    block = lax.dynamic_update_slice_in_dim(block, line, mine * small, 0)
    arrived, beside = together([hop(line, f, b) for f, b in hops], last(*beside))
    for (f, b), piece in zip(hops, arrived):
        target = (far ^ f) * 2 + (low ^ b)
        block = lax.dynamic_update_slice_in_dim(block, piece, target * small, 0)
    partner = swap(block, "group", group, 1)
    first = jnp.where(core == 0, block, partner)
    second = jnp.where(core == 0, partner, block)
    return jnp.concatenate([first, second], axis=0).astype(F32), beside


def encoding_tables(patch_count):
    quarter = D // 4
    half_width = D // 2
    power = lambda n: np.power(np.float32(10000.0), -np.arange(n, dtype=np.float32) / np.float32(n))
    at = np.arange(GRID).astype(np.float32)[:, None] * power(quarter)
    both = np.concatenate([np.sin(at), np.cos(at)], axis=-1)
    patch = np.arange(patch_count)
    rest = np.concatenate([both[patch // GRID], both[patch % GRID]], axis=-1).astype(np.float32)
    parts = []
    for _ in range(3):
        parts.append(rest.astype(ml_dtypes.bfloat16))
        rest = rest - parts[-1].astype(np.float32)
    group_at = np.arange(GROUPS).astype(np.float32)[:, None] * power(half_width)
    return np.stack(parts), np.concatenate([np.sin(group_at), np.cos(group_at)], axis=-1).astype(np.float32)


def on_device(dp, group, patches, vis_index, vis_count, w_stem, ln_gain, w_qkv, w_out, out_grad):
    scenes = patches.shape[0]
    tokens = scenes * TOK
    width = w_qkv.shape[2]
    fars = range(1, group // 2)
    rests = range(1, dp // 2)
    dp_low, dp_high = lax.axis_index("dp") % 2, lax.axis_index("dp") // 2
    low, high = dp_low.reshape(1), dp_high.reshape(1)
    core = (lax.axis_index("group") % 2).reshape(1)

    shard = pack_call(w_qkv, w_out)
    cross = lambda x, f: swap(x, "group", group, 2 * f)
    far_shards = [cross(shard, f) for f in fars]
    counts = vis_count.astype(jnp.int32).T
    counts_far = swap(counts, "group", group, 1)
    table, genc = encoding_tables(patches.shape[1])
    gain = ln_gain.reshape(1, D)
    stem = stem_call(
        counts,
        vis_index,
        patches,
        w_stem,
        gain,
        jnp.asarray(table),
        jnp.asarray(genc),
        out_grad.reshape(scenes, TOK, D),
    )
    stem, both_counts, far_shards = together(stem, jnp.stack([counts, counts_far]), far_shards)
    rings = [Ring(x, "dp", dp) for x in far_shards]
    ring = rings[0]
    owners = ring.owners(dp // 2 + 1, dp // 2)
    emb = stem[0].reshape(tokens, D)
    both = [stem[1].reshape(2, tokens, D)]
    cols = stem[2].reshape(tokens, stem[2].shape[2])
    both.append(swap(both[0], "group", group, 1))
    passed = []
    both, owners = step_all(rings, both, owners)
    while ring.steps < dp // 2:
        passed.append(cross(ring.ahead[-1], 1))
        if len(passed) > 1:
            (passed[-2],) = step_all(rings, passed[-2])
        else:
            step_all(rings)
    ring.ahead, ring.behind = together(ring.ahead, ring.behind)
    passed.append(cross(ring.ahead[-1], 1))
    passed.append(cross(jnp.concatenate(ring.behind[1:], axis=0), 1))

    packs, weights, crossing = [], [], []
    for f in list(fars) + [0]:
        if f:
            blocks = [(x, 0) for x in rings[f - 1].ahead + rings[f - 1].behind[1:]]
        else:
            blocks = [(x, 0) for x in [shard] + passed[:-1]] + [(passed[-1], b) for b in range(dp // 2 - 1)]
        made = attention_call(both_counts, owners, low, *both, None if f else (packs, weights), blocks, dp)
        if f == 1:
            made, passed[-3:] = together(made, passed[-3:])
        elif f:
            made = together(*made)
        else:
            made, arrived = together(made, [x[:3] for x in crossing])
        pack, weight, keep, other, back = made[0], made[1], made[2:4], made[4:6], made[6:]
        packs.append(pack)
        weights.append(weight)
        if f:
            crossing.append([cross(x, f) for x in (*other, *keep)])
    back_far = swap(back[1], "group", group, 1)
    coming = []
    for c in range(2):
        send = other[c]
        for x in arrived:
            send = send + x[c].astype(F32)
        coming.append(swap(send.astype(BF16), "dp", dp, 1))
    stem_made, coming[0], last_keeps = together(
        tail_call(core, back[0], back_far, emb, both[0], cols, gain), coming[0], [x[3] for x in crossing]
    )
    keeps = [[keep[0]] + [x[2] for x in arrived], [keep[1]] + list(last_keeps)]
    stem_keep, *stem_recv = stem_made
    stem_recv = [swap(x, "group", group, 1) for x in stem_recv]
    kinds = [F32 if j < 2 else BF16 for j in range(dp // 2)]
    second_leg = lambda c: combine_call(high, [[x] for x in keeps[c] + [coming[c]]], kinds)
    spread = lambda blocks, js: [swap(blocks[j], "dp", dp, 2 * j) for j in js]
    first = second_leg(0)
    stem_recv, share = together(stem_recv, first[0])
    first_rest = spread(first, rests[1:])
    stem_parts = halve_stem(stem_recv, stem_keep, group)
    _, coming[1], keeps[1] = together(stem_parts, coming[1], keeps[1])
    second = second_leg(1)
    near = dp // 2 * 3 // 4
    beside = [mixed_call(packs, weights), share, *first_rest, second[0]]
    def after_first(mixed, *arrived):
        return [swap(mixed, "group", group, 1), *arrived[:-1], *spread(first, [1]), arrived[-1]]

    def after_second(*arrived):
        return [*arrived, *spread(second, [1, *range(2, near)])]

    def last(mixed, *arrived):
        output = output_call(counts, mixed, emb, packs, weights)
        arrived = [*arrived, *spread(second, range(near, dp // 2))]
        half = len(arrived) // 2
        return output, *result_call(arrived[:half], arrived[half:])

    grad_w_stem, (output, grad_w_qkv, grad_w_out) = sum_stem(
        stem_parts, beside, (after_first, after_second), last, dp, group
    )
    return (output.reshape(scenes, GROUPS, CAP, D), grad_w_stem, grad_w_qkv, grad_w_out)


def solution(mesh):
    sizes = dict(mesh.shape)
    return jax.shard_map(
        functools.partial(on_device, sizes["dp"], sizes["group"]),
        mesh=mesh,
        in_specs=(
            P(("dp", "group"), None, None),
            P(("dp", "group"), None, None),
            P(("dp", "group"), None),
            P(),
            P(),
            P("dp", None, "group"),
            P("group", "dp"),
            P(("dp", "group"), None, None, None),
        ),
        out_specs=(
            P(("dp", "group"), None, None, None),
            P(),
            P("dp", None, "group"),
            P("group", "dp"),
        ),
        check_vma=False,
    )
```

```python
import functools

import jax
import jax.numpy as jnp
import ml_dtypes
import numpy as np
from jax import lax
from jax.experimental import pallas as pl
from jax.experimental.pallas import tpu as pltpu
from jax.sharding import PartitionSpec as P

D = 1024
HD = 64
GROUPS = 3
CAP = 48
GRID = 12
PIX = 64
TOK = GROUPS * CAP
PAIR = 128
GROUP_BANDS = ((0, 4), (4, 8), (8, 10))
NORM_EPS = 1e-06
F32 = jnp.float32
BF16 = jnp.bfloat16
VMEM_LIMIT = 60 * 1024 * 1024


def dot_nn(a, b):
    return lax.dot_general(a, b, (((1,), (0,)), ((), ())), preferred_element_type=F32)


def dot_nt(a, b):
    return lax.dot_general(a, b, (((1,), (1,)), ((), ())), preferred_element_type=F32)


def dot_tn(a, b):
    return lax.dot_general(a, b, (((0,), (0,)), ((), ())), preferred_element_type=F32)


def live_column(c0, c1, c2):
    row = lax.broadcasted_iota(jnp.int32, (TOK, 1), 0)
    return (
        (row < c0)
        | ((row >= CAP) & (row < CAP + c1))
        | ((row >= 2 * CAP) & (row < 2 * CAP + c2))
    )


def params():
    return pltpu.CompilerParams(vmem_limit_bytes=VMEM_LIMIT)


def cost(flops, nbytes):
    return pl.CostEstimate(flops=int(flops / 1000), bytes_accessed=int(nbytes / 1000), transcendentals=0)


def stem_kernel(
    cnt_ref, idx_ref, patch_ref, w_ref, gain_ref, parts, genc_ref, og_ref,
    emb_ref, rows_ref, cols_ref,
):
    step = pl.program_id(0)
    scenes = patch_ref.shape[0]
    patch_iota = lax.broadcasted_iota(jnp.int32, (parts.shape[1], CAP), 0)
    slot = lax.broadcasted_iota(jnp.int32, (CAP, 1), 0)
    for g, (start, end) in enumerate(GROUP_BANDS):
        rows = slice(g * CAP, (g + 1) * CAP)
        width = (end - start) * PIX
        picked, placed = [], []
        for s in range(scenes):
            onehot = (idx_ref[s, g : g + 1, :] == patch_iota).astype(F32).astype(BF16).T
            picked.append(dot_nn(onehot, patch_ref[s, :, start * PIX : end * PIX]).astype(BF16))
            placed.append(
                (dot_nn(onehot, parts[0]) + dot_nn(onehot, parts[1])) + dot_nn(onehot, parts[2])
            )
            live = slot < cnt_ref[g, step * scenes + s]
            rows_ref[1, s, rows, :] = jnp.where(live, og_ref[s, rows, :].astype(F32), 0.0).astype(BF16)
        summed = dot_nn(jnp.concatenate(picked, axis=0), w_ref[start * PIX : end * PIX, :])
        for s in range(scenes):
            values = summed[s * CAP : (s + 1) * CAP] + (placed[s] + genc_ref[g : g + 1, :])
            emb = values.astype(BF16)
            emb_ref[s, rows, :] = emb
            x = emb.astype(F32)
            centre = jnp.mean(x, axis=-1, keepdims=True)
            dev = x - centre
            spread = jnp.mean(dev * dev, axis=-1, keepdims=True)
            centred = dev * lax.rsqrt(spread + NORM_EPS)
            rows_ref[0, s, rows, :] = (centred * gain_ref[...]).astype(BF16)
            cols_ref[s, rows, :width] = picked[s]
            if width < cols_ref.shape[2]:
                cols_ref[s, rows, width:] = jnp.zeros((CAP, cols_ref.shape[2] - width), BF16)


def stem_call(counts, index, patches, w_stem, gain, table, genc, out_grad):
    scenes, patch_count, width = patches.shape
    block = 3 if scenes % 3 == 0 else 1
    col_width = max(e - s for s, e in GROUP_BANDS) * PIX
    per = lambda shape: pl.BlockSpec((block,) + shape, lambda i: (i, 0, 0))
    whole = lambda a: pl.BlockSpec(a.shape, lambda i: (0,) * a.ndim)
    return pl.pallas_call(
        stem_kernel,
        grid=(scenes // block,),
        in_specs=[
            pl.BlockSpec(memory_space=pltpu.SMEM),
            per((GROUPS, CAP)),
            per((patch_count, width)),
            whole(w_stem),
            whole(gain),
            whole(table),
            whole(genc),
            per((TOK, D)),
        ],
        out_specs=[
            per((TOK, D)),
            pl.BlockSpec((2, block, TOK, D), lambda i: (0, i, 0, 0)),
            per((TOK, col_width)),
        ],
        out_shape=[
            jax.ShapeDtypeStruct((scenes, TOK, D), BF16),
            jax.ShapeDtypeStruct((2, scenes, TOK, D), BF16),
            jax.ShapeDtypeStruct((scenes, TOK, col_width), BF16),
        ],
        compiler_params=params(),
        cost_estimate=cost(8e9, 12e6),
        name="stem_norm",
    )(counts, index, patches, w_stem, gain, table, genc, out_grad)


def pack_kernel(qkv_ref, out_w_ref, pack_ref):
    count, _, width = qkv_ref.shape
    for c in range(count):
        pack_ref[:, c * width : (c + 1) * width] = qkv_ref[c]
    pack_ref[:, count * width :] = out_w_ref[...].T


def pack_call(w_qkv, w_out):
    parts = jnp.transpose(w_qkv, (1, 0, 2))
    return pl.pallas_call(
        pack_kernel,
        out_shape=jax.ShapeDtypeStruct((w_qkv.shape[0], 3 * w_qkv.shape[2] + w_out.shape[0]), BF16),
        compiler_params=params(),
        cost_estimate=cost(1e6, 5e5),
        name="pack_weights",
    )(parts, w_out)


def attention_kernel(
    packs, blocks, dp, cnt_ref, owner_ref, low_ref, na_ref, nb_ref, ga_ref, gb_ref, *refs
):
    earlier, refs = refs[: 2 * (packs or 0)], refs[2 * (packs or 0) :]
    blocks, refs = refs[:blocks], refs[blocks:]
    out_ref, w_ref, *refs = refs
    keeps, others, refs = refs[:2], refs[2:4], refs[4:]
    n_s, g_s, qkv, total = refs[-4:]
    half, step = pl.program_id(0), pl.program_id(1)
    rows = n_s.shape[0]
    scenes = rows // TOK
    width = w_ref.shape[1] // 4

    @pl.when((half == 0) & (step == 0))
    def _():
        size = blocks[0].shape[0]
        for b, block in enumerate(blocks):
            w_ref[pl.ds(pl.multiple_of(owner_ref[b] * size, size), size), :] = block[...]
        total[...] = jnp.zeros_like(total)

    @pl.when(half == 0)
    def _():
        n_s[...] = na_ref[0]
        g_s[...] = ga_ref[0]

    @pl.when(half != 0)
    def _():
        n_s[...] = nb_ref[0]
        g_s[...] = gb_ref[0]

    qkv[:, : 3 * width] = dot_nn(n_s[...], w_ref[:, : 3 * width]).astype(BF16)
    qkv[:, 3 * width :] = dot_nn(g_s[...], w_ref[:, 3 * width :]).astype(BF16)
    heads = width // HD
    lane = lax.broadcasted_iota(jnp.int32, (1, width), 1)
    masks = [(lane // HD == h).astype(F32).astype(BF16) for h in range(heads)]
    scale = jnp.asarray(HD ** (-0.5), BF16)
    first_of_pair = lax.broadcasted_iota(jnp.int32, (1, PAIR), 1) < HD

    def own_lanes(tall):
        tiles = []
        for t in range(width // PAIR):
            at = slice(t * PAIR, (t + 1) * PAIR)
            one = tall[2 * t * TOK : (2 * t + 1) * TOK, at]
            two = tall[(2 * t + 1) * TOK : (2 * t + 2) * TOK, at]
            tiles.append(jnp.where(first_of_pair, one, two))
        return jnp.concatenate(tiles, axis=1)

    def scene_body(s, _):
        base = pl.multiple_of(s * TOK, 16)
        at = pl.ds(base, TOK)
        scene = step * scenes + s
        live = live_column(*[cnt_ref[half, g, scene] for g in range(GROUPS)])
        bias = jnp.where(live, 0.0, -1e30)
        q, k, v, dc = [qkv[at, c * width : (c + 1) * width] for c in range(4)]
        tall_q = jnp.concatenate([q * (m * scale) for m in masks], axis=0)
        tall_dc = jnp.concatenate([dc * m for m in masks], axis=0)
        scores = dot_nt(k, tall_q)
        grad_probs = dot_nt(v, tall_dc)
        probs_parts, score_parts = [], []
        for start in range(0, heads * TOK, PAIR):
            cols = slice(start, min(start + PAIR, heads * TOK))
            part = scores[:, cols] + bias
            lifted = jnp.exp(part - jnp.max(part, axis=0, keepdims=True))
            probs = lifted * (1.0 / jnp.sum(lifted, axis=0, keepdims=True))
            weighted = probs * grad_probs[:, cols]
            inner = jnp.sum(weighted, axis=0, keepdims=True)
            probs_parts.append(probs.astype(BF16))
            score_parts.append((weighted - probs * inner).astype(BF16))
        half_probs = jnp.concatenate(probs_parts, axis=1)
        grad_score = jnp.concatenate(score_parts, axis=1)
        out_ref[at, :width] = (own_lanes(dot_tn(grad_score, k)) * HD ** (-0.5)).astype(BF16)
        out_ref[at, width : 2 * width] = dot_nn(grad_score, tall_q).astype(BF16)
        out_ref[at, 2 * width : 3 * width] = dot_nn(half_probs, tall_dc).astype(BF16)
        out_ref[at, 3 * width :] = own_lanes(dot_tn(half_probs, v)).astype(BF16)
        return 0

    lax.fori_loop(0, scenes, scene_body, 0, unroll=True)
    total[:, : 3 * width] += dot_tn(n_s[...], out_ref[:, : 3 * width])
    total[:, 3 * width :] += dot_tn(g_s[...], out_ref[:, 3 * width :])

    @pl.when((half == pl.num_programs(0) - 1) & (step == pl.num_programs(1) - 1))
    def _():
        size = total.shape[0] // dp
        low = low_ref[0]
        for b in range(dp // 2):
            at = slice(b * size, (b + 1) * size)
            mine = pl.multiple_of((2 * b + low) * size, size)
            other = pl.multiple_of((2 * b + 1 - low) * size, size)
            for c in range(2):
                cols = slice(c * 2 * width, (c + 1) * 2 * width)
                keeps[c][at, :] = total[pl.ds(mine, size), cols].astype(keeps[c].dtype)
                others[c][at, :] = total[pl.ds(other, size), cols].astype(others[c].dtype)

    if packs is not None:
        back = dot_nt(out_ref[:, : 3 * width], w_ref[:, : 3 * width])
        for pack_ref, weight_ref in zip(earlier[:packs], earlier[packs:]):
            back = back + dot_nt(pack_ref[...], weight_ref[...])

        @pl.when(half == 0)
        def _():
            refs[0][...] = back

        @pl.when(half != 0)
        def _():
            refs[1][...] = back.astype(BF16)


def block_rows(tokens):
    return 3 * TOK if tokens % (3 * TOK) == 0 else TOK


def two_halves(rows, steps, lead):
    shape = (1,) * len(lead) + (rows, D)
    first = pl.BlockSpec(shape, lambda h, i: lead + (jnp.where(h == 0, i, steps - 1), 0))
    second = pl.BlockSpec(shape, lambda h, i: lead + (jnp.where(h == 0, 0, i), 0))
    return [first, second]


SCALARS = pl.BlockSpec(memory_space=pltpu.SMEM)


def attention_call(counts, owners, low, own, far, earlier, blocks, dp):
    tokens = own.shape[1]
    rows = block_rows(tokens)
    steps = tokens // rows
    cols = blocks[0][0].shape[1]
    whole = lambda shape: pl.BlockSpec(shape, lambda h, i: (0, 0))
    at = lambda h, i: (h * steps + i, 0)
    packs = None if earlier is None else len(earlier[0])
    back = [] if earlier is None else two_halves(rows, steps, ())
    kind = BF16 if earlier is None else F32
    grads = [jax.ShapeDtypeStruct((D // 2, c), kind) for c in [cols // 2] * 4]
    return pl.pallas_call(
        functools.partial(attention_kernel, packs, len(blocks), dp),
        grid=(2, steps),
        in_specs=[SCALARS] * 3
        + two_halves(rows, steps, (0,))
        + two_halves(rows, steps, (1,))
        + [pl.BlockSpec((rows, cols // 4 * 3), at)] * (packs or 0)
        + [whole((D, cols // 4 * 3))] * (packs or 0)
        + [pl.BlockSpec((D // dp, cols), functools.partial(lambda at, h, i: (at, 0), at)) for _, at in blocks],
        out_specs=[pl.BlockSpec((rows, cols), at), whole((D, cols))] + [whole(g.shape) for g in grads] + back,
        out_shape=[
            jax.ShapeDtypeStruct((2 * tokens, cols), BF16),
            jax.ShapeDtypeStruct((D, cols), BF16),
            *grads,
        ]
        + [jax.ShapeDtypeStruct((tokens, D), kind) for kind in (F32, BF16)[: len(back)]],
        scratch_shapes=[
            pltpu.VMEM((rows, D), BF16),
            pltpu.VMEM((rows, D), BF16),
            pltpu.VMEM((rows, cols), BF16),
            pltpu.VMEM((D, cols), F32),
        ],
        compiler_params=params(),
        cost_estimate=cost(20e9, 14e6),
        name="attention",
    )(counts, owners, low, own, far, own, far, *[x for group in earlier or () for x in group], *[b for b, _ in blocks])


def combine_kernel(counts, place_ref, *refs):
    ins, refs = refs[: sum(counts)], refs[sum(counts) :]
    rows = refs[0].shape[0]
    place = place_ref[0]
    for j, ref in enumerate(refs):
        at = pl.ds(pl.multiple_of((place ^ j) * rows, rows), rows)
        total = None
        first = 0
        for count in counts:
            pieces = [r[at, :].astype(F32) for r in ins[first : first + count]]
            new = pieces[0] if count == 1 else jnp.concatenate(pieces, axis=1)
            total = new if total is None else total + new
            first += count
        ref[...] = total.astype(ref.dtype)


def combine_call(place, parts, dtypes):
    ins = [piece for part in parts for piece in part]
    rows, cols = ins[0].shape[0] // len(dtypes), sum(piece.shape[1] for piece in parts[0])
    whole = lambda a: pl.BlockSpec(a.shape, lambda: (0, 0))
    return pl.pallas_call(
        functools.partial(combine_kernel, [len(part) for part in parts]),
        in_specs=[SCALARS] + [whole(a) for a in ins],
        out_specs=[pl.BlockSpec((rows, cols), lambda: (0, 0))] * len(dtypes),
        out_shape=[jax.ShapeDtypeStruct((rows, cols), d) for d in dtypes],
        compiler_params=params(),
        cost_estimate=cost(1e6, 5e6),
        name="combine",
    )(place, *ins)


def split_kernel(count, place_ref, *refs):
    total = refs[0][...]
    for ref in refs[1:count]:
        total = total + ref[...]
    outs = refs[count:]
    cols = outs[0].shape[1]
    place = place_ref[0]
    for j, out_ref in enumerate(outs):
        block = total[:, :cols]
        for b in range(1, len(outs)):
            block = jnp.where((place ^ j) == b, total[:, b * cols : (b + 1) * cols], block)
        out_ref[...] = block


def split_call(place, parts, blocks):
    rows, cols = parts[0].shape
    return pl.pallas_call(
        functools.partial(split_kernel, len(parts)),
        in_specs=[SCALARS] + [pl.BlockSpec((rows, cols), lambda: (0, 0))] * len(parts),
        out_specs=[pl.BlockSpec((rows, cols // blocks), lambda: (0, 0))] * blocks,
        out_shape=[jax.ShapeDtypeStruct((rows, cols // blocks), F32)] * blocks,
        compiler_params=params(),
        cost_estimate=cost(1e6, 2e6),
        name="split_sum",
    )(place, *parts)


def result_kernel(count, *refs):
    halves, qkv_ref, out_ref = (refs[:count], refs[count:-2]), refs[-2], refs[-1]
    first, second = [functools.reduce(lambda a, b: a + b, [r[...].astype(F32) for r in half]) for half in halves]
    width = first.shape[1] // 2
    qkv_ref[0] = first[:, :width]
    qkv_ref[1] = first[:, width:]
    qkv_ref[2] = second[:, :width]
    out_ref[...] = second[:, width:].T


def result_call(first, second):
    rows, cols = first[0].shape
    qkv, out = pl.pallas_call(
        functools.partial(result_kernel, len(first)),
        out_shape=[
            jax.ShapeDtypeStruct((3, rows, cols // 2), F32),
            jax.ShapeDtypeStruct((cols // 2, rows), F32),
        ],
        compiler_params=params(),
        cost_estimate=cost(1e6, 2e6),
        name="weight_results",
    )(*first, *second)
    return jnp.transpose(qkv, (1, 0, 2)), out


def mixed_product(context_refs, weight_refs):
    total = None
    for context_ref, w_ref in zip(context_refs, weight_refs):
        new = dot_nt(context_ref[...], w_ref[...])
        total = new if total is None else total + new
    return total


def context_specs(rows, packs, weights, first):
    width = packs[0].shape[1] // 4
    return [pl.BlockSpec((rows, width), lambda i: (first + i, 3))] * len(packs) + [
        pl.BlockSpec((D, width), lambda i: (0, 3))
    ] * len(weights)


def mixed_kernel(count, *refs):
    refs[-1][...] = mixed_product(refs[:count], refs[count : 2 * count]).astype(BF16)


def mixed_call(packs, weights):
    tokens = packs[0].shape[0] // 2
    rows = block_rows(tokens)
    return pl.pallas_call(
        functools.partial(mixed_kernel, len(packs)),
        grid=(tokens // rows,),
        in_specs=context_specs(rows, packs, weights, tokens // rows),
        out_specs=pl.BlockSpec((rows, D), lambda i: (i, 0)),
        out_shape=jax.ShapeDtypeStruct((tokens, D), BF16),
        compiler_params=params(),
        cost_estimate=cost(2e9, 5e6),
        name="mixed",
    )(*packs, *weights)


def tail_kernel(core_ref, own_ref, recv_ref, emb_ref, gl_ref, cols_ref, gain_ref, keep_ref, first_ref, second_ref, acc):
    step = pl.program_id(0)
    rows = emb_ref.shape[0]
    scenes = rows // TOK

    @pl.when(step == 0)
    def _():
        acc[...] = jnp.zeros_like(acc)

    grad_normed = own_ref[...] + recv_ref[...].astype(F32)
    x = emb_ref[...].astype(F32)
    dev = x - jnp.mean(x, axis=-1, keepdims=True)
    inv_std = lax.rsqrt(jnp.mean(dev * dev, axis=-1, keepdims=True) + NORM_EPS)
    centred = dev * inv_std
    scaled = grad_normed * gain_ref[...]
    first_mean = jnp.mean(scaled, axis=-1, keepdims=True)
    second_mean = jnp.mean(scaled * centred, axis=-1, keepdims=True)
    back = inv_std * (scaled - first_mean - centred * second_mean)
    grad_in = (gl_ref[0].astype(F32) + back).astype(BF16)
    for g, (start, end) in enumerate(GROUP_BANDS):
        at = [slice(s * TOK + g * CAP, s * TOK + (g + 1) * CAP) for s in range(scenes)]
        columns = jnp.concatenate([cols_ref[a, : (end - start) * PIX] for a in at], axis=0)
        grads = jnp.concatenate([grad_in[a] for a in at], axis=0)
        acc[start * PIX : end * PIX, :] += dot_tn(columns, grads)

    @pl.when(step == pl.num_programs(0) - 1)
    def _():
        size = keep_ref.shape[0]
        core = core_ref[0]
        keep_ref[...] = acc[pl.ds(pl.multiple_of(core * size, size), size), :]
        other = pl.ds(pl.multiple_of((1 - core) * size, size), size)
        first_ref[...] = acc[other, : D // 2]
        second_ref[...] = acc[other, D // 2 :]


def tail_call(core, own, recv, emb, rows_own, cols, gain):
    tokens = emb.shape[0]
    rows = 2 * TOK if tokens % (2 * TOK) == 0 else TOK
    per = lambda a: pl.BlockSpec((rows, a.shape[1]), lambda i: (i, 0))
    stem_rows = GROUP_BANDS[-1][1] * PIX
    keep = jax.ShapeDtypeStruct((stem_rows // 2, D), F32)
    send = jax.ShapeDtypeStruct((stem_rows // 2, D // 2), F32)
    return pl.pallas_call(
        tail_kernel,
        grid=(tokens // rows,),
        in_specs=[SCALARS, per(own), per(recv), per(emb), pl.BlockSpec((1, rows, D), lambda i: (1, i, 0)), per(cols)]
        + [pl.BlockSpec(gain.shape, lambda i: (0, 0))],
        out_specs=[pl.BlockSpec(a.shape, lambda i: (0, 0)) for a in (keep, send, send)],
        out_shape=[keep, send, send],
        scratch_shapes=[pltpu.VMEM((stem_rows, D), F32)],
        compiler_params=params(),
        cost_estimate=cost(10e9, 12e6),
        name="tail",
    )(core, own, recv, emb, rows_own, cols, gain)


def output_kernel(count, cnt_ref, recv_ref, emb_ref, *refs):
    out_ref = refs[-1]
    step = pl.program_id(0)
    scenes = emb_ref.shape[0] // TOK
    mixed = recv_ref[...].astype(F32) + mixed_product(refs[:count], refs[count : 2 * count])
    total = emb_ref[...].astype(F32) + mixed
    for s in range(scenes):
        scene = step * scenes + s
        live = live_column(*[cnt_ref[g, scene] for g in range(GROUPS)])
        at = slice(s * TOK, (s + 1) * TOK)
        out_ref[at, :] = jnp.where(live, total[at], 0.0).astype(BF16)


def output_call(counts, recv, emb, packs, weights):
    tokens = emb.shape[0]
    rows = 2 * TOK if tokens % (2 * TOK) == 0 else TOK
    per = lambda a: pl.BlockSpec((rows, a.shape[1]), lambda i: (i, 0))
    return pl.pallas_call(
        functools.partial(output_kernel, len(packs)),
        grid=(tokens // rows,),
        in_specs=[SCALARS, per(recv), per(emb)]
        + context_specs(rows, packs, weights, 0),
        out_specs=per(emb),
        out_shape=jax.ShapeDtypeStruct(emb.shape, BF16),
        compiler_params=params(),
        cost_estimate=cost(5e9, 10e6),
        name="layer_output",
    )(counts, recv, emb, *packs, *weights)


def swap(x, axis, size, bit):
    return lax.ppermute(x, axis, [(i, i ^ bit) for i in range(size)])


def together(*values):
    return lax.optimization_barrier(values)


class Ring:
    def __init__(self, x, axis, size):
        self.axis, self.size = axis, size
        order = list(range(0, size, 2)) + list(range(size - 1, 0, -2))
        self.forward = [(order[i], order[(i + 1) % size]) for i in range(size)]
        self.backward = [(order[(i + 1) % size], order[i]) for i in range(size)]
        self.ahead, self.behind = [x], [x]

    def send(self):
        moved = [lax.ppermute(self.ahead[-1], self.axis, self.forward)]
        if len(self.behind) <= (self.size - 1) // 2:
            moved.append(lax.ppermute(self.behind[-1], self.axis, self.backward))
        return moved

    def receive(self, moved):
        self.ahead.append(moved[0])
        self.behind.extend(moved[1:])

    @property
    def steps(self):
        return len(self.ahead) - 1

    def owners(self, ahead, behind):
        size = self.size
        me = lax.axis_index(self.axis)
        here = jnp.where(me % 2 == 0, me // 2, size - 1 - me // 2)
        distances = [-s for s in range(ahead)] + list(range(1, behind))
        at = (here + size + jnp.array(distances, jnp.int32)) % size
        return jnp.where(at < size // 2, 2 * at, 2 * (size - 1 - at) + 1)


def step_all(rings, *beside):
    moved, beside = together([ring.send() for ring in rings], beside)
    for ring, blocks in zip(rings, moved):
        ring.receive(blocks)
    return beside


def halve_stem(recv, keep, group):
    mine = lax.axis_index("group") // 2 * 2 + lax.axis_index("dp") % 2
    return combine_call(mine.reshape(1), [[keep], recv], [F32] * (group // 2 * 2))


def sum_stem(parts, beside, after, last, dp, group):
    core = lax.axis_index("group") % 2
    far = lax.axis_index("group") // 2
    low = lax.axis_index("dp") % 2
    high = lax.axis_index("dp") // 2
    fars, highs = group // 2, dp // 2
    mine = far * 2 + low
    small, width = parts[0].shape
    rows = 2 * fars * small

    def hop(block, f, b):
        if f:
            pairs = [
                (d * group + g, (d ^ b) * group + (g ^ (2 * f))) for d in range(dp) for g in range(group)
            ]
            return lax.ppermute(block, ("dp", "group"), pairs)
        return swap(block, "dp", dp, b)

    hops = [(k // 2, k % 2) for k in range(1, 2 * fars)]
    arrived = [hop(part, f, b) for part, (f, b) in zip(parts[1:], hops)]
    arrived, beside = together(arrived, beside)
    beside = after[0](*beside)
    cols = width // highs
    part, *away = split_call(high.reshape(1), [parts[0], *arrived], highs)
    arrived = [swap(a, "dp", dp, 2 * (j + 1)) for j, a in enumerate(away)]
    arrived, beside = together(arrived, beside)
    for block in arrived:
        part = part + block
    part = part.astype(BF16)
    line = jnp.zeros((small, width), BF16)
    line = lax.dynamic_update_slice_in_dim(line, part, high * cols, 1)
    arrived = [swap(part, "dp", dp, 2 * j) for j in range(1, highs)]
    arrived, beside = together(arrived, after[1](*beside))
    for j, block in enumerate(arrived):
        line = lax.dynamic_update_slice_in_dim(line, block, (high ^ (j + 1)) * cols, 1)
    block = jnp.zeros((rows, width), BF16)
    block = lax.dynamic_update_slice_in_dim(block, line, mine * small, 0)
    arrived, beside = together([hop(line, f, b) for f, b in hops], last(*beside))
    for (f, b), piece in zip(hops, arrived):
        target = (far ^ f) * 2 + (low ^ b)
        block = lax.dynamic_update_slice_in_dim(block, piece, target * small, 0)
    partner = swap(block, "group", group, 1)
    first = jnp.where(core == 0, block, partner)
    second = jnp.where(core == 0, partner, block)
    return jnp.concatenate([first, second], axis=0).astype(F32), beside


def encoding_tables(patch_count):
    quarter = D // 4
    half_width = D // 2
    power = lambda n: np.power(np.float32(10000.0), -np.arange(n, dtype=np.float32) / np.float32(n))
    at = np.arange(GRID).astype(np.float32)[:, None] * power(quarter)
    both = np.concatenate([np.sin(at), np.cos(at)], axis=-1)
    patch = np.arange(patch_count)
    rest = np.concatenate([both[patch // GRID], both[patch % GRID]], axis=-1).astype(np.float32)
    parts = []
    for _ in range(3):
        parts.append(rest.astype(ml_dtypes.bfloat16))
        rest = rest - parts[-1].astype(np.float32)
    group_at = np.arange(GROUPS).astype(np.float32)[:, None] * power(half_width)
    return np.stack(parts), np.concatenate([np.sin(group_at), np.cos(group_at)], axis=-1).astype(np.float32)


def on_device(dp, group, patches, vis_index, vis_count, w_stem, ln_gain, w_qkv, w_out, out_grad):
    scenes = patches.shape[0]
    tokens = scenes * TOK
    width = w_qkv.shape[2]
    fars = range(1, group // 2)
    rests = range(1, dp // 2)
    dp_low, dp_high = lax.axis_index("dp") % 2, lax.axis_index("dp") // 2
    low, high = dp_low.reshape(1), dp_high.reshape(1)
    core = (lax.axis_index("group") % 2).reshape(1)

    shard = pack_call(w_qkv, w_out)
    cross = lambda x, f: swap(x, "group", group, 2 * f)
    far_shards = [cross(shard, f) for f in fars]
    counts = vis_count.astype(jnp.int32).T
    counts_far = swap(counts, "group", group, 1)
    table, genc = encoding_tables(patches.shape[1])
    gain = ln_gain.reshape(1, D)
    stem = stem_call(
        counts,
        vis_index,
        patches,
        w_stem,
        gain,
        jnp.asarray(table),
        jnp.asarray(genc),
        out_grad.reshape(scenes, TOK, D),
    )
    stem, both_counts, far_shards = together(stem, jnp.stack([counts, counts_far]), far_shards)
    rings = [Ring(x, "dp", dp) for x in far_shards]
    ring = rings[0]
    owners = ring.owners(dp // 2 + 1, dp // 2)
    emb = stem[0].reshape(tokens, D)
    both = [stem[1].reshape(2, tokens, D)]
    cols = stem[2].reshape(tokens, stem[2].shape[2])
    both.append(swap(both[0], "group", group, 1))
    passed = []
    both, owners = step_all(rings, both, owners)
    while ring.steps < dp // 2:
        passed.append(cross(ring.ahead[-1], 1))
        if len(passed) > 1:
            (passed[-2],) = step_all(rings, passed[-2])
        else:
            step_all(rings)
    ring.ahead, ring.behind = together(ring.ahead, ring.behind)
    passed.append(cross(ring.ahead[-1], 1))
    passed.append(cross(jnp.concatenate(ring.behind[1:], axis=0), 1))

    packs, weights, crossing = [], [], []
    for f in list(fars) + [0]:
        if f:
            blocks = [(x, 0) for x in rings[f - 1].ahead + rings[f - 1].behind[1:]]
        else:
            blocks = [(x, 0) for x in [shard] + passed[:-1]] + [(passed[-1], b) for b in range(dp // 2 - 1)]
        made = attention_call(both_counts, owners, low, *both, None if f else (packs, weights), blocks, dp)
        if f == 1:
            made, passed[-3:] = together(made, passed[-3:])
        elif f:
            made = together(*made)
        else:
            made, arrived = together(made, [x[:3] for x in crossing])
        pack, weight, keep, other, back = made[0], made[1], made[2:4], made[4:6], made[6:]
        packs.append(pack)
        weights.append(weight)
        if f:
            crossing.append([cross(x, f) for x in (*other, *keep)])
    back_far = swap(back[1], "group", group, 1)
    coming = []
    for c in range(2):
        send = other[c]
        for x in arrived:
            send = send + x[c].astype(F32)
        coming.append(swap(send.astype(BF16), "dp", dp, 1))
    stem_made, coming[0], last_keeps = together(
        tail_call(core, back[0], back_far, emb, both[0], cols, gain), coming[0], [x[3] for x in crossing]
    )
    stem_keep, *stem_recv = stem_made
    stem_recv = [swap(x, "group", group, 1) for x in stem_recv]
    kinds = [F32 if j < 2 else BF16 for j in range(dp // 2)]
    second_leg = lambda c: combine_call(high, [[x] for x in keeps[c] + [coming[c]]], kinds)
    spread = lambda blocks, js: [swap(blocks[j], "dp", dp, 2 * j) for j in js]
    stem_recv = together(*stem_recv)
    keeps = [[keep[0]] + [x[2] for x in arrived], [keep[1]] + list(last_keeps)]
    stem_parts = halve_stem(stem_recv, stem_keep, group)
    _, coming[0], keeps = together(stem_parts, coming[0], keeps)
    first = second_leg(0)
    first_rest = spread(first, rests[1:])
    second = second_leg(1)
    near = dp // 2 * 3 // 4
    beside = [mixed_call(packs, weights), first[0], *first_rest, second[0]]
    def after_first(mixed, *arrived):
        output = output_call(counts, swap(mixed, "group", group, 1), emb, packs, weights)
        return [output, *arrived[:-1], *spread(first, [1]), arrived[-1]]

    def after_second(*arrived):
        return [*arrived, *spread(second, [1, *range(2, near)])]

    def last(output, *arrived):
        arrived = [*arrived, *spread(second, range(near, dp // 2))]
        half = len(arrived) // 2
        return output, *result_call(arrived[:half], arrived[half:])

    grad_w_stem, (output, grad_w_qkv, grad_w_out) = sum_stem(
        stem_parts, beside, (after_first, after_second), last, dp, group
    )
    return (output.reshape(scenes, GROUPS, CAP, D), grad_w_stem, grad_w_qkv, grad_w_out)


def solution(mesh):
    sizes = dict(mesh.shape)
    return jax.shard_map(
        functools.partial(on_device, sizes["dp"], sizes["group"]),
        mesh=mesh,
        in_specs=(
            P(("dp", "group"), None, None),
            P(("dp", "group"), None, None),
            P(("dp", "group"), None),
            P(),
            P(),
            P("dp", None, "group"),
            P("group", "dp"),
            P(("dp", "group"), None, None, None),
        ),
        out_specs=(
            P(("dp", "group"), None, None, None),
            P(),
            P("dp", None, "group"),
            P("group", "dp"),
        ),
        check_vma=False,
    )
```

```python
import functools

import jax
import jax.numpy as jnp
import ml_dtypes
import numpy as np
from jax import lax
from jax.experimental import pallas as pl
from jax.experimental.pallas import tpu as pltpu
from jax.sharding import PartitionSpec as P

D = 1024
HD = 64
GROUPS = 3
CAP = 48
GRID = 12
PIX = 64
TOK = GROUPS * CAP
PAIR = 128
GROUP_BANDS = ((0, 4), (4, 8), (8, 10))
NORM_EPS = 1e-06
F32 = jnp.float32
BF16 = jnp.bfloat16
VMEM_LIMIT = 60 * 1024 * 1024


def dot_nn(a, b):
    return lax.dot_general(a, b, (((1,), (0,)), ((), ())), preferred_element_type=F32)


def dot_nt(a, b):
    return lax.dot_general(a, b, (((1,), (1,)), ((), ())), preferred_element_type=F32)


def dot_tn(a, b):
    return lax.dot_general(a, b, (((0,), (0,)), ((), ())), preferred_element_type=F32)


def live_column(c0, c1, c2):
    row = lax.broadcasted_iota(jnp.int32, (TOK, 1), 0)
    return (
        (row < c0)
        | ((row >= CAP) & (row < CAP + c1))
        | ((row >= 2 * CAP) & (row < 2 * CAP + c2))
    )


def params():
    return pltpu.CompilerParams(vmem_limit_bytes=VMEM_LIMIT)


def cost(flops, nbytes):
    return pl.CostEstimate(flops=int(flops / 1000), bytes_accessed=int(nbytes / 1000), transcendentals=0)


def stem_kernel(
    cnt_ref, idx_ref, patch_ref, w_ref, gain_ref, parts, genc_ref, og_ref,
    emb_ref, rows_ref, cols_ref,
):
    step = pl.program_id(0)
    scenes = patch_ref.shape[0]
    patch_iota = lax.broadcasted_iota(jnp.int32, (parts.shape[1], CAP), 0)
    slot = lax.broadcasted_iota(jnp.int32, (CAP, 1), 0)
    for g, (start, end) in enumerate(GROUP_BANDS):
        rows = slice(g * CAP, (g + 1) * CAP)
        width = (end - start) * PIX
        picked, placed = [], []
        for s in range(scenes):
            onehot = (idx_ref[s, g : g + 1, :] == patch_iota).astype(F32).astype(BF16).T
            picked.append(dot_nn(onehot, patch_ref[s, :, start * PIX : end * PIX]).astype(BF16))
            placed.append(
                (dot_nn(onehot, parts[0]) + dot_nn(onehot, parts[1])) + dot_nn(onehot, parts[2])
            )
            live = slot < cnt_ref[g, step * scenes + s]
            rows_ref[1, s, rows, :] = jnp.where(live, og_ref[s, rows, :].astype(F32), 0.0).astype(BF16)
        summed = dot_nn(jnp.concatenate(picked, axis=0), w_ref[start * PIX : end * PIX, :])
        for s in range(scenes):
            values = summed[s * CAP : (s + 1) * CAP] + (placed[s] + genc_ref[g : g + 1, :])
            emb = values.astype(BF16)
            emb_ref[s, rows, :] = emb
            x = emb.astype(F32)
            centre = jnp.mean(x, axis=-1, keepdims=True)
            dev = x - centre
            spread = jnp.mean(dev * dev, axis=-1, keepdims=True)
            centred = dev * lax.rsqrt(spread + NORM_EPS)
            rows_ref[0, s, rows, :] = (centred * gain_ref[...]).astype(BF16)
            cols_ref[s, rows, :width] = picked[s]
            if width < cols_ref.shape[2]:
                cols_ref[s, rows, width:] = jnp.zeros((CAP, cols_ref.shape[2] - width), BF16)


def stem_call(counts, index, patches, w_stem, gain, table, genc, out_grad):
    scenes, patch_count, width = patches.shape
    block = 3 if scenes % 3 == 0 else 1
    col_width = max(e - s for s, e in GROUP_BANDS) * PIX
    per = lambda shape: pl.BlockSpec((block,) + shape, lambda i: (i, 0, 0))
    whole = lambda a: pl.BlockSpec(a.shape, lambda i: (0,) * a.ndim)
    return pl.pallas_call(
        stem_kernel,
        grid=(scenes // block,),
        in_specs=[
            pl.BlockSpec(memory_space=pltpu.SMEM),
            per((GROUPS, CAP)),
            per((patch_count, width)),
            whole(w_stem),
            whole(gain),
            whole(table),
            whole(genc),
            per((TOK, D)),
        ],
        out_specs=[
            per((TOK, D)),
            pl.BlockSpec((2, block, TOK, D), lambda i: (0, i, 0, 0)),
            per((TOK, col_width)),
        ],
        out_shape=[
            jax.ShapeDtypeStruct((scenes, TOK, D), BF16),
            jax.ShapeDtypeStruct((2, scenes, TOK, D), BF16),
            jax.ShapeDtypeStruct((scenes, TOK, col_width), BF16),
        ],
        compiler_params=params(),
        cost_estimate=cost(8e9, 12e6),
        name="stem_norm",
    )(counts, index, patches, w_stem, gain, table, genc, out_grad)


def pack_kernel(qkv_ref, out_w_ref, pack_ref):
    count, _, width = qkv_ref.shape
    for c in range(count):
        pack_ref[:, c * width : (c + 1) * width] = qkv_ref[c]
    pack_ref[:, count * width :] = out_w_ref[...].T


def pack_call(w_qkv, w_out):
    parts = jnp.transpose(w_qkv, (1, 0, 2))
    return pl.pallas_call(
        pack_kernel,
        out_shape=jax.ShapeDtypeStruct((w_qkv.shape[0], 3 * w_qkv.shape[2] + w_out.shape[0]), BF16),
        compiler_params=params(),
        cost_estimate=cost(1e6, 5e5),
        name="pack_weights",
    )(parts, w_out)


def attention_kernel(
    packs, blocks, dp, cnt_ref, owner_ref, low_ref, na_ref, nb_ref, ga_ref, gb_ref, *refs
):
    earlier, refs = refs[: 2 * (packs or 0)], refs[2 * (packs or 0) :]
    blocks, refs = refs[:blocks], refs[blocks:]
    out_ref, w_ref, *refs = refs
    keeps, others, refs = refs[:2], refs[2:4], refs[4:]
    n_all, g_all, pack_all, qkv, total = refs[-5:]
    half, step = pl.program_id(0), pl.program_id(1)
    rows = qkv.shape[0]
    here = pl.ds(pl.multiple_of((half * pl.num_programs(1) + step) * rows, 16), rows)
    scenes = rows // TOK
    width = w_ref.shape[1] // 4

    @pl.when((half == 0) & (step == 0))
    def _():
        size = blocks[0].shape[0]
        for b, block in enumerate(blocks):
            w_ref[pl.ds(pl.multiple_of(owner_ref[b] * size, size), size), :] = block[...]

    @pl.when(half == 0)
    def _():
        n_all[here, :] = na_ref[0]
        g_all[here, :] = ga_ref[0]

    @pl.when(half != 0)
    def _():
        n_all[here, :] = nb_ref[0]
        g_all[here, :] = gb_ref[0]

    qkv[:, : 3 * width] = dot_nn(n_all[here, :], w_ref[:, : 3 * width]).astype(BF16)
    qkv[:, 3 * width :] = dot_nn(g_all[here, :], w_ref[:, 3 * width :]).astype(BF16)
    heads = width // HD
    lane = lax.broadcasted_iota(jnp.int32, (1, width), 1)
    masks = [(lane // HD == h).astype(F32).astype(BF16) for h in range(heads)]
    scale = jnp.asarray(HD ** (-0.5), BF16)
    first_of_pair = lax.broadcasted_iota(jnp.int32, (1, PAIR), 1) < HD

    def own_lanes(tall):
        tiles = []
        for t in range(width // PAIR):
            at = slice(t * PAIR, (t + 1) * PAIR)
            one = tall[2 * t * TOK : (2 * t + 1) * TOK, at]
            two = tall[(2 * t + 1) * TOK : (2 * t + 2) * TOK, at]
            tiles.append(jnp.where(first_of_pair, one, two))
        return jnp.concatenate(tiles, axis=1)

    def scene_body(s, _):
        base = pl.multiple_of(s * TOK, 16)
        at = pl.ds(base, TOK)
        scene = step * scenes + s
        live = live_column(*[cnt_ref[half, g, scene] for g in range(GROUPS)])
        bias = jnp.where(live, 0.0, -1e30)
        q, k, v, dc = [qkv[at, c * width : (c + 1) * width] for c in range(4)]
        tall_q = jnp.concatenate([q * (m * scale) for m in masks], axis=0)
        tall_dc = jnp.concatenate([dc * m for m in masks], axis=0)
        scores = dot_nt(k, tall_q)
        grad_probs = dot_nt(v, tall_dc)
        probs_parts, score_parts = [], []
        for start in range(0, heads * TOK, PAIR):
            cols = slice(start, min(start + PAIR, heads * TOK))
            part = scores[:, cols] + bias
            lifted = jnp.exp(part - jnp.max(part, axis=0, keepdims=True))
            probs = lifted * (1.0 / jnp.sum(lifted, axis=0, keepdims=True))
            weighted = probs * grad_probs[:, cols]
            inner = jnp.sum(weighted, axis=0, keepdims=True)
            probs_parts.append(probs.astype(BF16))
            score_parts.append((weighted - probs * inner).astype(BF16))
        half_probs = jnp.concatenate(probs_parts, axis=1)
        grad_score = jnp.concatenate(score_parts, axis=1)
        out_ref[at, :width] = (own_lanes(dot_tn(grad_score, k)) * HD ** (-0.5)).astype(BF16)
        out_ref[at, width : 2 * width] = dot_nn(grad_score, tall_q).astype(BF16)
        out_ref[at, 2 * width : 3 * width] = dot_nn(half_probs, tall_dc).astype(BF16)
        out_ref[at, 3 * width :] = own_lanes(dot_tn(half_probs, v)).astype(BF16)
        return 0

    lax.fori_loop(0, scenes, scene_body, 0, unroll=True)
    pack_all[here, :] = out_ref[...]

    @pl.when((half == pl.num_programs(0) - 1) & (step == pl.num_programs(1) - 1))
    def _():
        total[:, : 3 * width] = dot_tn(n_all[...], pack_all[:, : 3 * width])
        total[:, 3 * width :] = dot_tn(g_all[...], pack_all[:, 3 * width :])
        size = total.shape[0] // dp
        low = low_ref[0]
        for b in range(dp // 2):
            at = slice(b * size, (b + 1) * size)
            mine = pl.multiple_of((2 * b + low) * size, size)
            other = pl.multiple_of((2 * b + 1 - low) * size, size)
            for c in range(2):
                cols = slice(c * 2 * width, (c + 1) * 2 * width)
                keeps[c][at, :] = total[pl.ds(mine, size), cols].astype(keeps[c].dtype)
                others[c][at, :] = total[pl.ds(other, size), cols].astype(others[c].dtype)

    if packs is not None:
        back = dot_nt(out_ref[:, : 3 * width], w_ref[:, : 3 * width])
        for pack_ref, weight_ref in zip(earlier[:packs], earlier[packs:]):
            back = back + dot_nt(pack_ref[...], weight_ref[...])

        @pl.when(half == 0)
        def _():
            refs[0][...] = back

        @pl.when(half != 0)
        def _():
            refs[1][...] = back.astype(BF16)


def block_rows(tokens):
    return 3 * TOK if tokens % (3 * TOK) == 0 else TOK


def two_halves(rows, steps, lead):
    shape = (1,) * len(lead) + (rows, D)
    first = pl.BlockSpec(shape, lambda h, i: lead + (jnp.where(h == 0, i, steps - 1), 0))
    second = pl.BlockSpec(shape, lambda h, i: lead + (jnp.where(h == 0, 0, i), 0))
    return [first, second]


SCALARS = pl.BlockSpec(memory_space=pltpu.SMEM)


def attention_call(counts, owners, low, own, far, earlier, blocks, dp):
    tokens = own.shape[1]
    rows = block_rows(tokens)
    steps = tokens // rows
    cols = blocks[0][0].shape[1]
    whole = lambda shape: pl.BlockSpec(shape, lambda h, i: (0, 0), pipeline_mode=pl.Buffered(1))
    at = lambda h, i: (h * steps + i, 0)
    packs = None if earlier is None else len(earlier[0])
    back = [] if earlier is None else two_halves(rows, steps, ())
    kind = BF16 if earlier is None else F32
    grads = [jax.ShapeDtypeStruct((D // 2, c), kind) for c in [cols // 2] * 4]
    return pl.pallas_call(
        functools.partial(attention_kernel, packs, len(blocks), dp),
        grid=(2, steps),
        in_specs=[SCALARS] * 3
        + two_halves(rows, steps, (0,))
        + two_halves(rows, steps, (1,))
        + [pl.BlockSpec((rows, cols // 4 * 3), at)] * (packs or 0)
        + [whole((D, cols // 4 * 3))] * (packs or 0)
        + [
            pl.BlockSpec((D // dp, cols), functools.partial(lambda at, h, i: (at, 0), at), pipeline_mode=pl.Buffered(1))
            for _, at in blocks
        ],
        out_specs=[pl.BlockSpec((rows, cols), at), whole((D, cols))] + [whole(g.shape) for g in grads] + back,
        out_shape=[
            jax.ShapeDtypeStruct((2 * tokens, cols), BF16),
            jax.ShapeDtypeStruct((D, cols), BF16),
            *grads,
        ]
        + [jax.ShapeDtypeStruct((tokens, D), kind) for kind in (F32, BF16)[: len(back)]],
        scratch_shapes=[
            pltpu.VMEM((2 * tokens, D), BF16),
            pltpu.VMEM((2 * tokens, D), BF16),
            pltpu.VMEM((2 * tokens, cols), BF16),
            pltpu.VMEM((rows, cols), BF16),
            pltpu.VMEM((D, cols), F32),
        ],
        compiler_params=params(),
        cost_estimate=cost(20e9, 14e6),
        name="attention",
    )(counts, owners, low, own, far, own, far, *[x for group in earlier or () for x in group], *[b for b, _ in blocks])


def combine_kernel(counts, place_ref, *refs):
    ins, refs = refs[: sum(counts)], refs[sum(counts) :]
    rows = refs[0].shape[0]
    place = place_ref[0]
    for j, ref in enumerate(refs):
        at = pl.ds(pl.multiple_of((place ^ j) * rows, rows), rows)
        total = None
        first = 0
        for count in counts:
            pieces = [r[at, :].astype(F32) for r in ins[first : first + count]]
            new = pieces[0] if count == 1 else jnp.concatenate(pieces, axis=1)
            total = new if total is None else total + new
            first += count
        ref[...] = total.astype(ref.dtype)


def combine_call(place, parts, dtypes):
    ins = [piece for part in parts for piece in part]
    rows, cols = ins[0].shape[0] // len(dtypes), sum(piece.shape[1] for piece in parts[0])
    whole = lambda a: pl.BlockSpec(a.shape, lambda: (0, 0))
    return pl.pallas_call(
        functools.partial(combine_kernel, [len(part) for part in parts]),
        in_specs=[SCALARS] + [whole(a) for a in ins],
        out_specs=[pl.BlockSpec((rows, cols), lambda: (0, 0))] * len(dtypes),
        out_shape=[jax.ShapeDtypeStruct((rows, cols), d) for d in dtypes],
        compiler_params=params(),
        cost_estimate=cost(1e6, 5e6),
        name="combine",
    )(place, *ins)


def split_kernel(count, place_ref, *refs):
    total = refs[0][...]
    for ref in refs[1:count]:
        total = total + ref[...]
    outs = refs[count:]
    cols = outs[0].shape[1]
    place = place_ref[0]
    for j, out_ref in enumerate(outs):
        block = total[:, :cols]
        for b in range(1, len(outs)):
            block = jnp.where((place ^ j) == b, total[:, b * cols : (b + 1) * cols], block)
        out_ref[...] = block


def split_call(place, parts, blocks):
    rows, cols = parts[0].shape
    return pl.pallas_call(
        functools.partial(split_kernel, len(parts)),
        in_specs=[SCALARS] + [pl.BlockSpec((rows, cols), lambda: (0, 0))] * len(parts),
        out_specs=[pl.BlockSpec((rows, cols // blocks), lambda: (0, 0))] * blocks,
        out_shape=[jax.ShapeDtypeStruct((rows, cols // blocks), F32)] * blocks,
        compiler_params=params(),
        cost_estimate=cost(1e6, 2e6),
        name="split_sum",
    )(place, *parts)


def result_kernel(count, *refs):
    halves, qkv_ref, out_ref = (refs[:count], refs[count:-2]), refs[-2], refs[-1]
    first, second = [functools.reduce(lambda a, b: a + b, [r[...].astype(F32) for r in half]) for half in halves]
    width = first.shape[1] // 2
    qkv_ref[0] = first[:, :width]
    qkv_ref[1] = first[:, width:]
    qkv_ref[2] = second[:, :width]
    out_ref[...] = second[:, width:].T


def result_call(first, second):
    rows, cols = first[0].shape
    qkv, out = pl.pallas_call(
        functools.partial(result_kernel, len(first)),
        out_shape=[
            jax.ShapeDtypeStruct((3, rows, cols // 2), F32),
            jax.ShapeDtypeStruct((cols // 2, rows), F32),
        ],
        compiler_params=params(),
        cost_estimate=cost(1e6, 2e6),
        name="weight_results",
    )(*first, *second)
    return jnp.transpose(qkv, (1, 0, 2)), out


def mixed_product(context_refs, weight_refs):
    total = None
    for context_ref, w_ref in zip(context_refs, weight_refs):
        new = dot_nt(context_ref[...], w_ref[...])
        total = new if total is None else total + new
    return total


def context_specs(rows, packs, weights, first):
    width = packs[0].shape[1] // 4
    return [pl.BlockSpec((rows, width), lambda i: (first + i, 3))] * len(packs) + [
        pl.BlockSpec((D, width), lambda i: (0, 3))
    ] * len(weights)


def mixed_kernel(count, *refs):
    refs[-1][...] = mixed_product(refs[:count], refs[count : 2 * count]).astype(BF16)


def mixed_call(packs, weights):
    tokens = packs[0].shape[0] // 2
    rows = block_rows(tokens)
    return pl.pallas_call(
        functools.partial(mixed_kernel, len(packs)),
        grid=(tokens // rows,),
        in_specs=context_specs(rows, packs, weights, tokens // rows),
        out_specs=pl.BlockSpec((rows, D), lambda i: (i, 0)),
        out_shape=jax.ShapeDtypeStruct((tokens, D), BF16),
        compiler_params=params(),
        cost_estimate=cost(2e9, 5e6),
        name="mixed",
    )(*packs, *weights)


def tail_kernel(core_ref, own_ref, recv_ref, emb_ref, gl_ref, cols_ref, gain_ref, keep_ref, first_ref, second_ref, acc):
    step = pl.program_id(0)
    rows = emb_ref.shape[0]
    scenes = rows // TOK

    @pl.when(step == 0)
    def _():
        acc[...] = jnp.zeros_like(acc)

    grad_normed = own_ref[...] + recv_ref[...].astype(F32)
    x = emb_ref[...].astype(F32)
    dev = x - jnp.mean(x, axis=-1, keepdims=True)
    inv_std = lax.rsqrt(jnp.mean(dev * dev, axis=-1, keepdims=True) + NORM_EPS)
    centred = dev * inv_std
    scaled = grad_normed * gain_ref[...]
    first_mean = jnp.mean(scaled, axis=-1, keepdims=True)
    second_mean = jnp.mean(scaled * centred, axis=-1, keepdims=True)
    back = inv_std * (scaled - first_mean - centred * second_mean)
    grad_in = (gl_ref[0].astype(F32) + back).astype(BF16)
    for g, (start, end) in enumerate(GROUP_BANDS):
        at = [slice(s * TOK + g * CAP, s * TOK + (g + 1) * CAP) for s in range(scenes)]
        columns = jnp.concatenate([cols_ref[a, : (end - start) * PIX] for a in at], axis=0)
        grads = jnp.concatenate([grad_in[a] for a in at], axis=0)
        acc[start * PIX : end * PIX, :] += dot_tn(columns, grads)

    @pl.when(step == pl.num_programs(0) - 1)
    def _():
        size = keep_ref.shape[0]
        core = core_ref[0]
        keep_ref[...] = acc[pl.ds(pl.multiple_of(core * size, size), size), :]
        other = pl.ds(pl.multiple_of((1 - core) * size, size), size)
        first_ref[...] = acc[other, : D // 2]
        second_ref[...] = acc[other, D // 2 :]


def tail_call(core, own, recv, emb, rows_own, cols, gain):
    tokens = emb.shape[0]
    rows = 2 * TOK if tokens % (2 * TOK) == 0 else TOK
    per = lambda a: pl.BlockSpec((rows, a.shape[1]), lambda i: (i, 0))
    stem_rows = GROUP_BANDS[-1][1] * PIX
    keep = jax.ShapeDtypeStruct((stem_rows // 2, D), F32)
    send = jax.ShapeDtypeStruct((stem_rows // 2, D // 2), F32)
    return pl.pallas_call(
        tail_kernel,
        grid=(tokens // rows,),
        in_specs=[SCALARS, per(own), per(recv), per(emb), pl.BlockSpec((1, rows, D), lambda i: (1, i, 0)), per(cols)]
        + [pl.BlockSpec(gain.shape, lambda i: (0, 0))],
        out_specs=[pl.BlockSpec(a.shape, lambda i: (0, 0)) for a in (keep, send, send)],
        out_shape=[keep, send, send],
        scratch_shapes=[pltpu.VMEM((stem_rows, D), F32)],
        compiler_params=params(),
        cost_estimate=cost(10e9, 12e6),
        name="tail",
    )(core, own, recv, emb, rows_own, cols, gain)


def output_kernel(count, cnt_ref, recv_ref, emb_ref, *refs):
    out_ref = refs[-1]
    step = pl.program_id(0)
    scenes = emb_ref.shape[0] // TOK
    mixed = recv_ref[...].astype(F32) + mixed_product(refs[:count], refs[count : 2 * count])
    total = emb_ref[...].astype(F32) + mixed
    for s in range(scenes):
        scene = step * scenes + s
        live = live_column(*[cnt_ref[g, scene] for g in range(GROUPS)])
        at = slice(s * TOK, (s + 1) * TOK)
        out_ref[at, :] = jnp.where(live, total[at], 0.0).astype(BF16)


def output_call(counts, recv, emb, packs, weights):
    tokens = emb.shape[0]
    rows = 2 * TOK if tokens % (2 * TOK) == 0 else TOK
    per = lambda a: pl.BlockSpec((rows, a.shape[1]), lambda i: (i, 0))
    return pl.pallas_call(
        functools.partial(output_kernel, len(packs)),
        grid=(tokens // rows,),
        in_specs=[SCALARS, per(recv), per(emb)]
        + context_specs(rows, packs, weights, 0),
        out_specs=per(emb),
        out_shape=jax.ShapeDtypeStruct(emb.shape, BF16),
        compiler_params=params(),
        cost_estimate=cost(5e9, 10e6),
        name="layer_output",
    )(counts, recv, emb, *packs, *weights)


def swap(x, axis, size, bit):
    return lax.ppermute(x, axis, [(i, i ^ bit) for i in range(size)])


def together(*values):
    return lax.optimization_barrier(values)


class Ring:
    def __init__(self, x, axis, size):
        self.axis, self.size = axis, size
        order = list(range(0, size, 2)) + list(range(size - 1, 0, -2))
        self.forward = [(order[i], order[(i + 1) % size]) for i in range(size)]
        self.backward = [(order[(i + 1) % size], order[i]) for i in range(size)]
        self.ahead, self.behind = [x], [x]

    def send(self):
        moved = [lax.ppermute(self.ahead[-1], self.axis, self.forward)]
        if len(self.behind) <= (self.size - 1) // 2:
            moved.append(lax.ppermute(self.behind[-1], self.axis, self.backward))
        return moved

    def receive(self, moved):
        self.ahead.append(moved[0])
        self.behind.extend(moved[1:])

    @property
    def steps(self):
        return len(self.ahead) - 1

    def owners(self, ahead, behind):
        size = self.size
        me = lax.axis_index(self.axis)
        here = jnp.where(me % 2 == 0, me // 2, size - 1 - me // 2)
        distances = [-s for s in range(ahead)] + list(range(1, behind))
        at = (here + size + jnp.array(distances, jnp.int32)) % size
        return jnp.where(at < size // 2, 2 * at, 2 * (size - 1 - at) + 1)


def step_all(rings, *beside):
    moved, beside = together([ring.send() for ring in rings], beside)
    for ring, blocks in zip(rings, moved):
        ring.receive(blocks)
    return beside


def halve_stem(recv, keep, group):
    mine = lax.axis_index("group") // 2 * 2 + lax.axis_index("dp") % 2
    return combine_call(mine.reshape(1), [[keep], recv], [F32] * (group // 2 * 2))


def sum_stem(parts, beside, after, last, dp, group):
    core = lax.axis_index("group") % 2
    far = lax.axis_index("group") // 2
    low = lax.axis_index("dp") % 2
    high = lax.axis_index("dp") // 2
    fars, highs = group // 2, dp // 2
    mine = far * 2 + low
    small, width = parts[0].shape
    rows = 2 * fars * small

    def hop(block, f, b):
        if f:
            pairs = [
                (d * group + g, (d ^ b) * group + (g ^ (2 * f))) for d in range(dp) for g in range(group)
            ]
            return lax.ppermute(block, ("dp", "group"), pairs)
        return swap(block, "dp", dp, b)

    hops = [(k // 2, k % 2) for k in range(1, 2 * fars)]
    arrived = [hop(part, f, b) for part, (f, b) in zip(parts[1:], hops)]
    arrived, beside = together(arrived, beside)
    beside = after[0](*beside)
    cols = width // highs
    part, *away = split_call(high.reshape(1), [parts[0], *arrived], highs)
    arrived = [swap(a, "dp", dp, 2 * (j + 1)) for j, a in enumerate(away)]
    arrived, beside = together(arrived, beside)
    for block in arrived:
        part = part + block
    part = part.astype(BF16)
    line = jnp.zeros((small, width), BF16)
    line = lax.dynamic_update_slice_in_dim(line, part, high * cols, 1)
    arrived = [swap(part, "dp", dp, 2 * j) for j in range(1, highs)]
    arrived, beside = together(arrived, after[1](*beside))
    for j, block in enumerate(arrived):
        line = lax.dynamic_update_slice_in_dim(line, block, (high ^ (j + 1)) * cols, 1)
    block = jnp.zeros((rows, width), BF16)
    block = lax.dynamic_update_slice_in_dim(block, line, mine * small, 0)
    arrived, beside = together([hop(line, f, b) for f, b in hops], last(*beside))
    for (f, b), piece in zip(hops, arrived):
        target = (far ^ f) * 2 + (low ^ b)
        block = lax.dynamic_update_slice_in_dim(block, piece, target * small, 0)
    partner = swap(block, "group", group, 1)
    first = jnp.where(core == 0, block, partner)
    second = jnp.where(core == 0, partner, block)
    return jnp.concatenate([first, second], axis=0).astype(F32), beside


def encoding_tables(patch_count):
    quarter = D // 4
    half_width = D // 2
    power = lambda n: np.power(np.float32(10000.0), -np.arange(n, dtype=np.float32) / np.float32(n))
    at = np.arange(GRID).astype(np.float32)[:, None] * power(quarter)
    both = np.concatenate([np.sin(at), np.cos(at)], axis=-1)
    patch = np.arange(patch_count)
    rest = np.concatenate([both[patch // GRID], both[patch % GRID]], axis=-1).astype(np.float32)
    parts = []
    for _ in range(3):
        parts.append(rest.astype(ml_dtypes.bfloat16))
        rest = rest - parts[-1].astype(np.float32)
    group_at = np.arange(GROUPS).astype(np.float32)[:, None] * power(half_width)
    return np.stack(parts), np.concatenate([np.sin(group_at), np.cos(group_at)], axis=-1).astype(np.float32)


def on_device(dp, group, patches, vis_index, vis_count, w_stem, ln_gain, w_qkv, w_out, out_grad):
    scenes = patches.shape[0]
    tokens = scenes * TOK
    width = w_qkv.shape[2]
    fars = range(1, group // 2)
    rests = range(1, dp // 2)
    dp_low, dp_high = lax.axis_index("dp") % 2, lax.axis_index("dp") // 2
    low, high = dp_low.reshape(1), dp_high.reshape(1)
    core = (lax.axis_index("group") % 2).reshape(1)

    shard = pack_call(w_qkv, w_out)
    cross = lambda x, f: swap(x, "group", group, 2 * f)
    far_shards = [cross(shard, f) for f in fars]
    counts = vis_count.astype(jnp.int32).T
    counts_far = swap(counts, "group", group, 1)
    table, genc = encoding_tables(patches.shape[1])
    gain = ln_gain.reshape(1, D)
    stem = stem_call(
        counts,
        vis_index,
        patches,
        w_stem,
        gain,
        jnp.asarray(table),
        jnp.asarray(genc),
        out_grad.reshape(scenes, TOK, D),
    )
    stem, both_counts, far_shards = together(stem, jnp.stack([counts, counts_far]), far_shards)
    rings = [Ring(x, "dp", dp) for x in far_shards]
    ring = rings[0]
    owners = ring.owners(dp // 2 + 1, dp // 2)
    emb = stem[0].reshape(tokens, D)
    both = [stem[1].reshape(2, tokens, D)]
    cols = stem[2].reshape(tokens, stem[2].shape[2])
    both.append(swap(both[0], "group", group, 1))
    passed = []
    both, owners = step_all(rings, both, owners)
    while ring.steps < dp // 2:
        passed.append(cross(ring.ahead[-1], 1))
        if len(passed) > 1:
            (passed[-2],) = step_all(rings, passed[-2])
        else:
            step_all(rings)
    ring.ahead, ring.behind = together(ring.ahead, ring.behind)
    passed.append(cross(ring.ahead[-1], 1))
    passed.append(cross(jnp.concatenate(ring.behind[1:], axis=0), 1))

    packs, weights, crossing = [], [], []
    for f in list(fars) + [0]:
        if f:
            blocks = [(x, 0) for x in rings[f - 1].ahead + rings[f - 1].behind[1:]]
        else:
            blocks = [(x, 0) for x in [shard] + passed[:-1]] + [(passed[-1], b) for b in range(dp // 2 - 1)]
        made = attention_call(both_counts, owners, low, *both, None if f else (packs, weights), blocks, dp)
        if f == 1:
            made, passed[-3:] = together(made, passed[-3:])
        elif f:
            made = together(*made)
        else:
            made, arrived = together(made, [x[:3] for x in crossing])
        pack, weight, keep, other, back = made[0], made[1], made[2:4], made[4:6], made[6:]
        packs.append(pack)
        weights.append(weight)
        if f:
            crossing.append([cross(x, f) for x in (*other, *keep)])
    back_far = swap(back[1], "group", group, 1)
    coming = []
    for c in range(2):
        send = other[c]
        for x in arrived:
            send = send + x[c].astype(F32)
        coming.append(swap(send.astype(BF16), "dp", dp, 1))
    stem_made, coming[0], last_keeps = together(
        tail_call(core, back[0], back_far, emb, both[0], cols, gain), coming[0], [x[3] for x in crossing]
    )
    stem_keep, *stem_recv = stem_made
    stem_recv = [swap(x, "group", group, 1) for x in stem_recv]
    kinds = [F32 if j < 2 else BF16 for j in range(dp // 2)]
    second_leg = lambda c: combine_call(high, [[x] for x in keeps[c] + [coming[c]]], kinds)
    spread = lambda blocks, js: [swap(blocks[j], "dp", dp, 2 * j) for j in js]
    stem_recv = together(*stem_recv)
    keeps = [[keep[0]] + [x[2] for x in arrived], [keep[1]] + list(last_keeps)]
    stem_parts = halve_stem(stem_recv, stem_keep, group)
    _, coming[0], keeps = together(stem_parts, coming[0], keeps)
    first = second_leg(0)
    first_rest = spread(first, rests[1:])
    second = second_leg(1)
    near = dp // 2 * 3 // 4
    beside = [mixed_call(packs, weights), first[0], *first_rest, second[0]]
    def after_first(mixed, *arrived):
        output = output_call(counts, swap(mixed, "group", group, 1), emb, packs, weights)
        return [output, *arrived[:-1], *spread(first, [1]), arrived[-1]]

    def after_second(*arrived):
        return [*arrived, *spread(second, [1, *range(2, near)])]

    def last(output, *arrived):
        arrived = [*arrived, *spread(second, range(near, dp // 2))]
        half = len(arrived) // 2
        return output, *result_call(arrived[:half], arrived[half:])

    grad_w_stem, (output, grad_w_qkv, grad_w_out) = sum_stem(
        stem_parts, beside, (after_first, after_second), last, dp, group
    )
    return (output.reshape(scenes, GROUPS, CAP, D), grad_w_stem, grad_w_qkv, grad_w_out)


def solution(mesh):
    sizes = dict(mesh.shape)
    return jax.shard_map(
        functools.partial(on_device, sizes["dp"], sizes["group"]),
        mesh=mesh,
        in_specs=(
            P(("dp", "group"), None, None),
            P(("dp", "group"), None, None),
            P(("dp", "group"), None),
            P(),
            P(),
            P("dp", None, "group"),
            P("group", "dp"),
            P(("dp", "group"), None, None, None),
        ),
        out_specs=(
            P(("dp", "group"), None, None, None),
            P(),
            P("dp", None, "group"),
            P("group", "dp"),
        ),
        check_vma=False,
    )
```

```python
import functools

import jax
import jax.numpy as jnp
import ml_dtypes
import numpy as np
from jax import lax
from jax.experimental import pallas as pl
from jax.experimental.pallas import tpu as pltpu
from jax.sharding import PartitionSpec as P

D = 1024
HD = 64
GROUPS = 3
CAP = 48
GRID = 12
PIX = 64
TOK = GROUPS * CAP
PAIR = 128
GROUP_BANDS = ((0, 4), (4, 8), (8, 10))
NORM_EPS = 1e-06
F32 = jnp.float32
BF16 = jnp.bfloat16
VMEM_LIMIT = 60 * 1024 * 1024


def dot_nn(a, b):
    return lax.dot_general(a, b, (((1,), (0,)), ((), ())), preferred_element_type=F32)


def dot_nt(a, b):
    return lax.dot_general(a, b, (((1,), (1,)), ((), ())), preferred_element_type=F32)


def dot_tn(a, b):
    return lax.dot_general(a, b, (((0,), (0,)), ((), ())), preferred_element_type=F32)


def live_column(c0, c1, c2):
    row = lax.broadcasted_iota(jnp.int32, (TOK, 1), 0)
    return (
        (row < c0)
        | ((row >= CAP) & (row < CAP + c1))
        | ((row >= 2 * CAP) & (row < 2 * CAP + c2))
    )


def params():
    return pltpu.CompilerParams(vmem_limit_bytes=VMEM_LIMIT)


def cost(flops, nbytes):
    return pl.CostEstimate(flops=int(flops / 1000), bytes_accessed=int(nbytes / 1000), transcendentals=0)


def stem_kernel(
    cnt_ref, idx_ref, patch_ref, w_ref, gain_ref, parts, genc_ref, og_ref,
    emb_ref, rows_ref, cols_ref,
):
    step = pl.program_id(0)
    scenes = patch_ref.shape[0]
    patch_iota = lax.broadcasted_iota(jnp.int32, (parts.shape[1], CAP), 0)
    slot = lax.broadcasted_iota(jnp.int32, (CAP, 1), 0)
    for g, (start, end) in enumerate(GROUP_BANDS):
        rows = slice(g * CAP, (g + 1) * CAP)
        width = (end - start) * PIX
        picked, placed = [], []
        for s in range(scenes):
            onehot = (idx_ref[s, g : g + 1, :] == patch_iota).astype(F32).astype(BF16).T
            picked.append(dot_nn(onehot, patch_ref[s, :, start * PIX : end * PIX]).astype(BF16))
            placed.append(
                (dot_nn(onehot, parts[0]) + dot_nn(onehot, parts[1])) + dot_nn(onehot, parts[2])
            )
            live = slot < cnt_ref[g, step * scenes + s]
            rows_ref[1, s, rows, :] = jnp.where(live, og_ref[s, rows, :].astype(F32), 0.0).astype(BF16)
        summed = dot_nn(jnp.concatenate(picked, axis=0), w_ref[start * PIX : end * PIX, :])
        for s in range(scenes):
            values = summed[s * CAP : (s + 1) * CAP] + (placed[s] + genc_ref[g : g + 1, :])
            emb = values.astype(BF16)
            emb_ref[s, rows, :] = emb
            x = emb.astype(F32)
            centre = jnp.mean(x, axis=-1, keepdims=True)
            dev = x - centre
            spread = jnp.mean(dev * dev, axis=-1, keepdims=True)
            centred = dev * lax.rsqrt(spread + NORM_EPS)
            rows_ref[0, s, rows, :] = (centred * gain_ref[...]).astype(BF16)
            cols_ref[s, rows, :width] = picked[s]
            if width < cols_ref.shape[2]:
                cols_ref[s, rows, width:] = jnp.zeros((CAP, cols_ref.shape[2] - width), BF16)


def stem_call(counts, index, patches, w_stem, gain, table, genc, out_grad):
    scenes, patch_count, width = patches.shape
    block = 3 if scenes % 3 == 0 else 1
    col_width = max(e - s for s, e in GROUP_BANDS) * PIX
    per = lambda shape: pl.BlockSpec((block,) + shape, lambda i: (i, 0, 0))
    whole = lambda a: pl.BlockSpec(a.shape, lambda i: (0,) * a.ndim)
    return pl.pallas_call(
        stem_kernel,
        grid=(scenes // block,),
        in_specs=[
            pl.BlockSpec(memory_space=pltpu.SMEM),
            per((GROUPS, CAP)),
            per((patch_count, width)),
            whole(w_stem),
            whole(gain),
            whole(table),
            whole(genc),
            per((TOK, D)),
        ],
        out_specs=[
            per((TOK, D)),
            pl.BlockSpec((2, block, TOK, D), lambda i: (0, i, 0, 0)),
            per((TOK, col_width)),
        ],
        out_shape=[
            jax.ShapeDtypeStruct((scenes, TOK, D), BF16),
            jax.ShapeDtypeStruct((2, scenes, TOK, D), BF16),
            jax.ShapeDtypeStruct((scenes, TOK, col_width), BF16),
        ],
        compiler_params=params(),
        cost_estimate=cost(8e9, 12e6),
        name="stem_norm",
    )(counts, index, patches, w_stem, gain, table, genc, out_grad)


def pack_kernel(qkv_ref, out_w_ref, pack_ref):
    count, _, width = qkv_ref.shape
    for c in range(count):
        pack_ref[:, c * width : (c + 1) * width] = qkv_ref[c]
    pack_ref[:, count * width :] = out_w_ref[...].T


def pack_call(w_qkv, w_out):
    parts = jnp.transpose(w_qkv, (1, 0, 2))
    return pl.pallas_call(
        pack_kernel,
        out_shape=jax.ShapeDtypeStruct((w_qkv.shape[0], 3 * w_qkv.shape[2] + w_out.shape[0]), BF16),
        compiler_params=params(),
        cost_estimate=cost(1e6, 5e5),
        name="pack_weights",
    )(parts, w_out)


def attention_kernel(
    packs, blocks, dp, cnt_ref, owner_ref, low_ref, na_ref, nb_ref, ga_ref, gb_ref, *refs
):
    earlier, refs = refs[: 2 * (packs or 0)], refs[2 * (packs or 0) :]
    blocks, refs = refs[:blocks], refs[blocks:]
    out_ref, w_ref, *refs = refs
    keeps, others, refs = refs[:2], refs[2:4], refs[4:]
    n_all, g_all, pack_all, qkv, total = refs[-5:]
    half, step = pl.program_id(0), pl.program_id(1)
    rows = qkv.shape[0]
    here = pl.ds(pl.multiple_of((half * pl.num_programs(1) + step) * rows, 16), rows)
    scenes = rows // TOK
    width = w_ref.shape[1] // 4

    @pl.when((half == 0) & (step == 0))
    def _():
        size = blocks[0].shape[0]
        for b, block in enumerate(blocks):
            w_ref[pl.ds(pl.multiple_of(owner_ref[b] * size, size), size), :] = block[...]

    @pl.when(half == 0)
    def _():
        n_all[here, :] = na_ref[0]
        g_all[here, :] = ga_ref[0]

    @pl.when(half != 0)
    def _():
        n_all[here, :] = nb_ref[0]
        g_all[here, :] = gb_ref[0]

    qkv[:, : 3 * width] = dot_nn(n_all[here, :], w_ref[:, : 3 * width]).astype(BF16)
    qkv[:, 3 * width :] = dot_nn(g_all[here, :], w_ref[:, 3 * width :]).astype(BF16)
    heads = width // HD
    lane = lax.broadcasted_iota(jnp.int32, (1, width), 1)
    masks = [(lane // HD == h).astype(F32).astype(BF16) for h in range(heads)]
    scale = jnp.asarray(HD ** (-0.5), BF16)
    first_of_pair = lax.broadcasted_iota(jnp.int32, (1, PAIR), 1) < HD

    def own_lanes(tall):
        tiles = []
        for t in range(width // PAIR):
            at = slice(t * PAIR, (t + 1) * PAIR)
            one = tall[2 * t * TOK : (2 * t + 1) * TOK, at]
            two = tall[(2 * t + 1) * TOK : (2 * t + 2) * TOK, at]
            tiles.append(jnp.where(first_of_pair, one, two))
        return jnp.concatenate(tiles, axis=1)

    def scene_body(s, _):
        base = pl.multiple_of(s * TOK, 16)
        at = pl.ds(base, TOK)
        scene = step * scenes + s
        live = live_column(*[cnt_ref[half, g, scene] for g in range(GROUPS)])
        bias = jnp.where(live, 0.0, -1e30)
        q, k, v, dc = [qkv[at, c * width : (c + 1) * width] for c in range(4)]
        tall_q = jnp.concatenate([q * (m * scale) for m in masks], axis=0)
        tall_dc = jnp.concatenate([dc * m for m in masks], axis=0)
        scores = dot_nt(k, tall_q)
        grad_probs = dot_nt(v, tall_dc)
        probs_parts, score_parts = [], []
        for start in range(0, heads * TOK, PAIR):
            cols = slice(start, min(start + PAIR, heads * TOK))
            part = scores[:, cols] + bias
            lifted = jnp.exp(part - jnp.max(part, axis=0, keepdims=True))
            probs = lifted * (1.0 / jnp.sum(lifted, axis=0, keepdims=True))
            weighted = probs * grad_probs[:, cols]
            inner = jnp.sum(weighted, axis=0, keepdims=True)
            probs_parts.append(probs.astype(BF16))
            score_parts.append((weighted - probs * inner).astype(BF16))
        half_probs = jnp.concatenate(probs_parts, axis=1)
        grad_score = jnp.concatenate(score_parts, axis=1)
        out_ref[at, :width] = (own_lanes(dot_tn(grad_score, k)) * HD ** (-0.5)).astype(BF16)
        out_ref[at, width : 2 * width] = dot_nn(grad_score, tall_q).astype(BF16)
        out_ref[at, 2 * width : 3 * width] = dot_nn(half_probs, tall_dc).astype(BF16)
        out_ref[at, 3 * width :] = own_lanes(dot_tn(half_probs, v)).astype(BF16)
        return 0

    lax.fori_loop(0, scenes, scene_body, 0, unroll=True)
    pack_all[here, :] = out_ref[...]

    @pl.when((half == pl.num_programs(0) - 1) & (step == pl.num_programs(1) - 1))
    def _():
        total[:, : 3 * width] = dot_tn(n_all[...], pack_all[:, : 3 * width])
        total[:, 3 * width :] = dot_tn(g_all[...], pack_all[:, 3 * width :])
        size = total.shape[0] // dp
        low = low_ref[0]
        for b in range(dp // 2):
            at = slice(b * size, (b + 1) * size)
            mine = pl.multiple_of((2 * b + low) * size, size)
            other = pl.multiple_of((2 * b + 1 - low) * size, size)
            for c in range(2):
                cols = slice(c * 2 * width, (c + 1) * 2 * width)
                keeps[c][at, :] = total[pl.ds(mine, size), cols].astype(keeps[c].dtype)
                others[c][at, :] = total[pl.ds(other, size), cols].astype(others[c].dtype)

    if packs is not None:
        back = dot_nt(out_ref[:, : 3 * width], w_ref[:, : 3 * width])
        for pack_ref, weight_ref in zip(earlier[:packs], earlier[packs:]):
            back = back + dot_nt(pack_ref[...], weight_ref[...])

        @pl.when(half == 0)
        def _():
            refs[0][...] = back

        @pl.when(half != 0)
        def _():
            refs[1][...] = back.astype(BF16)


def block_rows(tokens):
    return 3 * TOK if tokens % (3 * TOK) == 0 else TOK


def two_halves(rows, steps, lead):
    shape = (1,) * len(lead) + (rows, D)
    first = pl.BlockSpec(shape, lambda h, i: lead + (jnp.where(h == 0, i, steps - 1), 0))
    second = pl.BlockSpec(shape, lambda h, i: lead + (jnp.where(h == 0, 0, i), 0))
    return [first, second]


SCALARS = pl.BlockSpec(memory_space=pltpu.SMEM)


def attention_call(counts, owners, low, own, far, earlier, blocks, dp):
    tokens = own.shape[1]
    rows = block_rows(tokens)
    steps = tokens // rows
    cols = blocks[0].shape[1]
    whole = lambda shape: pl.BlockSpec(shape, lambda h, i: (0, 0), pipeline_mode=pl.Buffered(1))
    at = lambda h, i: (h * steps + i, 0)
    packs = None if earlier is None else len(earlier[0])
    back = [] if earlier is None else two_halves(rows, steps, ())
    kind = BF16 if earlier is None else F32
    grads = [jax.ShapeDtypeStruct((D // 2, c), kind) for c in [cols // 2] * 4]
    return pl.pallas_call(
        functools.partial(attention_kernel, packs, len(blocks), dp),
        grid=(2, steps),
        in_specs=[SCALARS] * 3
        + two_halves(rows, steps, (0,))
        + two_halves(rows, steps, (1,))
        + [pl.BlockSpec((rows, cols // 4 * 3), at)] * (packs or 0)
        + [whole((D, cols // 4 * 3))] * (packs or 0)
        + [whole(b.shape) for b in blocks],
        out_specs=[pl.BlockSpec((rows, cols), at), whole((D, cols))] + [whole(g.shape) for g in grads] + back,
        out_shape=[
            jax.ShapeDtypeStruct((2 * tokens, cols), BF16),
            jax.ShapeDtypeStruct((D, cols), BF16),
            *grads,
        ]
        + [jax.ShapeDtypeStruct((tokens, D), kind) for kind in (F32, BF16)[: len(back)]],
        scratch_shapes=[
            pltpu.VMEM((2 * tokens, D), BF16),
            pltpu.VMEM((2 * tokens, D), BF16),
            pltpu.VMEM((2 * tokens, cols), BF16),
            pltpu.VMEM((rows, cols), BF16),
            pltpu.VMEM((D, cols), F32),
        ],
        compiler_params=params(),
        cost_estimate=cost(20e9, 14e6),
        name="attention",
    )(counts, owners, low, own, far, own, far, *[x for group in earlier or () for x in group], *blocks)


def combine_kernel(counts, place_ref, *refs):
    ins, refs = refs[: sum(counts)], refs[sum(counts) :]
    rows = refs[0].shape[0]
    place = place_ref[0]
    for j, ref in enumerate(refs):
        at = pl.ds(pl.multiple_of((place ^ j) * rows, rows), rows)
        total = None
        first = 0
        for count in counts:
            pieces = [r[at, :].astype(F32) for r in ins[first : first + count]]
            new = pieces[0] if count == 1 else jnp.concatenate(pieces, axis=1)
            total = new if total is None else total + new
            first += count
        ref[...] = total.astype(ref.dtype)


def combine_call(place, parts, dtypes):
    ins = [piece for part in parts for piece in part]
    rows, cols = ins[0].shape[0] // len(dtypes), sum(piece.shape[1] for piece in parts[0])
    whole = lambda a: pl.BlockSpec(a.shape, lambda: (0, 0))
    return pl.pallas_call(
        functools.partial(combine_kernel, [len(part) for part in parts]),
        in_specs=[SCALARS] + [whole(a) for a in ins],
        out_specs=[pl.BlockSpec((rows, cols), lambda: (0, 0))] * len(dtypes),
        out_shape=[jax.ShapeDtypeStruct((rows, cols), d) for d in dtypes],
        compiler_params=params(),
        cost_estimate=cost(1e6, 5e6),
        name="combine",
    )(place, *ins)


def split_kernel(count, place_ref, *refs):
    total = refs[0][...]
    for ref in refs[1:count]:
        total = total + ref[...]
    outs = refs[count:]
    cols = outs[0].shape[1]
    place = place_ref[0]
    for j, out_ref in enumerate(outs):
        block = total[:, :cols]
        for b in range(1, len(outs)):
            block = jnp.where((place ^ j) == b, total[:, b * cols : (b + 1) * cols], block)
        out_ref[...] = block


def split_call(place, parts, blocks):
    rows, cols = parts[0].shape
    return pl.pallas_call(
        functools.partial(split_kernel, len(parts)),
        in_specs=[SCALARS] + [pl.BlockSpec((rows, cols), lambda: (0, 0))] * len(parts),
        out_specs=[pl.BlockSpec((rows, cols // blocks), lambda: (0, 0))] * blocks,
        out_shape=[jax.ShapeDtypeStruct((rows, cols // blocks), F32)] * blocks,
        compiler_params=params(),
        cost_estimate=cost(1e6, 2e6),
        name="split_sum",
    )(place, *parts)


def result_kernel(count, *refs):
    halves, qkv_ref, out_ref = (refs[:count], refs[count:-2]), refs[-2], refs[-1]
    first, second = [functools.reduce(lambda a, b: a + b, [r[...].astype(F32) for r in half]) for half in halves]
    width = first.shape[1] // 2
    qkv_ref[0] = first[:, :width]
    qkv_ref[1] = first[:, width:]
    qkv_ref[2] = second[:, :width]
    out_ref[...] = second[:, width:].T


def result_call(first, second):
    rows, cols = first[0].shape
    qkv, out = pl.pallas_call(
        functools.partial(result_kernel, len(first)),
        out_shape=[
            jax.ShapeDtypeStruct((3, rows, cols // 2), F32),
            jax.ShapeDtypeStruct((cols // 2, rows), F32),
        ],
        compiler_params=params(),
        cost_estimate=cost(1e6, 2e6),
        name="weight_results",
    )(*first, *second)
    return jnp.transpose(qkv, (1, 0, 2)), out


def mixed_product(context_refs, weight_refs):
    total = None
    for context_ref, w_ref in zip(context_refs, weight_refs):
        new = dot_nt(context_ref[...], w_ref[...])
        total = new if total is None else total + new
    return total


def context_specs(rows, packs, weights, first):
    width = packs[0].shape[1] // 4
    return [pl.BlockSpec((rows, width), lambda i: (first + i, 3))] * len(packs) + [
        pl.BlockSpec((D, width), lambda i: (0, 3))
    ] * len(weights)


def mixed_kernel(count, *refs):
    refs[-1][...] = mixed_product(refs[:count], refs[count : 2 * count]).astype(BF16)


def mixed_call(packs, weights):
    tokens = packs[0].shape[0] // 2
    rows = block_rows(tokens)
    return pl.pallas_call(
        functools.partial(mixed_kernel, len(packs)),
        grid=(tokens // rows,),
        in_specs=context_specs(rows, packs, weights, tokens // rows),
        out_specs=pl.BlockSpec((rows, D), lambda i: (i, 0)),
        out_shape=jax.ShapeDtypeStruct((tokens, D), BF16),
        compiler_params=params(),
        cost_estimate=cost(2e9, 5e6),
        name="mixed",
    )(*packs, *weights)


def tail_kernel(core_ref, own_ref, recv_ref, emb_ref, gl_ref, cols_ref, gain_ref, keep_ref, first_ref, second_ref, acc):
    step = pl.program_id(0)
    rows = emb_ref.shape[0]
    scenes = rows // TOK

    @pl.when(step == 0)
    def _():
        acc[...] = jnp.zeros_like(acc)

    grad_normed = own_ref[...] + recv_ref[...].astype(F32)
    x = emb_ref[...].astype(F32)
    dev = x - jnp.mean(x, axis=-1, keepdims=True)
    inv_std = lax.rsqrt(jnp.mean(dev * dev, axis=-1, keepdims=True) + NORM_EPS)
    centred = dev * inv_std
    scaled = grad_normed * gain_ref[...]
    first_mean = jnp.mean(scaled, axis=-1, keepdims=True)
    second_mean = jnp.mean(scaled * centred, axis=-1, keepdims=True)
    back = inv_std * (scaled - first_mean - centred * second_mean)
    grad_in = (gl_ref[0].astype(F32) + back).astype(BF16)
    for g, (start, end) in enumerate(GROUP_BANDS):
        at = [slice(s * TOK + g * CAP, s * TOK + (g + 1) * CAP) for s in range(scenes)]
        columns = jnp.concatenate([cols_ref[a, : (end - start) * PIX] for a in at], axis=0)
        grads = jnp.concatenate([grad_in[a] for a in at], axis=0)
        acc[start * PIX : end * PIX, :] += dot_tn(columns, grads)

    @pl.when(step == pl.num_programs(0) - 1)
    def _():
        size = keep_ref.shape[0]
        core = core_ref[0]
        keep_ref[...] = acc[pl.ds(pl.multiple_of(core * size, size), size), :]
        other = pl.ds(pl.multiple_of((1 - core) * size, size), size)
        first_ref[...] = acc[other, : D // 2]
        second_ref[...] = acc[other, D // 2 :]


def tail_call(core, own, recv, emb, rows_own, cols, gain):
    tokens = emb.shape[0]
    rows = 2 * TOK if tokens % (2 * TOK) == 0 else TOK
    per = lambda a: pl.BlockSpec((rows, a.shape[1]), lambda i: (i, 0))
    stem_rows = GROUP_BANDS[-1][1] * PIX
    keep = jax.ShapeDtypeStruct((stem_rows // 2, D), F32)
    send = jax.ShapeDtypeStruct((stem_rows // 2, D // 2), F32)
    return pl.pallas_call(
        tail_kernel,
        grid=(tokens // rows,),
        in_specs=[SCALARS, per(own), per(recv), per(emb), pl.BlockSpec((1, rows, D), lambda i: (1, i, 0)), per(cols)]
        + [pl.BlockSpec(gain.shape, lambda i: (0, 0))],
        out_specs=[pl.BlockSpec(a.shape, lambda i: (0, 0)) for a in (keep, send, send)],
        out_shape=[keep, send, send],
        scratch_shapes=[pltpu.VMEM((stem_rows, D), F32)],
        compiler_params=params(),
        cost_estimate=cost(10e9, 12e6),
        name="tail",
    )(core, own, recv, emb, rows_own, cols, gain)


def output_kernel(count, cnt_ref, recv_ref, emb_ref, *refs):
    out_ref = refs[-1]
    step = pl.program_id(0)
    scenes = emb_ref.shape[0] // TOK
    mixed = recv_ref[...].astype(F32) + mixed_product(refs[:count], refs[count : 2 * count])
    total = emb_ref[...].astype(F32) + mixed
    for s in range(scenes):
        scene = step * scenes + s
        live = live_column(*[cnt_ref[g, scene] for g in range(GROUPS)])
        at = slice(s * TOK, (s + 1) * TOK)
        out_ref[at, :] = jnp.where(live, total[at], 0.0).astype(BF16)


def output_call(counts, recv, emb, packs, weights):
    tokens = emb.shape[0]
    rows = 2 * TOK if tokens % (2 * TOK) == 0 else TOK
    per = lambda a: pl.BlockSpec((rows, a.shape[1]), lambda i: (i, 0))
    return pl.pallas_call(
        functools.partial(output_kernel, len(packs)),
        grid=(tokens // rows,),
        in_specs=[SCALARS, per(recv), per(emb)]
        + context_specs(rows, packs, weights, 0),
        out_specs=per(emb),
        out_shape=jax.ShapeDtypeStruct(emb.shape, BF16),
        compiler_params=params(),
        cost_estimate=cost(5e9, 10e6),
        name="layer_output",
    )(counts, recv, emb, *packs, *weights)


def swap(x, axis, size, bit):
    return lax.ppermute(x, axis, [(i, i ^ bit) for i in range(size)])


def together(*values):
    return lax.optimization_barrier(values)


class Ring:
    def __init__(self, x, axis, size):
        self.axis, self.size = axis, size
        order = list(range(0, size, 2)) + list(range(size - 1, 0, -2))
        self.forward = [(order[i], order[(i + 1) % size]) for i in range(size)]
        self.backward = [(order[(i + 1) % size], order[i]) for i in range(size)]
        self.ahead, self.behind = [x], [x]

    def send(self):
        moved = [lax.ppermute(self.ahead[-1], self.axis, self.forward)]
        if len(self.behind) <= (self.size - 1) // 2:
            moved.append(lax.ppermute(self.behind[-1], self.axis, self.backward))
        return moved

    def receive(self, moved):
        self.ahead.append(moved[0])
        self.behind.extend(moved[1:])

    @property
    def steps(self):
        return len(self.ahead) - 1

    def owners(self, ahead, behind):
        size = self.size
        me = lax.axis_index(self.axis)
        here = jnp.where(me % 2 == 0, me // 2, size - 1 - me // 2)
        distances = [-s for s in range(ahead)] + list(range(1, behind))
        at = (here + size + jnp.array(distances, jnp.int32)) % size
        return jnp.where(at < size // 2, 2 * at, 2 * (size - 1 - at) + 1)


def step_all(rings, *beside):
    moved, beside = together([ring.send() for ring in rings], beside)
    for ring, blocks in zip(rings, moved):
        ring.receive(blocks)
    return beside


def halve_stem(recv, keep, group):
    mine = lax.axis_index("group") // 2 * 2 + lax.axis_index("dp") % 2
    return combine_call(mine.reshape(1), [[keep], recv], [F32] * (group // 2 * 2))


def sum_stem(parts, beside, after, last, dp, group):
    core = lax.axis_index("group") % 2
    far = lax.axis_index("group") // 2
    low = lax.axis_index("dp") % 2
    high = lax.axis_index("dp") // 2
    fars, highs = group // 2, dp // 2
    mine = far * 2 + low
    small, width = parts[0].shape
    rows = 2 * fars * small

    def hop(block, f, b):
        if f:
            pairs = [
                (d * group + g, (d ^ b) * group + (g ^ (2 * f))) for d in range(dp) for g in range(group)
            ]
            return lax.ppermute(block, ("dp", "group"), pairs)
        return swap(block, "dp", dp, b)

    hops = [(k // 2, k % 2) for k in range(1, 2 * fars)]
    arrived = [hop(part, f, b) for part, (f, b) in zip(parts[1:], hops)]
    arrived, beside = together(arrived, beside)
    beside = after[0](*beside)
    cols = width // highs
    part, *away = split_call(high.reshape(1), [parts[0], *arrived], highs)
    arrived = [swap(a, "dp", dp, 2 * (j + 1)) for j, a in enumerate(away)]
    arrived, beside = together(arrived, beside)
    for block in arrived:
        part = part + block
    part = part.astype(BF16)
    line = jnp.zeros((small, width), BF16)
    line = lax.dynamic_update_slice_in_dim(line, part, high * cols, 1)
    arrived = [swap(part, "dp", dp, 2 * j) for j in range(1, highs)]
    arrived, beside = together(arrived, after[1](*beside))
    for j, block in enumerate(arrived):
        line = lax.dynamic_update_slice_in_dim(line, block, (high ^ (j + 1)) * cols, 1)
    block = jnp.zeros((rows, width), BF16)
    block = lax.dynamic_update_slice_in_dim(block, line, mine * small, 0)
    arrived, beside = together([hop(line, f, b) for f, b in hops], last(*beside))
    for (f, b), piece in zip(hops, arrived):
        target = (far ^ f) * 2 + (low ^ b)
        block = lax.dynamic_update_slice_in_dim(block, piece, target * small, 0)
    partner = swap(block, "group", group, 1)
    first = jnp.where(core == 0, block, partner)
    second = jnp.where(core == 0, partner, block)
    return jnp.concatenate([first, second], axis=0).astype(F32), beside


def encoding_tables(patch_count):
    quarter = D // 4
    half_width = D // 2
    power = lambda n: np.power(np.float32(10000.0), -np.arange(n, dtype=np.float32) / np.float32(n))
    at = np.arange(GRID).astype(np.float32)[:, None] * power(quarter)
    both = np.concatenate([np.sin(at), np.cos(at)], axis=-1)
    patch = np.arange(patch_count)
    rest = np.concatenate([both[patch // GRID], both[patch % GRID]], axis=-1).astype(np.float32)
    parts = []
    for _ in range(3):
        parts.append(rest.astype(ml_dtypes.bfloat16))
        rest = rest - parts[-1].astype(np.float32)
    group_at = np.arange(GROUPS).astype(np.float32)[:, None] * power(half_width)
    return np.stack(parts), np.concatenate([np.sin(group_at), np.cos(group_at)], axis=-1).astype(np.float32)


def on_device(dp, group, patches, vis_index, vis_count, w_stem, ln_gain, w_qkv, w_out, out_grad):
    scenes = patches.shape[0]
    tokens = scenes * TOK
    width = w_qkv.shape[2]
    fars = range(1, group // 2)
    rests = range(1, dp // 2)
    dp_low, dp_high = lax.axis_index("dp") % 2, lax.axis_index("dp") // 2
    low, high = dp_low.reshape(1), dp_high.reshape(1)
    core = (lax.axis_index("group") % 2).reshape(1)

    shard = pack_call(w_qkv, w_out)
    cross = lambda x, f: swap(x, "group", group, 2 * f)
    far_shards = [cross(shard, f) for f in fars]
    counts = vis_count.astype(jnp.int32).T
    counts_far = swap(counts, "group", group, 1)
    table, genc = encoding_tables(patches.shape[1])
    gain = ln_gain.reshape(1, D)
    stem = stem_call(
        counts,
        vis_index,
        patches,
        w_stem,
        gain,
        jnp.asarray(table),
        jnp.asarray(genc),
        out_grad.reshape(scenes, TOK, D),
    )
    stem, both_counts, far_shards = together(stem, jnp.stack([counts, counts_far]), far_shards)
    rings = [Ring(x, "dp", dp) for x in far_shards]
    ring = rings[0]
    owners = ring.owners(dp // 2 + 1, dp // 2)
    emb = stem[0].reshape(tokens, D)
    both = [stem[1].reshape(2, tokens, D)]
    cols = stem[2].reshape(tokens, stem[2].shape[2])
    both.append(swap(both[0], "group", group, 1))
    own_ahead, own_behind = [], []
    both, owners = step_all(rings, both, owners)
    while ring.steps < dp // 2:
        a, b = len(own_ahead), len(own_behind)
        own_ahead.append(cross(ring.ahead[-1], 1))
        if a:
            own_behind.append(cross(ring.behind[a], 1))
        last_ahead, last_behind = max(a - 1, 0), max(b - 1, 0)
        own_ahead[last_ahead:a], own_behind[last_behind:b] = step_all(
            rings, own_ahead[last_ahead:a], own_behind[last_behind:b]
        )
    ring.ahead, ring.behind = together(ring.ahead, ring.behind)
    own_ahead.append(cross(ring.ahead[-1], 1))
    own_behind.extend(cross(x, 1) for x in ring.behind[len(own_behind) + 1 :])

    packs, weights, crossing = [], [], []
    for f in list(fars) + [0]:
        if f:
            blocks = rings[f - 1].ahead + rings[f - 1].behind[1:]
        else:
            blocks = [shard] + own_ahead + own_behind
        made = attention_call(both_counts, owners, low, *both, None if f else (packs, weights), blocks, dp)
        if f == 1:
            made, own_ahead[-2:], own_behind[-2:] = together(made, own_ahead[-2:], own_behind[-2:])
        elif f:
            made = together(*made)
        else:
            made, arrived = together(made, [x[:3] for x in crossing])
        pack, weight, keep, other, back = made[0], made[1], made[2:4], made[4:6], made[6:]
        packs.append(pack)
        weights.append(weight)
        if f:
            crossing.append([cross(x, f) for x in (*other, *keep)])
    back_far = swap(back[1], "group", group, 1)
    coming = []
    for c in range(2):
        send = other[c]
        for x in arrived:
            send = send + x[c].astype(F32)
        coming.append(swap(send.astype(BF16), "dp", dp, 1))
    stem_made, coming[0], last_keeps = together(
        tail_call(core, back[0], back_far, emb, both[0], cols, gain), coming[0], [x[3] for x in crossing]
    )
    stem_keep, *stem_recv = stem_made
    stem_recv = [swap(x, "group", group, 1) for x in stem_recv]
    kinds = [F32 if j < 2 else BF16 for j in range(dp // 2)]
    second_leg = lambda c: combine_call(high, [[x] for x in keeps[c] + [coming[c]]], kinds)
    spread = lambda blocks, js: [swap(blocks[j], "dp", dp, 2 * j) for j in js]
    stem_recv = together(*stem_recv)
    keeps = [[keep[0]] + [x[2] for x in arrived], [keep[1]] + list(last_keeps)]
    stem_parts = halve_stem(stem_recv, stem_keep, group)
    _, coming[0], keeps = together(stem_parts, coming[0], keeps)
    first = second_leg(0)
    first_rest = spread(first, rests[1:])
    second = second_leg(1)
    near = dp // 2 * 3 // 4
    beside = [mixed_call(packs, weights), first[0], *first_rest, second[0]]
    def after_first(mixed, *arrived):
        output = output_call(counts, swap(mixed, "group", group, 1), emb, packs, weights)
        return [output, *arrived[:-1], *spread(first, [1]), arrived[-1]]

    def after_second(*arrived):
        return [*arrived, *spread(second, [1, *range(2, near)])]

    def last(output, *arrived):
        arrived = [*arrived, *spread(second, range(near, dp // 2))]
        half = len(arrived) // 2
        return output, *result_call(arrived[:half], arrived[half:])

    grad_w_stem, (output, grad_w_qkv, grad_w_out) = sum_stem(
        stem_parts, beside, (after_first, after_second), last, dp, group
    )
    return (output.reshape(scenes, GROUPS, CAP, D), grad_w_stem, grad_w_qkv, grad_w_out)


def solution(mesh):
    sizes = dict(mesh.shape)
    return jax.shard_map(
        functools.partial(on_device, sizes["dp"], sizes["group"]),
        mesh=mesh,
        in_specs=(
            P(("dp", "group"), None, None),
            P(("dp", "group"), None, None),
            P(("dp", "group"), None),
            P(),
            P(),
            P("dp", None, "group"),
            P("group", "dp"),
            P(("dp", "group"), None, None, None),
        ),
        out_specs=(
            P(("dp", "group"), None, None, None),
            P(),
            P("dp", None, "group"),
            P("group", "dp"),
        ),
        check_vma=False,
    )
```

```python
import functools

import jax
import jax.numpy as jnp
import ml_dtypes
import numpy as np
from jax import lax
from jax.experimental import pallas as pl
from jax.experimental.pallas import tpu as pltpu
from jax.sharding import PartitionSpec as P

D = 1024
HD = 64
GROUPS = 3
CAP = 48
GRID = 12
PIX = 64
TOK = GROUPS * CAP
PAIR = 128
GROUP_BANDS = ((0, 4), (4, 8), (8, 10))
NORM_EPS = 1e-06
F32 = jnp.float32
BF16 = jnp.bfloat16
VMEM_LIMIT = 60 * 1024 * 1024


def dot_nn(a, b):
    return lax.dot_general(a, b, (((1,), (0,)), ((), ())), preferred_element_type=F32)


def dot_nt(a, b):
    return lax.dot_general(a, b, (((1,), (1,)), ((), ())), preferred_element_type=F32)


def dot_tn(a, b):
    return lax.dot_general(a, b, (((0,), (0,)), ((), ())), preferred_element_type=F32)


def live_column(c0, c1, c2):
    row = lax.broadcasted_iota(jnp.int32, (TOK, 1), 0)
    return (
        (row < c0)
        | ((row >= CAP) & (row < CAP + c1))
        | ((row >= 2 * CAP) & (row < 2 * CAP + c2))
    )


def params():
    return pltpu.CompilerParams(vmem_limit_bytes=VMEM_LIMIT)


def cost(flops, nbytes):
    return pl.CostEstimate(flops=int(flops / 1000), bytes_accessed=int(nbytes / 1000), transcendentals=0)


def stem_kernel(
    cnt_ref, idx_ref, patch_ref, w_ref, gain_ref, parts, genc_ref, og_ref,
    emb_ref, rows_ref, cols_ref,
):
    step = pl.program_id(0)
    scenes = patch_ref.shape[0]
    patch_iota = lax.broadcasted_iota(jnp.int32, (parts.shape[1], CAP), 0)
    slot = lax.broadcasted_iota(jnp.int32, (CAP, 1), 0)
    for g, (start, end) in enumerate(GROUP_BANDS):
        rows = slice(g * CAP, (g + 1) * CAP)
        width = (end - start) * PIX
        picked, placed = [], []
        for s in range(scenes):
            onehot = (idx_ref[s, g : g + 1, :] == patch_iota).astype(F32).astype(BF16).T
            picked.append(dot_nn(onehot, patch_ref[s, :, start * PIX : end * PIX]).astype(BF16))
            placed.append(
                (dot_nn(onehot, parts[0]) + dot_nn(onehot, parts[1])) + dot_nn(onehot, parts[2])
            )
            live = slot < cnt_ref[g, step * scenes + s]
            rows_ref[1, s, rows, :] = jnp.where(live, og_ref[s, rows, :].astype(F32), 0.0).astype(BF16)
        summed = dot_nn(jnp.concatenate(picked, axis=0), w_ref[start * PIX : end * PIX, :])
        for s in range(scenes):
            values = summed[s * CAP : (s + 1) * CAP] + (placed[s] + genc_ref[g : g + 1, :])
            emb = values.astype(BF16)
            emb_ref[s, rows, :] = emb
            x = emb.astype(F32)
            centre = jnp.mean(x, axis=-1, keepdims=True)
            dev = x - centre
            spread = jnp.mean(dev * dev, axis=-1, keepdims=True)
            centred = dev * lax.rsqrt(spread + NORM_EPS)
            rows_ref[0, s, rows, :] = (centred * gain_ref[...]).astype(BF16)
            cols_ref[s, rows, :width] = picked[s]
            if width < cols_ref.shape[2]:
                cols_ref[s, rows, width:] = jnp.zeros((CAP, cols_ref.shape[2] - width), BF16)


def stem_call(counts, index, patches, w_stem, gain, table, genc, out_grad):
    scenes, patch_count, width = patches.shape
    block = 3 if scenes % 3 == 0 else 1
    col_width = max(e - s for s, e in GROUP_BANDS) * PIX
    per = lambda shape: pl.BlockSpec((block,) + shape, lambda i: (i, 0, 0))
    whole = lambda a: pl.BlockSpec(a.shape, lambda i: (0,) * a.ndim)
    return pl.pallas_call(
        stem_kernel,
        grid=(scenes // block,),
        in_specs=[
            pl.BlockSpec(memory_space=pltpu.SMEM),
            per((GROUPS, CAP)),
            per((patch_count, width)),
            whole(w_stem),
            whole(gain),
            whole(table),
            whole(genc),
            per((TOK, D)),
        ],
        out_specs=[
            per((TOK, D)),
            pl.BlockSpec((2, block, TOK, D), lambda i: (0, i, 0, 0)),
            per((TOK, col_width)),
        ],
        out_shape=[
            jax.ShapeDtypeStruct((scenes, TOK, D), BF16),
            jax.ShapeDtypeStruct((2, scenes, TOK, D), BF16),
            jax.ShapeDtypeStruct((scenes, TOK, col_width), BF16),
        ],
        compiler_params=params(),
        cost_estimate=cost(8e9, 12e6),
        name="stem_norm",
    )(counts, index, patches, w_stem, gain, table, genc, out_grad)


def pack_kernel(qkv_ref, out_w_ref, pack_ref):
    count, _, width = qkv_ref.shape
    for c in range(count):
        pack_ref[:, c * width : (c + 1) * width] = qkv_ref[c]
    pack_ref[:, count * width :] = out_w_ref[...].T


def pack_call(w_qkv, w_out):
    parts = jnp.transpose(w_qkv, (1, 0, 2))
    return pl.pallas_call(
        pack_kernel,
        out_shape=jax.ShapeDtypeStruct((w_qkv.shape[0], 3 * w_qkv.shape[2] + w_out.shape[0]), BF16),
        compiler_params=params(),
        cost_estimate=cost(1e6, 5e5),
        name="pack_weights",
    )(parts, w_out)


def attention_kernel(
    packs, blocks, dp, cnt_ref, owner_ref, low_ref, na_ref, nb_ref, ga_ref, gb_ref, *refs
):
    earlier, refs = refs[: 2 * (packs or 0)], refs[2 * (packs or 0) :]
    blocks, refs = refs[:blocks], refs[blocks:]
    out_ref, w_ref, *refs = refs
    keeps, others, refs = refs[:2], refs[2:4], refs[4:]
    n_all, g_all, pack_all, qkv, total = refs[-5:]
    half, step = pl.program_id(0), pl.program_id(1)
    rows = qkv.shape[0]
    here = pl.ds(pl.multiple_of((half * pl.num_programs(1) + step) * rows, 16), rows)
    scenes = rows // TOK
    width = w_ref.shape[1] // 4

    @pl.when((half == 0) & (step == 0))
    def _():
        size = blocks[0].shape[0]
        for b, block in enumerate(blocks):
            w_ref[pl.ds(pl.multiple_of(owner_ref[b] * size, size), size), :] = block[...]

    @pl.when(half == 0)
    def _():
        n_all[here, :] = na_ref[0]
        g_all[here, :] = ga_ref[0]

    @pl.when(half != 0)
    def _():
        n_all[here, :] = nb_ref[0]
        g_all[here, :] = gb_ref[0]

    qkv[:, : 3 * width] = dot_nn(n_all[here, :], w_ref[:, : 3 * width]).astype(BF16)
    qkv[:, 3 * width :] = dot_nn(g_all[here, :], w_ref[:, 3 * width :]).astype(BF16)
    heads = width // HD
    lane = lax.broadcasted_iota(jnp.int32, (1, width), 1)
    masks = [(lane // HD == h).astype(F32).astype(BF16) for h in range(heads)]
    scale = jnp.asarray(HD ** (-0.5), BF16)
    first_of_pair = lax.broadcasted_iota(jnp.int32, (1, PAIR), 1) < HD

    def own_lanes(tall):
        tiles = []
        for t in range(width // PAIR):
            at = slice(t * PAIR, (t + 1) * PAIR)
            one = tall[2 * t * TOK : (2 * t + 1) * TOK, at]
            two = tall[(2 * t + 1) * TOK : (2 * t + 2) * TOK, at]
            tiles.append(jnp.where(first_of_pair, one, two))
        return jnp.concatenate(tiles, axis=1)

    def scene_body(s, _):
        base = pl.multiple_of(s * TOK, 16)
        at = pl.ds(base, TOK)
        scene = step * scenes + s
        live = live_column(*[cnt_ref[half, g, scene] for g in range(GROUPS)])
        bias = jnp.where(live, 0.0, -1e30)
        q, k, v, dc = [qkv[at, c * width : (c + 1) * width] for c in range(4)]
        tall_q = jnp.concatenate([q * (m * scale) for m in masks], axis=0)
        tall_dc = jnp.concatenate([dc * m for m in masks], axis=0)
        scores = dot_nt(k, tall_q)
        grad_probs = dot_nt(v, tall_dc)
        probs_parts, score_parts = [], []
        for start in range(0, heads * TOK, PAIR):
            cols = slice(start, min(start + PAIR, heads * TOK))
            part = scores[:, cols] + bias
            lifted = jnp.exp(part - jnp.max(part, axis=0, keepdims=True))
            probs = lifted * (1.0 / jnp.sum(lifted, axis=0, keepdims=True))
            weighted = probs * grad_probs[:, cols]
            inner = jnp.sum(weighted, axis=0, keepdims=True)
            probs_parts.append(probs.astype(BF16))
            score_parts.append((weighted - probs * inner).astype(BF16))
        half_probs = jnp.concatenate(probs_parts, axis=1)
        grad_score = jnp.concatenate(score_parts, axis=1)
        out_ref[at, :width] = (own_lanes(dot_tn(grad_score, k)) * HD ** (-0.5)).astype(BF16)
        out_ref[at, width : 2 * width] = dot_nn(grad_score, tall_q).astype(BF16)
        out_ref[at, 2 * width : 3 * width] = dot_nn(half_probs, tall_dc).astype(BF16)
        out_ref[at, 3 * width :] = own_lanes(dot_tn(half_probs, v)).astype(BF16)
        return 0

    lax.fori_loop(0, scenes, scene_body, 0, unroll=True)
    pack_all[here, :] = out_ref[...]

    @pl.when((half == pl.num_programs(0) - 1) & (step == pl.num_programs(1) - 1))
    def _():
        total[:, : 3 * width] = dot_tn(n_all[...], pack_all[:, : 3 * width])
        total[:, 3 * width :] = dot_tn(g_all[...], pack_all[:, 3 * width :])
        size = total.shape[0] // dp
        low = low_ref[0]
        for b in range(dp // 2):
            at = slice(b * size, (b + 1) * size)
            mine = pl.multiple_of((2 * b + low) * size, size)
            other = pl.multiple_of((2 * b + 1 - low) * size, size)
            for c in range(2):
                cols = slice(c * 2 * width, (c + 1) * 2 * width)
                keeps[c][at, :] = total[pl.ds(mine, size), cols].astype(keeps[c].dtype)
                others[c][at, :] = total[pl.ds(other, size), cols].astype(others[c].dtype)

    if packs is not None:
        back = dot_nt(out_ref[:, : 3 * width], w_ref[:, : 3 * width])
        for pack_ref, weight_ref in zip(earlier[:packs], earlier[packs:]):
            back = back + dot_nt(pack_ref[...], weight_ref[...])

        @pl.when(half == 0)
        def _():
            refs[0][...] = back

        @pl.when(half != 0)
        def _():
            refs[1][...] = back.astype(BF16)


def block_rows(tokens):
    return 3 * TOK if tokens % (3 * TOK) == 0 else TOK


def two_halves(rows, steps, lead):
    shape = (1,) * len(lead) + (rows, D)
    first = pl.BlockSpec(shape, lambda h, i: lead + (jnp.where(h == 0, i, steps - 1), 0))
    second = pl.BlockSpec(shape, lambda h, i: lead + (jnp.where(h == 0, 0, i), 0))
    return [first, second]


SCALARS = pl.BlockSpec(memory_space=pltpu.SMEM)


def attention_call(counts, owners, low, own, far, earlier, blocks, dp):
    tokens = own.shape[1]
    rows = block_rows(tokens)
    steps = tokens // rows
    cols = blocks[0].shape[1]
    whole = lambda shape: pl.BlockSpec(shape, lambda h, i: (0, 0), pipeline_mode=pl.Buffered(1))
    at = lambda h, i: (h * steps + i, 0)
    packs = None if earlier is None else len(earlier[0])
    back = [] if earlier is None else two_halves(rows, steps, ())
    kind = BF16 if earlier is None else F32
    grads = [jax.ShapeDtypeStruct((D // 2, c), kind) for c in [cols // 2] * 4]
    return pl.pallas_call(
        functools.partial(attention_kernel, packs, len(blocks), dp),
        grid=(2, steps),
        in_specs=[SCALARS] * 3
        + two_halves(rows, steps, (0,))
        + two_halves(rows, steps, (1,))
        + [pl.BlockSpec((rows, cols // 4 * 3), at)] * (packs or 0)
        + [whole((D, cols // 4 * 3))] * (packs or 0)
        + [whole(b.shape) for b in blocks],
        out_specs=[pl.BlockSpec((rows, cols), at), whole((D, cols))] + [whole(g.shape) for g in grads] + back,
        out_shape=[
            jax.ShapeDtypeStruct((2 * tokens, cols), BF16),
            jax.ShapeDtypeStruct((D, cols), BF16),
            *grads,
        ]
        + [jax.ShapeDtypeStruct((tokens, D), kind) for kind in (F32, BF16)[: len(back)]],
        scratch_shapes=[
            pltpu.VMEM((2 * tokens, D), BF16),
            pltpu.VMEM((2 * tokens, D), BF16),
            pltpu.VMEM((2 * tokens, cols), BF16),
            pltpu.VMEM((rows, cols), BF16),
            pltpu.VMEM((D, cols), F32),
        ],
        compiler_params=params(),
        cost_estimate=cost(20e9, 14e6),
        name="attention",
    )(counts, owners, low, own, far, own, far, *[x for group in earlier or () for x in group], *blocks)


def combine_kernel(counts, place_ref, *refs):
    ins, refs = refs[: sum(counts)], refs[sum(counts) :]
    rows = refs[0].shape[0]
    place = place_ref[0]
    for j, ref in enumerate(refs):
        at = pl.ds(pl.multiple_of((place ^ j) * rows, rows), rows)
        total = None
        first = 0
        for count in counts:
            pieces = [r[at, :].astype(F32) for r in ins[first : first + count]]
            new = pieces[0] if count == 1 else jnp.concatenate(pieces, axis=1)
            total = new if total is None else total + new
            first += count
        ref[...] = total.astype(ref.dtype)


def combine_call(place, parts, dtypes):
    ins = [piece for part in parts for piece in part]
    rows, cols = ins[0].shape[0] // len(dtypes), sum(piece.shape[1] for piece in parts[0])
    whole = lambda a: pl.BlockSpec(a.shape, lambda: (0, 0))
    return pl.pallas_call(
        functools.partial(combine_kernel, [len(part) for part in parts]),
        in_specs=[SCALARS] + [whole(a) for a in ins],
        out_specs=[pl.BlockSpec((rows, cols), lambda: (0, 0))] * len(dtypes),
        out_shape=[jax.ShapeDtypeStruct((rows, cols), d) for d in dtypes],
        compiler_params=params(),
        cost_estimate=cost(1e6, 5e6),
        name="combine",
    )(place, *ins)


def split_kernel(count, place_ref, *refs):
    total = refs[0][...]
    for ref in refs[1:count]:
        total = total + ref[...]
    outs = refs[count:]
    cols = outs[0].shape[1]
    place = place_ref[0]
    for j, out_ref in enumerate(outs):
        block = total[:, :cols]
        for b in range(1, len(outs)):
            block = jnp.where((place ^ j) == b, total[:, b * cols : (b + 1) * cols], block)
        out_ref[...] = block


def split_call(place, parts, blocks):
    rows, cols = parts[0].shape
    return pl.pallas_call(
        functools.partial(split_kernel, len(parts)),
        in_specs=[SCALARS] + [pl.BlockSpec((rows, cols), lambda: (0, 0))] * len(parts),
        out_specs=[pl.BlockSpec((rows, cols // blocks), lambda: (0, 0))] * blocks,
        out_shape=[jax.ShapeDtypeStruct((rows, cols // blocks), F32)] * blocks,
        compiler_params=params(),
        cost_estimate=cost(1e6, 2e6),
        name="split_sum",
    )(place, *parts)


def result_kernel(count, *refs):
    halves, qkv_ref, out_ref = (refs[:count], refs[count:-2]), refs[-2], refs[-1]
    first, second = [functools.reduce(lambda a, b: a + b, [r[...].astype(F32) for r in half]) for half in halves]
    width = first.shape[1] // 2
    qkv_ref[0] = first[:, :width]
    qkv_ref[1] = first[:, width:]
    qkv_ref[2] = second[:, :width]
    out_ref[...] = second[:, width:].T


def result_call(first, second):
    rows, cols = first[0].shape
    qkv, out = pl.pallas_call(
        functools.partial(result_kernel, len(first)),
        out_shape=[
            jax.ShapeDtypeStruct((3, rows, cols // 2), F32),
            jax.ShapeDtypeStruct((cols // 2, rows), F32),
        ],
        compiler_params=params(),
        cost_estimate=cost(1e6, 2e6),
        name="weight_results",
    )(*first, *second)
    return jnp.transpose(qkv, (1, 0, 2)), out


def mixed_product(context_refs, weight_refs):
    total = None
    for context_ref, w_ref in zip(context_refs, weight_refs):
        new = dot_nt(context_ref[...], w_ref[...])
        total = new if total is None else total + new
    return total


def context_specs(rows, packs, weights, first):
    width = packs[0].shape[1] // 4
    return [pl.BlockSpec((rows, width), lambda i: (first + i, 3))] * len(packs) + [
        pl.BlockSpec((D, width), lambda i: (0, 3))
    ] * len(weights)


def mixed_kernel(count, *refs):
    refs[-1][...] = mixed_product(refs[:count], refs[count : 2 * count]).astype(BF16)


def mixed_call(packs, weights):
    tokens = packs[0].shape[0] // 2
    rows = block_rows(tokens)
    return pl.pallas_call(
        functools.partial(mixed_kernel, len(packs)),
        grid=(tokens // rows,),
        in_specs=context_specs(rows, packs, weights, tokens // rows),
        out_specs=pl.BlockSpec((rows, D), lambda i: (i, 0)),
        out_shape=jax.ShapeDtypeStruct((tokens, D), BF16),
        compiler_params=params(),
        cost_estimate=cost(2e9, 5e6),
        name="mixed",
    )(*packs, *weights)


def tail_kernel(core_ref, own_ref, recv_ref, emb_ref, gl_ref, cols_ref, gain_ref, keep_ref, first_ref, second_ref, acc):
    step = pl.program_id(0)
    rows = emb_ref.shape[0]
    scenes = rows // TOK

    @pl.when(step == 0)
    def _():
        acc[...] = jnp.zeros_like(acc)

    grad_normed = own_ref[...] + recv_ref[...].astype(F32)
    x = emb_ref[...].astype(F32)
    dev = x - jnp.mean(x, axis=-1, keepdims=True)
    inv_std = lax.rsqrt(jnp.mean(dev * dev, axis=-1, keepdims=True) + NORM_EPS)
    centred = dev * inv_std
    scaled = grad_normed * gain_ref[...]
    first_mean = jnp.mean(scaled, axis=-1, keepdims=True)
    second_mean = jnp.mean(scaled * centred, axis=-1, keepdims=True)
    back = inv_std * (scaled - first_mean - centred * second_mean)
    grad_in = (gl_ref[0].astype(F32) + back).astype(BF16)
    for g, (start, end) in enumerate(GROUP_BANDS):
        at = [slice(s * TOK + g * CAP, s * TOK + (g + 1) * CAP) for s in range(scenes)]
        columns = jnp.concatenate([cols_ref[a, : (end - start) * PIX] for a in at], axis=0)
        grads = jnp.concatenate([grad_in[a] for a in at], axis=0)
        acc[start * PIX : end * PIX, :] += dot_tn(columns, grads)

    @pl.when(step == pl.num_programs(0) - 1)
    def _():
        size = keep_ref.shape[0]
        core = core_ref[0]
        keep_ref[...] = acc[pl.ds(pl.multiple_of(core * size, size), size), :]
        other = pl.ds(pl.multiple_of((1 - core) * size, size), size)
        first_ref[...] = acc[other, : D // 2]
        second_ref[...] = acc[other, D // 2 :]


def tail_call(core, own, recv, emb, rows_own, cols, gain):
    tokens = emb.shape[0]
    rows = 2 * TOK if tokens % (2 * TOK) == 0 else TOK
    per = lambda a: pl.BlockSpec((rows, a.shape[1]), lambda i: (i, 0))
    stem_rows = GROUP_BANDS[-1][1] * PIX
    keep = jax.ShapeDtypeStruct((stem_rows // 2, D), F32)
    send = jax.ShapeDtypeStruct((stem_rows // 2, D // 2), F32)
    return pl.pallas_call(
        tail_kernel,
        grid=(tokens // rows,),
        in_specs=[SCALARS, per(own), per(recv), per(emb), pl.BlockSpec((1, rows, D), lambda i: (1, i, 0)), per(cols)]
        + [pl.BlockSpec(gain.shape, lambda i: (0, 0))],
        out_specs=[pl.BlockSpec(a.shape, lambda i: (0, 0)) for a in (keep, send, send)],
        out_shape=[keep, send, send],
        scratch_shapes=[pltpu.VMEM((stem_rows, D), F32)],
        compiler_params=params(),
        cost_estimate=cost(10e9, 12e6),
        name="tail",
    )(core, own, recv, emb, rows_own, cols, gain)


def output_kernel(count, cnt_ref, recv_ref, emb_ref, *refs):
    out_ref = refs[-1]
    step = pl.program_id(0)
    scenes = emb_ref.shape[0] // TOK
    mixed = recv_ref[...].astype(F32) + mixed_product(refs[:count], refs[count : 2 * count])
    total = emb_ref[...].astype(F32) + mixed
    for s in range(scenes):
        scene = step * scenes + s
        live = live_column(*[cnt_ref[g, scene] for g in range(GROUPS)])
        at = slice(s * TOK, (s + 1) * TOK)
        out_ref[at, :] = jnp.where(live, total[at], 0.0).astype(BF16)


def output_call(counts, recv, emb, packs, weights):
    tokens = emb.shape[0]
    rows = 2 * TOK if tokens % (2 * TOK) == 0 else TOK
    per = lambda a: pl.BlockSpec((rows, a.shape[1]), lambda i: (i, 0))
    return pl.pallas_call(
        functools.partial(output_kernel, len(packs)),
        grid=(tokens // rows,),
        in_specs=[SCALARS, per(recv), per(emb)]
        + context_specs(rows, packs, weights, 0),
        out_specs=per(emb),
        out_shape=jax.ShapeDtypeStruct(emb.shape, BF16),
        compiler_params=params(),
        cost_estimate=cost(5e9, 10e6),
        name="layer_output",
    )(counts, recv, emb, *packs, *weights)


def swap(x, axis, size, bit):
    return lax.ppermute(x, axis, [(i, i ^ bit) for i in range(size)])


def together(*values):
    return lax.optimization_barrier(values)


class Ring:
    def __init__(self, x, axis, size):
        self.axis, self.size = axis, size
        order = list(range(0, size, 2)) + list(range(size - 1, 0, -2))
        self.forward = [(order[i], order[(i + 1) % size]) for i in range(size)]
        self.backward = [(order[(i + 1) % size], order[i]) for i in range(size)]
        self.ahead, self.behind = [x], [x]

    def send(self):
        moved = [lax.ppermute(self.ahead[-1], self.axis, self.forward)]
        if len(self.behind) <= (self.size - 1) // 2:
            moved.append(lax.ppermute(self.behind[-1], self.axis, self.backward))
        return moved

    def receive(self, moved):
        self.ahead.append(moved[0])
        self.behind.extend(moved[1:])

    @property
    def steps(self):
        return len(self.ahead) - 1

    def owners(self, ahead, behind):
        size = self.size
        me = lax.axis_index(self.axis)
        here = jnp.where(me % 2 == 0, me // 2, size - 1 - me // 2)
        distances = [-s for s in range(ahead)] + list(range(1, behind))
        at = (here + size + jnp.array(distances, jnp.int32)) % size
        return jnp.where(at < size // 2, 2 * at, 2 * (size - 1 - at) + 1)


def step_all(rings, *beside):
    moved, beside = together([ring.send() for ring in rings], beside)
    for ring, blocks in zip(rings, moved):
        ring.receive(blocks)
    return beside


def halve_stem(recv, keep, group):
    mine = lax.axis_index("group") // 2 * 2 + lax.axis_index("dp") % 2
    return combine_call(mine.reshape(1), [[keep], recv], [F32] * (group // 2 * 2))


def sum_stem(parts, beside, after, last, dp, group):
    core = lax.axis_index("group") % 2
    far = lax.axis_index("group") // 2
    low = lax.axis_index("dp") % 2
    high = lax.axis_index("dp") // 2
    fars, highs = group // 2, dp // 2
    mine = far * 2 + low
    small, width = parts[0].shape
    rows = 2 * fars * small

    def hop(block, f, b):
        if f:
            pairs = [
                (d * group + g, (d ^ b) * group + (g ^ (2 * f))) for d in range(dp) for g in range(group)
            ]
            return lax.ppermute(block, ("dp", "group"), pairs)
        return swap(block, "dp", dp, b)

    hops = [(k // 2, k % 2) for k in range(1, 2 * fars)]
    arrived = [hop(part, f, b) for part, (f, b) in zip(parts[1:], hops)]
    arrived, beside = together(arrived, beside)
    beside = after[0](*beside)
    cols = width // highs
    part, *away = split_call(high.reshape(1), [parts[0], *arrived], highs)
    arrived = [swap(a, "dp", dp, 2 * (j + 1)) for j, a in enumerate(away)]
    arrived, beside = together(arrived, beside)
    for block in arrived:
        part = part + block
    part = part.astype(BF16)
    line = jnp.zeros((small, width), BF16)
    line = lax.dynamic_update_slice_in_dim(line, part, high * cols, 1)
    arrived = [swap(part, "dp", dp, 2 * j) for j in range(1, highs)]
    arrived, beside = together(arrived, after[1](*beside))
    for j, block in enumerate(arrived):
        line = lax.dynamic_update_slice_in_dim(line, block, (high ^ (j + 1)) * cols, 1)
    block = jnp.zeros((rows, width), BF16)
    block = lax.dynamic_update_slice_in_dim(block, line, mine * small, 0)
    arrived, beside = together([hop(line, f, b) for f, b in hops], last(*beside))
    for (f, b), piece in zip(hops, arrived):
        target = (far ^ f) * 2 + (low ^ b)
        block = lax.dynamic_update_slice_in_dim(block, piece, target * small, 0)
    partner = swap(block, "group", group, 1)
    whole = jnp.zeros((2 * rows, width), F32)
    whole = lax.dynamic_update_slice_in_dim(whole, block.astype(F32), core * rows, 0)
    whole = lax.dynamic_update_slice_in_dim(whole, partner.astype(F32), (1 - core) * rows, 0)
    return whole, beside


def encoding_tables(patch_count):
    quarter = D // 4
    half_width = D // 2
    power = lambda n: np.power(np.float32(10000.0), -np.arange(n, dtype=np.float32) / np.float32(n))
    at = np.arange(GRID).astype(np.float32)[:, None] * power(quarter)
    both = np.concatenate([np.sin(at), np.cos(at)], axis=-1)
    patch = np.arange(patch_count)
    rest = np.concatenate([both[patch // GRID], both[patch % GRID]], axis=-1).astype(np.float32)
    parts = []
    for _ in range(3):
        parts.append(rest.astype(ml_dtypes.bfloat16))
        rest = rest - parts[-1].astype(np.float32)
    group_at = np.arange(GROUPS).astype(np.float32)[:, None] * power(half_width)
    return np.stack(parts), np.concatenate([np.sin(group_at), np.cos(group_at)], axis=-1).astype(np.float32)


def on_device(dp, group, patches, vis_index, vis_count, w_stem, ln_gain, w_qkv, w_out, out_grad):
    scenes = patches.shape[0]
    tokens = scenes * TOK
    width = w_qkv.shape[2]
    fars = range(1, group // 2)
    rests = range(1, dp // 2)
    dp_low, dp_high = lax.axis_index("dp") % 2, lax.axis_index("dp") // 2
    low, high = dp_low.reshape(1), dp_high.reshape(1)
    core = (lax.axis_index("group") % 2).reshape(1)

    shard = pack_call(w_qkv, w_out)
    cross = lambda x, f: swap(x, "group", group, 2 * f)
    far_shards = [cross(shard, f) for f in fars]
    counts = vis_count.astype(jnp.int32).T
    counts_far = swap(counts, "group", group, 1)
    table, genc = encoding_tables(patches.shape[1])
    gain = ln_gain.reshape(1, D)
    stem = stem_call(
        counts,
        vis_index,
        patches,
        w_stem,
        gain,
        jnp.asarray(table),
        jnp.asarray(genc),
        out_grad.reshape(scenes, TOK, D),
    )
    stem, both_counts, far_shards = together(stem, jnp.stack([counts, counts_far]), far_shards)
    rings = [Ring(x, "dp", dp) for x in far_shards]
    ring = rings[0]
    owners = ring.owners(dp // 2 + 1, dp // 2)
    emb = stem[0].reshape(tokens, D)
    both = [stem[1].reshape(2, tokens, D)]
    cols = stem[2].reshape(tokens, stem[2].shape[2])
    both.append(swap(both[0], "group", group, 1))
    own_ahead, own_behind = [], []
    both, owners = step_all(rings, both, owners)
    while ring.steps < dp // 2:
        a, b = len(own_ahead), len(own_behind)
        own_ahead.append(cross(ring.ahead[-1], 1))
        if a:
            own_behind.append(cross(ring.behind[a], 1))
        ahead, behind = slice(max(a - 1, 0), a), slice(max(b - 2, 0), max(b - 1, 0))
        own_ahead[ahead], own_behind[behind] = step_all(rings, own_ahead[ahead], own_behind[behind])
    ring.ahead, ring.behind = together(ring.ahead, ring.behind)
    own_ahead.append(cross(ring.ahead[-1], 1))
    own_behind.extend(cross(x, 1) for x in ring.behind[len(own_behind) + 1 :])

    packs, weights, crossing = [], [], []
    for f in list(fars) + [0]:
        if f:
            blocks = rings[f - 1].ahead + rings[f - 1].behind[1:]
        else:
            blocks = [shard] + own_ahead + own_behind
        made = attention_call(both_counts, owners, low, *both, None if f else (packs, weights), blocks, dp)
        if f == 1:
            made, own_ahead[-2:], own_behind[-3:] = together(made, own_ahead[-2:], own_behind[-3:])
        elif f:
            made = together(*made)
        else:
            made, arrived = together(made, [x[:3] for x in crossing])
        pack, weight, keep, other, back = made[0], made[1], made[2:4], made[4:6], made[6:]
        packs.append(pack)
        weights.append(weight)
        if f:
            crossing.append([cross(x, f) for x in (*other, keep[0])] + [keep[1]])
    back_far = swap(back[1], "group", group, 1)
    coming = []
    for c in range(2):
        send = other[c]
        for x in arrived:
            send = send + x[c].astype(F32)
        send = send.astype(BF16)
        if c == 0:
            send, last_keeps = together(send, [x[3] for x in crossing])
        coming.append(swap(send, "dp", dp, 1))
    last_keeps = [cross(x, f) for f, x in zip(fars, last_keeps)]
    stem_made, coming[0], last_keeps = together(
        tail_call(core, back[0], back_far, emb, both[0], cols, gain), coming[0], last_keeps
    )
    stem_keep, *stem_recv = stem_made
    stem_recv = [swap(x, "group", group, 1) for x in stem_recv]
    kinds = [F32 if j < 2 else BF16 for j in range(dp // 2)]
    second_leg = lambda c: combine_call(high, [[x] for x in keeps[c] + [coming[c]]], kinds)
    spread = lambda blocks, js: [swap(blocks[j], "dp", dp, 2 * j) for j in js]
    stem_recv = together(*stem_recv)
    keeps = [[keep[0]] + [x[2] for x in arrived], [keep[1]] + list(last_keeps)]
    stem_parts = halve_stem(stem_recv, stem_keep, group)
    _, coming[0], keeps = together(stem_parts, coming[0], keeps)
    first = second_leg(0)
    first_rest = spread(first, rests[1:])
    second = second_leg(1)
    near = dp // 2 * 3 // 4
    beside = [mixed_call(packs, weights), first[0], *first_rest, second[0]]
    def after_first(mixed, *arrived):
        output = output_call(counts, swap(mixed, "group", group, 1), emb, packs, weights)
        return [output, *arrived[:-1], *spread(first, [1]), arrived[-1]]

    def after_second(*arrived):
        return [*arrived, *spread(second, [1, *range(2, near)])]

    def last(output, *arrived):
        arrived = [*arrived, *spread(second, range(near, dp // 2))]
        half = len(arrived) // 2
        return output, *result_call(arrived[:half], arrived[half:])

    grad_w_stem, (output, grad_w_qkv, grad_w_out) = sum_stem(
        stem_parts, beside, (after_first, after_second), last, dp, group
    )
    return (output.reshape(scenes, GROUPS, CAP, D), grad_w_stem, grad_w_qkv, grad_w_out)


def solution(mesh):
    sizes = dict(mesh.shape)
    return jax.shard_map(
        functools.partial(on_device, sizes["dp"], sizes["group"]),
        mesh=mesh,
        in_specs=(
            P(("dp", "group"), None, None),
            P(("dp", "group"), None, None),
            P(("dp", "group"), None),
            P(),
            P(),
            P("dp", None, "group"),
            P("group", "dp"),
            P(("dp", "group"), None, None, None),
        ),
        out_specs=(
            P(("dp", "group"), None, None, None),
            P(),
            P("dp", None, "group"),
            P("group", "dp"),
        ),
        check_vma=False,
    )
```

```python
import functools

import jax
import jax.numpy as jnp
import ml_dtypes
import numpy as np
from jax import lax
from jax.experimental import pallas as pl
from jax.experimental.pallas import tpu as pltpu
from jax.sharding import PartitionSpec as P

D = 1024
HD = 64
GROUPS = 3
CAP = 48
GRID = 12
PIX = 64
TOK = GROUPS * CAP
PAIR = 128
GROUP_BANDS = ((0, 4), (4, 8), (8, 10))
NORM_EPS = 1e-06
F32 = jnp.float32
BF16 = jnp.bfloat16
VMEM_LIMIT = 60 * 1024 * 1024


def dot_nn(a, b):
    return lax.dot_general(a, b, (((1,), (0,)), ((), ())), preferred_element_type=F32)


def dot_nt(a, b):
    return lax.dot_general(a, b, (((1,), (1,)), ((), ())), preferred_element_type=F32)


def dot_tn(a, b):
    return lax.dot_general(a, b, (((0,), (0,)), ((), ())), preferred_element_type=F32)


def live_column(c0, c1, c2):
    row = lax.broadcasted_iota(jnp.int32, (TOK, 1), 0)
    return (
        (row < c0)
        | ((row >= CAP) & (row < CAP + c1))
        | ((row >= 2 * CAP) & (row < 2 * CAP + c2))
    )


def params():
    return pltpu.CompilerParams(vmem_limit_bytes=VMEM_LIMIT)


def cost(flops, nbytes):
    return pl.CostEstimate(flops=int(flops / 1000), bytes_accessed=int(nbytes / 1000), transcendentals=0)


def stem_kernel(
    cnt_ref, idx_ref, patch_ref, w_ref, gain_ref, parts, genc_ref, og_ref,
    emb_ref, rows_ref, cols_ref,
):
    step = pl.program_id(0)
    scenes = patch_ref.shape[0]
    patch_iota = lax.broadcasted_iota(jnp.int32, (parts.shape[1], CAP), 0)
    slot = lax.broadcasted_iota(jnp.int32, (CAP, 1), 0)
    for g, (start, end) in enumerate(GROUP_BANDS):
        rows = slice(g * CAP, (g + 1) * CAP)
        width = (end - start) * PIX
        picked, placed = [], []
        for s in range(scenes):
            onehot = (idx_ref[s, g : g + 1, :] == patch_iota).astype(F32).astype(BF16).T
            picked.append(dot_nn(onehot, patch_ref[s, :, start * PIX : end * PIX]).astype(BF16))
            placed.append(
                (dot_nn(onehot, parts[0]) + dot_nn(onehot, parts[1])) + dot_nn(onehot, parts[2])
            )
            live = slot < cnt_ref[g, step * scenes + s]
            rows_ref[1, s, rows, :] = jnp.where(live, og_ref[s, rows, :].astype(F32), 0.0).astype(BF16)
        summed = dot_nn(jnp.concatenate(picked, axis=0), w_ref[start * PIX : end * PIX, :])
        for s in range(scenes):
            values = summed[s * CAP : (s + 1) * CAP] + (placed[s] + genc_ref[g : g + 1, :])
            emb = values.astype(BF16)
            emb_ref[s, rows, :] = emb
            x = emb.astype(F32)
            centre = jnp.mean(x, axis=-1, keepdims=True)
            dev = x - centre
            spread = jnp.mean(dev * dev, axis=-1, keepdims=True)
            centred = dev * lax.rsqrt(spread + NORM_EPS)
            rows_ref[0, s, rows, :] = (centred * gain_ref[...]).astype(BF16)
            cols_ref[s, rows, :width] = picked[s]
            if width < cols_ref.shape[2]:
                cols_ref[s, rows, width:] = jnp.zeros((CAP, cols_ref.shape[2] - width), BF16)


def stem_call(counts, index, patches, w_stem, gain, table, genc, out_grad):
    scenes, patch_count, width = patches.shape
    block = 3 if scenes % 3 == 0 else 1
    col_width = max(e - s for s, e in GROUP_BANDS) * PIX
    per = lambda shape: pl.BlockSpec((block,) + shape, lambda i: (i, 0, 0))
    whole = lambda a: pl.BlockSpec(a.shape, lambda i: (0,) * a.ndim)
    return pl.pallas_call(
        stem_kernel,
        grid=(scenes // block,),
        in_specs=[
            pl.BlockSpec(memory_space=pltpu.SMEM),
            per((GROUPS, CAP)),
            per((patch_count, width)),
            whole(w_stem),
            whole(gain),
            whole(table),
            whole(genc),
            per((TOK, D)),
        ],
        out_specs=[
            per((TOK, D)),
            pl.BlockSpec((2, block, TOK, D), lambda i: (0, i, 0, 0)),
            per((TOK, col_width)),
        ],
        out_shape=[
            jax.ShapeDtypeStruct((scenes, TOK, D), BF16),
            jax.ShapeDtypeStruct((2, scenes, TOK, D), BF16),
            jax.ShapeDtypeStruct((scenes, TOK, col_width), BF16),
        ],
        compiler_params=params(),
        cost_estimate=cost(8e9, 12e6),
        name="stem_norm",
    )(counts, index, patches, w_stem, gain, table, genc, out_grad)


def pack_kernel(qkv_ref, out_w_ref, pack_ref):
    count, _, width = qkv_ref.shape
    for c in range(count):
        pack_ref[:, c * width : (c + 1) * width] = qkv_ref[c]
    pack_ref[:, count * width :] = out_w_ref[...].T


def pack_call(w_qkv, w_out):
    parts = jnp.transpose(w_qkv, (1, 0, 2))
    return pl.pallas_call(
        pack_kernel,
        out_shape=jax.ShapeDtypeStruct((w_qkv.shape[0], 3 * w_qkv.shape[2] + w_out.shape[0]), BF16),
        compiler_params=params(),
        cost_estimate=cost(1e6, 5e5),
        name="pack_weights",
    )(parts, w_out)


def attention_kernel(
    packs, blocks, dp, cnt_ref, owner_ref, low_ref, na_ref, nb_ref, ga_ref, gb_ref, *refs
):
    earlier, refs = refs[: 2 * (packs or 0)], refs[2 * (packs or 0) :]
    blocks, refs = refs[:blocks], refs[blocks:]
    out_ref, w_ref, *refs = refs
    keeps, others, refs = refs[:2], refs[2:4], refs[4:]
    n_all, g_all, pack_all, qkv, total = refs[-5:]
    half, step = pl.program_id(0), pl.program_id(1)
    rows = qkv.shape[0]
    here = pl.ds(pl.multiple_of((half * pl.num_programs(1) + step) * rows, 16), rows)
    scenes = rows // TOK
    width = w_ref.shape[1] // 4

    @pl.when((half == 0) & (step == 0))
    def _():
        size = blocks[0].shape[0]
        for b, block in enumerate(blocks):
            w_ref[pl.ds(pl.multiple_of(owner_ref[b] * size, size), size), :] = block[...]

    @pl.when(half == 0)
    def _():
        n_all[here, :] = na_ref[0]
        g_all[here, :] = ga_ref[0]

    @pl.when(half != 0)
    def _():
        n_all[here, :] = nb_ref[0]
        g_all[here, :] = gb_ref[0]

    qkv[:, : 3 * width] = dot_nn(n_all[here, :], w_ref[:, : 3 * width]).astype(BF16)
    qkv[:, 3 * width :] = dot_nn(g_all[here, :], w_ref[:, 3 * width :]).astype(BF16)
    heads = width // HD
    lane = lax.broadcasted_iota(jnp.int32, (1, width), 1)
    masks = [(lane // HD == h).astype(F32).astype(BF16) for h in range(heads)]
    scale = jnp.asarray(HD ** (-0.5), BF16)
    first_of_pair = lax.broadcasted_iota(jnp.int32, (1, PAIR), 1) < HD

    def own_lanes(tall):
        tiles = []
        for t in range(width // PAIR):
            at = slice(t * PAIR, (t + 1) * PAIR)
            one = tall[2 * t * TOK : (2 * t + 1) * TOK, at]
            two = tall[(2 * t + 1) * TOK : (2 * t + 2) * TOK, at]
            tiles.append(jnp.where(first_of_pair, one, two))
        return jnp.concatenate(tiles, axis=1)

    def scene_body(s, _):
        base = pl.multiple_of(s * TOK, 16)
        at = pl.ds(base, TOK)
        scene = step * scenes + s
        live = live_column(*[cnt_ref[half, g, scene] for g in range(GROUPS)])
        bias = jnp.where(live, 0.0, -1e30)
        q, k, v, dc = [qkv[at, c * width : (c + 1) * width] for c in range(4)]
        tall_q = jnp.concatenate([q * (m * scale) for m in masks], axis=0)
        tall_dc = jnp.concatenate([dc * m for m in masks], axis=0)
        scores = dot_nt(k, tall_q)
        grad_probs = dot_nt(v, tall_dc)
        probs_parts, score_parts = [], []
        for start in range(0, heads * TOK, PAIR):
            cols = slice(start, min(start + PAIR, heads * TOK))
            part = scores[:, cols] + bias
            lifted = jnp.exp(part - jnp.max(part, axis=0, keepdims=True))
            probs = lifted * (1.0 / jnp.sum(lifted, axis=0, keepdims=True))
            weighted = probs * grad_probs[:, cols]
            inner = jnp.sum(weighted, axis=0, keepdims=True)
            probs_parts.append(probs.astype(BF16))
            score_parts.append((weighted - probs * inner).astype(BF16))
        half_probs = jnp.concatenate(probs_parts, axis=1)
        grad_score = jnp.concatenate(score_parts, axis=1)
        out_ref[at, :width] = (own_lanes(dot_tn(grad_score, k)) * HD ** (-0.5)).astype(BF16)
        out_ref[at, width : 2 * width] = dot_nn(grad_score, tall_q).astype(BF16)
        out_ref[at, 2 * width : 3 * width] = dot_nn(half_probs, tall_dc).astype(BF16)
        out_ref[at, 3 * width :] = own_lanes(dot_tn(half_probs, v)).astype(BF16)
        return 0

    lax.fori_loop(0, scenes, scene_body, 0, unroll=True)
    pack_all[here, :] = out_ref[...]

    @pl.when((half == pl.num_programs(0) - 1) & (step == pl.num_programs(1) - 1))
    def _():
        total[:, : 3 * width] = dot_tn(n_all[...], pack_all[:, : 3 * width])
        total[:, 3 * width :] = dot_tn(g_all[...], pack_all[:, 3 * width :])
        size = total.shape[0] // dp
        low = low_ref[0]
        for b in range(dp // 2):
            at = slice(b * size, (b + 1) * size)
            mine = pl.multiple_of((2 * b + low) * size, size)
            other = pl.multiple_of((2 * b + 1 - low) * size, size)
            for c in range(2):
                cols = slice(c * 2 * width, (c + 1) * 2 * width)
                keeps[c][at, :] = total[pl.ds(mine, size), cols].astype(keeps[c].dtype)
                others[c][at, :] = total[pl.ds(other, size), cols].astype(others[c].dtype)

    if packs is not None:
        back = dot_nt(out_ref[:, : 3 * width], w_ref[:, : 3 * width])
        for pack_ref, weight_ref in zip(earlier[:packs], earlier[packs:]):
            back = back + dot_nt(pack_ref[...], weight_ref[...])

        @pl.when(half == 0)
        def _():
            refs[0][...] = back

        @pl.when(half != 0)
        def _():
            refs[1][...] = back.astype(BF16)


def block_rows(tokens):
    return 3 * TOK if tokens % (3 * TOK) == 0 else TOK


def two_halves(rows, steps, lead):
    shape = (1,) * len(lead) + (rows, D)
    first = pl.BlockSpec(shape, lambda h, i: lead + (jnp.where(h == 0, i, steps - 1), 0))
    second = pl.BlockSpec(shape, lambda h, i: lead + (jnp.where(h == 0, 0, i), 0))
    return [first, second]


SCALARS = pl.BlockSpec(memory_space=pltpu.SMEM)


def attention_call(counts, owners, low, own, far, earlier, blocks, dp):
    tokens = own.shape[1]
    rows = block_rows(tokens)
    steps = tokens // rows
    cols = blocks[0].shape[1]
    whole = lambda shape: pl.BlockSpec(shape, lambda h, i: (0, 0), pipeline_mode=pl.Buffered(1))
    at = lambda h, i: (h * steps + i, 0)
    packs = None if earlier is None else len(earlier[0])
    back = [] if earlier is None else two_halves(rows, steps, ())
    kind = BF16 if earlier is None else F32
    grads = [jax.ShapeDtypeStruct((D // 2, c), kind) for c in [cols // 2] * 4]
    return pl.pallas_call(
        functools.partial(attention_kernel, packs, len(blocks), dp),
        grid=(2, steps),
        in_specs=[SCALARS] * 3
        + two_halves(rows, steps, (0,))
        + two_halves(rows, steps, (1,))
        + [pl.BlockSpec((rows, cols // 4 * 3), at)] * (packs or 0)
        + [whole((D, cols // 4 * 3))] * (packs or 0)
        + [whole(b.shape) for b in blocks],
        out_specs=[pl.BlockSpec((rows, cols), at), whole((D, cols))] + [whole(g.shape) for g in grads] + back,
        out_shape=[
            jax.ShapeDtypeStruct((2 * tokens, cols), BF16),
            jax.ShapeDtypeStruct((D, cols), BF16),
            *grads,
        ]
        + [jax.ShapeDtypeStruct((tokens, D), kind) for kind in (F32, BF16)[: len(back)]],
        scratch_shapes=[
            pltpu.VMEM((2 * tokens, D), BF16),
            pltpu.VMEM((2 * tokens, D), BF16),
            pltpu.VMEM((2 * tokens, cols), BF16),
            pltpu.VMEM((rows, cols), BF16),
            pltpu.VMEM((D, cols), F32),
        ],
        compiler_params=params(),
        cost_estimate=cost(20e9, 14e6),
        name="attention",
    )(counts, owners, low, own, far, own, far, *[x for group in earlier or () for x in group], *blocks)


def combine_kernel(counts, place_ref, *refs):
    ins, refs = refs[: sum(counts)], refs[sum(counts) :]
    rows = refs[0].shape[0]
    place = place_ref[0]
    for j, ref in enumerate(refs):
        at = pl.ds(pl.multiple_of((place ^ j) * rows, rows), rows)
        total = None
        first = 0
        for count in counts:
            pieces = [r[at, :].astype(F32) for r in ins[first : first + count]]
            new = pieces[0] if count == 1 else jnp.concatenate(pieces, axis=1)
            total = new if total is None else total + new
            first += count
        ref[...] = total.astype(ref.dtype)


def combine_call(place, parts, dtypes):
    ins = [piece for part in parts for piece in part]
    rows, cols = ins[0].shape[0] // len(dtypes), sum(piece.shape[1] for piece in parts[0])
    whole = lambda a: pl.BlockSpec(a.shape, lambda: (0, 0))
    return pl.pallas_call(
        functools.partial(combine_kernel, [len(part) for part in parts]),
        in_specs=[SCALARS] + [whole(a) for a in ins],
        out_specs=[pl.BlockSpec((rows, cols), lambda: (0, 0))] * len(dtypes),
        out_shape=[jax.ShapeDtypeStruct((rows, cols), d) for d in dtypes],
        compiler_params=params(),
        cost_estimate=cost(1e6, 5e6),
        name="combine",
    )(place, *ins)


def split_kernel(count, place_ref, *refs):
    total = refs[0][...]
    for ref in refs[1:count]:
        total = total + ref[...]
    outs = refs[count:]
    cols = outs[0].shape[1]
    place = place_ref[0]
    for j, out_ref in enumerate(outs):
        block = total[:, :cols]
        for b in range(1, len(outs)):
            block = jnp.where((place ^ j) == b, total[:, b * cols : (b + 1) * cols], block)
        out_ref[...] = block


def split_call(place, parts, blocks):
    rows, cols = parts[0].shape
    return pl.pallas_call(
        functools.partial(split_kernel, len(parts)),
        in_specs=[SCALARS] + [pl.BlockSpec((rows, cols), lambda: (0, 0))] * len(parts),
        out_specs=[pl.BlockSpec((rows, cols // blocks), lambda: (0, 0))] * blocks,
        out_shape=[jax.ShapeDtypeStruct((rows, cols // blocks), F32)] * blocks,
        compiler_params=params(),
        cost_estimate=cost(1e6, 2e6),
        name="split_sum",
    )(place, *parts)


def result_kernel(count, *refs):
    halves, qkv_ref, out_ref = (refs[:count], refs[count:-2]), refs[-2], refs[-1]
    first, second = [functools.reduce(lambda a, b: a + b, [r[...].astype(F32) for r in half]) for half in halves]
    width = first.shape[1] // 2
    qkv_ref[0] = first[:, :width]
    qkv_ref[1] = first[:, width:]
    qkv_ref[2] = second[:, :width]
    out_ref[...] = second[:, width:].T


def result_call(first, second):
    rows, cols = first[0].shape
    qkv, out = pl.pallas_call(
        functools.partial(result_kernel, len(first)),
        out_shape=[
            jax.ShapeDtypeStruct((3, rows, cols // 2), F32),
            jax.ShapeDtypeStruct((cols // 2, rows), F32),
        ],
        compiler_params=params(),
        cost_estimate=cost(1e6, 2e6),
        name="weight_results",
    )(*first, *second)
    return jnp.transpose(qkv, (1, 0, 2)), out


def mixed_product(context_refs, weight_refs):
    total = None
    for context_ref, w_ref in zip(context_refs, weight_refs):
        new = dot_nt(context_ref[...], w_ref[...])
        total = new if total is None else total + new
    return total


def context_specs(rows, packs, weights, first):
    width = packs[0].shape[1] // 4
    return [pl.BlockSpec((rows, width), lambda i: (first + i, 3))] * len(packs) + [
        pl.BlockSpec((D, width), lambda i: (0, 3))
    ] * len(weights)


def mixed_kernel(count, *refs):
    refs[-1][...] = mixed_product(refs[:count], refs[count : 2 * count]).astype(BF16)


def mixed_call(packs, weights):
    tokens = packs[0].shape[0] // 2
    rows = block_rows(tokens)
    return pl.pallas_call(
        functools.partial(mixed_kernel, len(packs)),
        grid=(tokens // rows,),
        in_specs=context_specs(rows, packs, weights, tokens // rows),
        out_specs=pl.BlockSpec((rows, D), lambda i: (i, 0)),
        out_shape=jax.ShapeDtypeStruct((tokens, D), BF16),
        compiler_params=params(),
        cost_estimate=cost(2e9, 5e6),
        name="mixed",
    )(*packs, *weights)


def tail_kernel(core_ref, own_ref, recv_ref, emb_ref, gl_ref, cols_ref, gain_ref, keep_ref, first_ref, second_ref, acc):
    step = pl.program_id(0)
    rows = emb_ref.shape[0]
    scenes = rows // TOK

    @pl.when(step == 0)
    def _():
        acc[...] = jnp.zeros_like(acc)

    grad_normed = own_ref[...] + recv_ref[...].astype(F32)
    x = emb_ref[...].astype(F32)
    dev = x - jnp.mean(x, axis=-1, keepdims=True)
    inv_std = lax.rsqrt(jnp.mean(dev * dev, axis=-1, keepdims=True) + NORM_EPS)
    centred = dev * inv_std
    scaled = grad_normed * gain_ref[...]
    first_mean = jnp.mean(scaled, axis=-1, keepdims=True)
    second_mean = jnp.mean(scaled * centred, axis=-1, keepdims=True)
    back = inv_std * (scaled - first_mean - centred * second_mean)
    grad_in = (gl_ref[0].astype(F32) + back).astype(BF16)
    for g, (start, end) in enumerate(GROUP_BANDS):
        at = [slice(s * TOK + g * CAP, s * TOK + (g + 1) * CAP) for s in range(scenes)]
        columns = jnp.concatenate([cols_ref[a, : (end - start) * PIX] for a in at], axis=0)
        grads = jnp.concatenate([grad_in[a] for a in at], axis=0)
        acc[start * PIX : end * PIX, :] += dot_tn(columns, grads)

    @pl.when(step == pl.num_programs(0) - 1)
    def _():
        size = keep_ref.shape[0]
        core = core_ref[0]
        keep_ref[...] = acc[pl.ds(pl.multiple_of(core * size, size), size), :]
        other = pl.ds(pl.multiple_of((1 - core) * size, size), size)
        first_ref[...] = acc[other, : D // 2]
        second_ref[...] = acc[other, D // 2 :]


def tail_call(core, own, recv, emb, rows_own, cols, gain):
    tokens = emb.shape[0]
    rows = 2 * TOK if tokens % (2 * TOK) == 0 else TOK
    per = lambda a: pl.BlockSpec((rows, a.shape[1]), lambda i: (i, 0))
    stem_rows = GROUP_BANDS[-1][1] * PIX
    keep = jax.ShapeDtypeStruct((stem_rows // 2, D), F32)
    send = jax.ShapeDtypeStruct((stem_rows // 2, D // 2), F32)
    return pl.pallas_call(
        tail_kernel,
        grid=(tokens // rows,),
        in_specs=[SCALARS, per(own), per(recv), per(emb), pl.BlockSpec((1, rows, D), lambda i: (1, i, 0)), per(cols)]
        + [pl.BlockSpec(gain.shape, lambda i: (0, 0))],
        out_specs=[pl.BlockSpec(a.shape, lambda i: (0, 0)) for a in (keep, send, send)],
        out_shape=[keep, send, send],
        scratch_shapes=[pltpu.VMEM((stem_rows, D), F32)],
        compiler_params=params(),
        cost_estimate=cost(10e9, 12e6),
        name="tail",
    )(core, own, recv, emb, rows_own, cols, gain)


def output_kernel(count, cnt_ref, recv_ref, emb_ref, *refs):
    out_ref = refs[-1]
    step = pl.program_id(0)
    scenes = emb_ref.shape[0] // TOK
    mixed = recv_ref[...].astype(F32) + mixed_product(refs[:count], refs[count : 2 * count])
    total = emb_ref[...].astype(F32) + mixed
    for s in range(scenes):
        scene = step * scenes + s
        live = live_column(*[cnt_ref[g, scene] for g in range(GROUPS)])
        at = slice(s * TOK, (s + 1) * TOK)
        out_ref[at, :] = jnp.where(live, total[at], 0.0).astype(BF16)


def output_call(counts, recv, emb, packs, weights):
    tokens = emb.shape[0]
    rows = 2 * TOK if tokens % (2 * TOK) == 0 else TOK
    per = lambda a: pl.BlockSpec((rows, a.shape[1]), lambda i: (i, 0))
    return pl.pallas_call(
        functools.partial(output_kernel, len(packs)),
        grid=(tokens // rows,),
        in_specs=[SCALARS, per(recv), per(emb)]
        + context_specs(rows, packs, weights, 0),
        out_specs=per(emb),
        out_shape=jax.ShapeDtypeStruct(emb.shape, BF16),
        compiler_params=params(),
        cost_estimate=cost(5e9, 10e6),
        name="layer_output",
    )(counts, recv, emb, *packs, *weights)


def swap(x, axis, size, bit):
    return lax.ppermute(x, axis, [(i, i ^ bit) for i in range(size)])


def together(*values):
    return lax.optimization_barrier(values)


class Ring:
    def __init__(self, x, axis, size):
        self.axis, self.size = axis, size
        order = list(range(0, size, 2)) + list(range(size - 1, 0, -2))
        self.forward = [(order[i], order[(i + 1) % size]) for i in range(size)]
        self.backward = [(order[(i + 1) % size], order[i]) for i in range(size)]
        self.ahead, self.behind = [x], [x]

    def send(self):
        moved = [lax.ppermute(self.ahead[-1], self.axis, self.forward)]
        if len(self.behind) <= (self.size - 1) // 2:
            moved.append(lax.ppermute(self.behind[-1], self.axis, self.backward))
        return moved

    def receive(self, moved):
        self.ahead.append(moved[0])
        self.behind.extend(moved[1:])

    @property
    def steps(self):
        return len(self.ahead) - 1

    def owners(self, ahead, behind):
        size = self.size
        me = lax.axis_index(self.axis)
        here = jnp.where(me % 2 == 0, me // 2, size - 1 - me // 2)
        distances = [-s for s in range(ahead)] + list(range(1, behind))
        at = (here + size + jnp.array(distances, jnp.int32)) % size
        return jnp.where(at < size // 2, 2 * at, 2 * (size - 1 - at) + 1)


def step_all(rings, *beside):
    moved, beside = together([ring.send() for ring in rings], beside)
    for ring, blocks in zip(rings, moved):
        ring.receive(blocks)
    return beside


def halve_stem(recv, keep, group):
    mine = lax.axis_index("group") // 2 * 2 + lax.axis_index("dp") % 2
    return combine_call(mine.reshape(1), [[keep], recv], [F32] * (group // 2 * 2))


def sum_stem(parts, beside, after, last, dp, group):
    core = lax.axis_index("group") % 2
    far = lax.axis_index("group") // 2
    low = lax.axis_index("dp") % 2
    high = lax.axis_index("dp") // 2
    fars, highs = group // 2, dp // 2
    mine = far * 2 + low
    small, width = parts[0].shape
    rows = 2 * fars * small

    def hop(block, f, b):
        if f:
            pairs = [
                (d * group + g, (d ^ b) * group + (g ^ (2 * f))) for d in range(dp) for g in range(group)
            ]
            return lax.ppermute(block, ("dp", "group"), pairs)
        return swap(block, "dp", dp, b)

    hops = [(k // 2, k % 2) for k in range(1, 2 * fars)]
    arrived = [hop(part, f, b) for part, (f, b) in zip(parts[1:], hops)]
    arrived, beside = together(arrived, beside)
    beside = after[0](*beside)
    cols = width // highs
    part, *away = split_call(high.reshape(1), [parts[0], *arrived], highs)
    arrived = [swap(a, "dp", dp, 2 * (j + 1)) for j, a in enumerate(away)]
    arrived, beside = together(arrived, beside)
    for block in arrived:
        part = part + block
    part = part.astype(BF16)
    line = jnp.zeros((small, width), BF16)
    line = lax.dynamic_update_slice_in_dim(line, part, high * cols, 1)
    arrived = [swap(part, "dp", dp, 2 * j) for j in range(1, highs)]
    arrived, beside = together(arrived, after[1](*beside))
    for j, block in enumerate(arrived):
        line = lax.dynamic_update_slice_in_dim(line, block, (high ^ (j + 1)) * cols, 1)
    block = jnp.zeros((rows, width), BF16)
    block = lax.dynamic_update_slice_in_dim(block, line, mine * small, 0)
    arrived, beside = together([hop(line, f, b) for f, b in hops], last(*beside))
    for (f, b), piece in zip(hops, arrived):
        target = (far ^ f) * 2 + (low ^ b)
        block = lax.dynamic_update_slice_in_dim(block, piece, target * small, 0)
    partner = swap(block, "group", group, 1)
    whole = jnp.zeros((2 * rows, width), F32)
    whole = lax.dynamic_update_slice_in_dim(whole, block.astype(F32), core * rows, 0)
    whole = lax.dynamic_update_slice_in_dim(whole, partner.astype(F32), (1 - core) * rows, 0)
    return whole, beside


def encoding_tables(patch_count):
    quarter = D // 4
    half_width = D // 2
    power = lambda n: np.power(np.float32(10000.0), -np.arange(n, dtype=np.float32) / np.float32(n))
    at = np.arange(GRID).astype(np.float32)[:, None] * power(quarter)
    both = np.concatenate([np.sin(at), np.cos(at)], axis=-1)
    patch = np.arange(patch_count)
    rest = np.concatenate([both[patch // GRID], both[patch % GRID]], axis=-1).astype(np.float32)
    parts = []
    for _ in range(3):
        parts.append(rest.astype(ml_dtypes.bfloat16))
        rest = rest - parts[-1].astype(np.float32)
    group_at = np.arange(GROUPS).astype(np.float32)[:, None] * power(half_width)
    return np.stack(parts), np.concatenate([np.sin(group_at), np.cos(group_at)], axis=-1).astype(np.float32)


def on_device(dp, group, patches, vis_index, vis_count, w_stem, ln_gain, w_qkv, w_out, out_grad):
    scenes = patches.shape[0]
    tokens = scenes * TOK
    width = w_qkv.shape[2]
    fars = range(1, group // 2)
    rests = range(1, dp // 2)
    dp_low, dp_high = lax.axis_index("dp") % 2, lax.axis_index("dp") // 2
    low, high = dp_low.reshape(1), dp_high.reshape(1)
    core = (lax.axis_index("group") % 2).reshape(1)

    shard = pack_call(w_qkv, w_out)
    cross = lambda x, f: swap(x, "group", group, 2 * f)
    far_shards = [cross(shard, f) for f in fars]
    counts = vis_count.astype(jnp.int32).T
    counts_far = swap(counts, "group", group, 1)
    table, genc = encoding_tables(patches.shape[1])
    gain = ln_gain.reshape(1, D)
    stem = stem_call(
        counts,
        vis_index,
        patches,
        w_stem,
        gain,
        jnp.asarray(table),
        jnp.asarray(genc),
        out_grad.reshape(scenes, TOK, D),
    )
    stem, both_counts, far_shards = together(stem, jnp.stack([counts, counts_far]), far_shards)
    rings = [Ring(x, "dp", dp) for x in far_shards]
    ring = rings[0]
    owners = ring.owners(dp // 2 + 1, dp // 2)
    emb = stem[0].reshape(tokens, D)
    both = [stem[1].reshape(2, tokens, D)]
    cols = stem[2].reshape(tokens, stem[2].shape[2])
    both.append(swap(both[0], "group", group, 1))
    own_ahead, own_behind = [], []
    both, owners = step_all(rings, both, owners)
    while ring.steps < dp // 2:
        a, b = len(own_ahead), len(own_behind)
        own_ahead.append(cross(ring.ahead[-1], 1))
        if a:
            own_behind.append(cross(ring.behind[a], 1))
        ahead, behind = slice(max(a - 1, 0), a), slice(max(b - 2, 0), max(b - 1, 0))
        own_ahead[ahead], own_behind[behind] = step_all(rings, own_ahead[ahead], own_behind[behind])
    ring.ahead, ring.behind = together(ring.ahead, ring.behind)
    own_ahead.append(cross(ring.ahead[-1], 1))
    own_behind.extend(cross(x, 1) for x in ring.behind[len(own_behind) + 1 :])

    packs, weights, crossing = [], [], []
    for f in list(fars) + [0]:
        if f:
            blocks = rings[f - 1].ahead + rings[f - 1].behind[1:]
        else:
            blocks = [shard] + own_ahead + own_behind
        made = attention_call(both_counts, owners, low, *both, None if f else (packs, weights), blocks, dp)
        if f == 1:
            made, own_ahead[-2:], own_behind[-3:] = together(made, own_ahead[-2:], own_behind[-3:])
        elif f:
            made = together(*made)
        else:
            made, arrived = together(made, [x[:3] for x in crossing])
        pack, weight, keep, other, back = made[0], made[1], made[2:4], made[4:6], made[6:]
        packs.append(pack)
        weights.append(weight)
        if f:
            crossing.append([cross(x, f) for x in (*other, keep[0])] + [keep[1]])
    back_far = swap(back[1], "group", group, 1)
    coming = []
    for c in range(2):
        send = other[c]
        for x in arrived:
            send = send + x[c].astype(F32)
        send = send.astype(BF16)
        if c == 0:
            send, last_keeps = together(send, [x[3] for x in crossing])
        coming.append(swap(send, "dp", dp, 1))
    last_keeps = [cross(x, f) for f, x in zip(fars, last_keeps)]
    stem_made, coming[0], last_keeps = together(
        tail_call(core, back[0], back_far, emb, both[0], cols, gain), coming[0], last_keeps
    )
    stem_keep, *stem_recv = stem_made
    stem_recv = [swap(x, "group", group, 1) for x in stem_recv]
    kinds = [F32 if j < 2 else BF16 for j in range(dp // 2)]
    second_leg = lambda c: combine_call(high, [[x] for x in keeps[c] + [coming[c]]], kinds)
    spread = lambda blocks, js: [swap(blocks[j], "dp", dp, 2 * j) for j in js]
    stem_recv = together(*stem_recv)
    keeps = [[keep[0]] + [x[2] for x in arrived], [keep[1]] + list(last_keeps)]
    stem_parts = halve_stem(stem_recv, stem_keep, group)
    _, coming[0], keeps = together(stem_parts, coming[0], keeps)
    first = second_leg(0)
    first_rest = spread(first, rests[1:])
    second = second_leg(1)
    near = dp // 2 * 3 // 4
    beside = [mixed_call(packs, weights), first[0], *first_rest, second[0]]
    def after_first(mixed, *arrived):
        output = output_call(counts, swap(mixed, "group", group, 1), emb, packs, weights)
        return [output, *arrived[:-1], *spread(first, [1]), arrived[-1]]

    def after_second(*arrived):
        return [*arrived, *spread(second, [1, *range(2, near)]), second[near:]]

    def last(*arrived):
        blocks = dict(enumerate(arrived[-1], near))
        return [*arrived[:-1], *spread(blocks, blocks)]

    grad_w_stem, (output, *arrived) = sum_stem(
        stem_parts, beside, (after_first, after_second), last, dp, group
    )
    half = len(arrived) // 2
    grad_w_qkv, grad_w_out = result_call(arrived[:half], arrived[half:])
    return (output.reshape(scenes, GROUPS, CAP, D), grad_w_stem, grad_w_qkv, grad_w_out)


def solution(mesh):
    sizes = dict(mesh.shape)
    return jax.shard_map(
        functools.partial(on_device, sizes["dp"], sizes["group"]),
        mesh=mesh,
        in_specs=(
            P(("dp", "group"), None, None),
            P(("dp", "group"), None, None),
            P(("dp", "group"), None),
            P(),
            P(),
            P("dp", None, "group"),
            P("group", "dp"),
            P(("dp", "group"), None, None, None),
        ),
        out_specs=(
            P(("dp", "group"), None, None, None),
            P(),
            P("dp", None, "group"),
            P("group", "dp"),
        ),
        check_vma=False,
    )
```

```python
import functools

import jax
import jax.numpy as jnp
import ml_dtypes
import numpy as np
from jax import lax
from jax.experimental import pallas as pl
from jax.experimental.pallas import tpu as pltpu
from jax.sharding import PartitionSpec as P

D = 1024
HD = 64
GROUPS = 3
CAP = 48
GRID = 12
PIX = 64
TOK = GROUPS * CAP
PAIR = 128
GROUP_BANDS = ((0, 4), (4, 8), (8, 10))
NORM_EPS = 1e-06
F32 = jnp.float32
BF16 = jnp.bfloat16
VMEM_LIMIT = 60 * 1024 * 1024
SMALL_LIMIT = 16 * 1024 * 1024


def dot_nn(a, b):
    return lax.dot_general(a, b, (((1,), (0,)), ((), ())), preferred_element_type=F32)


def dot_nt(a, b):
    return lax.dot_general(a, b, (((1,), (1,)), ((), ())), preferred_element_type=F32)


def dot_tn(a, b):
    return lax.dot_general(a, b, (((0,), (0,)), ((), ())), preferred_element_type=F32)


def live_column(c0, c1, c2):
    row = lax.broadcasted_iota(jnp.int32, (TOK, 1), 0)
    return (
        (row < c0)
        | ((row >= CAP) & (row < CAP + c1))
        | ((row >= 2 * CAP) & (row < 2 * CAP + c2))
    )


def params(limit=VMEM_LIMIT):
    return pltpu.CompilerParams(vmem_limit_bytes=limit)


def cost(flops, nbytes):
    return pl.CostEstimate(flops=int(flops / 1000), bytes_accessed=int(nbytes / 1000), transcendentals=0)


def stem_kernel(
    cnt_ref, idx_ref, patch_ref, w_ref, gain_ref, parts, genc_ref, og_ref,
    emb_ref, rows_ref, cols_ref,
):
    step = pl.program_id(0)
    scenes = patch_ref.shape[0]
    patch_iota = lax.broadcasted_iota(jnp.int32, (parts.shape[1], CAP), 0)
    slot = lax.broadcasted_iota(jnp.int32, (CAP, 1), 0)
    for g, (start, end) in enumerate(GROUP_BANDS):
        rows = slice(g * CAP, (g + 1) * CAP)
        width = (end - start) * PIX
        picked, placed = [], []
        for s in range(scenes):
            onehot = (idx_ref[s, g : g + 1, :] == patch_iota).astype(F32).astype(BF16).T
            picked.append(dot_nn(onehot, patch_ref[s, :, start * PIX : end * PIX]).astype(BF16))
            placed.append(
                (dot_nn(onehot, parts[0]) + dot_nn(onehot, parts[1])) + dot_nn(onehot, parts[2])
            )
            live = slot < cnt_ref[g, step * scenes + s]
            rows_ref[1, s, rows, :] = jnp.where(live, og_ref[s, rows, :].astype(F32), 0.0).astype(BF16)
        summed = dot_nn(jnp.concatenate(picked, axis=0), w_ref[start * PIX : end * PIX, :])
        for s in range(scenes):
            values = summed[s * CAP : (s + 1) * CAP] + (placed[s] + genc_ref[g : g + 1, :])
            emb = values.astype(BF16)
            emb_ref[s, rows, :] = emb
            x = emb.astype(F32)
            centre = jnp.mean(x, axis=-1, keepdims=True)
            dev = x - centre
            spread = jnp.mean(dev * dev, axis=-1, keepdims=True)
            centred = dev * lax.rsqrt(spread + NORM_EPS)
            rows_ref[0, s, rows, :] = (centred * gain_ref[...]).astype(BF16)
            cols_ref[s, rows, :width] = picked[s]
            if width < cols_ref.shape[2]:
                cols_ref[s, rows, width:] = jnp.zeros((CAP, cols_ref.shape[2] - width), BF16)


def stem_call(counts, index, patches, w_stem, gain, table, genc, out_grad):
    scenes, patch_count, width = patches.shape
    block = 3 if scenes % 3 == 0 else 1
    col_width = max(e - s for s, e in GROUP_BANDS) * PIX
    per = lambda shape: pl.BlockSpec((block,) + shape, lambda i: (i, 0, 0))
    whole = lambda a: pl.BlockSpec(a.shape, lambda i: (0,) * a.ndim)
    return pl.pallas_call(
        stem_kernel,
        grid=(scenes // block,),
        in_specs=[
            pl.BlockSpec(memory_space=pltpu.SMEM),
            per((GROUPS, CAP)),
            per((patch_count, width)),
            whole(w_stem),
            whole(gain),
            whole(table),
            whole(genc),
            per((TOK, D)),
        ],
        out_specs=[
            per((TOK, D)),
            pl.BlockSpec((2, block, TOK, D), lambda i: (0, i, 0, 0)),
            per((TOK, col_width)),
        ],
        out_shape=[
            jax.ShapeDtypeStruct((scenes, TOK, D), BF16),
            jax.ShapeDtypeStruct((2, scenes, TOK, D), BF16),
            jax.ShapeDtypeStruct((scenes, TOK, col_width), BF16),
        ],
        compiler_params=params(),
        cost_estimate=cost(8e9, 12e6),
        name="stem_norm",
    )(counts, index, patches, w_stem, gain, table, genc, out_grad)


def pack_kernel(qkv_ref, out_w_ref, pack_ref):
    count, _, width = qkv_ref.shape
    for c in range(count):
        pack_ref[:, c * width : (c + 1) * width] = qkv_ref[c]
    pack_ref[:, count * width :] = out_w_ref[...].T


def pack_call(w_qkv, w_out):
    parts = jnp.transpose(w_qkv, (1, 0, 2))
    return pl.pallas_call(
        pack_kernel,
        out_shape=jax.ShapeDtypeStruct((w_qkv.shape[0], 3 * w_qkv.shape[2] + w_out.shape[0]), BF16),
        compiler_params=params(),
        cost_estimate=cost(1e6, 5e5),
        name="pack_weights",
    )(parts, w_out)


def attention_kernel(
    packs, blocks, dp, cnt_ref, owner_ref, low_ref, na_ref, nb_ref, ga_ref, gb_ref, *refs
):
    earlier, refs = refs[: 2 * (packs or 0)], refs[2 * (packs or 0) :]
    blocks, refs = refs[:blocks], refs[blocks:]
    out_ref, w_ref, *refs = refs
    keeps, others, refs = refs[:2], refs[2:4], refs[4:]
    n_all, g_all, pack_all, qkv, total = refs[-5:]
    half, step = pl.program_id(0), pl.program_id(1)
    rows = qkv.shape[0]
    here = pl.ds(pl.multiple_of((half * pl.num_programs(1) + step) * rows, 16), rows)
    scenes = rows // TOK
    width = w_ref.shape[1] // 4

    @pl.when((half == 0) & (step == 0))
    def _():
        size = blocks[0].shape[0]
        for b, block in enumerate(blocks):
            w_ref[pl.ds(pl.multiple_of(owner_ref[b] * size, size), size), :] = block[...]

    @pl.when(half == 0)
    def _():
        n_all[here, :] = na_ref[0]
        g_all[here, :] = ga_ref[0]

    @pl.when(half != 0)
    def _():
        n_all[here, :] = nb_ref[0]
        g_all[here, :] = gb_ref[0]

    qkv[:, : 3 * width] = dot_nn(n_all[here, :], w_ref[:, : 3 * width]).astype(BF16)
    qkv[:, 3 * width :] = dot_nn(g_all[here, :], w_ref[:, 3 * width :]).astype(BF16)
    heads = width // HD
    lane = lax.broadcasted_iota(jnp.int32, (1, width), 1)
    masks = [(lane // HD == h).astype(F32).astype(BF16) for h in range(heads)]
    scale = jnp.asarray(HD ** (-0.5), BF16)
    first_of_pair = lax.broadcasted_iota(jnp.int32, (1, PAIR), 1) < HD

    def own_lanes(tall):
        tiles = []
        for t in range(width // PAIR):
            at = slice(t * PAIR, (t + 1) * PAIR)
            one = tall[2 * t * TOK : (2 * t + 1) * TOK, at]
            two = tall[(2 * t + 1) * TOK : (2 * t + 2) * TOK, at]
            tiles.append(jnp.where(first_of_pair, one, two))
        return jnp.concatenate(tiles, axis=1)

    def scene_body(s, _):
        base = pl.multiple_of(s * TOK, 16)
        at = pl.ds(base, TOK)
        scene = step * scenes + s
        live = live_column(*[cnt_ref[half, g, scene] for g in range(GROUPS)])
        bias = jnp.where(live, 0.0, -1e30)
        q, k, v, dc = [qkv[at, c * width : (c + 1) * width] for c in range(4)]
        tall_q = jnp.concatenate([q * (m * scale) for m in masks], axis=0)
        tall_dc = jnp.concatenate([dc * m for m in masks], axis=0)
        scores = dot_nt(k, tall_q)
        grad_probs = dot_nt(v, tall_dc)
        probs_parts, score_parts = [], []
        for start in range(0, heads * TOK, PAIR):
            cols = slice(start, min(start + PAIR, heads * TOK))
            part = scores[:, cols] + bias
            lifted = jnp.exp(part - jnp.max(part, axis=0, keepdims=True))
            probs = lifted * (1.0 / jnp.sum(lifted, axis=0, keepdims=True))
            weighted = probs * grad_probs[:, cols]
            inner = jnp.sum(weighted, axis=0, keepdims=True)
            probs_parts.append(probs.astype(BF16))
            score_parts.append((weighted - probs * inner).astype(BF16))
        half_probs = jnp.concatenate(probs_parts, axis=1)
        grad_score = jnp.concatenate(score_parts, axis=1)
        out_ref[at, :width] = (own_lanes(dot_tn(grad_score, k)) * HD ** (-0.5)).astype(BF16)
        out_ref[at, width : 2 * width] = dot_nn(grad_score, tall_q).astype(BF16)
        out_ref[at, 2 * width : 3 * width] = dot_nn(half_probs, tall_dc).astype(BF16)
        out_ref[at, 3 * width :] = own_lanes(dot_tn(half_probs, v)).astype(BF16)
        return 0

    lax.fori_loop(0, scenes, scene_body, 0, unroll=True)
    pack_all[here, :] = out_ref[...]

    @pl.when((half == pl.num_programs(0) - 1) & (step == pl.num_programs(1) - 1))
    def _():
        total[:, : 3 * width] = dot_tn(n_all[...], pack_all[:, : 3 * width])
        total[:, 3 * width :] = dot_tn(g_all[...], pack_all[:, 3 * width :])
        size = total.shape[0] // dp
        low = low_ref[0]
        for b in range(dp // 2):
            at = slice(b * size, (b + 1) * size)
            mine = pl.multiple_of((2 * b + low) * size, size)
            other = pl.multiple_of((2 * b + 1 - low) * size, size)
            for c in range(2):
                cols = slice(c * 2 * width, (c + 1) * 2 * width)
                keeps[c][at, :] = total[pl.ds(mine, size), cols].astype(keeps[c].dtype)
                others[c][at, :] = total[pl.ds(other, size), cols].astype(others[c].dtype)

    if packs is not None:
        back = dot_nt(out_ref[:, : 3 * width], w_ref[:, : 3 * width])
        for pack_ref, weight_ref in zip(earlier[:packs], earlier[packs:]):
            back = back + dot_nt(pack_ref[...], weight_ref[...])

        @pl.when(half == 0)
        def _():
            refs[0][...] = back

        @pl.when(half != 0)
        def _():
            refs[1][...] = back.astype(BF16)


def block_rows(tokens):
    return 3 * TOK if tokens % (3 * TOK) == 0 else TOK


def two_halves(rows, steps, lead):
    shape = (1,) * len(lead) + (rows, D)
    first = pl.BlockSpec(shape, lambda h, i: lead + (jnp.where(h == 0, i, steps - 1), 0))
    second = pl.BlockSpec(shape, lambda h, i: lead + (jnp.where(h == 0, 0, i), 0))
    return [first, second]


SCALARS = pl.BlockSpec(memory_space=pltpu.SMEM)


def attention_call(counts, owners, low, own, far, earlier, blocks, dp):
    tokens = own.shape[1]
    rows = block_rows(tokens)
    steps = tokens // rows
    cols = blocks[0].shape[1]
    whole = lambda shape: pl.BlockSpec(shape, lambda h, i: (0, 0), pipeline_mode=pl.Buffered(1))
    at = lambda h, i: (h * steps + i, 0)
    packs = None if earlier is None else len(earlier[0])
    back = [] if earlier is None else two_halves(rows, steps, ())
    kind = BF16 if earlier is None else F32
    grads = [jax.ShapeDtypeStruct((D // 2, c), kind) for c in [cols // 2] * 4]
    return pl.pallas_call(
        functools.partial(attention_kernel, packs, len(blocks), dp),
        grid=(2, steps),
        in_specs=[SCALARS] * 3
        + two_halves(rows, steps, (0,))
        + two_halves(rows, steps, (1,))
        + [pl.BlockSpec((rows, cols // 4 * 3), at)] * (packs or 0)
        + [whole((D, cols // 4 * 3))] * (packs or 0)
        + [whole(b.shape) for b in blocks],
        out_specs=[pl.BlockSpec((rows, cols), at), whole((D, cols))] + [whole(g.shape) for g in grads] + back,
        out_shape=[
            jax.ShapeDtypeStruct((2 * tokens, cols), BF16),
            jax.ShapeDtypeStruct((D, cols), BF16),
            *grads,
        ]
        + [jax.ShapeDtypeStruct((tokens, D), kind) for kind in (F32, BF16)[: len(back)]],
        scratch_shapes=[
            pltpu.VMEM((2 * tokens, D), BF16),
            pltpu.VMEM((2 * tokens, D), BF16),
            pltpu.VMEM((2 * tokens, cols), BF16),
            pltpu.VMEM((rows, cols), BF16),
            pltpu.VMEM((D, cols), F32),
        ],
        compiler_params=params(),
        cost_estimate=cost(20e9, 14e6),
        name="attention",
    )(counts, owners, low, own, far, own, far, *[x for group in earlier or () for x in group], *blocks)


def combine_kernel(counts, place_ref, *refs):
    ins, refs = refs[: sum(counts)], refs[sum(counts) :]
    rows = refs[0].shape[0]
    place = place_ref[0]
    for j, ref in enumerate(refs):
        at = pl.ds(pl.multiple_of((place ^ j) * rows, rows), rows)
        total = None
        first = 0
        for count in counts:
            pieces = [r[at, :].astype(F32) for r in ins[first : first + count]]
            new = pieces[0] if count == 1 else jnp.concatenate(pieces, axis=1)
            total = new if total is None else total + new
            first += count
        ref[...] = total.astype(ref.dtype)


def combine_call(place, parts, dtypes):
    ins = [piece for part in parts for piece in part]
    rows, cols = ins[0].shape[0] // len(dtypes), sum(piece.shape[1] for piece in parts[0])
    whole = lambda a: pl.BlockSpec(a.shape, lambda: (0, 0))
    return pl.pallas_call(
        functools.partial(combine_kernel, [len(part) for part in parts]),
        in_specs=[SCALARS] + [whole(a) for a in ins],
        out_specs=[pl.BlockSpec((rows, cols), lambda: (0, 0))] * len(dtypes),
        out_shape=[jax.ShapeDtypeStruct((rows, cols), d) for d in dtypes],
        compiler_params=params(SMALL_LIMIT),
        cost_estimate=cost(1e6, 5e6),
        name="combine",
    )(place, *ins)


def split_kernel(count, place_ref, *refs):
    total = refs[0][...]
    for ref in refs[1:count]:
        total = total + ref[...]
    outs = refs[count:]
    cols = outs[0].shape[1]
    place = place_ref[0]
    for j, out_ref in enumerate(outs):
        block = total[:, :cols]
        for b in range(1, len(outs)):
            block = jnp.where((place ^ j) == b, total[:, b * cols : (b + 1) * cols], block)
        out_ref[...] = block


def split_call(place, parts, blocks):
    rows, cols = parts[0].shape
    return pl.pallas_call(
        functools.partial(split_kernel, len(parts)),
        in_specs=[SCALARS] + [pl.BlockSpec((rows, cols), lambda: (0, 0))] * len(parts),
        out_specs=[pl.BlockSpec((rows, cols // blocks), lambda: (0, 0))] * blocks,
        out_shape=[jax.ShapeDtypeStruct((rows, cols // blocks), F32)] * blocks,
        compiler_params=params(SMALL_LIMIT),
        cost_estimate=cost(1e6, 2e6),
        name="split_sum",
    )(place, *parts)


def result_kernel(count, *refs):
    halves, qkv_ref, out_ref = (refs[:count], refs[count:-2]), refs[-2], refs[-1]
    first, second = [functools.reduce(lambda a, b: a + b, [r[...].astype(F32) for r in half]) for half in halves]
    width = first.shape[1] // 2
    qkv_ref[0] = first[:, :width]
    qkv_ref[1] = first[:, width:]
    qkv_ref[2] = second[:, :width]
    out_ref[...] = second[:, width:].T


def result_call(first, second):
    rows, cols = first[0].shape
    qkv, out = pl.pallas_call(
        functools.partial(result_kernel, len(first)),
        out_shape=[
            jax.ShapeDtypeStruct((3, rows, cols // 2), F32),
            jax.ShapeDtypeStruct((cols // 2, rows), F32),
        ],
        compiler_params=params(SMALL_LIMIT),
        cost_estimate=cost(1e6, 2e6),
        name="weight_results",
    )(*first, *second)
    return jnp.transpose(qkv, (1, 0, 2)), out


def mixed_product(context_refs, weight_refs):
    total = None
    for context_ref, w_ref in zip(context_refs, weight_refs):
        new = dot_nt(context_ref[...], w_ref[...])
        total = new if total is None else total + new
    return total


def context_specs(rows, packs, weights, first):
    width = packs[0].shape[1] // 4
    return [pl.BlockSpec((rows, width), lambda i: (first + i, 3))] * len(packs) + [
        pl.BlockSpec((D, width), lambda i: (0, 3))
    ] * len(weights)


def mixed_kernel(count, *refs):
    refs[-1][...] = mixed_product(refs[:count], refs[count : 2 * count]).astype(BF16)


def mixed_call(packs, weights):
    tokens = packs[0].shape[0] // 2
    rows = block_rows(tokens)
    return pl.pallas_call(
        functools.partial(mixed_kernel, len(packs)),
        grid=(tokens // rows,),
        in_specs=context_specs(rows, packs, weights, tokens // rows),
        out_specs=pl.BlockSpec((rows, D), lambda i: (i, 0)),
        out_shape=jax.ShapeDtypeStruct((tokens, D), BF16),
        compiler_params=params(),
        cost_estimate=cost(2e9, 5e6),
        name="mixed",
    )(*packs, *weights)


def tail_kernel(core_ref, own_ref, recv_ref, emb_ref, gl_ref, cols_ref, gain_ref, keep_ref, first_ref, second_ref, acc):
    step = pl.program_id(0)
    rows = emb_ref.shape[0]
    scenes = rows // TOK

    @pl.when(step == 0)
    def _():
        acc[...] = jnp.zeros_like(acc)

    grad_normed = own_ref[...] + recv_ref[...].astype(F32)
    x = emb_ref[...].astype(F32)
    dev = x - jnp.mean(x, axis=-1, keepdims=True)
    inv_std = lax.rsqrt(jnp.mean(dev * dev, axis=-1, keepdims=True) + NORM_EPS)
    centred = dev * inv_std
    scaled = grad_normed * gain_ref[...]
    first_mean = jnp.mean(scaled, axis=-1, keepdims=True)
    second_mean = jnp.mean(scaled * centred, axis=-1, keepdims=True)
    back = inv_std * (scaled - first_mean - centred * second_mean)
    grad_in = (gl_ref[0].astype(F32) + back).astype(BF16)
    for g, (start, end) in enumerate(GROUP_BANDS):
        at = [slice(s * TOK + g * CAP, s * TOK + (g + 1) * CAP) for s in range(scenes)]
        columns = jnp.concatenate([cols_ref[a, : (end - start) * PIX] for a in at], axis=0)
        grads = jnp.concatenate([grad_in[a] for a in at], axis=0)
        acc[start * PIX : end * PIX, :] += dot_tn(columns, grads)

    @pl.when(step == pl.num_programs(0) - 1)
    def _():
        size = keep_ref.shape[0]
        core = core_ref[0]
        keep_ref[...] = acc[pl.ds(pl.multiple_of(core * size, size), size), :]
        other = pl.ds(pl.multiple_of((1 - core) * size, size), size)
        first_ref[...] = acc[other, : D // 2]
        second_ref[...] = acc[other, D // 2 :]


def tail_call(core, own, recv, emb, rows_own, cols, gain):
    tokens = emb.shape[0]
    rows = 2 * TOK if tokens % (2 * TOK) == 0 else TOK
    per = lambda a: pl.BlockSpec((rows, a.shape[1]), lambda i: (i, 0))
    stem_rows = GROUP_BANDS[-1][1] * PIX
    keep = jax.ShapeDtypeStruct((stem_rows // 2, D), F32)
    send = jax.ShapeDtypeStruct((stem_rows // 2, D // 2), F32)
    return pl.pallas_call(
        tail_kernel,
        grid=(tokens // rows,),
        in_specs=[SCALARS, per(own), per(recv), per(emb), pl.BlockSpec((1, rows, D), lambda i: (1, i, 0)), per(cols)]
        + [pl.BlockSpec(gain.shape, lambda i: (0, 0))],
        out_specs=[pl.BlockSpec(a.shape, lambda i: (0, 0)) for a in (keep, send, send)],
        out_shape=[keep, send, send],
        scratch_shapes=[pltpu.VMEM((stem_rows, D), F32)],
        compiler_params=params(),
        cost_estimate=cost(10e9, 12e6),
        name="tail",
    )(core, own, recv, emb, rows_own, cols, gain)


def output_kernel(count, cnt_ref, recv_ref, emb_ref, *refs):
    out_ref = refs[-1]
    step = pl.program_id(0)
    scenes = emb_ref.shape[0] // TOK
    mixed = recv_ref[...].astype(F32) + mixed_product(refs[:count], refs[count : 2 * count])
    total = emb_ref[...].astype(F32) + mixed
    for s in range(scenes):
        scene = step * scenes + s
        live = live_column(*[cnt_ref[g, scene] for g in range(GROUPS)])
        at = slice(s * TOK, (s + 1) * TOK)
        out_ref[at, :] = jnp.where(live, total[at], 0.0).astype(BF16)


def output_call(counts, recv, emb, packs, weights):
    tokens = emb.shape[0]
    rows = 2 * TOK if tokens % (2 * TOK) == 0 else TOK
    per = lambda a: pl.BlockSpec((rows, a.shape[1]), lambda i: (i, 0))
    return pl.pallas_call(
        functools.partial(output_kernel, len(packs)),
        grid=(tokens // rows,),
        in_specs=[SCALARS, per(recv), per(emb)]
        + context_specs(rows, packs, weights, 0),
        out_specs=per(emb),
        out_shape=jax.ShapeDtypeStruct(emb.shape, BF16),
        compiler_params=params(),
        cost_estimate=cost(5e9, 10e6),
        name="layer_output",
    )(counts, recv, emb, *packs, *weights)


def swap(x, axis, size, bit):
    return lax.ppermute(x, axis, [(i, i ^ bit) for i in range(size)])


def together(*values):
    return lax.optimization_barrier(values)


class Ring:
    def __init__(self, x, axis, size):
        self.axis, self.size = axis, size
        order = list(range(0, size, 2)) + list(range(size - 1, 0, -2))
        self.forward = [(order[i], order[(i + 1) % size]) for i in range(size)]
        self.backward = [(order[(i + 1) % size], order[i]) for i in range(size)]
        self.ahead, self.behind = [x], [x]

    def send(self):
        moved = [lax.ppermute(self.ahead[-1], self.axis, self.forward)]
        if len(self.behind) <= (self.size - 1) // 2:
            moved.append(lax.ppermute(self.behind[-1], self.axis, self.backward))
        return moved

    def receive(self, moved):
        self.ahead.append(moved[0])
        self.behind.extend(moved[1:])

    @property
    def steps(self):
        return len(self.ahead) - 1

    def owners(self, ahead, behind):
        size = self.size
        me = lax.axis_index(self.axis)
        here = jnp.where(me % 2 == 0, me // 2, size - 1 - me // 2)
        distances = [-s for s in range(ahead)] + list(range(1, behind))
        at = (here + size + jnp.array(distances, jnp.int32)) % size
        return jnp.where(at < size // 2, 2 * at, 2 * (size - 1 - at) + 1)


def step_all(rings, *beside):
    moved, beside = together([ring.send() for ring in rings], beside)
    for ring, blocks in zip(rings, moved):
        ring.receive(blocks)
    return beside


def halve_stem(recv, keep, group):
    mine = lax.axis_index("group") // 2 * 2 + lax.axis_index("dp") % 2
    return combine_call(mine.reshape(1), [[keep], recv], [F32] * (group // 2 * 2))


def sum_stem(parts, beside, after, last, dp, group):
    core = lax.axis_index("group") % 2
    far = lax.axis_index("group") // 2
    low = lax.axis_index("dp") % 2
    high = lax.axis_index("dp") // 2
    fars, highs = group // 2, dp // 2
    mine = far * 2 + low
    small, width = parts[0].shape
    rows = 2 * fars * small

    def hop(block, f, b):
        if f:
            pairs = [
                (d * group + g, (d ^ b) * group + (g ^ (2 * f))) for d in range(dp) for g in range(group)
            ]
            return lax.ppermute(block, ("dp", "group"), pairs)
        return swap(block, "dp", dp, b)

    hops = [(k // 2, k % 2) for k in range(1, 2 * fars)]
    arrived = [hop(part, f, b) for part, (f, b) in zip(parts[1:], hops)]
    arrived, beside = together(arrived, beside)
    beside = after[0](*beside)
    cols = width // highs
    part, *away = split_call(high.reshape(1), [parts[0], *arrived], highs)
    arrived = [swap(a, "dp", dp, 2 * (j + 1)) for j, a in enumerate(away)]
    arrived, beside = together(arrived, beside)
    for block in arrived:
        part = part + block
    part = part.astype(BF16)
    line = jnp.zeros((small, width), BF16)
    line = lax.dynamic_update_slice_in_dim(line, part, high * cols, 1)
    arrived = [swap(part, "dp", dp, 2 * j) for j in range(1, highs)]
    arrived, beside = together(arrived, after[1](*beside))
    for j, block in enumerate(arrived):
        line = lax.dynamic_update_slice_in_dim(line, block, (high ^ (j + 1)) * cols, 1)
    block = jnp.zeros((rows, width), BF16)
    block = lax.dynamic_update_slice_in_dim(block, line, mine * small, 0)
    arrived, beside = together([hop(line, f, b) for f, b in hops], last(*beside))
    for (f, b), piece in zip(hops, arrived):
        target = (far ^ f) * 2 + (low ^ b)
        block = lax.dynamic_update_slice_in_dim(block, piece, target * small, 0)
    partner = swap(block, "group", group, 1)
    whole = jnp.zeros((2 * rows, width), F32)
    whole = lax.dynamic_update_slice_in_dim(whole, block.astype(F32), core * rows, 0)
    whole = lax.dynamic_update_slice_in_dim(whole, partner.astype(F32), (1 - core) * rows, 0)
    return whole, beside


def encoding_tables(patch_count):
    quarter = D // 4
    half_width = D // 2
    power = lambda n: np.power(np.float32(10000.0), -np.arange(n, dtype=np.float32) / np.float32(n))
    at = np.arange(GRID).astype(np.float32)[:, None] * power(quarter)
    both = np.concatenate([np.sin(at), np.cos(at)], axis=-1)
    patch = np.arange(patch_count)
    rest = np.concatenate([both[patch // GRID], both[patch % GRID]], axis=-1).astype(np.float32)
    parts = []
    for _ in range(3):
        parts.append(rest.astype(ml_dtypes.bfloat16))
        rest = rest - parts[-1].astype(np.float32)
    group_at = np.arange(GROUPS).astype(np.float32)[:, None] * power(half_width)
    return np.stack(parts), np.concatenate([np.sin(group_at), np.cos(group_at)], axis=-1).astype(np.float32)


def on_device(dp, group, patches, vis_index, vis_count, w_stem, ln_gain, w_qkv, w_out, out_grad):
    scenes = patches.shape[0]
    tokens = scenes * TOK
    width = w_qkv.shape[2]
    fars = range(1, group // 2)
    rests = range(1, dp // 2)
    dp_low, dp_high = lax.axis_index("dp") % 2, lax.axis_index("dp") // 2
    low, high = dp_low.reshape(1), dp_high.reshape(1)
    core = (lax.axis_index("group") % 2).reshape(1)

    shard = pack_call(w_qkv, w_out)
    cross = lambda x, f: swap(x, "group", group, 2 * f)
    far_shards = [cross(shard, f) for f in fars]
    counts = vis_count.astype(jnp.int32).T
    counts_far = swap(counts, "group", group, 1)
    table, genc = encoding_tables(patches.shape[1])
    gain = ln_gain.reshape(1, D)
    stem = stem_call(
        counts,
        vis_index,
        patches,
        w_stem,
        gain,
        jnp.asarray(table),
        jnp.asarray(genc),
        out_grad.reshape(scenes, TOK, D),
    )
    stem, counts_far, far_shards = together(stem, counts_far, far_shards)
    rings = [Ring(x, "dp", dp) for x in far_shards]
    ring = rings[0]
    owners = ring.owners(dp // 2 + 1, dp // 2)
    emb = stem[0].reshape(tokens, D)
    both = [stem[1].reshape(2, tokens, D)]
    cols = stem[2].reshape(tokens, stem[2].shape[2])
    both.append(swap(both[0], "group", group, 1))
    own_ahead, own_behind = [], []
    both, owners, both_counts = step_all(rings, both, owners, jnp.stack([counts, counts_far]))
    while ring.steps < dp // 2:
        a, b = len(own_ahead), len(own_behind)
        own_ahead.append(cross(ring.ahead[-1], 1))
        if a:
            own_behind.append(cross(ring.behind[a], 1))
        ahead, behind = slice(max(a - 1, 0), a), slice(max(b - 2, 0), max(b - 1, 0))
        own_ahead[ahead], own_behind[behind] = step_all(rings, own_ahead[ahead], own_behind[behind])
    ring.ahead, ring.behind = together(ring.ahead, ring.behind)
    own_ahead.append(cross(ring.ahead[-1], 1))
    own_behind.extend(cross(x, 1) for x in ring.behind[len(own_behind) + 1 :])

    packs, weights, crossing = [], [], []
    for f in list(fars) + [0]:
        if f:
            blocks = rings[f - 1].ahead + rings[f - 1].behind[1:]
        else:
            blocks = [shard] + own_ahead + own_behind
        made = attention_call(both_counts, owners, low, *both, None if f else (packs, weights), blocks, dp)
        if f == 1:
            made, own_ahead[-2:], own_behind[-3:] = together(made, own_ahead[-2:], own_behind[-3:])
        elif f:
            made = together(*made)
        else:
            made, arrived = together(made, [x[:3] for x in crossing])
        pack, weight, keep, other, back = made[0], made[1], made[2:4], made[4:6], made[6:]
        packs.append(pack)
        weights.append(weight)
        if f:
            crossing.append([cross(x, f) for x in (*other, keep[0])] + [keep[1]])
    back_far = swap(back[1], "group", group, 1)
    coming = []
    for c in range(2):
        send = other[c]
        for x in arrived:
            send = send + x[c].astype(F32)
        send = send.astype(BF16)
        if c == 0:
            send, last_keeps = together(send, [x[3] for x in crossing])
        coming.append(swap(send, "dp", dp, 1))
    last_keeps = [cross(x, f) for f, x in zip(fars, last_keeps)]
    stem_made, coming[0], last_keeps = together(
        tail_call(core, back[0], back_far, emb, both[0], cols, gain), coming[0], last_keeps
    )
    stem_keep, *stem_recv = stem_made
    stem_recv = [swap(x, "group", group, 1) for x in stem_recv]
    kinds = [F32 if j < 2 else BF16 for j in range(dp // 2)]
    second_leg = lambda c: combine_call(high, [[x] for x in keeps[c] + [coming[c]]], kinds)
    spread = lambda blocks, js: [swap(blocks[j], "dp", dp, 2 * j) for j in js]
    stem_recv = together(*stem_recv)
    keeps = [[keep[0]] + [x[2] for x in arrived], [keep[1]] + list(last_keeps)]
    stem_parts = halve_stem(stem_recv, stem_keep, group)
    _, coming[0], keeps = together(stem_parts, coming[0], keeps)
    first = second_leg(0)
    first_rest = spread(first, rests[1:])
    second = second_leg(1)
    near = dp // 2 * 3 // 4
    beside = [mixed_call(packs, weights), first[0], *first_rest, second[0]]
    def after_first(mixed, *arrived):
        output = output_call(counts, swap(mixed, "group", group, 1), emb, packs, weights)
        return [output, *arrived[:-1], *spread(first, [1]), arrived[-1]]

    def after_second(*arrived):
        return [*arrived, *spread(second, [1, *range(2, near)]), second[near:]]

    def last(*arrived):
        blocks = dict(enumerate(arrived[-1], near))
        return [*arrived[:-1], *spread(blocks, blocks)]

    grad_w_stem, (output, *arrived) = sum_stem(
        stem_parts, beside, (after_first, after_second), last, dp, group
    )
    half = len(arrived) // 2
    grad_w_qkv, grad_w_out = result_call(arrived[:half], arrived[half:])
    return (output.reshape(scenes, GROUPS, CAP, D), grad_w_stem, grad_w_qkv, grad_w_out)


def solution(mesh):
    sizes = dict(mesh.shape)
    return jax.shard_map(
        functools.partial(on_device, sizes["dp"], sizes["group"]),
        mesh=mesh,
        in_specs=(
            P(("dp", "group"), None, None),
            P(("dp", "group"), None, None),
            P(("dp", "group"), None),
            P(),
            P(),
            P("dp", None, "group"),
            P("group", "dp"),
            P(("dp", "group"), None, None, None),
        ),
        out_specs=(
            P(("dp", "group"), None, None, None),
            P(),
            P("dp", None, "group"),
            P("group", "dp"),
        ),
        check_vma=False,
    )
```

```python
import functools

import jax
import jax.numpy as jnp
import ml_dtypes
import numpy as np
from jax import lax
from jax.experimental import pallas as pl
from jax.experimental.pallas import tpu as pltpu
from jax.sharding import PartitionSpec as P

D = 1024
HD = 64
GROUPS = 3
CAP = 48
GRID = 12
PIX = 64
TOK = GROUPS * CAP
PAIR = 128
GROUP_BANDS = ((0, 4), (4, 8), (8, 10))
NORM_EPS = 1e-06
F32 = jnp.float32
BF16 = jnp.bfloat16
VMEM_LIMIT = 60 * 1024 * 1024
SMALL_LIMIT = 16 * 1024 * 1024


def dot_nn(a, b):
    return lax.dot_general(a, b, (((1,), (0,)), ((), ())), preferred_element_type=F32)


def dot_nt(a, b):
    return lax.dot_general(a, b, (((1,), (1,)), ((), ())), preferred_element_type=F32)


def dot_tn(a, b):
    return lax.dot_general(a, b, (((0,), (0,)), ((), ())), preferred_element_type=F32)


def live_column(c0, c1, c2):
    row = lax.broadcasted_iota(jnp.int32, (TOK, 1), 0)
    return (
        (row < c0)
        | ((row >= CAP) & (row < CAP + c1))
        | ((row >= 2 * CAP) & (row < 2 * CAP + c2))
    )


def params(limit=VMEM_LIMIT):
    return pltpu.CompilerParams(vmem_limit_bytes=limit)


def cost(flops, nbytes):
    return pl.CostEstimate(flops=int(flops / 1000), bytes_accessed=int(nbytes / 1000), transcendentals=0)


def stem_kernel(
    cnt_ref, idx_ref, patch_ref, w_ref, gain_ref, parts, genc_ref, og_ref,
    emb_ref, rows_ref, cols_ref,
):
    step = pl.program_id(0)
    scenes = patch_ref.shape[0]
    patch_iota = lax.broadcasted_iota(jnp.int32, (parts.shape[1], CAP), 0)
    slot = lax.broadcasted_iota(jnp.int32, (CAP, 1), 0)
    for g, (start, end) in enumerate(GROUP_BANDS):
        rows = slice(g * CAP, (g + 1) * CAP)
        width = (end - start) * PIX
        picked, placed = [], []
        for s in range(scenes):
            onehot = (idx_ref[s, g : g + 1, :] == patch_iota).astype(F32).astype(BF16).T
            picked.append(dot_nn(onehot, patch_ref[s, :, start * PIX : end * PIX]).astype(BF16))
            placed.append(
                (dot_nn(onehot, parts[0]) + dot_nn(onehot, parts[1])) + dot_nn(onehot, parts[2])
            )
            live = slot < cnt_ref[g, step * scenes + s]
            rows_ref[1, s, rows, :] = jnp.where(live, og_ref[s, rows, :].astype(F32), 0.0).astype(BF16)
        summed = dot_nn(jnp.concatenate(picked, axis=0), w_ref[start * PIX : end * PIX, :])
        for s in range(scenes):
            values = summed[s * CAP : (s + 1) * CAP] + (placed[s] + genc_ref[g : g + 1, :])
            emb = values.astype(BF16)
            emb_ref[s, rows, :] = emb
            x = emb.astype(F32)
            centre = jnp.mean(x, axis=-1, keepdims=True)
            dev = x - centre
            spread = jnp.mean(dev * dev, axis=-1, keepdims=True)
            centred = dev * lax.rsqrt(spread + NORM_EPS)
            rows_ref[0, s, rows, :] = (centred * gain_ref[...]).astype(BF16)
            cols_ref[s, rows, :width] = picked[s]
            if width < cols_ref.shape[2]:
                cols_ref[s, rows, width:] = jnp.zeros((CAP, cols_ref.shape[2] - width), BF16)


def stem_call(counts, index, patches, w_stem, gain, table, genc, out_grad):
    scenes, patch_count, width = patches.shape
    block = 3 if scenes % 3 == 0 else 1
    col_width = max(e - s for s, e in GROUP_BANDS) * PIX
    per = lambda shape: pl.BlockSpec((block,) + shape, lambda i: (i, 0, 0))
    whole = lambda a: pl.BlockSpec(a.shape, lambda i: (0,) * a.ndim)
    return pl.pallas_call(
        stem_kernel,
        grid=(scenes // block,),
        in_specs=[
            pl.BlockSpec(memory_space=pltpu.SMEM),
            per((GROUPS, CAP)),
            per((patch_count, width)),
            whole(w_stem),
            whole(gain),
            whole(table),
            whole(genc),
            per((TOK, D)),
        ],
        out_specs=[
            per((TOK, D)),
            pl.BlockSpec((2, block, TOK, D), lambda i: (0, i, 0, 0)),
            per((TOK, col_width)),
        ],
        out_shape=[
            jax.ShapeDtypeStruct((scenes, TOK, D), BF16),
            jax.ShapeDtypeStruct((2, scenes, TOK, D), BF16),
            jax.ShapeDtypeStruct((scenes, TOK, col_width), BF16),
        ],
        compiler_params=params(),
        cost_estimate=cost(8e9, 12e6),
        name="stem_norm",
    )(counts, index, patches, w_stem, gain, table, genc, out_grad)


def pack_kernel(qkv_ref, out_w_ref, pack_ref):
    count, _, width = qkv_ref.shape
    for c in range(count):
        pack_ref[:, c * width : (c + 1) * width] = qkv_ref[c]
    pack_ref[:, count * width :] = out_w_ref[...].T


def pack_call(w_qkv, w_out):
    parts = jnp.transpose(w_qkv, (1, 0, 2))
    return pl.pallas_call(
        pack_kernel,
        out_shape=jax.ShapeDtypeStruct((w_qkv.shape[0], 3 * w_qkv.shape[2] + w_out.shape[0]), BF16),
        compiler_params=params(),
        cost_estimate=cost(1e6, 5e5),
        name="pack_weights",
    )(parts, w_out)


def attention_kernel(
    packs, blocks, dp, cnt_ref, owner_ref, low_ref, na_ref, nb_ref, ga_ref, gb_ref, *refs
):
    earlier, refs = refs[: 2 * (packs or 0)], refs[2 * (packs or 0) :]
    blocks, refs = refs[:blocks], refs[blocks:]
    out_ref, w_ref, *refs = refs
    keeps, others, refs = refs[:2], refs[2:4], refs[4:]
    n_all, g_all, pack_all, qkv, total = refs[-5:]
    half, step = pl.program_id(0), pl.program_id(1)
    rows = qkv.shape[0]
    here = pl.ds(pl.multiple_of((half * pl.num_programs(1) + step) * rows, 16), rows)
    scenes = rows // TOK
    width = w_ref.shape[1] // 4

    @pl.when((half == 0) & (step == 0))
    def _():
        size = blocks[0].shape[0]
        for b, block in enumerate(blocks):
            w_ref[pl.ds(pl.multiple_of(owner_ref[b] * size, size), size), :] = block[...]

    @pl.when(half == 0)
    def _():
        n_all[here, :] = na_ref[0]
        g_all[here, :] = ga_ref[0]

    @pl.when(half != 0)
    def _():
        n_all[here, :] = nb_ref[0]
        g_all[here, :] = gb_ref[0]

    qkv[:, : 3 * width] = dot_nn(n_all[here, :], w_ref[:, : 3 * width]).astype(BF16)
    qkv[:, 3 * width :] = dot_nn(g_all[here, :], w_ref[:, 3 * width :]).astype(BF16)
    heads = width // HD
    lane = lax.broadcasted_iota(jnp.int32, (1, width), 1)
    masks = [(lane // HD == h).astype(F32).astype(BF16) for h in range(heads)]
    scale = jnp.asarray(HD ** (-0.5), BF16)
    first_of_pair = lax.broadcasted_iota(jnp.int32, (1, PAIR), 1) < HD

    def own_lanes(tall):
        tiles = []
        for t in range(width // PAIR):
            at = slice(t * PAIR, (t + 1) * PAIR)
            one = tall[2 * t * TOK : (2 * t + 1) * TOK, at]
            two = tall[(2 * t + 1) * TOK : (2 * t + 2) * TOK, at]
            tiles.append(jnp.where(first_of_pair, one, two))
        return jnp.concatenate(tiles, axis=1)

    def scene_body(s, _):
        base = pl.multiple_of(s * TOK, 16)
        at = pl.ds(base, TOK)
        scene = step * scenes + s
        live = live_column(*[cnt_ref[half, g, scene] for g in range(GROUPS)])
        bias = jnp.where(live, 0.0, -1e30)
        q, k, v, dc = [qkv[at, c * width : (c + 1) * width] for c in range(4)]
        tall_q = jnp.concatenate([q * (m * scale) for m in masks], axis=0)
        tall_dc = jnp.concatenate([dc * m for m in masks], axis=0)
        scores = dot_nt(k, tall_q)
        grad_probs = dot_nt(v, tall_dc)
        probs_parts, score_parts = [], []
        for start in range(0, heads * TOK, PAIR):
            cols = slice(start, min(start + PAIR, heads * TOK))
            part = scores[:, cols] + bias
            lifted = jnp.exp(part - jnp.max(part, axis=0, keepdims=True))
            probs = lifted * (1.0 / jnp.sum(lifted, axis=0, keepdims=True))
            weighted = probs * grad_probs[:, cols]
            inner = jnp.sum(weighted, axis=0, keepdims=True)
            probs_parts.append(probs.astype(BF16))
            score_parts.append((weighted - probs * inner).astype(BF16))
        half_probs = jnp.concatenate(probs_parts, axis=1)
        grad_score = jnp.concatenate(score_parts, axis=1)
        out_ref[at, :width] = (own_lanes(dot_tn(grad_score, k)) * HD ** (-0.5)).astype(BF16)
        out_ref[at, width : 2 * width] = dot_nn(grad_score, tall_q).astype(BF16)
        out_ref[at, 2 * width : 3 * width] = dot_nn(half_probs, tall_dc).astype(BF16)
        out_ref[at, 3 * width :] = own_lanes(dot_tn(half_probs, v)).astype(BF16)
        return 0

    lax.fori_loop(0, scenes, scene_body, 0, unroll=True)
    pack_all[here, :] = out_ref[...]

    @pl.when((half == pl.num_programs(0) - 1) & (step == pl.num_programs(1) - 1))
    def _():
        total[:, : 3 * width] = dot_tn(n_all[...], pack_all[:, : 3 * width])
        total[:, 3 * width :] = dot_tn(g_all[...], pack_all[:, 3 * width :])
        size = total.shape[0] // dp
        low = low_ref[0]
        for b in range(dp // 2):
            at = slice(b * size, (b + 1) * size)
            mine = pl.multiple_of((2 * b + low) * size, size)
            other = pl.multiple_of((2 * b + 1 - low) * size, size)
            for c in range(2):
                cols = slice(c * 2 * width, (c + 1) * 2 * width)
                keeps[c][at, :] = total[pl.ds(mine, size), cols].astype(keeps[c].dtype)
                others[c][at, :] = total[pl.ds(other, size), cols].astype(others[c].dtype)

    if packs is not None:
        back = dot_nt(out_ref[:, : 3 * width], w_ref[:, : 3 * width])
        for pack_ref, weight_ref in zip(earlier[:packs], earlier[packs:]):
            back = back + dot_nt(pack_ref[...], weight_ref[...])

        @pl.when(half == 0)
        def _():
            refs[0][...] = back

        @pl.when(half != 0)
        def _():
            refs[1][...] = back.astype(BF16)


def block_rows(tokens):
    return 3 * TOK if tokens % (3 * TOK) == 0 else TOK


def two_halves(rows, steps, lead):
    shape = (1,) * len(lead) + (rows, D)
    first = pl.BlockSpec(shape, lambda h, i: lead + (jnp.where(h == 0, i, steps - 1), 0))
    second = pl.BlockSpec(shape, lambda h, i: lead + (jnp.where(h == 0, 0, i), 0))
    return [first, second]


SCALARS = pl.BlockSpec(memory_space=pltpu.SMEM)


def attention_call(counts, owners, low, own, far, earlier, blocks, dp):
    tokens = own.shape[1]
    rows = block_rows(tokens)
    steps = tokens // rows
    cols = blocks[0].shape[1]
    whole = lambda shape: pl.BlockSpec(shape, lambda h, i: (0, 0), pipeline_mode=pl.Buffered(1))
    at = lambda h, i: (h * steps + i, 0)
    packs = None if earlier is None else len(earlier[0])
    back = [] if earlier is None else two_halves(rows, steps, ())
    kind = BF16 if earlier is None else F32
    grads = [jax.ShapeDtypeStruct((D // 2, c), kind) for c in [cols // 2] * 4]
    return pl.pallas_call(
        functools.partial(attention_kernel, packs, len(blocks), dp),
        grid=(2, steps),
        in_specs=[SCALARS] * 3
        + two_halves(rows, steps, (0,))
        + two_halves(rows, steps, (1,))
        + [pl.BlockSpec((rows, cols // 4 * 3), at)] * (packs or 0)
        + [whole((D, cols // 4 * 3))] * (packs or 0)
        + [whole(b.shape) for b in blocks],
        out_specs=[pl.BlockSpec((rows, cols), at), whole((D, cols))] + [whole(g.shape) for g in grads] + back,
        out_shape=[
            jax.ShapeDtypeStruct((2 * tokens, cols), BF16),
            jax.ShapeDtypeStruct((D, cols), BF16),
            *grads,
        ]
        + [jax.ShapeDtypeStruct((tokens, D), kind) for kind in (F32, BF16)[: len(back)]],
        scratch_shapes=[
            pltpu.VMEM((2 * tokens, D), BF16),
            pltpu.VMEM((2 * tokens, D), BF16),
            pltpu.VMEM((2 * tokens, cols), BF16),
            pltpu.VMEM((rows, cols), BF16),
            pltpu.VMEM((D, cols), F32),
        ],
        compiler_params=params(),
        cost_estimate=cost(20e9, 14e6),
        name="attention",
    )(counts, owners, low, own, far, own, far, *[x for group in earlier or () for x in group], *blocks)


def combine_kernel(counts, place_ref, *refs):
    ins, refs = refs[: sum(counts)], refs[sum(counts) :]
    rows = refs[0].shape[0]
    place = place_ref[0]
    for j, ref in enumerate(refs):
        at = pl.ds(pl.multiple_of((place ^ j) * rows, rows), rows)
        total = None
        first = 0
        for count in counts:
            pieces = [r[at, :].astype(F32) for r in ins[first : first + count]]
            new = pieces[0] if count == 1 else jnp.concatenate(pieces, axis=1)
            total = new if total is None else total + new
            first += count
        ref[...] = total.astype(ref.dtype)


def combine_call(place, parts, dtypes):
    ins = [piece for part in parts for piece in part]
    rows, cols = ins[0].shape[0] // len(dtypes), sum(piece.shape[1] for piece in parts[0])
    whole = lambda a: pl.BlockSpec(a.shape, lambda: (0, 0))
    return pl.pallas_call(
        functools.partial(combine_kernel, [len(part) for part in parts]),
        in_specs=[SCALARS] + [whole(a) for a in ins],
        out_specs=[pl.BlockSpec((rows, cols), lambda: (0, 0))] * len(dtypes),
        out_shape=[jax.ShapeDtypeStruct((rows, cols), d) for d in dtypes],
        compiler_params=params(SMALL_LIMIT),
        cost_estimate=cost(1e6, 5e6),
        name="combine",
    )(place, *ins)


def split_kernel(count, place_ref, *refs):
    total = refs[0][...]
    for ref in refs[1:count]:
        total = total + ref[...]
    outs = refs[count:]
    cols = outs[0].shape[1]
    place = place_ref[0]
    for j, out_ref in enumerate(outs):
        block = total[:, :cols]
        for b in range(1, len(outs)):
            block = jnp.where((place ^ j) == b, total[:, b * cols : (b + 1) * cols], block)
        out_ref[...] = block


def split_call(place, parts, blocks):
    rows, cols = parts[0].shape
    return pl.pallas_call(
        functools.partial(split_kernel, len(parts)),
        in_specs=[SCALARS] + [pl.BlockSpec((rows, cols), lambda: (0, 0))] * len(parts),
        out_specs=[pl.BlockSpec((rows, cols // blocks), lambda: (0, 0))] * blocks,
        out_shape=[jax.ShapeDtypeStruct((rows, cols // blocks), F32)] * blocks,
        compiler_params=params(SMALL_LIMIT),
        cost_estimate=cost(1e6, 2e6),
        name="split_sum",
    )(place, *parts)


def result_kernel(count, *refs):
    halves, qkv_ref, out_ref = (refs[:count], refs[count:-2]), refs[-2], refs[-1]
    first, second = [functools.reduce(lambda a, b: a + b, [r[...].astype(F32) for r in half]) for half in halves]
    width = first.shape[1] // 2
    qkv_ref[0] = first[:, :width]
    qkv_ref[1] = first[:, width:]
    qkv_ref[2] = second[:, :width]
    out_ref[...] = second[:, width:].T


def result_call(first, second):
    rows, cols = first[0].shape
    qkv, out = pl.pallas_call(
        functools.partial(result_kernel, len(first)),
        out_shape=[
            jax.ShapeDtypeStruct((3, rows, cols // 2), F32),
            jax.ShapeDtypeStruct((cols // 2, rows), F32),
        ],
        compiler_params=params(SMALL_LIMIT),
        cost_estimate=cost(1e6, 2e6),
        name="weight_results",
    )(*first, *second)
    return jnp.transpose(qkv, (1, 0, 2)), out


def mixed_product(context_refs, weight_refs):
    total = None
    for context_ref, w_ref in zip(context_refs, weight_refs):
        new = dot_nt(context_ref[...], w_ref[...])
        total = new if total is None else total + new
    return total


def context_specs(rows, packs, weights, first):
    width = packs[0].shape[1] // 4
    return [pl.BlockSpec((rows, width), lambda i: (first + i, 3))] * len(packs) + [
        pl.BlockSpec((D, width), lambda i: (0, 3))
    ] * len(weights)


def mixed_kernel(count, *refs):
    refs[-1][...] = mixed_product(refs[:count], refs[count : 2 * count]).astype(BF16)


def mixed_call(packs, weights):
    tokens = packs[0].shape[0] // 2
    rows = block_rows(tokens)
    return pl.pallas_call(
        functools.partial(mixed_kernel, len(packs)),
        grid=(tokens // rows,),
        in_specs=context_specs(rows, packs, weights, tokens // rows),
        out_specs=pl.BlockSpec((rows, D), lambda i: (i, 0)),
        out_shape=jax.ShapeDtypeStruct((tokens, D), BF16),
        compiler_params=params(),
        cost_estimate=cost(2e9, 5e6),
        name="mixed",
    )(*packs, *weights)


def tail_kernel(core_ref, own_ref, recv_ref, emb_ref, gl_ref, cols_ref, gain_ref, keep_ref, first_ref, second_ref, acc):
    step = pl.program_id(0)
    rows = emb_ref.shape[0]
    scenes = rows // TOK

    @pl.when(step == 0)
    def _():
        acc[...] = jnp.zeros_like(acc)

    grad_normed = own_ref[...] + recv_ref[...].astype(F32)
    x = emb_ref[...].astype(F32)
    dev = x - jnp.mean(x, axis=-1, keepdims=True)
    inv_std = lax.rsqrt(jnp.mean(dev * dev, axis=-1, keepdims=True) + NORM_EPS)
    centred = dev * inv_std
    scaled = grad_normed * gain_ref[...]
    first_mean = jnp.mean(scaled, axis=-1, keepdims=True)
    second_mean = jnp.mean(scaled * centred, axis=-1, keepdims=True)
    back = inv_std * (scaled - first_mean - centred * second_mean)
    grad_in = (gl_ref[0].astype(F32) + back).astype(BF16)
    for g, (start, end) in enumerate(GROUP_BANDS):
        at = [slice(s * TOK + g * CAP, s * TOK + (g + 1) * CAP) for s in range(scenes)]
        columns = jnp.concatenate([cols_ref[a, : (end - start) * PIX] for a in at], axis=0)
        grads = jnp.concatenate([grad_in[a] for a in at], axis=0)
        acc[start * PIX : end * PIX, :] += dot_tn(columns, grads)

    @pl.when(step == pl.num_programs(0) - 1)
    def _():
        size = keep_ref.shape[0]
        core = core_ref[0]
        keep_ref[...] = acc[pl.ds(pl.multiple_of(core * size, size), size), :]
        other = pl.ds(pl.multiple_of((1 - core) * size, size), size)
        first_ref[...] = acc[other, : D // 2]
        second_ref[...] = acc[other, D // 2 :]


def tail_call(core, own, recv, emb, rows_own, cols, gain):
    tokens = emb.shape[0]
    rows = 2 * TOK if tokens % (2 * TOK) == 0 else TOK
    per = lambda a: pl.BlockSpec((rows, a.shape[1]), lambda i: (i, 0))
    stem_rows = GROUP_BANDS[-1][1] * PIX
    keep = jax.ShapeDtypeStruct((stem_rows // 2, D), F32)
    send = jax.ShapeDtypeStruct((stem_rows // 2, D // 2), F32)
    return pl.pallas_call(
        tail_kernel,
        grid=(tokens // rows,),
        in_specs=[SCALARS, per(own), per(recv), per(emb), pl.BlockSpec((1, rows, D), lambda i: (1, i, 0)), per(cols)]
        + [pl.BlockSpec(gain.shape, lambda i: (0, 0))],
        out_specs=[pl.BlockSpec(a.shape, lambda i: (0, 0)) for a in (keep, send, send)],
        out_shape=[keep, send, send],
        scratch_shapes=[pltpu.VMEM((stem_rows, D), F32)],
        compiler_params=params(),
        cost_estimate=cost(10e9, 12e6),
        name="tail",
    )(core, own, recv, emb, rows_own, cols, gain)


def output_kernel(count, cnt_ref, recv_ref, emb_ref, *refs):
    out_ref = refs[-1]
    step = pl.program_id(0)
    scenes = emb_ref.shape[0] // TOK
    mixed = recv_ref[...].astype(F32) + mixed_product(refs[:count], refs[count : 2 * count])
    total = emb_ref[...].astype(F32) + mixed
    for s in range(scenes):
        scene = step * scenes + s
        live = live_column(*[cnt_ref[g, scene] for g in range(GROUPS)])
        at = slice(s * TOK, (s + 1) * TOK)
        out_ref[at, :] = jnp.where(live, total[at], 0.0).astype(BF16)


def output_call(counts, recv, emb, packs, weights):
    tokens = emb.shape[0]
    rows = 2 * TOK if tokens % (2 * TOK) == 0 else TOK
    per = lambda a: pl.BlockSpec((rows, a.shape[1]), lambda i: (i, 0))
    return pl.pallas_call(
        functools.partial(output_kernel, len(packs)),
        grid=(tokens // rows,),
        in_specs=[SCALARS, per(recv), per(emb)]
        + context_specs(rows, packs, weights, 0),
        out_specs=per(emb),
        out_shape=jax.ShapeDtypeStruct(emb.shape, BF16),
        compiler_params=params(),
        cost_estimate=cost(5e9, 10e6),
        name="layer_output",
    )(counts, recv, emb, *packs, *weights)


def swap(x, axis, size, bit):
    return lax.ppermute(x, axis, [(i, i ^ bit) for i in range(size)])


def together(*values):
    return lax.optimization_barrier(values)


class Ring:
    def __init__(self, x, axis, size):
        self.axis, self.size = axis, size
        order = list(range(0, size, 2)) + list(range(size - 1, 0, -2))
        self.forward = [(order[i], order[(i + 1) % size]) for i in range(size)]
        self.backward = [(order[(i + 1) % size], order[i]) for i in range(size)]
        self.ahead, self.behind = [x], [x]

    def send(self):
        moved = [lax.ppermute(self.ahead[-1], self.axis, self.forward)]
        if len(self.behind) <= (self.size - 1) // 2:
            moved.append(lax.ppermute(self.behind[-1], self.axis, self.backward))
        return moved

    def receive(self, moved):
        self.ahead.append(moved[0])
        self.behind.extend(moved[1:])

    @property
    def steps(self):
        return len(self.ahead) - 1

    def owners(self, ahead, behind):
        size = self.size
        me = lax.axis_index(self.axis)
        here = jnp.where(me % 2 == 0, me // 2, size - 1 - me // 2)
        distances = [-s for s in range(ahead)] + list(range(1, behind))
        at = (here + size + jnp.array(distances, jnp.int32)) % size
        return jnp.where(at < size // 2, 2 * at, 2 * (size - 1 - at) + 1)


def step_all(rings, *beside):
    moved, beside = together([ring.send() for ring in rings], beside)
    for ring, blocks in zip(rings, moved):
        ring.receive(blocks)
    return beside


def halve_stem(recv, keep, group):
    mine = lax.axis_index("group") // 2 * 2 + lax.axis_index("dp") % 2
    return combine_call(mine.reshape(1), [[keep], recv], [F32] * (group // 2 * 2))


def sum_stem(parts, beside, after, last, dp, group):
    core = lax.axis_index("group") % 2
    far = lax.axis_index("group") // 2
    low = lax.axis_index("dp") % 2
    high = lax.axis_index("dp") // 2
    fars, highs = group // 2, dp // 2
    mine = far * 2 + low
    small, width = parts[0].shape
    rows = 2 * fars * small

    def hop(block, f, b):
        if f:
            pairs = [
                (d * group + g, (d ^ b) * group + (g ^ (2 * f))) for d in range(dp) for g in range(group)
            ]
            return lax.ppermute(block, ("dp", "group"), pairs)
        return swap(block, "dp", dp, b)

    hops = [(k // 2, k % 2) for k in range(1, 2 * fars)]
    arrived = [hop(part, f, b) for part, (f, b) in zip(parts[1:], hops)]
    arrived, beside = together(arrived, beside)
    beside = after[0](*beside)
    cols = width // highs
    part, *away = split_call(high.reshape(1), [parts[0], *arrived], highs)
    arrived = [swap(a, "dp", dp, 2 * (j + 1)) for j, a in enumerate(away)]
    arrived, beside = together(arrived, beside)
    for block in arrived:
        part = part + block
    part = part.astype(BF16)
    line = jnp.zeros((small, width), BF16)
    line = lax.dynamic_update_slice_in_dim(line, part, high * cols, 1)
    arrived = [swap(part, "dp", dp, 2 * j) for j in range(1, highs)]
    arrived, beside = together(arrived, after[1](*beside))
    for j, block in enumerate(arrived):
        line = lax.dynamic_update_slice_in_dim(line, block, (high ^ (j + 1)) * cols, 1)
    block = jnp.zeros((rows, width), BF16)
    block = lax.dynamic_update_slice_in_dim(block, line, mine * small, 0)
    arrived, beside = together([hop(line, f, b) for f, b in hops], last(*beside))
    for (f, b), piece in zip(hops, arrived):
        target = (far ^ f) * 2 + (low ^ b)
        block = lax.dynamic_update_slice_in_dim(block, piece, target * small, 0)
    partner = swap(block, "group", group, 1)
    whole = jnp.zeros((2 * rows, width), F32)
    whole = lax.dynamic_update_slice_in_dim(whole, block.astype(F32), core * rows, 0)
    whole = lax.dynamic_update_slice_in_dim(whole, partner.astype(F32), (1 - core) * rows, 0)
    return whole, beside


def encoding_tables(patch_count):
    quarter = D // 4
    half_width = D // 2
    power = lambda n: np.power(np.float32(10000.0), -np.arange(n, dtype=np.float32) / np.float32(n))
    at = np.arange(GRID).astype(np.float32)[:, None] * power(quarter)
    both = np.concatenate([np.sin(at), np.cos(at)], axis=-1)
    patch = np.arange(patch_count)
    rest = np.concatenate([both[patch // GRID], both[patch % GRID]], axis=-1).astype(np.float32)
    parts = []
    for _ in range(3):
        parts.append(rest.astype(ml_dtypes.bfloat16))
        rest = rest - parts[-1].astype(np.float32)
    group_at = np.arange(GROUPS).astype(np.float32)[:, None] * power(half_width)
    return np.stack(parts), np.concatenate([np.sin(group_at), np.cos(group_at)], axis=-1).astype(np.float32)


def on_device(dp, group, patches, vis_index, vis_count, w_stem, ln_gain, w_qkv, w_out, out_grad):
    scenes = patches.shape[0]
    tokens = scenes * TOK
    width = w_qkv.shape[2]
    fars = range(1, group // 2)
    rests = range(1, dp // 2)
    dp_low, dp_high = lax.axis_index("dp") % 2, lax.axis_index("dp") // 2
    low, high = dp_low.reshape(1), dp_high.reshape(1)
    core = (lax.axis_index("group") % 2).reshape(1)

    shard = pack_call(w_qkv, w_out)
    cross = lambda x, f: swap(x, "group", group, 2 * f)
    far_shards = [cross(shard, f) for f in fars]
    counts = vis_count.astype(jnp.int32).T
    counts_far = swap(counts, "group", group, 1)
    table, genc = encoding_tables(patches.shape[1])
    gain = ln_gain.reshape(1, D)
    stem = stem_call(
        counts,
        vis_index,
        patches,
        w_stem,
        gain,
        jnp.asarray(table),
        jnp.asarray(genc),
        out_grad.reshape(scenes, TOK, D),
    )
    stem, counts_far, far_shards = together(stem, counts_far, far_shards)
    rings = [Ring(x, "dp", dp) for x in far_shards]
    ring = rings[0]
    owners = ring.owners(dp // 2 + 1, dp // 2)
    emb = stem[0].reshape(tokens, D)
    both = [stem[1].reshape(2, tokens, D)]
    cols = stem[2].reshape(tokens, stem[2].shape[2])
    both.append(swap(both[0], "group", group, 1))
    own_ahead, own_behind = [], []
    both, owners, both_counts = step_all(rings, both, owners, jnp.stack([counts, counts_far]))
    while ring.steps < dp // 2:
        a, b = len(own_ahead), len(own_behind)
        own_ahead.append(cross(ring.ahead[-1], 1))
        if a:
            own_behind.append(cross(ring.behind[a], 1))
        ahead, behind = slice(max(a - 1, 0), a), slice(max(b - 2, 0), max(b - 1, 0))
        own_ahead[ahead], own_behind[behind] = step_all(rings, own_ahead[ahead], own_behind[behind])
    ring.ahead, ring.behind = together(ring.ahead, ring.behind)
    own_ahead.append(cross(ring.ahead[-1], 1))
    own_behind.extend(cross(x, 1) for x in ring.behind[len(own_behind) + 1 :])

    packs, weights, crossing = [], [], []
    for f in list(fars) + [0]:
        if f:
            blocks = rings[f - 1].ahead + rings[f - 1].behind[1:]
        else:
            blocks = [shard] + own_ahead + own_behind
        made = attention_call(both_counts, owners, low, *both, None if f else (packs, weights), blocks, dp)
        if f == 1:
            made, own_ahead[-2:], own_behind[-3:] = together(made, own_ahead[-2:], own_behind[-3:])
        elif f:
            made = together(*made)
        else:
            made, arrived = together(made, [x[:3] for x in crossing])
        pack, weight, keep, other, back = made[0], made[1], made[2:4], made[4:6], made[6:]
        packs.append(pack)
        weights.append(weight)
        if f:
            crossing.append([cross(x, f) for x in (*other, keep[0])] + [keep[1]])
    back_far = swap(back[1], "group", group, 1)
    coming = []
    for c in range(2):
        send = other[c]
        for x in arrived:
            send = send + x[c].astype(F32)
        send = send.astype(BF16)
        if c == 0:
            send, last_keeps = together(send, [x[3] for x in crossing])
        coming.append(swap(send, "dp", dp, 1))
    last_keeps = [cross(x, f) for f, x in zip(fars, last_keeps)]
    stem_made, coming[0], last_keeps = together(
        tail_call(core, back[0], back_far, emb, both[0], cols, gain), coming[0], last_keeps
    )
    stem_keep, *stem_recv = stem_made
    stem_recv = [swap(x, "group", group, 1) for x in stem_recv]
    kinds = [F32 if j < 2 else BF16 for j in range(dp // 2)]
    second_leg = lambda c: combine_call(high, [[x] for x in keeps[c] + [coming[c]]], kinds)
    spread = lambda blocks, js: [swap(blocks[j], "dp", dp, 2 * j) for j in js]
    stem_recv = together(*stem_recv)
    keeps = [[keep[0]] + [x[2] for x in arrived], [keep[1]] + list(last_keeps)]
    stem_parts = halve_stem(stem_recv, stem_keep, group)
    _, coming[0], keeps = together(stem_parts, coming[0], keeps)
    first = second_leg(0)
    first_rest = spread(first, rests[1:])
    mixed, coming[1], first_rest[0] = together(mixed_call(packs, weights), coming[1], first_rest[0])
    second = second_leg(1)
    near = dp // 2 * 3 // 4
    beside = [mixed, first[0], first_rest[0], second[0]]
    def after_first(mixed, *arrived):
        output = output_call(counts, swap(mixed, "group", group, 1), emb, packs, weights)
        return [output, *arrived[:-1], *first_rest[1:], *spread(first, [1]), arrived[-1]]

    def after_second(*arrived):
        return [*arrived, *spread(second, [1, *range(2, near)]), second[near:]]

    def last(*arrived):
        blocks = dict(enumerate(arrived[-1], near))
        return [*arrived[:-1], *spread(blocks, blocks)]

    grad_w_stem, (output, *arrived) = sum_stem(
        stem_parts, beside, (after_first, after_second), last, dp, group
    )
    half = len(arrived) // 2
    grad_w_qkv, grad_w_out = result_call(arrived[:half], arrived[half:])
    return (output.reshape(scenes, GROUPS, CAP, D), grad_w_stem, grad_w_qkv, grad_w_out)


def solution(mesh):
    sizes = dict(mesh.shape)
    return jax.shard_map(
        functools.partial(on_device, sizes["dp"], sizes["group"]),
        mesh=mesh,
        in_specs=(
            P(("dp", "group"), None, None),
            P(("dp", "group"), None, None),
            P(("dp", "group"), None),
            P(),
            P(),
            P("dp", None, "group"),
            P("group", "dp"),
            P(("dp", "group"), None, None, None),
        ),
        out_specs=(
            P(("dp", "group"), None, None, None),
            P(),
            P("dp", None, "group"),
            P("group", "dp"),
        ),
        check_vma=False,
    )
```
